32 devices in a mesh: section: 2 (over x), dp: 16 (over z, y, core).
Axes of the slice: x: 2, y: 2, z: 4, core: 2. Of those that a mesh axis runs over, the one named last changes fastest.
Arguments:
- boundary: bfloat16 [2, 32, 1024, 512], P('section', 'dp'), may hold values from -6 to 6
- segments: int32 [32, 1024], P('dp'), may hold values from 0 to 3, never falling along the last dimension, each value on 1 to 512 neighbouring positions
- code_index: int32 [32, 1024], P('dp'), may hold values from 0 to 8191
- attention_in: bfloat16 [2, 512, 1536], P('section'), may hold values from -0.25 to 0.25
- attention_out: bfloat16 [2, 512, 512], P('section'), may hold values from -2 to 2
- hidden_in: bfloat16 [2, 512, 2048], P('section'), may hold values from -0.25 to 0.25
- hidden_out: bfloat16 [2, 2048, 512], P('section'), may hold values from -0.125 to 0.125
- block_gains: float32 [2, 2, 512], P('section'), may hold values from 0.5 to 1.5
- block_biases: float32 [2, 6, 512], P('section'), may hold values from -2.5 to 2.5
- hidden_bias: float32 [2, 2048], P('section'), may hold values from -2.5 to 2.5
- output_gain: float32 [512], replicated, may hold values from 0.5 to 1.5
- head_bias: float32 [2, 512], replicated, may hold values from -2.5 to 2.5
- down_weight: float32 [512, 32], replicated, may hold values from -0.25 to 0.25
- down_bias: float32 [32], replicated, may hold values from -2.5 to 2.5
- up_weight: float32 [32, 512], replicated, may hold values from -3 to 3
- codebook: float32 [8192, 32], replicated, may hold values from -6 to 6
Outputs:
- edge_result: float32 [2, 32, 1024, 512], P('section', 'dp')
- attention_in_grad: float32 [2, 512, 1536], P('section')
- attention_out_grad: float32 [2, 512, 512], P('section')
- hidden_in_grad: float32 [2, 512, 2048], P('section')
- hidden_out_grad: float32 [2, 2048, 512], P('section')
- gains_grad: float32 [2, 2, 512], P('section')
- biases_grad: float32 [2, 6, 512], P('section')
- hidden_bias_grad: float32 [2, 2048], P('section')
- output_gain_grad: float32 [512], replicated
- head_bias_grad: float32 [2, 512], replicated
- down_weight_grad: float32 [512, 32], replicated
- down_bias_grad: float32 [32], replicated
- up_weight_grad: float32 [32, 512], replicated
- codebook_grad: float32 [8192, 32], replicated
The draws below stay inside these ranges and needn't reach their ends.
Inputs may be any that keep to these rules, and one draw needn't show every extreme that they name: `segments`: within each packed row segment numbers never fall; each segment has 1 to 512 tokens, and one has exactly 512.
All inputs are finite; a program needn't handle non-finite values.
Results may differ from the reference program's by a relative error of at most 0.012.
Values sent between devices are 32-bit elements; how exact they have to be, the bound alone decides.
A program may use at most 320 MiB of HBM per device.

```python
import math
import jax
import jax.numpy as jnp
import numpy as np
from jax import lax

D = 512
HEADS = 8
HEAD = 64
FF = 2048
LATENT = 32
CODES = 8192
SEQ = 1024
ROWS = 32


def touch_ends(drawn, stream_key, least, top_value):
    longest = drawn.shape.index(max(drawn.shape))
    spots = []
    for shift in (0, 1):
        where = [jax.random.randint(jax.random.fold_in(stream_key, axis), (), 0, length) for axis, length in enumerate(drawn.shape)]
        where[longest] = (where[longest] + shift) % drawn.shape[longest]
        spots.append(tuple(where))
    return drawn.at[spots[0]].set(least).at[spots[1]].set(top_value)


def block_scale(rng, dims, cuts, smallest, high):
    level, own = 1.0, jax.random.fold_in(rng, 6)
    for axis_at, blocks in cuts:
        steps = jnp.exp(jax.random.uniform(jax.random.fold_in(own, axis_at), (blocks,), jnp.float32, smallest / len(cuts), high / len(cuts)))
        level = level * jnp.repeat(steps, dims[axis_at] // blocks).reshape([-1 if axis == axis_at else 1 for axis in range(len(dims))])
    return level


def length_profile(amount, total, bound, skew):
    loads = [(1 << 20) // math.isqrt(grade ** skew) + 1 for grade in range(2, amount + 1)]
    surplus, given = total - bound - (amount - 1), [1] * (amount - 1)
    while surplus > 0:
        candidates = [i for i in range(amount - 1) if given[i] < bound]
        mass, budget = sum([loads[i] for i in candidates]), surplus
        for i in candidates:
            more = min(bound - given[i], max(1, budget * loads[i] // mass), surplus)
            given[i] = given[i] + more
            surplus = surplus - more
    return np.array([bound] + given)


def uneven(own_key, count, total, reach, lean):
    if count == 2:
        one = jax.random.randint(own_key, (), max(1, total - reach), min(reach, total - 1) + 1)
        return jnp.stack([one, total - one])
    lengths = jnp.asarray(length_profile(count, total, reach, lean), jnp.int32)
    twos = (count - 1) // 2
    donor, sink = lengths[1:1 + 2 * twos:2], lengths[2:2 + 2 * twos:2]
    margin = jnp.minimum(donor - 1, reach - sink)
    moved = jax.random.randint(jax.random.fold_in(own_key, 1), (twos,), 0, 1 << 20) % (margin + 1)
    lengths = lengths.at[1:1 + 2 * twos:2].set(donor - moved).at[2:2 + 2 * twos:2].set(sink + moved)
    return lengths[jax.random.permutation(jax.random.fold_in(own_key, 2), count)]


def normal_values(rng, shape, scale, limit, cuts=(), kind=jnp.bfloat16):
    level = block_scale(rng, shape, cuts, -0.22, 0.18) if cuts else 1.0
    values = jax.random.normal(rng, shape, jnp.float32) * scale * level
    return jnp.minimum(jnp.maximum(values, -limit), limit).astype(kind)


def setup_inputs(seed: int = 0) -> dict:
    arg_keys = jax.random.split(jax.random.key(seed), 17)
    boundary = normal_values(arg_keys[0], (2, ROWS, SEQ, D), 1.0, 6.0, ((0, 2), (1, 16)))
    segments = jax.vmap(lambda own: jnp.searchsorted(jnp.cumsum(uneven(own, max(3, SEQ // 256), SEQ, SEQ // 2, 0)), jnp.arange(SEQ), side="right"))(jax.random.split(arg_keys[1], ROWS)).reshape((ROWS, SEQ)).astype(jnp.int32)
    code_index = touch_ends(jax.random.randint(arg_keys[2], (ROWS, SEQ), 0, CODES), jax.random.fold_in(arg_keys[2], 1), 0, CODES - 1).astype(jnp.int32)
    attention_in = normal_values(arg_keys[3], (2, D, 3 * D), D ** -0.5, 0.25, ((0, 2),))
    attention_out = normal_values(arg_keys[4], (2, D, D), (D // 64) ** -0.5, 2.0, ((0, 2),))
    hidden_in = normal_values(arg_keys[5], (2, D, FF), D ** -0.5, 0.25, ((0, 2),))
    hidden_out = normal_values(arg_keys[6], (2, FF, D), FF ** -0.5, 0.125, ((0, 2),))
    block_gains = jnp.clip(1.0 + 0.1 * jax.random.normal(arg_keys[7], (2, 2, D), jnp.float32), 0.5, 1.5)
    block_biases = normal_values(arg_keys[8], (2, 6, D), 0.3, 2.5, ((0, 2),), jnp.float32)
    hidden_bias = normal_values(arg_keys[9], (2, FF), 0.3, 2.5, ((0, 2),), jnp.float32)
    output_gain = jnp.clip(1.0 + 0.1 * jax.random.normal(arg_keys[10], (D,), jnp.float32), 0.5, 1.5)
    head_bias = normal_values(arg_keys[11], (2, D), 0.3, 2.5, (), jnp.float32)
    down_weight = normal_values(arg_keys[12], (D, LATENT), D ** -0.5, 0.25, (), jnp.float32)
    down_bias = normal_values(arg_keys[13], (LATENT,), 0.3, 2.5, (), jnp.float32)
    up_weight = normal_values(arg_keys[14], (LATENT, D), (LATENT // 8) ** -0.5, 3.0, (), jnp.float32)
    codebook = normal_values(arg_keys[15], (CODES, LATENT), 1.0, 6.0, (), jnp.float32)
    return dict(boundary=boundary, segments=segments, code_index=code_index, attention_in=attention_in, attention_out=attention_out, hidden_in=hidden_in, hidden_out=hidden_out, block_gains=block_gains, block_biases=block_biases, hidden_bias=hidden_bias, output_gain=output_gain, head_bias=head_bias, down_weight=down_weight, down_bias=down_bias, up_weight=up_weight, codebook=codebook)


highest = lax.Precision.HIGHEST
norm_eps = 1e-06
masked_score = -1e+30
commit_weight = 0.25
gelu_coef = 0.7978845608028654

@jax.custom_vjp
def low(v):
    return lax.optimization_barrier(v.astype(jnp.bfloat16)).astype(jnp.float32)

@jax.custom_vjp
def low_back(v):
    return v

def low_keep(v):
    return (low(v), None)

def low_pass(kept, grad):
    return (grad,)

def back_keep(v):
    return (v, None)

def back_low(kept, grad):
    return (low(grad),)
low.defvjp(low_keep, low_pass)
low_back.defvjp(back_keep, back_low)

def layer_norm(values, gain, offset):
    center = values - lax.optimization_barrier(jnp.mean(values, -1, keepdims=True))
    spread = lax.optimization_barrier(jnp.mean(center * center, -1, keepdims=True))
    return center * lax.rsqrt(spread + norm_eps) * gain + offset

def gelu_tanh(values):
    return 0.5 * values * (1.0 + jnp.tanh(gelu_coef * (values + 0.044715 * values * values * values)))

def unit_rows(values):
    return values * lax.rsqrt(lax.optimization_barrier(jnp.sum(values * values, -1, keepdims=True)) + norm_eps)

def encode_tail(hidden, gain, offset, weight, bias):
    normed = layer_norm(hidden, gain, offset)
    latent = jnp.matmul(normed, weight, precision=highest) + bias
    return unit_rows(latent)

def residual_block(values, segment, params):
    attention_in, attention_out, hidden_in, hidden_out, gains, biases, hidden_bias = params
    model_width = attention_out.shape[0]
    groups, length = (values.shape[0], values.shape[1])
    normed_first = low(layer_norm(values, gains[0], biases[3]))
    projected = jnp.einsum('gsd,de->gse', normed_first, attention_in, precision=highest)
    query = low_back(low(projected[..., :model_width] + biases[0]))
    key_rows = low_back(low(projected[..., model_width:2 * model_width]))
    value_rows = low_back(low(projected[..., 2 * model_width:] + biases[1]))
    query = query.reshape(groups, length, HEADS, HEAD)
    key_rows = key_rows.reshape(groups, length, HEADS, HEAD)
    value_rows = value_rows.reshape(groups, length, HEADS, HEAD)
    scores = jnp.einsum('gqhe,gkhe->ghqk', query, key_rows, precision=highest) * HEAD ** (-0.5)
    same = (segment[:, :, None] == segment[:, None, :])[:, None]
    scores = low_back(jnp.where(same, scores, masked_score))
    row_max = lax.optimization_barrier(jnp.max(scores, -1, keepdims=True))
    raised = jnp.exp(scores - row_max)
    attention = low(raised / lax.optimization_barrier(jnp.sum(raised, -1, keepdims=True)))
    context = jnp.einsum('ghqk,gkhe->gqhe', attention, value_rows, precision=highest)
    context = low_back(low(context.reshape(groups, length, model_width)))
    midway = values + low_back(jnp.einsum('gsd,de->gse', context, attention_out, precision=highest) + biases[2])
    normed_second = low(layer_norm(midway, gains[1], biases[4]))
    preact = low_back(jnp.einsum('gsd,df->gsf', normed_second, hidden_in, precision=highest) + hidden_bias)
    activated = low(gelu_tanh(preact))
    return midway + low_back(jnp.einsum('gsf,fd->gsd', activated, hidden_out, precision=highest) + biases[5])

def section_params(params, which):
    return tuple((params[number][which] for number in range(7)))

def encode(params, values, segment):
    hidden = residual_block(values, segment, section_params(params, 0))
    return encode_tail(hidden, params[7], params[8][0], params[9], params[10])

def reference(boundary, segments, code_index, attention_in, attention_out, hidden_in, hidden_out, block_gains, block_biases, hidden_bias, output_gain, head_bias, down_weight, down_bias, up_weight, codebook):
    group = math.gcd(ROWS, max(1, 4096 // SEQ))
    turns = ROWS // group

    def grouped(array):
        return array.reshape((turns, group) + array.shape[1:])
    edges = boundary.astype(jnp.float32)
    inputs = grouped(edges[0])
    cotangent = grouped(edges[1])
    segment_groups = grouped(segments)
    code_groups = grouped(code_index)
    params = (attention_in.astype(jnp.float32), attention_out.astype(jnp.float32), hidden_in.astype(jnp.float32), hidden_out.astype(jnp.float32), block_gains, block_biases, hidden_bias, output_gain, head_bias, down_weight, down_bias, up_weight, codebook)
    fixed_latent = lax.map(lambda pieces: encode(params, pieces[0], pieces[1]), (inputs, segment_groups))
    fixed_code = jnp.take(unit_rows(codebook), code_groups, axis=0)

    def forward(entry, params):
        book = unit_rows(params[12])

        def one_group(running, pieces):
            values, segment, index_rows, latent_fix, code_fix, cotan = pieces
            latent = encode(params, values, segment)
            chosen = jnp.take(book, index_rows, axis=0)
            passed = latent + (code_fix - latent_fix)
            decoder_in = jnp.matmul(passed, params[11], precision=highest) + params[8][1]
            decoded = residual_block(decoder_in, segment, section_params(params, 1))
            book_gap = latent_fix - chosen
            commit_gap = latent - code_fix
            objective = jnp.sum(decoded * cotan) + jnp.sum(book_gap * book_gap) + commit_weight * jnp.sum(commit_gap * commit_gap)
            return (running + objective, decoded)
        total, decoded = lax.scan(jax.checkpoint(one_group), jnp.zeros((), jnp.float32), (entry, segment_groups, code_groups, fixed_latent, fixed_code, cotangent))
        return (total, decoded)
    total, back_fn, decoded = jax.vjp(forward, inputs, params, has_aux=True)
    entry_grad, grads = back_fn(jnp.ones((), jnp.float32))
    edge_result = jnp.stack([entry_grad.reshape(ROWS, SEQ, D), decoded.reshape(ROWS, SEQ, D)])
    return (edge_result, grads[0], grads[1], grads[2], grads[3], grads[4], grads[5], grads[6], grads[7], grads[8], grads[9], grads[10], grads[11], grads[12])
```

```python
import functools
import math

import jax
import jax.numpy as jnp
from jax import lax
from jax.experimental import pallas as pl
from jax.experimental.pallas import tpu as pltpu
from jax.sharding import PartitionSpec as P

HEAD = 64
BF = jnp.bfloat16
F32 = jnp.float32
LOG2E = math.log2(math.e)
NORM_EPS = 1e-06
MASKED = -1e30
GELU = 0.7978845608028654
CUBIC = 0.044715
NN = (((1,), (0,)), ((), ()))
NT = (((1,), (1,)), ((), ()))
TN = (((0,), (0,)), ((), ()))
TOKENS = 256
WINDOW = 256
PARAMS = pltpu.CompilerParams(vmem_limit_bytes=56 << 20)


def dot(a, b, dims):
    return lax.dot_general(a, b, dims, preferred_element_type=F32)


def lanes(shape):
    return lax.broadcasted_iota(jnp.int32, shape, 1)


def split(values):
    high = values.astype(BF)
    return high, (values - high.astype(F32)).astype(BF)


def dot3(left, right, dims):
    return dot(left[0], right[0], dims) + dot(left[0], right[1], dims) + dot(left[1], right[0], dims)


def norm_parts(values):
    center = values - jnp.mean(values, -1, keepdims=True)
    inverse = lax.rsqrt(jnp.mean(center * center, -1, keepdims=True) + NORM_EPS)
    return center * inverse, inverse


def norm_back(grad, gain, hat, inverse):
    scaled = grad * gain
    return inverse * (
        scaled
        - jnp.mean(scaled, -1, keepdims=True)
        - hat * jnp.mean(scaled * hat, -1, keepdims=True)
    )


def column_sum(values):
    return jnp.sum(values, 0, keepdims=True)


def code_kernel(index, table, unit, wide, raw):
    count = raw.shape[0]

    def some(step, carry):
        for inner in range(8):
            token = step * 8 + inner
            raw[pl.ds(token, 1), :] = table[pl.ds(index[token], 1), :]
        return carry

    lax.fori_loop(0, count // 8, some, 0)
    values = raw[...]
    values = values * lax.rsqrt(jnp.sum(values * values, -1, keepdims=True) + NORM_EPS)
    unit[...] = values
    high, low = split(values)
    wide[...] = jnp.concatenate([high, low, high, jnp.zeros_like(high)], 1)


def gather_codes(index, table):
    count, width = index.shape[0], table.shape[1]
    return pl.pallas_call(
        code_kernel,
        in_specs=[pl.BlockSpec(memory_space=pltpu.SMEM), pl.BlockSpec(memory_space=pltpu.VMEM)],
        out_specs=[pl.BlockSpec(memory_space=pltpu.VMEM)] * 2,
        out_shape=(
            jax.ShapeDtypeStruct((count, width), F32),
            jax.ShapeDtypeStruct((count, 4 * width), BF),
        ),
        scratch_shapes=[pltpu.VMEM((count, width), F32)],
        compiler_params=PARAMS,
        name="gather_codes",
    )(index, table)


def scatter_kernel(index, unit, latent, table, out, total, rows):
    count = rows.shape[0]
    width = unit.shape[1]
    total[...] = jnp.zeros_like(total)
    rows[...] = 2.0 * (unit[...] - latent[...])

    def some(step, carry):
        for inner in range(8):
            token = step * 8 + inner
            here = pl.ds(index[token], 1)
            total[here, :] = total[here, :] + rows[pl.ds(token, 1), :]
        return carry

    lax.fori_loop(0, count // 8, some, 0)
    block = 1024

    def back(step, carry):
        here = pl.ds(pl.multiple_of(step * block, block), block)
        values = table[here, :]
        grad = total[here, :]
        inverse = lax.rsqrt(jnp.sum(values * values, -1, keepdims=True) + NORM_EPS)
        book = values * inverse
        out[here, :] = inverse * (grad - book * jnp.sum(book * grad, -1, keepdims=True))
        return carry

    lax.fori_loop(0, total.shape[0] // block, back, 0)


def scatter_codes(index, unit, latent, table):
    return pl.pallas_call(
        scatter_kernel,
        in_specs=[pl.BlockSpec(memory_space=pltpu.SMEM)] + [pl.BlockSpec(memory_space=pltpu.VMEM)] * 3,
        out_specs=pl.BlockSpec(memory_space=pltpu.VMEM),
        out_shape=jax.ShapeDtypeStruct(table.shape, F32),
        scratch_shapes=[pltpu.VMEM(table.shape, F32), pltpu.VMEM(unit.shape, F32)],
        compiler_params=PARAMS,
        name="scatter_codes",
    )(index, unit, latent, table)


def entry_values(encoder, edge, wide, up, head_bias):
    return jnp.where(encoder, edge.astype(F32), dot(wide, up, NN) + head_bias[1:2, :])


def project_kernel(side, edge, wide, up, head_bias, gains, biases, weight, n1, query, key, value):
    width = edge.shape[1]
    encoder = side[0] == 0
    values = entry_values(encoder, edge[...], wide[...], up[...], head_bias[...])
    hat, unused = norm_parts(values)
    normed = (hat * gains[0:1, :] + biases[3:4, :]).astype(BF)
    n1[...] = normed
    query[...] = (
        (dot(normed, weight[:, :width], NN) + biases[0:1, :]) * (LOG2E * HEAD ** (-0.5))
    ).astype(BF)
    key[...] = dot(normed, weight[:, width : 2 * width], NN).astype(BF)
    value[...] = (dot(normed, weight[:, 2 * width :], NN) + biases[1:2, :]).astype(BF)


def merge(low_half, left, right):
    return jnp.where(low_half, left, right)


def attend_kernel(windows, query, key, value, query_mark, key_mark, context, marks, *, row):
    count = query.shape[0]
    size = TOKENS
    pairs = query.shape[1] // 128
    low_query = lanes((size, 128)) < 64
    mark_lane = lanes((size, 128)) & 63

    def block(number, start, extent):
        rows = pl.ds(pl.multiple_of(number * size, size), size)
        keys = pl.ds(pl.multiple_of(start, WINDOW), extent)
        low_key = lanes((extent, 128)) < 64
        query_aug, key_aug = query_mark[rows, :], key_mark[keys, :]
        ones = jnp.ones((extent, 128), BF)
        scores = []
        for pair in range(pairs):
            here = slice(pair * 128, pair * 128 + 128)
            query_pair, key_pair = query[rows, here], key[keys, here]
            scores.append(
                dot(merge(low_query, query_pair, query_aug), merge(low_key, key_pair, key_aug), NT)
            )
            scores.append(
                dot(merge(low_query, query_aug, query_pair), merge(low_key, key_aug, key_pair), NT)
            )
        tops = [jnp.max(score, -1, keepdims=True) for score in scores]
        raised = [jnp.exp2(score - top).astype(BF) for score, top in zip(scores, tops)]
        for pair in range(pairs):
            here = slice(pair * 128, pair * 128 + 128)
            value_pair = value[keys, here]
            even = dot(raised[2 * pair], merge(low_key, value_pair, ones), NN)
            odd = dot(raised[2 * pair + 1], merge(low_key, ones, value_pair), NN)
            total = merge(low_query, odd, even)
            context[rows, here] = (
                merge(low_query, even, odd) / pltpu.roll(total, 64, 1)
            ).astype(BF)
            level = -(merge(low_query, tops[2 * pair + 1], tops[2 * pair]) + jnp.log2(total))
            first = level.astype(BF)
            rest = level - first.astype(F32)
            second, third = split(rest)
            marks[rows, here] = merge(
                mark_lane == 4, first, merge(mark_lane == 5, second, merge(mark_lane == 6, third, query_aug))
            )

    def one(number, carry):
        base = (row * (count // size) + number) * 2
        for_windows(windows[base], windows[base + 1], count, functools.partial(block, number))
        return carry

    lax.fori_loop(0, count // size, one, 0)


def for_windows(start, steps, count, run):
    extents = list(range(2 * WINDOW, count + 1, WINDOW))
    for position, extent in enumerate(extents):
        take = steps * WINDOW <= extent
        if position:
            take = take & (steps * WINDOW > extents[position - 1])

        @pl.when(take)
        def _():
            run(jnp.minimum(start * WINDOW, count - extent), extent)


def gelu_parts(values):
    square = values * values
    half = 0.5 + 0.5 * jnp.tanh(values * (GELU + (GELU * CUBIC) * square))
    active = values * half
    slope = half + active * (1.0 - half) * (2.0 * GELU + (6.0 * GELU * CUBIC) * square)
    return active, slope


def hidden_kernel(
    side, edge, wide, up, head_bias, context, weight_out, gains, biases, weight_in, hidden_bias,
    weight_last, output_gain, down, down_bias,
    mid, n2, active_out, slope_out, result, latent_out,
):
    encoder = side[0] == 0
    width = edge.shape[1]
    values = entry_values(encoder, edge[...], wide[...], up[...], head_bias[...])
    midway = values + (dot(context[...], weight_out[...], NN) + biases[2:3, :])
    mid[...] = midway
    hat, unused = norm_parts(midway)
    normed = (hat * gains[1:2, :] + biases[4:5, :]).astype(BF)
    n2[...] = normed
    total = midway + biases[5:6, :]
    chunk = 512
    for start in range(0, weight_in.shape[1], chunk):
        here = slice(start, start + chunk)
        active, slope = gelu_parts(dot(normed, weight_in[:, here], NN) + hidden_bias[0:1, here])
        active = active.astype(BF)
        active_out[:, here] = active
        slope_out[:, here] = slope.astype(BF)
        total = total + dot(active, weight_last[here, :], NN)
    result[...] = total

    @pl.when(encoder)
    def _():
        last_hat, unused = norm_parts(total)
        code = last_hat * output_gain[0:1, :] + head_bias[0:1, :]
        latent = code_product(code, down[...]) + down_bias[0:1, :]
        scale = lax.rsqrt(jnp.sum(latent * latent, -1, keepdims=True) + NORM_EPS)
        latent_out[...] = latent * scale


def code_product(values, weight):
    narrow = weight.shape[1] // 2
    high, low = split(values)
    both = dot(high, weight, NN)
    return both[:, :narrow] + both[:, narrow:] + dot(low, weight[:, :narrow], NN)


def tail_back_kernel(
    side, result, cotangent, unit, latent_in, output_gain, head_bias, down, down_bias, down_turned,
    weight_last, slope, weight_in, mid, gains, biases, weight_out,
    out_low, preact_low, mid_grad, branch_low, context_grad, sums, head_weight,
    upstream,
):
    encoder = side[0] == 0
    width = result.shape[1]
    narrow = unit.shape[1]

    @pl.when(pl.program_id(0) == 0)
    def _():
        sums[...] = jnp.zeros_like(sums)
        head_weight[...] = jnp.zeros_like(head_weight)

    @pl.when(encoder)
    def _():
        hat, inverse = norm_parts(result[...])
        normed = hat * output_gain[0:1, :] + head_bias[0:1, :]
        latent = code_product(normed, down[...]) + down_bias[0:1, :]
        scale = lax.rsqrt(jnp.sum(latent * latent, -1, keepdims=True) + NORM_EPS)
        code = latent * scale
        code_grad = latent_in[...] + 0.5 * (code - unit[...])
        latent_grad = scale * (code_grad - code * jnp.sum(code * code_grad, -1, keepdims=True))
        pieces = split(latent_grad)
        normed_grad = dot3(pieces, (down_turned[:narrow, :], down_turned[narrow:, :]), NN)
        head_weight[...] += dot3(pieces, split(normed), TN)
        sums[2:3, :width] += column_sum(normed_grad * hat)
        sums[2:3, width : 2 * width] += column_sum(normed_grad)
        sums[3:4, :narrow] += column_sum(latent_grad)
        upstream[...] = norm_back(normed_grad, output_gain[0:1, :], hat, inverse)

    @pl.when(jnp.logical_not(encoder))
    def _():
        upstream[...] = cotangent[...].astype(F32)

    above = upstream[...]
    low = above.astype(BF)
    out_low[...] = low
    sums[1:2, :width] += column_sum(low.astype(F32))
    normed_grad = None
    chunk = 512
    for start in range(0, weight_in.shape[1], chunk):
        here = slice(start, start + chunk)
        active_grad = dot(low, weight_last[here, :], NT)
        inner = (active_grad * slope[:, here].astype(F32)).astype(BF)
        preact_low[:, here] = inner
        sums[0:1, here] += column_sum(inner.astype(F32))
        term = dot(inner, weight_in[:, here], NT)
        normed_grad = term if normed_grad is None else normed_grad + term
    hat, inverse = norm_parts(mid[...])
    sums[1:2, 2 * width : 3 * width] += column_sum(normed_grad * hat)
    sums[1:2, 3 * width :] += column_sum(normed_grad)
    middle = above + norm_back(normed_grad, gains[1:2, :], hat, inverse)
    mid_grad[...] = middle
    branch = middle.astype(BF)
    branch_low[...] = branch
    sums[1:2, width : 2 * width] += column_sum(branch.astype(F32))
    context_grad[...] = dot(branch, weight_out[...], NT).astype(BF)


def attend_back_kernel(
    windows, query, marks, key, value, context_grad, context, key_mark,
    query_grad, key_grad, value_grad, grad_mark, key_total, value_total, *, row
):
    count = query.shape[0]
    size = TOKENS
    pairs = query.shape[1] // 128
    low_all = lanes((count, 128)) < 64
    low_query = lanes((size, 128)) < 64
    lane_all = lanes((count, 128)) & 63
    across = (
        lax.broadcasted_iota(jnp.int32, (128, 128), 0) // 64 != lanes((128, 128)) // 64
    ).astype(BF)
    zero = jnp.zeros((count, 128), BF)
    for pair in range(pairs):
        here = slice(pair * 128, pair * 128 + 128)
        product = split(context_grad[:, here].astype(F32) * context[:, here].astype(F32))
        level = -(dot(product[0], across, NN) + dot(product[1], across, NN))
        first = level.astype(BF)
        second, third = split(level - first.astype(F32))
        grad_mark[:, here] = merge(
            lane_all == 0, first, merge(lane_all == 1, second, merge(lane_all == 2, third, zero))
        )
    key_total[...] = jnp.zeros_like(key_total)
    value_total[...] = jnp.zeros_like(value_total)

    def block(number, start, extent):
        rows = pl.ds(pl.multiple_of(number * size, size), size)
        keys = pl.ds(pl.multiple_of(start, WINDOW), extent)
        low_key = lanes((extent, 128)) < 64
        key_aug = key_mark[keys, :]
        ones = jnp.where((lanes((extent, 128)) & 63) < 3, 1.0, 0.0).astype(BF)
        none = jnp.zeros((extent, 128), BF)
        for pair in range(pairs):
            here = slice(pair * 128, pair * 128 + 128)
            query_pair, key_pair, value_pair = query[rows, here], key[keys, here], value[keys, here]
            grad_pair, query_aug, grad_aug = context_grad[rows, here], marks[rows, here], grad_mark[rows, here]
            found = []
            for swap in (False, True):

                def both(low, left, right):
                    return merge(low, right, left) if swap else merge(low, left, right)

                scores = dot(both(low_key, key_pair, key_aug), both(low_query, query_pair, query_aug), NT)
                rise = dot(both(low_key, value_pair, ones), both(low_query, grad_pair, grad_aug), NT)
                chance = jnp.exp2(scores)
                score_grad = (chance * rise).astype(BF)
                found.append(
                    (
                        dot(score_grad, query_pair, NN),
                        dot(chance.astype(BF), grad_pair, NN),
                        dot(score_grad, both(low_key, key_pair, none), TN),
                    )
                )
            key_total[keys, here] += merge(low_key, found[0][0], found[1][0])
            value_total[keys, here] += merge(low_key, found[0][1], found[1][1])
            query_grad[rows, here] = ((found[0][2] + found[1][2]) * HEAD ** (-0.5)).astype(BF)

    def one(number, carry):
        base = (row * (count // size) + number) * 2
        for_windows(windows[base], windows[base + 1], count, functools.partial(block, number))
        return carry

    lax.fori_loop(0, count // size, one, 0)
    key_grad[...] = (key_total[...] * (1.0 / LOG2E)).astype(BF)
    value_grad[...] = value_total[...].astype(BF)


def entry_back_kernel(
    side, edge, wide, up, head_bias, unit, query_grad, key_grad, value_grad, weight, gains, biases,
    mid_grad, up_turned,
    entry, latent_out, sums, head_weight,
):
    encoder = side[0] == 0
    width = edge.shape[1]
    narrow = unit.shape[1]

    @pl.when(pl.program_id(0) == 0)
    def _():
        sums[...] = jnp.zeros_like(sums)
        head_weight[...] = jnp.zeros_like(head_weight)

    values = entry_values(encoder, edge[...], wide[...], up[...], head_bias[...])
    normed_grad = (
        dot(query_grad[...], weight[:, :width], NT)
        + dot(key_grad[...], weight[:, width : 2 * width], NT)
        + dot(value_grad[...], weight[:, 2 * width :], NT)
    )
    hat, inverse = norm_parts(values)
    sums[0:1, :width] += column_sum(query_grad[...].astype(F32))
    sums[0:1, width : 2 * width] += column_sum(value_grad[...].astype(F32))
    sums[0:1, 2 * width : 3 * width] += column_sum(normed_grad * hat)
    sums[0:1, 3 * width :] += column_sum(normed_grad)
    total = mid_grad[...] + norm_back(normed_grad, gains[0:1, :], hat, inverse)
    entry[...] = total

    @pl.when(jnp.logical_not(encoder))
    def _():
        sums[1:2, :width] += column_sum(total)
        latent_out[...] = code_product(total, up_turned[...])
        head_weight[...] += dot3(split(unit[...]), split(total), TN)


def weight_kernel(*refs, turns, adding):
    operands, refs = refs[:10], refs[10:]
    if adding:
        before, refs = refs[:4], refs[4:]
    active, out_low, n2, preact_low, context, branch_low, n1 = operands[:7]
    step = pl.program_id(0)
    first, second, third = turns

    def put(number, value):
        if adding:
            value = value + before[number][...]
        refs[number][...] = value

    @pl.when(step < first)
    def _():
        put(3, dot(active[...], out_low[...], TN))

    @pl.when((step >= first) & (step < second))
    def _():
        put(2, dot(n2[...], preact_low[...], TN))

    @pl.when((step >= second) & (step < third))
    def _():
        put(1, dot(context[...], branch_low[...], TN))

    for place in range(3):

        @pl.when(step == third + place)
        def _():
            put(0, dot(n1[...], operands[7 + place][...], TN))


def weight_grads(kept, back, before=None):
    active, n2, context, n1 = kept["active"], kept["n2"], kept["context"], kept["n1"]
    out_low, preact_low, branch_low = back["out_low"], back["preact_low"], back["branch_low"]
    count, width = n1.shape
    hidden = active.shape[1]
    tile = 512
    first = hidden // tile
    second = 2 * first
    third = second + 1
    whole = lambda step: (0, 0)
    down_rows = lambda step: (jnp.minimum(step, first - 1), 0)
    active_columns = lambda step: (0, jnp.minimum(step, first - 1))
    hidden_columns = lambda step: (0, jnp.clip(step - first, 0, first - 1))
    last_columns = lambda step: (0, jnp.clip(step - third, 0, 2))
    full = pl.BlockSpec((count, width), whole)
    in_specs = [
        pl.BlockSpec((count, tile), active_columns),
        full,
        full,
        pl.BlockSpec((count, tile), hidden_columns),
        full,
        full,
        full,
        full,
        full,
        full,
    ]
    out_specs = [
        pl.BlockSpec((width, tile), last_columns),
        pl.BlockSpec((width, width), whole),
        pl.BlockSpec((width, tile), hidden_columns),
        pl.BlockSpec((tile, width), down_rows),
    ]
    shapes = ((width, 3 * width), (width, width), (width, hidden), (hidden, width))
    operands = [active, out_low, n2, preact_low, context, branch_low, n1]
    operands += [back["query_grad"], back["key_grad"], back["value_grad"]]
    adding = before is not None
    if adding:
        operands += list(before)
        in_specs = in_specs + out_specs
    return pl.pallas_call(
        functools.partial(weight_kernel, turns=(first, second, third), adding=adding),
        grid=(third + 3,),
        in_specs=in_specs,
        out_specs=out_specs,
        out_shape=tuple(jax.ShapeDtypeStruct(shape, F32) for shape in shapes),
        input_output_aliases={10 + number: number for number in range(4)} if adding else {},
        compiler_params=PARAMS,
        name="weight_grads",
    )(*operands)


def nothing_kernel(*refs):
    pass


def unwritten(shapes):
    return pl.pallas_call(
        nothing_kernel,
        out_specs=[pl.BlockSpec(memory_space=pl.ANY)] * len(shapes),
        out_shape=tuple(shapes),
        name="unwritten",
    )()


KEPT = ("n1", "query", "key", "value", "context", "marks", "mid", "n2", "active", "slope", "result", "latent")
BACK = (
    "out_low", "preact_low", "mid_grad", "branch_low", "query_grad", "key_grad", "value_grad",
    "entry", "latent_out", "sums_late", "sums_early", "head_late", "head_early",
)


class Rows:
    def __init__(self, side, edges, wide, unit, windows, query_mark, key_mark, weights, head):
        self.side, self.edges, self.wide, self.unit = side, edges, wide, unit
        self.windows, self.query_mark, self.key_mark = windows, query_mark, key_mark
        (
            self.attention_in, self.attention_out, self.hidden_in, self.hidden_out,
            self.gains, self.biases, self.hidden_bias,
        ) = weights
        (
            self.output_gain, self.head_bias, self.down, self.down_bias, self.down_turned,
            self.up, self.up_turned,
        ) = head
        self.rows, self.count, self.width = edges.shape
        self.hidden = self.hidden_in.shape[1]
        self.narrow = unit.shape[1]

    def kept_shapes(self):
        n, d, f = self.count, self.width, self.hidden
        table = dict(
            n1=(d, BF), query=(d, BF), key=(d, BF), value=(d, BF), context=(d, BF), marks=(d, BF),
            mid=(d, F32), n2=(d, BF), active=(f, BF), slope=(f, BF), result=(d, F32), latent=(self.narrow, F32),
        )
        return {name: jax.ShapeDtypeStruct((n, size), kind) for name, (size, kind) in table.items()}

    def back_shapes(self):
        n, d, f = self.count, self.width, self.hidden
        table = dict(
            out_low=(n, d, BF), preact_low=(n, f, BF), mid_grad=(n, d, F32), branch_low=(n, d, BF),
            query_grad=(n, d, BF), key_grad=(n, d, BF), value_grad=(n, d, BF), entry=(n, d, F32),
            latent_out=(n, self.narrow, F32), sums_late=(8, f, F32), sums_early=(8, f, F32),
            head_late=(self.narrow, d, F32), head_early=(self.narrow, d, F32),
        )
        return {name: jax.ShapeDtypeStruct((a, b), kind) for name, (a, b, kind) in table.items()}

    def side_spec(self):
        return pl.BlockSpec(memory_space=pltpu.SMEM)

    def tokens(self, array):
        return pl.BlockSpec((TOKENS, array.shape[1]), lambda step: (step, 0))

    def whole(self, array):
        return pl.BlockSpec(array.shape, lambda step: (0,) * len(array.shape))

    def entry_specs(self, row):
        steps = self.count // TOKENS
        return [
            pl.BlockSpec((None, TOKENS, self.width), lambda step: (row, step, 0)),
            pl.BlockSpec((TOKENS, self.wide.shape[1]), lambda step: (row * steps + step, 0)),
            self.whole(self.up),
            self.whole(self.head_bias),
        ]

    def unit_spec(self, row):
        steps = self.count // TOKENS
        return pl.BlockSpec((TOKENS, self.narrow), lambda step: (row * steps + step, 0))

    def call(self, kernel, in_specs, operands, outs, out_specs, name, scratch=()):
        return pl.pallas_call(
            kernel,
            grid=(self.count // TOKENS,),
            in_specs=in_specs,
            out_specs=out_specs,
            out_shape=tuple(outs),
            scratch_shapes=list(scratch),
            compiler_params=PARAMS,
            name=name,
        )(*operands)

    def attention_call(self, kernel, row, operands, outs, name, scratch=()):
        half = self.width // 2

        def spec(array):
            if array.ndim == 3:
                return pl.BlockSpec((None, self.count, array.shape[2]), lambda step, info: (row, 0, 0))
            return pl.BlockSpec((self.count, half), lambda step, info: (0, step))

        return pl.pallas_call(
            functools.partial(kernel, row=row),
            grid_spec=pltpu.PrefetchScalarGridSpec(
                num_scalar_prefetch=1,
                grid=(2,),
                in_specs=[spec(array) for array in operands],
                out_specs=[spec(array) for array in outs],
                scratch_shapes=list(scratch),
            ),
            out_shape=tuple(outs),
            compiler_params=PARAMS,
            name=name,
        )(self.windows, *operands)

    def forward(self, row):
        shapes = self.kept_shapes()
        entry = (self.edges, self.wide, self.up, self.head_bias)
        kept = {}
        names = ("n1", "query", "key", "value")
        outs = self.call(
            project_kernel,
            [self.side_spec()] + self.entry_specs(row)
            + [self.whole(self.gains), self.whole(self.biases), self.whole(self.attention_in)],
            (self.side,) + entry + (self.gains, self.biases, self.attention_in),
            [shapes[name] for name in names],
            [self.tokens(shapes[name]) for name in names],
            "project",
        )
        kept.update(zip(names, outs))
        names = ("context", "marks")
        outs = self.attention_call(
            attend_kernel, row,
            (kept["query"], kept["key"], kept["value"], self.query_mark, self.key_mark),
            [shapes[name] for name in names],
            "attend",
        )
        kept.update(zip(names, outs))
        names = ("mid", "n2", "active", "slope", "result", "latent")
        consts = (
            self.attention_out, self.gains, self.biases, self.hidden_in, self.hidden_bias, self.hidden_out,
            self.output_gain, self.down, self.down_bias,
        )
        outs = self.call(
            hidden_kernel,
            [self.side_spec()] + self.entry_specs(row) + [self.tokens(kept["context"])]
            + [self.whole(array) for array in consts],
            (self.side,) + entry + (kept["context"],) + consts,
            [shapes[name] for name in names],
            [self.tokens(shapes[name]) for name in names],
            "hidden",
        )
        kept.update(zip(names, outs))
        return kept

    def backward(self, row, kept, latent_in):
        shapes = self.back_shapes()
        back = {}
        names = ("out_low", "preact_low", "mid_grad", "branch_low", "context_grad", "sums_late", "head_late")
        shapes["context_grad"] = shapes["out_low"]
        consts = (self.output_gain, self.head_bias, self.down, self.down_bias, self.down_turned, self.hidden_out)
        late = (self.gains, self.biases, self.attention_out)
        outs = self.call(
            tail_back_kernel,
            [self.side_spec(), self.tokens(kept["result"]), self.entry_specs(row)[0], self.unit_spec(row),
             self.tokens(latent_in)]
            + [self.whole(array) for array in consts]
            + [self.tokens(kept["slope"]), self.whole(self.hidden_in), self.tokens(kept["mid"])]
            + [self.whole(array) for array in late],
            (self.side, kept["result"], self.edges, self.unit, latent_in) + consts
            + (kept["slope"], self.hidden_in, kept["mid"]) + late,
            [shapes[name] for name in names],
            [self.tokens(shapes[name]) for name in names[:5]] + [self.whole(shapes[name]) for name in names[5:]],
            "tail_back",
            scratch=[pltpu.VMEM((TOKENS, self.width), F32)],
        )
        back.update(zip(names, outs))
        names = ("query_grad", "key_grad", "value_grad")
        half = self.width // 2
        outs = self.attention_call(
            attend_back_kernel, row,
            (kept["query"], kept["marks"], kept["key"], kept["value"], back.pop("context_grad"), kept["context"],
             self.key_mark),
            [shapes[name] for name in names],
            "attend_back",
            scratch=[
                pltpu.VMEM((self.count, half), BF),
                pltpu.VMEM((self.count, half), F32),
                pltpu.VMEM((self.count, half), F32),
            ],
        )
        back.update(zip(names, outs))
        names = ("entry", "latent_out", "sums_early", "head_early")
        grads = (back["query_grad"], back["key_grad"], back["value_grad"])
        outs = self.call(
            entry_back_kernel,
            [self.side_spec()] + self.entry_specs(row) + [self.unit_spec(row)]
            + [self.tokens(array) for array in grads]
            + [self.whole(self.attention_in), self.whole(self.gains), self.whole(self.biases),
               self.tokens(back["mid_grad"]), self.whole(self.up_turned)],
            (self.side, self.edges, self.wide, self.up, self.head_bias, self.unit) + grads
            + (self.attention_in, self.gains, self.biases, back["mid_grad"], self.up_turned),
            [shapes[name] for name in names],
            [self.tokens(shapes[name]) for name in names[:2]] + [self.whole(shapes[name]) for name in names[2:]],
            "entry_back",
        )
        back.update(zip(names, outs))
        return back


def pair_of(values, axis):
    return jnp.concatenate(split(values), axis)


def as_list(table, names):
    return [table[name] for name in names]


def marks_of(segments):
    lane = jnp.arange(128) & 63
    same = segments[..., None] == lane
    inside = lane < 4
    query_mark = jnp.where(inside & ~same, MASKED, 0.0).astype(BF)
    key_mark = jnp.where((inside & same) | ((lane > 3) & (lane < 7)), 1.0, 0.0).astype(BF)
    return query_mark, key_mark


def windows_of(segments):
    rows, count = segments.shape
    steps = count // WINDOW
    blocks = segments.reshape(rows, steps, WINDOW)
    least, most = blocks[:, :, 0], blocks[:, :, -1]
    meets = (most[:, :, None] >= least[:, None, :]) & (least[:, :, None] <= most[:, None, :])
    place = jnp.arange(steps)
    start = jnp.min(jnp.where(meets, place, steps), -1)
    stop = jnp.max(jnp.where(meets, place, -1), -1) + 1
    return jnp.stack([start, stop - start], -1).reshape(-1).astype(jnp.int32)


def on_device(
    boundary, segments, code_index, attention_in, attention_out, hidden_in, hidden_out, block_gains,
    block_biases, hidden_bias, output_gain, head_bias, down_weight, down_bias, up_weight, codebook,
):
    section = lax.axis_index("section")
    encoder = section == 0
    side = section.astype(jnp.int32)[None]
    edges = boundary[0]
    rows, count, width = edges.shape
    hidden = hidden_in.shape[2]
    index = code_index.reshape(-1)
    unit, wide = gather_codes(index, codebook)
    query_mark, key_mark = marks_of(segments)
    up_high, up_low = split(up_weight)
    work = Rows(
        side, edges, wide, unit, windows_of(segments), query_mark, key_mark,
        (
            attention_in[0], attention_out[0], hidden_in[0], hidden_out[0], block_gains[0], block_biases[0],
            hidden_bias,
        ),
        (
            output_gain[None], head_bias, pair_of(down_weight, 1), down_bias[None], pair_of(down_weight.T, 0),
            jnp.concatenate([up_high, up_high, up_low, jnp.zeros_like(up_low)], 0), pair_of(up_weight.T, 1),
        ),
    )
    kept_shapes = as_list(work.kept_shapes(), KEPT)
    back_shapes = as_list(work.back_shapes(), BACK)
    book_shape = jax.ShapeDtypeStruct(codebook.shape, F32)
    weight_shapes = [
        jax.ShapeDtypeStruct(shape, F32)
        for shape in ((width, 3 * width), (width, width), (width, hidden), (hidden, width))
    ]
    quiet = jnp.zeros((count, unit.shape[1]), F32)
    first_kept = work.forward(0)

    def encoder_second():
        kept = work.forward(1)
        latent = jnp.concatenate([first_kept["latent"], kept["latent"]], 0)
        book = scatter_codes(index, unit, latent, codebook)
        return as_list(kept, KEPT), list(unwritten(back_shapes)), book

    def decoder_first():
        back = work.backward(0, first_kept, quiet)
        return list(unwritten(kept_shapes)), as_list(back, BACK), unwritten([book_shape])[0]

    kept_a, back_a, book = lax.cond(encoder, encoder_second, decoder_first)
    back_a = dict(zip(BACK, back_a))
    kept_a = dict(zip(KEPT, kept_a))
    latent_in = lax.ppermute(back_a["latent_out"], "section", [(1, 0)])

    def encoder_third():
        return list(unwritten(kept_shapes)), as_list(work.backward(0, first_kept, latent_in), BACK)

    def decoder_third():
        return as_list(work.forward(1), KEPT), list(unwritten(back_shapes))

    kept_b, back_b = lax.cond(encoder, encoder_third, decoder_third)
    kept_b, back_b = dict(zip(KEPT, kept_b)), dict(zip(BACK, back_b))

    def encoder_fourth():
        return list(unwritten(back_shapes)), list(weight_grads(first_kept, back_b))

    def decoder_fourth():
        return as_list(work.backward(1, kept_b, quiet), BACK), list(unwritten(weight_shapes))

    back_c, weights_c = lax.cond(encoder, encoder_fourth, decoder_fourth)
    back_c = dict(zip(BACK, back_c))
    latent_in_second = lax.ppermute(back_c["latent_out"], "section", [(1, 0)])

    def encoder_fifth():
        back = work.backward(1, kept_a, latent_in_second)
        total = weight_grads(kept_a, back, weights_c)
        sums = [back[name] + back_b[name] for name in BACK[-4:]]
        edge = jnp.stack([back_b["entry"], back["entry"]])
        return list(total), sums, edge

    def decoder_fifth():
        total = weight_grads(first_kept, back_a)
        total = weight_grads(kept_b, back_c, total)
        sums = [back_a[name] + back_c[name] for name in BACK[-4:]]
        edge = jnp.stack([first_kept["result"], kept_b["result"]])
        return list(total), sums, edge

    totals, sums, edge = lax.cond(encoder, encoder_fifth, decoder_fifth)
    head_weight = jnp.where(encoder, sums[2], sums[3])
    book = jnp.where(encoder, book, 0.0).reshape(-1, 128)
    totals, sums_late, sums_early, head_weight, book = lax.psum(
        (totals, sums[0], sums[1], head_weight, book), "dp"
    )
    from_encoder = jnp.where(
        encoder,
        jnp.concatenate([sums_late[2].reshape(-1, 128), sums_late[3].reshape(-1, 128)], 0), 0.0
    )
    from_decoder = jnp.where(encoder, 0.0, sums_early[1].reshape(-1, 128))
    empty = jnp.zeros_like(head_weight)
    book, head_sums, down_grad, up_grad = lax.psum(
        (
            book,
            jnp.concatenate([from_encoder, from_decoder], 0),
            jnp.where(encoder, head_weight, empty),
            jnp.where(encoder, empty, head_weight),
        ),
        "section",
    )
    head_sums = head_sums.reshape(3, -1)
    late, early = sums_late[1].reshape(4, width), sums_early[0].reshape(4, width)
    return (
        edge[None],
        totals[0][None],
        totals[1][None],
        totals[2][None],
        totals[3][None],
        jnp.stack([early[2], late[2]])[None],
        jnp.stack([early[0], early[1], late[1], early[3], late[3], late[0]])[None],
        sums_late[0][None],
        head_sums[0, :width],
        jnp.stack([head_sums[0, width : 2 * width], head_sums[2, :width]]),
        down_grad.T,
        head_sums[1, : unit.shape[1]],
        up_grad,
        book.reshape(codebook.shape),
    )


def solution(mesh):
    return jax.shard_map(
        on_device,
        mesh=mesh,
        in_specs=(
            P("section", "dp", None, None), P("dp", None), P("dp", None),
            P("section", None, None), P("section", None, None), P("section", None, None),
            P("section", None, None), P("section", None, None), P("section", None, None),
            P("section", None), P(), P(), P(), P(), P(), P(),
        ),
        out_specs=(
            P("section", "dp", None, None), P("section", None, None), P("section", None, None),
            P("section", None, None), P("section", None, None), P("section", None, None),
            P("section", None, None), P("section", None), P(), P(), P(), P(), P(), P(),
        ),
        check_vma=False,
    )
```

```python
import functools
import math

import jax
import jax.numpy as jnp
from jax import lax
from jax.experimental import pallas as pl
from jax.experimental.pallas import tpu as pltpu
from jax.sharding import PartitionSpec as P

HEAD = 64
BF = jnp.bfloat16
F32 = jnp.float32
LOG2E = math.log2(math.e)
NORM_EPS = 1e-06
MASKED = -1e30
GELU = 0.7978845608028654
CUBIC = 0.044715
NN = (((1,), (0,)), ((), ()))
NT = (((1,), (1,)), ((), ()))
TN = (((0,), (0,)), ((), ()))
TOKENS = 256
WINDOW = 256
PARAMS = pltpu.CompilerParams(vmem_limit_bytes=56 << 20)


def dot(a, b, dims):
    return lax.dot_general(a, b, dims, preferred_element_type=F32)


def lanes(shape):
    return lax.broadcasted_iota(jnp.int32, shape, 1)


def split(values):
    high = values.astype(BF)
    return high, (values - high.astype(F32)).astype(BF)


def dot3(left, right, dims):
    return dot(left[0], right[0], dims) + dot(left[0], right[1], dims) + dot(left[1], right[0], dims)


def norm_parts(values):
    center = values - jnp.mean(values, -1, keepdims=True)
    inverse = lax.rsqrt(jnp.mean(center * center, -1, keepdims=True) + NORM_EPS)
    return center * inverse, inverse


def norm_back(grad, gain, hat, inverse):
    scaled = grad * gain
    return inverse * (
        scaled
        - jnp.mean(scaled, -1, keepdims=True)
        - hat * jnp.mean(scaled * hat, -1, keepdims=True)
    )


def column_sum(values):
    return jnp.sum(values, 0, keepdims=True)


def code_kernel(index, table_turned, unit, wide, table, raw):
    count = raw.shape[0]
    block = 512

    def turn(step, carry):
        start = pl.multiple_of(step * block, block)
        table[pl.ds(start, block), :] = table_turned[:, pl.ds(start, block)].T
        return carry

    lax.fori_loop(0, table.shape[0] // block, turn, 0)

    def some(step, carry):
        for inner in range(8):
            token = step * 8 + inner
            raw[pl.ds(token, 1), :] = table[pl.ds(index[token], 1), :]
        return carry

    lax.fori_loop(0, count // 8, some, 0)
    values = raw[...]
    values = values * lax.rsqrt(jnp.sum(values * values, -1, keepdims=True) + NORM_EPS)
    unit[...] = values
    high, low = split(values)
    wide[...] = jnp.concatenate([high, low, high, jnp.zeros_like(high)], 1)


def gather_codes(index, table_turned):
    count, width = index.shape[0], table_turned.shape[0]
    return pl.pallas_call(
        code_kernel,
        in_specs=[pl.BlockSpec(memory_space=pltpu.SMEM), pl.BlockSpec(memory_space=pltpu.VMEM)],
        out_specs=[pl.BlockSpec(memory_space=pltpu.VMEM)] * 2,
        out_shape=(
            jax.ShapeDtypeStruct((count, width), F32),
            jax.ShapeDtypeStruct((count, 4 * width), BF),
        ),
        scratch_shapes=[pltpu.VMEM(table_turned.shape[::-1], F32), pltpu.VMEM((count, width), F32)],
        compiler_params=PARAMS,
        name="gather_codes",
    )(index, table_turned)


def scatter_kernel(index, unit, latent_first, latent_second, table_turned, out, total, rows):
    count = rows.shape[0]
    width = unit.shape[1]
    half = count // 2
    total[...] = jnp.zeros_like(total)
    rows[:half, :] = 2.0 * (unit[:half, :] - latent_first[...])
    rows[half:, :] = 2.0 * (unit[half:, :] - latent_second[...])

    def some(step, carry):
        for inner in range(8):
            token = step * 8 + inner
            here = pl.ds(index[token], 1)
            total[here, :] = total[here, :] + rows[pl.ds(token, 1), :]
        return carry

    lax.fori_loop(0, count // 8, some, 0)
    block = out.shape[1]

    def back(step, carry):
        start = pl.multiple_of(step * block, block)
        values = table_turned[:, pl.ds(start, block)]
        grad = total[pl.ds(start, block), :].T
        inverse = lax.rsqrt(jnp.sum(values * values, 0, keepdims=True) + NORM_EPS)
        book = values * inverse
        out[pl.ds(pl.multiple_of(step * width, width), width), :] = inverse * (
            grad - book * jnp.sum(book * grad, 0, keepdims=True)
        )
        return carry

    lax.fori_loop(0, total.shape[0] // block, back, 0)


def book_shape(table_turned, width):
    return jax.ShapeDtypeStruct((table_turned.size // width, width), F32)


def scatter_codes(index, unit, latents, table_turned, width):
    return pl.pallas_call(
        scatter_kernel,
        in_specs=[pl.BlockSpec(memory_space=pltpu.SMEM)] + [pl.BlockSpec(memory_space=pltpu.VMEM)] * 4,
        out_specs=pl.BlockSpec(memory_space=pltpu.VMEM),
        out_shape=book_shape(table_turned, width),
        scratch_shapes=[pltpu.VMEM(table_turned.shape[::-1], F32), pltpu.VMEM(unit.shape, F32)],
        compiler_params=PARAMS,
        name="scatter_codes",
    )(index, unit, *latents, table_turned)


def entry_values(encoder, edge, wide, up, head_bias):
    return jnp.where(encoder, edge.astype(F32), dot(wide, up, NN) + head_bias[1:2, :])


def project_kernel(side, edge, wide, up, head_bias, gains, biases, weight, n1, query, key, value):
    width = edge.shape[1]
    encoder = side[0] == 0
    values = entry_values(encoder, edge[...], wide[...], up[...], head_bias[...])
    hat, unused = norm_parts(values)
    normed = (hat * gains[0:1, :] + biases[3:4, :]).astype(BF)
    n1[...] = normed
    query[...] = (
        (dot(normed, weight[:, :width], NN) + biases[0:1, :]) * (LOG2E * HEAD ** (-0.5))
    ).astype(BF)
    key[...] = dot(normed, weight[:, width : 2 * width], NN).astype(BF)
    value[...] = (dot(normed, weight[:, 2 * width :], NN) + biases[1:2, :]).astype(BF)


def merge(low_half, left, right):
    return jnp.where(low_half, left, right)


def attend_kernel(windows, query, key, value, query_mark, key_mark, context, marks, *, row):
    count = query.shape[0]
    size = TOKENS
    pairs = query.shape[1] // 128
    low_query = lanes((size, 128)) < 64
    mark_lane = lanes((size, 128)) & 63

    def block(number, start, extent):
        rows = pl.ds(pl.multiple_of(number * size, size), size)
        keys = pl.ds(pl.multiple_of(start, WINDOW), extent)
        low_key = lanes((extent, 128)) < 64
        query_aug, key_aug = query_mark[rows, :], key_mark[keys, :]
        ones = jnp.ones((extent, 128), BF)
        scores = []
        for pair in range(pairs):
            here = slice(pair * 128, pair * 128 + 128)
            query_pair, key_pair = query[rows, here], key[keys, here]
            scores.append(
                dot(merge(low_query, query_pair, query_aug), merge(low_key, key_pair, key_aug), NT)
            )
            scores.append(
                dot(merge(low_query, query_aug, query_pair), merge(low_key, key_aug, key_pair), NT)
            )
        tops = [jnp.max(score, -1, keepdims=True) for score in scores]
        raised = [jnp.exp2(score - top).astype(BF) for score, top in zip(scores, tops)]
        for pair in range(pairs):
            here = slice(pair * 128, pair * 128 + 128)
            value_pair = value[keys, here]
            even = dot(raised[2 * pair], merge(low_key, value_pair, ones), NN)
            odd = dot(raised[2 * pair + 1], merge(low_key, ones, value_pair), NN)
            total = merge(low_query, odd, even)
            context[rows, here] = (
                merge(low_query, even, odd) / pltpu.roll(total, 64, 1)
            ).astype(BF)
            level = -(merge(low_query, tops[2 * pair + 1], tops[2 * pair]) + jnp.log2(total))
            first = level.astype(BF)
            rest = level - first.astype(F32)
            second, third = split(rest)
            marks[rows, here] = merge(
                mark_lane == 4, first, merge(mark_lane == 5, second, merge(mark_lane == 6, third, query_aug))
            )

    def one(number, carry):
        base = (row * (count // size) + number) * 2
        for_windows(windows[base], windows[base + 1], count, functools.partial(block, number))
        return carry

    lax.fori_loop(0, count // size, one, 0)


def for_windows(start, steps, count, run):
    extents = list(range(2 * WINDOW, count + 1, WINDOW))
    for position, extent in enumerate(extents):
        take = steps * WINDOW <= extent
        if position:
            take = take & (steps * WINDOW > extents[position - 1])

        @pl.when(take)
        def _():
            run(jnp.minimum(start * WINDOW, count - extent), extent)


def gelu_parts(values):
    square = values * values
    half = 0.5 + 0.5 * jnp.tanh(values * (GELU + (GELU * CUBIC) * square))
    active = values * half
    slope = half + active * (1.0 - half) * (2.0 * GELU + (6.0 * GELU * CUBIC) * square)
    return active, slope


def hidden_kernel(
    side, edge, wide, up, head_bias, context, weight_out, gains, biases, weight_in, hidden_bias,
    weight_last, output_gain, down, down_bias,
    mid, n2, active_out, slope_out, result, latent_out,
):
    encoder = side[0] == 0
    width = edge.shape[1]
    values = entry_values(encoder, edge[...], wide[...], up[...], head_bias[...])
    midway = values + (dot(context[...], weight_out[...], NN) + biases[2:3, :])
    mid[...] = midway
    hat, unused = norm_parts(midway)
    normed = (hat * gains[1:2, :] + biases[4:5, :]).astype(BF)
    n2[...] = normed
    total = midway + biases[5:6, :]
    chunk = 512
    for start in range(0, weight_in.shape[1], chunk):
        here = slice(start, start + chunk)
        active, slope = gelu_parts(dot(normed, weight_in[:, here], NN) + hidden_bias[0:1, here])
        active = active.astype(BF)
        active_out[:, here] = active
        slope_out[:, here] = slope.astype(BF)
        total = total + dot(active, weight_last[here, :], NN)
    result[...] = total

    @pl.when(encoder)
    def _():
        last_hat, unused = norm_parts(total)
        code = last_hat * output_gain[0:1, :] + head_bias[0:1, :]
        latent = code_product(code, down[...]) + down_bias[0:1, :]
        scale = lax.rsqrt(jnp.sum(latent * latent, -1, keepdims=True) + NORM_EPS)
        latent_out[...] = latent * scale


def code_product(values, weight):
    narrow = weight.shape[1] // 2
    high, low = split(values)
    both = dot(high, weight, NN)
    return both[:, :narrow] + both[:, narrow:] + dot(low, weight[:, :narrow], NN)


def tail_back_kernel(
    side, result, cotangent, unit, latent_in, output_gain, head_bias, down, down_bias, down_turned,
    weight_last, slope, weight_in, mid, gains, biases, weight_out,
    out_low, preact_low, mid_grad, branch_low, context_grad, sums, head_weight,
    upstream,
):
    encoder = side[0] == 0
    width = result.shape[1]
    narrow = unit.shape[1]

    @pl.when(pl.program_id(0) == 0)
    def _():
        sums[...] = jnp.zeros_like(sums)
        head_weight[...] = jnp.zeros_like(head_weight)

    @pl.when(encoder)
    def _():
        hat, inverse = norm_parts(result[...])
        normed = hat * output_gain[0:1, :] + head_bias[0:1, :]
        latent = code_product(normed, down[...]) + down_bias[0:1, :]
        scale = lax.rsqrt(jnp.sum(latent * latent, -1, keepdims=True) + NORM_EPS)
        code = latent * scale
        code_grad = latent_in[...] + 0.5 * (code - unit[...])
        latent_grad = scale * (code_grad - code * jnp.sum(code * code_grad, -1, keepdims=True))
        pieces = split(latent_grad)
        normed_grad = dot3(pieces, (down_turned[:narrow, :], down_turned[narrow:, :]), NN)
        head_weight[...] += dot3(pieces, split(normed), TN)
        sums[8:9, :] += column_sum(normed_grad * hat)
        sums[9:10, :] += column_sum(normed_grad)
        sums[10:11, :narrow] += column_sum(latent_grad)
        upstream[...] = norm_back(normed_grad, output_gain[0:1, :], hat, inverse)

    @pl.when(jnp.logical_not(encoder))
    def _():
        upstream[...] = cotangent[...].astype(F32)

    above = upstream[...]
    low = above.astype(BF)
    out_low[...] = low
    sums[4:5, :] += column_sum(low.astype(F32))
    normed_grad = None
    chunk = 512
    for start in range(0, weight_in.shape[1], chunk):
        here = slice(start, start + chunk)
        active_grad = dot(low, weight_last[here, :], NT)
        inner = (active_grad * slope[:, here].astype(F32)).astype(BF)
        preact_low[:, here] = inner
        sums[start // chunk : start // chunk + 1, :] += column_sum(inner.astype(F32))
        term = dot(inner, weight_in[:, here], NT)
        normed_grad = term if normed_grad is None else normed_grad + term
    hat, inverse = norm_parts(mid[...])
    sums[6:7, :] += column_sum(normed_grad * hat)
    sums[7:8, :] += column_sum(normed_grad)
    middle = above + norm_back(normed_grad, gains[1:2, :], hat, inverse)
    mid_grad[...] = middle
    branch = middle.astype(BF)
    branch_low[...] = branch
    sums[5:6, :] += column_sum(branch.astype(F32))
    context_grad[...] = dot(branch, weight_out[...], NT).astype(BF)


def attend_back_kernel(
    windows, query, marks, key, value, context_grad, context, key_mark,
    query_grad, key_grad, value_grad, grad_mark, key_total, value_total, *, row
):
    count = query.shape[0]
    size = TOKENS
    pairs = query.shape[1] // 128
    low_all = lanes((count, 128)) < 64
    low_query = lanes((size, 128)) < 64
    lane_all = lanes((count, 128)) & 63
    across = (
        lax.broadcasted_iota(jnp.int32, (128, 128), 0) // 64 != lanes((128, 128)) // 64
    ).astype(BF)
    zero = jnp.zeros((count, 128), BF)
    for pair in range(pairs):
        here = slice(pair * 128, pair * 128 + 128)
        product = split(context_grad[:, here].astype(F32) * context[:, here].astype(F32))
        level = -(dot(product[0], across, NN) + dot(product[1], across, NN))
        first = level.astype(BF)
        second, third = split(level - first.astype(F32))
        grad_mark[:, here] = merge(
            lane_all == 0, first, merge(lane_all == 1, second, merge(lane_all == 2, third, zero))
        )
    key_total[...] = jnp.zeros_like(key_total)
    value_total[...] = jnp.zeros_like(value_total)

    def block(number, start, extent):
        rows = pl.ds(pl.multiple_of(number * size, size), size)
        keys = pl.ds(pl.multiple_of(start, WINDOW), extent)
        low_key = lanes((extent, 128)) < 64
        key_aug = key_mark[keys, :]
        ones = jnp.where((lanes((extent, 128)) & 63) < 3, 1.0, 0.0).astype(BF)
        none = jnp.zeros((extent, 128), BF)
        for pair in range(pairs):
            here = slice(pair * 128, pair * 128 + 128)
            query_pair, key_pair, value_pair = query[rows, here], key[keys, here], value[keys, here]
            grad_pair, query_aug, grad_aug = context_grad[rows, here], marks[rows, here], grad_mark[rows, here]
            found = []
            for swap in (False, True):

                def both(low, left, right):
                    return merge(low, right, left) if swap else merge(low, left, right)

                scores = dot(both(low_key, key_pair, key_aug), both(low_query, query_pair, query_aug), NT)
                rise = dot(both(low_key, value_pair, ones), both(low_query, grad_pair, grad_aug), NT)
                chance = jnp.exp2(scores)
                score_grad = (chance * rise).astype(BF)
                found.append(
                    (
                        dot(score_grad, query_pair, NN),
                        dot(chance.astype(BF), grad_pair, NN),
                        dot(score_grad, both(low_key, key_pair, none), TN),
                    )
                )
            key_total[keys, here] += merge(low_key, found[0][0], found[1][0])
            value_total[keys, here] += merge(low_key, found[0][1], found[1][1])
            query_grad[rows, here] = ((found[0][2] + found[1][2]) * HEAD ** (-0.5)).astype(BF)

    def one(number, carry):
        base = (row * (count // size) + number) * 2
        for_windows(windows[base], windows[base + 1], count, functools.partial(block, number))
        return carry

    lax.fori_loop(0, count // size, one, 0)
    key_grad[...] = (key_total[...] * (1.0 / LOG2E)).astype(BF)
    value_grad[...] = value_total[...].astype(BF)


def entry_back_kernel(
    side, edge, wide, up, head_bias, unit, query_grad, key_grad, value_grad, weight, gains, biases,
    mid_grad, up_turned,
    entry, latent_out, sums, head_weight,
):
    encoder = side[0] == 0
    width = edge.shape[1]
    narrow = unit.shape[1]

    @pl.when(pl.program_id(0) == 0)
    def _():
        sums[...] = jnp.zeros_like(sums)
        head_weight[...] = jnp.zeros_like(head_weight)

    values = entry_values(encoder, edge[...], wide[...], up[...], head_bias[...])
    normed_grad = (
        dot(query_grad[...], weight[:, :width], NT)
        + dot(key_grad[...], weight[:, width : 2 * width], NT)
        + dot(value_grad[...], weight[:, 2 * width :], NT)
    )
    hat, inverse = norm_parts(values)
    sums[0:1, :] += column_sum(query_grad[...].astype(F32))
    sums[1:2, :] += column_sum(value_grad[...].astype(F32))
    sums[2:3, :] += column_sum(normed_grad * hat)
    sums[3:4, :] += column_sum(normed_grad)
    total = mid_grad[...] + norm_back(normed_grad, gains[0:1, :], hat, inverse)
    entry[...] = total

    @pl.when(jnp.logical_not(encoder))
    def _():
        sums[4:5, :] += column_sum(total)
        latent_out[...] = code_product(total, up_turned[...])
        head_weight[...] += dot3(split(unit[...]), split(total), TN)


def weight_kernel(*refs, turns, adding):
    operands, out = refs[:10], refs[-1]
    active, out_low, n2, preact_low, context, branch_low, n1 = operands[:7]
    step = pl.program_id(0)
    first, second, third = turns

    def put(left, right):
        value = dot(left[...], right[...], TN)
        out[...] = value + refs[10][...] if adding else value

    @pl.when(step < first)
    def _():
        put(active, out_low)

    @pl.when((step >= first) & (step < second))
    def _():
        put(n2, preact_low)

    @pl.when((step >= second) & (step < third))
    def _():
        put(context, branch_low)

    for place in range(3):

        @pl.when(step == third + place)
        def _():
            put(n1, operands[7 + place])


def weight_grads(kept, back, before=None):
    active, n2, context, n1 = kept["active"], kept["n2"], kept["context"], kept["n1"]
    out_low, preact_low, branch_low = back["out_low"], back["preact_low"], back["branch_low"]
    count, width = n1.shape
    first = active.shape[1] // width
    second = 2 * first
    third = second + 1
    whole = lambda step: (0, 0)
    full = pl.BlockSpec((count, width), whole)
    in_specs = [full] * 10
    in_specs[0] = pl.BlockSpec((count, width), lambda step: (0, jnp.minimum(step, first - 1)))
    in_specs[3] = pl.BlockSpec((count, width), lambda step: (0, jnp.clip(step - first, 0, first - 1)))
    out_spec = pl.BlockSpec((width, width), lambda step: (step, 0))
    operands = [active, out_low, n2, preact_low, context, branch_low, n1]
    operands += [back["query_grad"], back["key_grad"], back["value_grad"]]
    adding = before is not None
    if adding:
        operands.append(before)
        in_specs.append(out_spec)
    return pl.pallas_call(
        functools.partial(weight_kernel, turns=(first, second, third), adding=adding),
        grid=(third + 3,),
        in_specs=in_specs,
        out_specs=out_spec,
        out_shape=jax.ShapeDtypeStruct(((third + 3) * width, width), F32),
        input_output_aliases={10: 0} if adding else {},
        compiler_params=PARAMS,
        name="weight_grads",
    )(*operands)


MESH = pl.DeviceIdType.MESH


def ring_chip(position, chips):
    odd = position // (chips // 2)
    return (1 - odd) * (2 * position) + odd * (2 * (chips - 1 - position) + 1)


def sum_kernel(
    chips, main, misc, main_out, misc_out,
    own_main, own_misc, pair_main, pair_misc, run_main, run_misc, far_misc,
    load_sems, pair_send, pair_recv, run_send, run_recv, far_send, far_recv,
    keep_sems, spread_send, spread_recv, side_send, side_recv,
):
    place = lax.axis_index("dp")
    section = lax.axis_index("section")
    chip, core = place // 2, place % 2
    column, odd = chip // 2, chip % 2
    position = (1 - odd) * column + odd * (chips - 1 - column)
    other = {"dp": chip * 2 + (1 - core)}
    far = {"section": 1 - section}
    ahead = {"dp": ring_chip((position + 1) % chips, chips) * 2 + core}
    behind = {"dp": ring_chip((position + chips - 1) % chips, chips) * 2 + core}
    targets = (ahead, behind)
    sizes = (main.shape[0] // (4 * chips), misc.shape[0] // (4 * chips))
    sources, results = (main, misc), (main_out, misc_out)
    own, pair, run = (own_main, own_misc), (pair_main, pair_misc), (run_main, run_misc)

    barrier = pltpu.get_barrier_semaphore()
    for device in (other, far, ahead, behind):
        pl.semaphore_signal(barrier, inc=1, device_id=device, device_id_type=MESH)

    def piece(step, way):
        return (position + (2 * chips - step if way == 0 else step)) % chips

    def rows(which, half, way, number):
        size = sizes[which]
        return pl.ds(pl.multiple_of(((half * 2 + way) * chips + number) * size, 8), size)

    def load(which, way, step):
        return pltpu.make_async_copy(
            sources[which].at[rows(which, core, way, piece(step, way))],
            own[which].at[way, step],
            load_sems.at[which, way, step],
        )

    def swap(which, way, step):
        return pltpu.make_async_remote_copy(
            src_ref=sources[which].at[rows(which, 1 - core, way, piece(step, way))],
            dst_ref=pair[which].at[way, step],
            send_sem=pair_send.at[which, way, step],
            recv_sem=pair_recv.at[which, way, step],
            device_id=other,
            device_id_type=MESH,
        )

    def pass_on(which, way, step):
        return pltpu.make_async_remote_copy(
            src_ref=run[which].at[way, step],
            dst_ref=run[which].at[way, step + 1],
            send_sem=run_send.at[which, way, step],
            recv_sem=run_recv.at[which, way, step + 1],
            device_id=targets[way],
            device_id_type=MESH,
        )

    def cross(way):
        return pltpu.make_async_remote_copy(
            src_ref=run_misc.at[way, chips - 1],
            dst_ref=far_misc.at[way],
            send_sem=far_send.at[way],
            recv_sem=far_recv.at[way],
            device_id=far,
            device_id_type=MESH,
        )

    def final_rows(which, way, step):
        return rows(which, core, way, piece(step + chips - 1, way))

    def keep(which, way):
        return pltpu.make_async_copy(
            run[which].at[way, chips - 1], results[which].at[final_rows(which, way, 0)], keep_sems.at[which, way]
        )

    def spread(which, way, step, first=False):
        here = results[which].at[final_rows(which, way, step)]
        return pltpu.make_async_remote_copy(
            src_ref=run[which].at[way, chips - 1] if first else here,
            dst_ref=here,
            send_sem=spread_send.at[which, way, step],
            recv_sem=spread_recv.at[which, way, step],
            device_id=targets[way],
            device_id_type=MESH,
        )

    def aside(which, way, step, first=False):
        here = results[which].at[final_rows(which, way, step)]
        return pltpu.make_async_remote_copy(
            src_ref=run[which].at[way, chips - 1] if first else here,
            dst_ref=here,
            send_sem=side_send.at[which, way, step],
            recv_sem=side_recv.at[which, way, step],
            device_id=other,
            device_id_type=MESH,
        )

    def beside(which, way, step):
        here = results[which].at[rows(which, 1 - core, way, piece(step + chips - 1, way))]
        return pltpu.make_async_remote_copy(
            src_ref=here, dst_ref=here, send_sem=side_send.at[which, way, step],
            recv_sem=side_recv.at[which, way, step], device_id=other, device_id_type=MESH,
        )

    def incoming(which, way, step):
        here = results[which].at[final_rows(which, way, step)]
        return pltpu.make_async_remote_copy(
            src_ref=here, dst_ref=here, send_sem=spread_send.at[which, way, step],
            recv_sem=spread_recv.at[which, way, step - 1], device_id=targets[way], device_id_type=MESH,
        )

    both = [(which, way) for way in range(2) for which in range(2)]

    def begin(step, carry):
        for which, way in both:
            load(which, way, step).start()
        return carry

    lax.fori_loop(0, chips, begin, 0)
    pl.semaphore_wait(barrier, 4)

    def begin_swap(step, carry):
        for which, way in both:
            swap(which, way, step).start()
        return carry

    lax.fori_loop(0, chips, begin_swap, 0)

    for which, way in both:
        load(which, way, 0).wait()
        swap(which, way, 0).wait_recv()
        run[which][way, 0] = own[which][way, 0] + pair[which][way, 0]
        pass_on(which, way, 0).start()

    def gather_step(step, carry):
        for which, way in both:
            load(which, way, step).wait()
            swap(which, way, step).wait_recv()
            pass_on(which, way, step - 1).wait_recv()
            run[which][way, step] = run[which][way, step] + own[which][way, step] + pair[which][way, step]

            @pl.when(step < chips - 1)
            def _():
                pass_on(which, way, step).start()

        return carry

    lax.fori_loop(1, chips, gather_step, 0)

    for way in range(2):
        cross(way).start()
        keep(0, way).start()
        spread(0, way, 0, True).start()
        aside(0, way, 0, True).start()
    for way in range(2):
        cross(way).wait()
        run_misc[way, chips - 1] = run_misc[way, chips - 1] + far_misc[way]
        keep(1, way).start()
        spread(1, way, 0, True).start()
        aside(1, way, 0, True).start()

    def spread_step(step, carry):
        for which, way in both:
            incoming(which, way, step).wait_recv()

            @pl.when(step < chips - 1)
            def _():
                spread(which, way, step).start()

            aside(which, way, step).start()
        return carry

    lax.fori_loop(1, chips, spread_step, 0)

    def finish(step, carry):
        for which, way in both:
            swap(which, way, step).wait_send()
            beside(which, way, step).wait_recv()
            aside(which, way, step).wait_send()

            @pl.when(step < chips - 1)
            def _():
                pass_on(which, way, step).wait_send()
                spread(which, way, step).wait_send()

        return carry

    lax.fori_loop(0, chips, finish, 0)
    for which, way in both:
        keep(which, way).wait()


def sum_over_dp(main, misc):
    chips = lax.axis_size("dp") // 2
    width = main.shape[1]
    sizes = (main.shape[0] // (4 * chips), misc.shape[0] // (4 * chips))
    slots = lambda which: pltpu.VMEM((2, chips, sizes[which], width), F32)
    sems = lambda *shape: pltpu.SemaphoreType.DMA(shape)
    return pl.pallas_call(
        functools.partial(sum_kernel, chips),
        in_specs=[pl.BlockSpec(memory_space=pl.ANY)] * 2,
        out_specs=[pl.BlockSpec(memory_space=pl.ANY)] * 2,
        out_shape=(jax.ShapeDtypeStruct(main.shape, F32), jax.ShapeDtypeStruct(misc.shape, F32)),
        scratch_shapes=[slots(0), slots(1)] * 3
        + [pltpu.VMEM((2, sizes[1], width), F32)]
        + [sems(2, 2, chips)] * 5
        + [sems(2)] * 2
        + [sems(2, 2)]
        + [sems(2, 2, chips)] * 4,
        compiler_params=pltpu.CompilerParams(
            collective_id=0, has_side_effects=True, vmem_limit_bytes=48 << 20
        ),
        name="sum_over_dp",
    )(main, misc)


def nothing_kernel(*refs):
    pass


def unwritten(shapes):
    return pl.pallas_call(
        nothing_kernel,
        out_specs=[pl.BlockSpec(memory_space=pl.ANY)] * len(shapes),
        out_shape=tuple(shapes),
        name="unwritten",
    )()


KEPT = ("n1", "query", "key", "value", "context", "marks", "mid", "n2", "active", "slope", "result", "latent")
BACK = (
    "out_low", "preact_low", "mid_grad", "branch_low", "query_grad", "key_grad", "value_grad",
    "entry", "latent_out", "sums_late", "sums_early", "head_late", "head_early",
)


class Rows:
    def __init__(self, side, edges, wide, unit, windows, query_mark, key_mark, weights, head):
        self.side, self.edges, self.wide, self.unit = side, edges, wide, unit
        self.windows, self.query_mark, self.key_mark = windows, query_mark, key_mark
        (
            self.attention_in, self.attention_out, self.hidden_in, self.hidden_out,
            self.gains, self.biases, self.hidden_bias,
        ) = weights
        (
            self.output_gain, self.head_bias, self.down, self.down_bias, self.down_turned,
            self.up, self.up_turned,
        ) = head
        self.rows, self.count, self.width = edges.shape
        self.hidden = self.hidden_in.shape[1]
        self.narrow = unit.shape[1]

    def kept_shapes(self):
        n, d, f = self.count, self.width, self.hidden
        table = dict(
            n1=(d, BF), query=(d, BF), key=(d, BF), value=(d, BF), context=(d, BF), marks=(d, BF),
            mid=(d, F32), n2=(d, BF), active=(f, BF), slope=(f, BF), latent=(self.narrow, F32),
        )
        shapes = {name: jax.ShapeDtypeStruct((n, size), kind) for name, (size, kind) in table.items()}
        shapes["result"] = jax.ShapeDtypeStruct((self.rows, n, d), F32)
        return shapes

    def back_shapes(self):
        n, d, f = self.count, self.width, self.hidden
        table = dict(
            out_low=(n, d, BF), preact_low=(n, f, BF), mid_grad=(n, d, F32), branch_low=(n, d, BF),
            query_grad=(n, d, BF), key_grad=(n, d, BF), value_grad=(n, d, BF),
            latent_out=(n, self.narrow, F32), sums_late=(16, d, F32), sums_early=(16, d, F32),
            head_late=(self.narrow, d, F32), head_early=(self.narrow, d, F32),
        )
        shapes = {name: jax.ShapeDtypeStruct((a, b), kind) for name, (a, b, kind) in table.items()}
        shapes["entry"] = jax.ShapeDtypeStruct((self.rows, n, d), F32)
        return shapes

    def side_spec(self):
        return pl.BlockSpec(memory_space=pltpu.SMEM)

    def tokens(self, array):
        return pl.BlockSpec((TOKENS, array.shape[1]), lambda step: (step, 0))

    def whole(self, array):
        return pl.BlockSpec(array.shape, lambda step: (0,) * len(array.shape))

    def entry_specs(self, row):
        steps = self.count // TOKENS
        return [
            pl.BlockSpec((None, TOKENS, self.width), lambda step: (row, step, 0)),
            pl.BlockSpec((TOKENS, self.wide.shape[1]), lambda step: (row * steps + step, 0)),
            self.whole(self.up),
            self.whole(self.head_bias),
        ]

    def row_spec(self, row):
        return pl.BlockSpec((None, TOKENS, self.width), lambda step: (row, step, 0))

    def unit_spec(self, row):
        steps = self.count // TOKENS
        return pl.BlockSpec((TOKENS, self.narrow), lambda step: (row * steps + step, 0))

    def call(self, kernel, in_specs, operands, outs, out_specs, name, scratch=(), rest=None, place=0):
        aliases = {}
        if rest is not None:
            inner, number = kernel, len(operands)

            def kernel(*refs):
                inner(*refs[:number], *refs[number + 1 :])

            in_specs, operands = in_specs + [pl.BlockSpec(memory_space=pl.ANY)], operands + (rest,)
            aliases = {number: place}
        return pl.pallas_call(
            kernel,
            input_output_aliases=aliases,
            grid=(self.count // TOKENS,),
            in_specs=in_specs,
            out_specs=out_specs,
            out_shape=tuple(outs),
            scratch_shapes=list(scratch),
            compiler_params=PARAMS,
            name=name,
        )(*operands)

    def attention_call(self, kernel, row, operands, outs, name, scratch=()):
        half = self.width // 2

        def spec(array):
            if array.ndim == 3:
                return pl.BlockSpec((None, self.count, array.shape[2]), lambda step, info: (row, 0, 0))
            return pl.BlockSpec((self.count, half), lambda step, info: (0, step))

        return pl.pallas_call(
            functools.partial(kernel, row=row),
            grid_spec=pltpu.PrefetchScalarGridSpec(
                num_scalar_prefetch=1,
                grid=(2,),
                in_specs=[spec(array) for array in operands],
                out_specs=[spec(array) for array in outs],
                scratch_shapes=list(scratch),
            ),
            out_shape=tuple(outs),
            compiler_params=PARAMS,
            name=name,
        )(self.windows, *operands)

    def forward(self, row, rest=None):
        shapes = self.kept_shapes()
        entry = (self.edges, self.wide, self.up, self.head_bias)
        kept = {}
        names = ("n1", "query", "key", "value")
        outs = self.call(
            project_kernel,
            [self.side_spec()] + self.entry_specs(row)
            + [self.whole(self.gains), self.whole(self.biases), self.whole(self.attention_in)],
            (self.side,) + entry + (self.gains, self.biases, self.attention_in),
            [shapes[name] for name in names],
            [self.tokens(shapes[name]) for name in names],
            "project",
        )
        kept.update(zip(names, outs))
        names = ("context", "marks")
        outs = self.attention_call(
            attend_kernel, row,
            (kept["query"], kept["key"], kept["value"], self.query_mark, self.key_mark),
            [shapes[name] for name in names],
            "attend",
        )
        kept.update(zip(names, outs))
        names = ("mid", "n2", "active", "slope", "result", "latent")
        consts = (
            self.attention_out, self.gains, self.biases, self.hidden_in, self.hidden_bias, self.hidden_out,
            self.output_gain, self.down, self.down_bias,
        )
        outs = self.call(
            hidden_kernel,
            [self.side_spec()] + self.entry_specs(row) + [self.tokens(kept["context"])]
            + [self.whole(array) for array in consts],
            (self.side,) + entry + (kept["context"],) + consts,
            [shapes[name] for name in names],
            [self.row_spec(row) if name == "result" else self.tokens(shapes[name]) for name in names],
            "hidden",
            rest=rest,
            place=names.index("result"),
        )
        kept.update(zip(names, outs))
        return kept

    def backward(self, row, kept, latent_in, rest=None):
        shapes = self.back_shapes()
        back = {}
        names = ("out_low", "preact_low", "mid_grad", "branch_low", "context_grad", "sums_late", "head_late")
        shapes["context_grad"] = shapes["out_low"]
        consts = (self.output_gain, self.head_bias, self.down, self.down_bias, self.down_turned, self.hidden_out)
        late = (self.gains, self.biases, self.attention_out)
        outs = self.call(
            tail_back_kernel,
            [self.side_spec(), self.row_spec(row), self.entry_specs(row)[0], self.unit_spec(row),
             self.tokens(latent_in)]
            + [self.whole(array) for array in consts]
            + [self.tokens(kept["slope"]), self.whole(self.hidden_in), self.tokens(kept["mid"])]
            + [self.whole(array) for array in late],
            (self.side, kept["result"], self.edges, self.unit, latent_in) + consts
            + (kept["slope"], self.hidden_in, kept["mid"]) + late,
            [shapes[name] for name in names],
            [self.tokens(shapes[name]) for name in names[:5]] + [self.whole(shapes[name]) for name in names[5:]],
            "tail_back",
            scratch=[pltpu.VMEM((TOKENS, self.width), F32)],
        )
        back.update(zip(names, outs))
        names = ("query_grad", "key_grad", "value_grad")
        half = self.width // 2
        outs = self.attention_call(
            attend_back_kernel, row,
            (kept["query"], kept["marks"], kept["key"], kept["value"], back.pop("context_grad"), kept["context"],
             self.key_mark),
            [shapes[name] for name in names],
            "attend_back",
            scratch=[
                pltpu.VMEM((self.count, half), BF),
                pltpu.VMEM((self.count, half), F32),
                pltpu.VMEM((self.count, half), F32),
            ],
        )
        back.update(zip(names, outs))
        names = ("entry", "latent_out", "sums_early", "head_early")
        grads = (back["query_grad"], back["key_grad"], back["value_grad"])
        outs = self.call(
            entry_back_kernel,
            [self.side_spec()] + self.entry_specs(row) + [self.unit_spec(row)]
            + [self.tokens(array) for array in grads]
            + [self.whole(self.attention_in), self.whole(self.gains), self.whole(self.biases),
               self.tokens(back["mid_grad"]), self.whole(self.up_turned)],
            (self.side, self.edges, self.wide, self.up, self.head_bias, self.unit) + grads
            + (self.attention_in, self.gains, self.biases, back["mid_grad"], self.up_turned),
            [shapes[name] for name in names],
            [self.row_spec(row), self.tokens(shapes["latent_out"])] + [self.whole(shapes[name]) for name in names[2:]],
            "entry_back",
            rest=rest,
        )
        back.update(zip(names, outs))
        return back


def pair_of(values, axis):
    return jnp.concatenate(split(values), axis)


def as_list(table, names):
    return [table[name] for name in names]


def marks_of(segments):
    lane = jnp.arange(128) & 63
    same = segments[..., None] == lane
    inside = lane < 4
    query_mark = jnp.where(inside & ~same, MASKED, 0.0).astype(BF)
    key_mark = jnp.where((inside & same) | ((lane > 3) & (lane < 7)), 1.0, 0.0).astype(BF)
    return query_mark, key_mark


def windows_of(segments):
    rows, count = segments.shape
    steps = count // WINDOW
    blocks = segments.reshape(rows, steps, WINDOW)
    least, most = blocks[:, :, 0], blocks[:, :, -1]
    meets = (most[:, :, None] >= least[:, None, :]) & (least[:, :, None] <= most[:, None, :])
    place = jnp.arange(steps)
    start = jnp.min(jnp.where(meets, place, steps), -1)
    stop = jnp.max(jnp.where(meets, place, -1), -1) + 1
    return jnp.stack([start, stop - start], -1).reshape(-1).astype(jnp.int32)


def on_device(
    boundary, segments, code_index, attention_in, attention_out, hidden_in, hidden_out, block_gains,
    block_biases, hidden_bias, output_gain, head_bias, down_weight, down_bias, up_weight, codebook,
):
    section = lax.axis_index("section")
    encoder = section == 0
    side = section.astype(jnp.int32)[None]
    edges = boundary[0]
    rows, count, width = edges.shape
    hidden = hidden_in.shape[2]
    index = code_index.reshape(-1)
    table_turned = codebook.T
    unit, wide = gather_codes(index, table_turned)
    query_mark, key_mark = marks_of(segments)
    up_high, up_low = split(up_weight)
    work = Rows(
        side, edges, wide, unit, windows_of(segments), query_mark, key_mark,
        (
            attention_in[0], attention_out[0], hidden_in[0], hidden_out[0], block_gains[0], block_biases[0],
            hidden_bias,
        ),
        (
            output_gain[None], head_bias, pair_of(down_weight, 1), down_bias[None], pair_of(down_weight.T, 0),
            jnp.concatenate([up_high, up_high, up_low, jnp.zeros_like(up_low)], 0), pair_of(up_weight.T, 1),
        ),
    )
    kept_shapes = as_list(work.kept_shapes(), KEPT)
    back_shapes = as_list(work.back_shapes(), BACK)
    book_out = book_shape(table_turned, width)
    weight_out = jax.ShapeDtypeStruct((2 * hidden + 4 * width, width), F32)
    quiet = jnp.zeros((count, unit.shape[1]), F32)
    first_kept = work.forward(0)

    def encoder_second():
        return as_list(work.forward(1), KEPT), list(unwritten(back_shapes))

    def decoder_first():
        return list(unwritten(kept_shapes)), as_list(work.backward(0, first_kept, quiet), BACK)

    kept_a, back_a = lax.cond(encoder, encoder_second, decoder_first)
    back_a = dict(zip(BACK, back_a))
    kept_a = dict(zip(KEPT, kept_a))
    latent_in = lax.ppermute(back_a["latent_out"], "section", [(1, 0)])

    def encoder_third():
        return list(unwritten(kept_shapes)), as_list(work.backward(0, first_kept, latent_in), BACK)

    def decoder_third():
        return as_list(work.forward(1, first_kept["result"]), KEPT), list(unwritten(back_shapes))

    kept_b, back_b = lax.cond(encoder, encoder_third, decoder_third)
    kept_b, back_b = dict(zip(KEPT, kept_b)), dict(zip(BACK, back_b))

    def encoder_fourth():
        book = scatter_codes(index, unit, (first_kept["latent"], kept_a["latent"]), table_turned, width)
        return list(unwritten(back_shapes)), weight_grads(first_kept, back_b), book

    def decoder_fourth():
        weights, book = unwritten([weight_out, book_out])
        return as_list(work.backward(1, kept_b, quiet), BACK), weights, book

    back_c, weights_c, book = lax.cond(encoder, encoder_fourth, decoder_fourth)
    back_c = dict(zip(BACK, back_c))
    latent_in_second = lax.ppermute(back_c["latent_out"], "section", [(1, 0)])

    def encoder_fifth():
        back = work.backward(1, kept_a, latent_in_second, back_b["entry"])
        total = weight_grads(kept_a, back, weights_c)
        late, early, down, unused = [back[name] + back_b[name] for name in BACK[-4:]]
        empty = jnp.zeros_like(down)
        none = jnp.zeros_like(jnp.concatenate([late, early]))
        return total, jnp.concatenate([book, down, empty, late, early, none]), back["entry"]

    def decoder_fifth():
        total = weight_grads(first_kept, back_a)
        total = weight_grads(kept_b, back_c, total)
        late, early, unused, up = [back_a[name] + back_c[name] for name in BACK[-4:]]
        empty = jnp.zeros_like(up)
        none = jnp.zeros_like(jnp.concatenate([late, early]))
        return total, jnp.concatenate([jnp.zeros(book.shape, F32), empty, up, none, late, early]), kept_b["result"]

    totals, misc, edge = lax.cond(encoder, encoder_fifth, decoder_fifth)
    totals, misc = sum_all(totals, misc)
    pieces, at = [], 0
    for size in (book_out.shape[0], unit.shape[1], unit.shape[1], 16, 16, 16, 16):
        pieces.append(misc[at : at + size])
        at += size
    book, down_grad, up_grad, first_late, first_early, second_late, second_early = pieces
    late = jnp.where(encoder, first_late, second_late)
    early = jnp.where(encoder, first_early, second_early)
    steps = hidden // width
    narrow = unit.shape[1]
    book = book.reshape(-1, narrow, width).transpose(1, 0, 2).reshape(table_turned.shape)
    tiles = totals.reshape(-1, width, width)

    def columns(part):
        return part.transpose(1, 0, 2).reshape(1, width, -1)

    return (
        edge[None],
        columns(tiles[2 * steps + 1 :]),
        tiles[2 * steps][None],
        columns(tiles[steps : 2 * steps]),
        totals[None, :hidden],
        jnp.stack([early[2], late[6]])[None],
        jnp.stack([early[0], early[1], late[5], early[3], late[7], late[4]])[None],
        late[:steps].reshape(1, hidden),
        first_late[8],
        jnp.stack([first_late[9], second_early[4]]),
        down_grad.T,
        first_late[10, :narrow],
        up_grad,
        book.T,
    )


def sum_all(main, misc):
    devices = lax.axis_size("dp")
    if devices < 4:
        return main, lax.psum(misc, "section")
    unit = 16 * devices
    extra = -misc.shape[0] % unit
    return sum_over_dp(main, jnp.pad(misc, ((0, extra), (0, 0))))


def solution(mesh):
    return jax.shard_map(
        on_device,
        mesh=mesh,
        in_specs=(
            P("section", "dp", None, None), P("dp", None), P("dp", None),
            P("section", None, None), P("section", None, None), P("section", None, None),
            P("section", None, None), P("section", None, None), P("section", None, None),
            P("section", None), P(), P(), P(), P(), P(), P(),
        ),
        out_specs=(
            P("section", "dp", None, None), P("section", None, None), P("section", None, None),
            P("section", None, None), P("section", None, None), P("section", None, None),
            P("section", None, None), P("section", None), P(), P(), P(), P(), P(), P(),
        ),
        check_vma=False,
    )
```

```python
import functools
import math

import jax
import jax.numpy as jnp
from jax import lax
from jax.experimental import pallas as pl
from jax.experimental.pallas import tpu as pltpu
from jax.sharding import PartitionSpec as P

HEAD = 64
BF = jnp.bfloat16
F32 = jnp.float32
LOG2E = math.log2(math.e)
NORM_EPS = 1e-06
MASKED = -1e30
GELU = 0.7978845608028654
CUBIC = 0.044715
NN = (((1,), (0,)), ((), ()))
NT = (((1,), (1,)), ((), ()))
TN = (((0,), (0,)), ((), ()))
TOKENS = 256
WINDOW = 256
PARAMS = pltpu.CompilerParams(vmem_limit_bytes=56 << 20)


def dot(a, b, dims):
    return lax.dot_general(a, b, dims, preferred_element_type=F32)


def lanes(shape):
    return lax.broadcasted_iota(jnp.int32, shape, 1)


def split(values):
    high = values.astype(BF)
    return high, (values - high.astype(F32)).astype(BF)


def dot3(left, right, dims):
    return dot(left[0], right[0], dims) + dot(left[0], right[1], dims) + dot(left[1], right[0], dims)


def norm_parts(values):
    center = values - jnp.mean(values, -1, keepdims=True)
    inverse = lax.rsqrt(jnp.mean(center * center, -1, keepdims=True) + NORM_EPS)
    return center * inverse, inverse


def norm_back(grad, gain, hat, inverse):
    scaled = grad * gain
    return inverse * (
        scaled
        - jnp.mean(scaled, -1, keepdims=True)
        - hat * jnp.mean(scaled * hat, -1, keepdims=True)
    )


def column_sum(values):
    return jnp.sum(values, 0, keepdims=True)


def code_kernel(index, table_turned, segments, unit, wide, query_mark, key_mark, table, raw):
    count = raw.shape[0]
    block = 512

    def turn(step, carry):
        start = pl.multiple_of(step * block, block)
        table[pl.ds(start, block), :] = table_turned[:, pl.ds(start, block)].T
        return carry

    lax.fori_loop(0, table.shape[0] // block, turn, 0)

    def some(step, carry):
        for inner in range(16):
            token = step * 16 + inner
            raw[pl.ds(token, 1), :] = table[pl.ds(index[token], 1), :]
        return carry

    lax.fori_loop(0, count // 16, some, 0)
    values = raw[...]
    values = values * lax.rsqrt(jnp.sum(values * values, -1, keepdims=True) + NORM_EPS)
    unit[...] = values
    high, low = split(values)
    wide[...] = jnp.concatenate([high, low, high, jnp.zeros_like(high)], 1)
    length = segments.shape[1]
    lane = lanes((length, 128)) & 63
    for row in range(segments.shape[0]):
        owner = jnp.broadcast_to(segments[row : row + 1, :], (128, length)).T
        same = owner == lane
        query_mark[row] = jnp.where((lane < 4) & jnp.logical_not(same), MASKED, 0.0).astype(BF)
        key_mark[row] = jnp.where(((lane < 4) & same) | ((lane > 3) & (lane < 7)), 1.0, 0.0).astype(BF)


def gather_codes(index, table_turned, segments):
    count, width = index.shape[0], table_turned.shape[0]
    vmem = pl.BlockSpec(memory_space=pltpu.VMEM)
    mark = jax.ShapeDtypeStruct(segments.shape + (128,), BF)
    return pl.pallas_call(
        code_kernel,
        in_specs=[pl.BlockSpec(memory_space=pltpu.SMEM), vmem, vmem],
        out_specs=[vmem] * 4,
        out_shape=(
            jax.ShapeDtypeStruct((count, width), F32),
            jax.ShapeDtypeStruct((count, 4 * width), BF),
            mark,
            mark,
        ),
        scratch_shapes=[pltpu.VMEM(table_turned.shape[::-1], F32), pltpu.VMEM((count, width), F32)],
        compiler_params=PARAMS,
        name="gather_codes",
    )(index, table_turned, segments)


def scatter_kernel(index, unit, latent_first, latent_second, table_turned, out, total, rows):
    count = rows.shape[0]
    width = unit.shape[1]
    half = count // 2
    total[...] = jnp.zeros_like(total)
    rows[:half, :] = 2.0 * (unit[:half, :] - latent_first[...])
    rows[half:, :] = 2.0 * (unit[half:, :] - latent_second[...])

    def some(step, carry):
        for inner in range(8):
            token = step * 8 + inner
            here = pl.ds(index[token], 1)
            total[here, :] = total[here, :] + rows[pl.ds(token, 1), :]
        return carry

    lax.fori_loop(0, count // 8, some, 0)
    block = out.shape[1]

    def back(step, carry):
        start = pl.multiple_of(step * block, block)
        values = table_turned[:, pl.ds(start, block)]
        grad = total[pl.ds(start, block), :].T
        inverse = lax.rsqrt(jnp.sum(values * values, 0, keepdims=True) + NORM_EPS)
        book = values * inverse
        out[pl.ds(pl.multiple_of(step * width, width), width), :] = inverse * (
            grad - book * jnp.sum(book * grad, 0, keepdims=True)
        )
        return carry

    lax.fori_loop(0, total.shape[0] // block, back, 0)


def book_shape(table_turned, width):
    return jax.ShapeDtypeStruct((table_turned.size // width, width), F32)


def scatter_codes(index, unit, latents, table_turned, width):
    return pl.pallas_call(
        scatter_kernel,
        in_specs=[pl.BlockSpec(memory_space=pltpu.SMEM)] + [pl.BlockSpec(memory_space=pltpu.VMEM)] * 4,
        out_specs=pl.BlockSpec(memory_space=pltpu.VMEM),
        out_shape=book_shape(table_turned, width),
        scratch_shapes=[pltpu.VMEM(table_turned.shape[::-1], F32), pltpu.VMEM(unit.shape, F32)],
        compiler_params=PARAMS,
        name="scatter_codes",
    )(index, unit, *latents, table_turned)


def entry_values(encoder, edge, wide, up, head_bias):
    high, low = split(up)
    parts = jnp.concatenate([high, high, low, jnp.zeros_like(low)], 0)
    return jnp.where(encoder, edge.astype(F32), dot(wide, parts, NN) + head_bias[1:2, :])


def project_kernel(side, edge, wide, up, head_bias, gains, biases, weight, n1, query, key, value):
    width = edge.shape[1]
    encoder = side[0] == 0
    values = entry_values(encoder, edge[...], wide[...], up[...], head_bias[...])
    hat, unused = norm_parts(values)
    normed = (hat * gains[0:1, :] + biases[3:4, :]).astype(BF)
    n1[...] = normed
    query[...] = (
        (dot(normed, weight[:, :width], NN) + biases[0:1, :]) * (LOG2E * HEAD ** (-0.5))
    ).astype(BF)
    key[...] = dot(normed, weight[:, width : 2 * width], NN).astype(BF)
    value[...] = (dot(normed, weight[:, 2 * width :], NN) + biases[1:2, :]).astype(BF)


def merge(low_half, left, right):
    return jnp.where(low_half, left, right)


def attend_kernel(windows, query, key, value, query_mark, key_mark, context, marks, *, row):
    count = query.shape[0]
    size = TOKENS
    pairs = query.shape[1] // 128
    low_query = lanes((size, 128)) < 64
    mark_lane = lanes((size, 128)) & 63

    def block(number, start, extent):
        rows = pl.ds(pl.multiple_of(number * size, size), size)
        keys = pl.ds(pl.multiple_of(start, WINDOW), extent)
        low_key = lanes((extent, 128)) < 64
        query_aug, key_aug = query_mark[rows, :], key_mark[keys, :]
        ones = jnp.ones((extent, 128), BF)
        scores = []
        for pair in range(pairs):
            here = slice(pair * 128, pair * 128 + 128)
            query_pair, key_pair = query[rows, here], key[keys, here]
            scores.append(
                dot(merge(low_query, query_pair, query_aug), merge(low_key, key_pair, key_aug), NT)
            )
            scores.append(
                dot(merge(low_query, query_aug, query_pair), merge(low_key, key_aug, key_pair), NT)
            )
        tops = [jnp.max(score, -1, keepdims=True) for score in scores]
        raised = [jnp.exp2(score - top).astype(BF) for score, top in zip(scores, tops)]
        for pair in range(pairs):
            here = slice(pair * 128, pair * 128 + 128)
            value_pair = value[keys, here]
            even = dot(raised[2 * pair], merge(low_key, value_pair, ones), NN)
            odd = dot(raised[2 * pair + 1], merge(low_key, ones, value_pair), NN)
            total = merge(low_query, odd, even)
            context[rows, here] = (
                merge(low_query, even, odd) / pltpu.roll(total, 64, 1)
            ).astype(BF)
            level = -(merge(low_query, tops[2 * pair + 1], tops[2 * pair]) + jnp.log2(total))
            first = level.astype(BF)
            rest = level - first.astype(F32)
            second, third = split(rest)
            marks[rows, here] = merge(
                mark_lane == 4, first, merge(mark_lane == 5, second, merge(mark_lane == 6, third, query_aug))
            )

    def one(number, carry):
        base = (row * (count // size) + number) * 2
        for_windows(windows[base], windows[base + 1], count, functools.partial(block, number))
        return carry

    lax.fori_loop(0, count // size, one, 0)


def for_windows(start, steps, count, run):
    extents = list(range(2 * WINDOW, count + 1, WINDOW))
    for position, extent in enumerate(extents):
        take = steps * WINDOW <= extent
        if position:
            take = take & (steps * WINDOW > extents[position - 1])

        @pl.when(take)
        def _():
            run(jnp.minimum(start * WINDOW, count - extent), extent)


def gelu_parts(values):
    square = values * values
    half = 0.5 + 0.5 * jnp.tanh(values * (GELU + (GELU * CUBIC) * square))
    active = values * half
    slope = half + active * (1.0 - half) * (2.0 * GELU + (6.0 * GELU * CUBIC) * square)
    return active, slope


def hidden_kernel(
    side, edge, wide, up, head_bias, context, weight_out, gains, biases, weight_in, hidden_bias,
    weight_last, output_gain, down, down_bias,
    mid, n2, active_out, slope_out, result, latent_out,
):
    encoder = side[0] == 0
    width = edge.shape[1]
    values = entry_values(encoder, edge[...], wide[...], up[...], head_bias[...])
    midway = values + (dot(context[...], weight_out[...], NN) + biases[2:3, :])
    mid[...] = midway
    hat, unused = norm_parts(midway)
    normed = (hat * gains[1:2, :] + biases[4:5, :]).astype(BF)
    n2[...] = normed
    total = midway + biases[5:6, :]
    chunk = 256
    for start in range(0, weight_in.shape[1], chunk):
        here = slice(start, start + chunk)
        active, slope = gelu_parts(dot(normed, weight_in[:, here], NN) + hidden_bias[0:1, here])
        active = active.astype(BF)
        active_out[:, here] = active
        slope_out[:, here] = slope.astype(BF)
        total = total + dot(active, weight_last[here, :], NN)
    result[...] = total

    @pl.when(encoder)
    def _():
        last_hat, unused = norm_parts(total)
        code = last_hat * output_gain[0:1, :] + head_bias[0:1, :]
        latent = code_product(code, down[...]) + down_bias[0:1, :]
        scale = lax.rsqrt(jnp.sum(latent * latent, -1, keepdims=True) + NORM_EPS)
        latent_out[...] = latent * scale


def code_product(values, weight):
    return dot3(split(values), split(weight), NT)


def tail_back_kernel(
    side, result, cotangent, unit, latent_in, output_gain, head_bias, down, down_bias,
    weight_last, slope, weight_in, mid, gains, biases, weight_out, *refs, adding
):
    before, refs = refs[: 2 * adding], refs[2 * adding :]
    out_low, preact_low, mid_grad, branch_low, context_grad, sums, head_weight, upstream = refs
    encoder = side[0] == 0
    width = result.shape[1]
    narrow = unit.shape[1]

    @pl.when(pl.program_id(0) == 0)
    def _():
        sums[...] = before[0][...] if adding else jnp.zeros_like(sums)
        head_weight[...] = before[1][...] if adding else jnp.zeros_like(head_weight)

    @pl.when(encoder)
    def _():
        hat, inverse = norm_parts(result[...])
        normed = hat * output_gain[0:1, :] + head_bias[0:1, :]
        latent = code_product(normed, down[...]) + down_bias[0:1, :]
        scale = lax.rsqrt(jnp.sum(latent * latent, -1, keepdims=True) + NORM_EPS)
        code = latent * scale
        code_grad = latent_in[...].T + 0.5 * (code - unit[...])
        latent_grad = scale * (code_grad - code * jnp.sum(code * code_grad, -1, keepdims=True))
        pieces = split(latent_grad)
        normed_grad = dot3(pieces, split(down[...]), NN)
        head_weight[...] += dot3(pieces, split(normed), TN)
        sums[8:9, :] += column_sum(normed_grad * hat)
        sums[9:10, :] += column_sum(normed_grad)
        sums[10:11, :narrow] += column_sum(latent_grad)
        upstream[...] = norm_back(normed_grad, output_gain[0:1, :], hat, inverse)

    @pl.when(jnp.logical_not(encoder))
    def _():
        upstream[...] = cotangent[...].astype(F32)

    above = upstream[...]
    low = above.astype(BF)
    out_low[...] = low
    sums[4:5, :] += column_sum(low.astype(F32))
    normed_grad = None
    chunk = 1024
    for start in range(0, weight_in.shape[1], chunk):
        here = slice(start, start + chunk)
        active_grad = dot(low, weight_last[here, :], NT)
        inner = (active_grad * slope[:, here].astype(F32)).astype(BF)
        preact_low[:, here] = inner
        part = column_sum(inner.astype(F32))
        for at in range(0, chunk, min(chunk, width)):
            row, lane = (start + at) // width, (start + at) % width
            size = min(chunk, width)
            sums[row : row + 1, lane : lane + size] += part[:, at : at + size]
        term = dot(inner, weight_in[:, here], NT)
        normed_grad = term if normed_grad is None else normed_grad + term
    hat, inverse = norm_parts(mid[...])
    sums[6:7, :] += column_sum(normed_grad * hat)
    sums[7:8, :] += column_sum(normed_grad)
    middle = above + norm_back(normed_grad, gains[1:2, :], hat, inverse)
    mid_grad[...] = middle
    branch = middle.astype(BF)
    branch_low[...] = branch
    sums[5:6, :] += column_sum(branch.astype(F32))
    context_grad[...] = dot(branch, weight_out[...], NT).astype(BF)


def attend_back_kernel(
    windows, query, marks, key, value, context_grad, context, key_mark,
    query_grad, key_grad, value_grad, grad_mark, key_total, value_total, *, row
):
    count = query.shape[0]
    size = TOKENS
    pairs = query.shape[1] // 128
    low_all = lanes((count, 128)) < 64
    low_query = lanes((size, 128)) < 64
    lane_all = lanes((count, 128)) & 63
    across = (
        lax.broadcasted_iota(jnp.int32, (128, 128), 0) // 64 != lanes((128, 128)) // 64
    ).astype(BF)
    zero = jnp.zeros((count, 128), BF)
    for pair in range(pairs):
        here = slice(pair * 128, pair * 128 + 128)
        product = split(context_grad[:, here].astype(F32) * context[:, here].astype(F32))
        level = -(dot(product[0], across, NN) + dot(product[1], across, NN))
        first = level.astype(BF)
        second, third = split(level - first.astype(F32))
        grad_mark[:, here] = merge(
            lane_all == 0, first, merge(lane_all == 1, second, merge(lane_all == 2, third, zero))
        )
    key_total[...] = jnp.zeros_like(key_total)
    value_total[...] = jnp.zeros_like(value_total)

    def block(number, start, extent):
        rows = pl.ds(pl.multiple_of(number * size, size), size)
        keys = pl.ds(pl.multiple_of(start, WINDOW), extent)
        low_key = lanes((extent, 128)) < 64
        key_aug = key_mark[keys, :]
        ones = jnp.where((lanes((extent, 128)) & 63) < 3, 1.0, 0.0).astype(BF)
        none = jnp.zeros((extent, 128), BF)
        for pair in range(pairs):
            here = slice(pair * 128, pair * 128 + 128)
            query_pair, key_pair, value_pair = query[rows, here], key[keys, here], value[keys, here]
            grad_pair, query_aug, grad_aug = context_grad[rows, here], marks[rows, here], grad_mark[rows, here]
            found = []
            for swap in (False, True):

                def both(low, left, right):
                    return merge(low, right, left) if swap else merge(low, left, right)

                scores = dot(both(low_key, key_pair, key_aug), both(low_query, query_pair, query_aug), NT)
                rise = dot(both(low_key, value_pair, ones), both(low_query, grad_pair, grad_aug), NT)
                chance = jnp.exp2(scores)
                score_grad = (chance * rise).astype(BF)
                found.append(
                    (
                        dot(score_grad, query_pair, NN),
                        dot(chance.astype(BF), grad_pair, NN),
                        dot(score_grad, both(low_key, key_pair, none), TN),
                    )
                )
            key_total[keys, here] += merge(low_key, found[0][0], found[1][0])
            value_total[keys, here] += merge(low_key, found[0][1], found[1][1])
            query_grad[rows, here] = ((found[0][2] + found[1][2]) * HEAD ** (-0.5)).astype(BF)

    def one(number, carry):
        base = (row * (count // size) + number) * 2
        for_windows(windows[base], windows[base + 1], count, functools.partial(block, number))
        return carry

    lax.fori_loop(0, count // size, one, 0)
    key_grad[...] = (key_total[...] * (1.0 / LOG2E)).astype(BF)
    value_grad[...] = value_total[...].astype(BF)


def entry_back_kernel(
    side, edge, wide, up, head_bias, unit, query_grad, key_grad, value_grad, weight, gains, biases,
    mid_grad, *refs, adding
):
    before, refs = refs[: 2 * adding], refs[2 * adding :]
    entry, latent_out, sums, head_weight = refs
    encoder = side[0] == 0
    width = edge.shape[1]
    narrow = unit.shape[1]

    @pl.when(pl.program_id(0) == 0)
    def _():
        sums[...] = before[0][...] if adding else jnp.zeros_like(sums)
        head_weight[...] = before[1][...] if adding else jnp.zeros_like(head_weight)

    values = entry_values(encoder, edge[...], wide[...], up[...], head_bias[...])
    normed_grad = (
        dot(query_grad[...], weight[:, :width], NT)
        + dot(key_grad[...], weight[:, width : 2 * width], NT)
        + dot(value_grad[...], weight[:, 2 * width :], NT)
    )
    hat, inverse = norm_parts(values)
    sums[0:1, :] += column_sum(query_grad[...].astype(F32))
    sums[1:2, :] += column_sum(value_grad[...].astype(F32))
    sums[2:3, :] += column_sum(normed_grad * hat)
    sums[3:4, :] += column_sum(normed_grad)
    total = mid_grad[...] + norm_back(normed_grad, gains[0:1, :], hat, inverse)
    entry[...] = total

    @pl.when(jnp.logical_not(encoder))
    def _():
        sums[4:5, :] += column_sum(total)
        latent_out[...] = code_product(total, up[...]).T
        head_weight[...] += dot3(split(unit[...]), split(total), TN)


def weight_kernel(*refs, turns, adding):
    operands, out = refs[:10], refs[-1]
    active, out_low, n2, preact_low, context, branch_low, n1 = operands[:7]
    step = pl.program_id(0)
    first, second, third = turns

    def put(left, right):
        value = dot(left[...], right[...], TN)
        out[...] = value + refs[10][...] if adding else value

    @pl.when(step < first)
    def _():
        put(active, out_low)

    @pl.when((step >= first) & (step < second))
    def _():
        put(n2, preact_low)

    @pl.when((step >= second) & (step < third))
    def _():
        put(context, branch_low)

    for place in range(3):

        @pl.when(step == third + place)
        def _():
            put(n1, operands[7 + place])


def weight_grads(kept, back, before=None):
    active, n2, context, n1 = kept["active"], kept["n2"], kept["context"], kept["n1"]
    out_low, preact_low, branch_low = back["out_low"], back["preact_low"], back["branch_low"]
    count, width = n1.shape
    first = active.shape[1] // width
    second = 2 * first
    third = second + 1
    whole = lambda step: (0, 0)
    full = pl.BlockSpec((count, width), whole)
    in_specs = [full] * 10
    in_specs[0] = pl.BlockSpec((count, width), lambda step: (0, jnp.minimum(step, first - 1)))
    in_specs[3] = pl.BlockSpec((count, width), lambda step: (0, jnp.clip(step - first, 0, first - 1)))
    out_spec = pl.BlockSpec((width, width), lambda step: (step, 0))
    operands = [active, out_low, n2, preact_low, context, branch_low, n1]
    operands += [back["query_grad"], back["key_grad"], back["value_grad"]]
    adding = before is not None
    if adding:
        operands.append(before)
        in_specs.append(out_spec)
    return pl.pallas_call(
        functools.partial(weight_kernel, turns=(first, second, third), adding=adding),
        grid=(third + 3,),
        in_specs=in_specs,
        out_specs=out_spec,
        out_shape=jax.ShapeDtypeStruct(((third + 3) * width, width), F32),
        input_output_aliases={10: 0} if adding else {},
        compiler_params=PARAMS,
        name="weight_grads",
    )(*operands)


MESH = pl.DeviceIdType.MESH


def ring_chip(position, chips):
    odd = position // (chips // 2)
    return (1 - odd) * (2 * position) + odd * (2 * (chips - 1 - position) + 1)


def sum_kernel(
    chips, main, misc, main_out, misc_out,
    own_main, own_misc, pair_main, pair_misc, run_main, run_misc, far_misc,
    load_sems, pair_send, pair_recv, run_send, run_recv, far_send, far_recv,
    keep_sems, spread_send, spread_recv, side_send, side_recv,
):
    place = lax.axis_index("dp")
    section = lax.axis_index("section")
    chip, core = place // 2, place % 2
    column, odd = chip // 2, chip % 2
    position = (1 - odd) * column + odd * (chips - 1 - column)
    other = {"dp": chip * 2 + (1 - core)}
    far = {"section": 1 - section}
    ahead = {"dp": ring_chip((position + 1) % chips, chips) * 2 + core}
    behind = {"dp": ring_chip((position + chips - 1) % chips, chips) * 2 + core}
    targets = (ahead, behind)
    sizes = (main.shape[0] // (4 * chips), misc.shape[0] // (4 * chips))
    sources, results = (main, misc), (main_out, misc_out)
    own, pair, run = (own_main, own_misc), (pair_main, pair_misc), (run_main, run_misc)

    barrier = pltpu.get_barrier_semaphore()
    for device in (other, far, ahead, behind):
        pl.semaphore_signal(barrier, inc=1, device_id=device, device_id_type=MESH)

    def piece(step, way):
        return (position + (2 * chips - step if way == 0 else step)) % chips

    def rows(which, half, way, number):
        size = sizes[which]
        return pl.ds(pl.multiple_of(((half * 2 + way) * chips + number) * size, 8), size)

    def load(which, way, step):
        return pltpu.make_async_copy(
            sources[which].at[rows(which, core, way, piece(step, way))],
            own[which].at[way, step],
            load_sems.at[which, way, step],
        )

    def swap(which, way, step):
        return pltpu.make_async_remote_copy(
            src_ref=sources[which].at[rows(which, 1 - core, way, piece(step, way))],
            dst_ref=pair[which].at[way, step],
            send_sem=pair_send.at[which, way, step],
            recv_sem=pair_recv.at[which, way, step],
            device_id=other,
            device_id_type=MESH,
        )

    def pass_on(which, way, step):
        return pltpu.make_async_remote_copy(
            src_ref=run[which].at[way, step],
            dst_ref=run[which].at[way, step + 1],
            send_sem=run_send.at[which, way, step],
            recv_sem=run_recv.at[which, way, step + 1],
            device_id=targets[way],
            device_id_type=MESH,
        )

    def cross(way):
        return pltpu.make_async_remote_copy(
            src_ref=run_misc.at[way, chips - 1],
            dst_ref=far_misc.at[way],
            send_sem=far_send.at[way],
            recv_sem=far_recv.at[way],
            device_id=far,
            device_id_type=MESH,
        )

    def final_rows(which, way, step):
        return rows(which, core, way, piece(step + chips - 1, way))

    def keep(which, way):
        return pltpu.make_async_copy(
            run[which].at[way, chips - 1], results[which].at[final_rows(which, way, 0)], keep_sems.at[which, way]
        )

    def spread(which, way, step, first=False):
        here = results[which].at[final_rows(which, way, step)]
        return pltpu.make_async_remote_copy(
            src_ref=run[which].at[way, chips - 1] if first else here,
            dst_ref=here,
            send_sem=spread_send.at[which, way, step],
            recv_sem=spread_recv.at[which, way, step],
            device_id=targets[way],
            device_id_type=MESH,
        )

    def aside(which, way, step, first=False):
        here = results[which].at[final_rows(which, way, step)]
        return pltpu.make_async_remote_copy(
            src_ref=run[which].at[way, chips - 1] if first else here,
            dst_ref=here,
            send_sem=side_send.at[which, way, step],
            recv_sem=side_recv.at[which, way, step],
            device_id=other,
            device_id_type=MESH,
        )

    def beside(which, way, step):
        here = results[which].at[rows(which, 1 - core, way, piece(step + chips - 1, way))]
        return pltpu.make_async_remote_copy(
            src_ref=here, dst_ref=here, send_sem=side_send.at[which, way, step],
            recv_sem=side_recv.at[which, way, step], device_id=other, device_id_type=MESH,
        )

    def incoming(which, way, step):
        here = results[which].at[final_rows(which, way, step)]
        return pltpu.make_async_remote_copy(
            src_ref=here, dst_ref=here, send_sem=spread_send.at[which, way, step],
            recv_sem=spread_recv.at[which, way, step - 1], device_id=targets[way], device_id_type=MESH,
        )

    both = [(which, way) for way in range(2) for which in range(2)]

    def begin(step, carry):
        for which, way in both:
            load(which, way, step).start()
        return carry

    lax.fori_loop(0, chips, begin, 0)
    pl.semaphore_wait(barrier, 4)

    def begin_swap(step, carry):
        for which, way in both:
            swap(which, way, step).start()
        return carry

    lax.fori_loop(0, chips, begin_swap, 0)

    for which, way in both:
        load(which, way, 0).wait()
        swap(which, way, 0).wait_recv()
        run[which][way, 0] = own[which][way, 0] + pair[which][way, 0]
        pass_on(which, way, 0).start()

    def gather_step(step, carry):
        for which, way in both:
            load(which, way, step).wait()
            swap(which, way, step).wait_recv()
            pass_on(which, way, step - 1).wait_recv()
            run[which][way, step] = run[which][way, step] + own[which][way, step] + pair[which][way, step]

            @pl.when(step < chips - 1)
            def _():
                pass_on(which, way, step).start()

        return carry

    lax.fori_loop(1, chips, gather_step, 0)

    for way in range(2):
        cross(way).start()
        keep(0, way).start()
        spread(0, way, 0, True).start()
        aside(0, way, 0, True).start()
    for way in range(2):
        cross(way).wait()
        run_misc[way, chips - 1] = run_misc[way, chips - 1] + far_misc[way]
        keep(1, way).start()
        spread(1, way, 0, True).start()
        aside(1, way, 0, True).start()

    def spread_step(step, carry):
        for which, way in both:
            incoming(which, way, step).wait_recv()

            @pl.when(step < chips - 1)
            def _():
                spread(which, way, step).start()

            aside(which, way, step).start()
        return carry

    lax.fori_loop(1, chips, spread_step, 0)

    def finish(step, carry):
        for which, way in both:
            swap(which, way, step).wait_send()
            beside(which, way, step).wait_recv()
            aside(which, way, step).wait_send()

            @pl.when(step < chips - 1)
            def _():
                pass_on(which, way, step).wait_send()
                spread(which, way, step).wait_send()

        return carry

    lax.fori_loop(0, chips, finish, 0)
    for which, way in both:
        keep(which, way).wait()


def head_kernel(side, book, down, up, late, early, out):
    encoder = side[0] == 0
    out[...] = jnp.zeros_like(out)
    size = book.shape[0]
    narrow = down.shape[0]
    at = size + 2 * narrow

    @pl.when(encoder)
    def _():
        out[:size, :] = book[...]
        out[size : size + narrow, :] = down[...]
        out[at : at + 16, :] = late[...]
        out[at + 16 : at + 32, :] = early[...]

    @pl.when(jnp.logical_not(encoder))
    def _():
        out[size + narrow : at, :] = up[...]
        out[at + 32 : at + 48, :] = late[...]
        out[at + 48 : at + 64, :] = early[...]


def gather_head(side, book, down, up, late, early):
    rows = book.shape[0] + 2 * down.shape[0] + 64
    unit = 16 * lax.axis_size("dp")
    vmem = pl.BlockSpec(memory_space=pltpu.VMEM)
    return pl.pallas_call(
        head_kernel,
        in_specs=[pl.BlockSpec(memory_space=pltpu.SMEM)] + [vmem] * 5,
        out_specs=vmem,
        out_shape=jax.ShapeDtypeStruct((rows + (-rows % unit), book.shape[1]), F32),
        compiler_params=PARAMS,
        name="gather_head",
    )(side, book, down, up, late, early)


def unpack_kernel(main, misc, hidden_out, hidden_in, attention_out, attention_in, book, sems):
    width = main.shape[1]
    narrow = book.shape[0]
    steps = hidden_out.shape[0] // width
    copies = [(main.at[pl.ds(0, steps * width)], hidden_out)]
    at = steps
    for out, count in ((hidden_in, steps), (attention_out, 1), (attention_in, 3)):
        for number in range(count):
            copies.append((main.at[pl.ds((at + number) * width, width)], out.at[:, pl.ds(number * width, width)]))
        at += count
    for number in range(book.shape[1] // width):
        copies.append((misc.at[pl.ds(number * narrow, narrow)], book.at[:, pl.ds(number * width, width)]))
    copies = [pltpu.make_async_copy(*pair, sems.at[number]) for number, pair in enumerate(copies)]
    for copy in copies:
        copy.start()
    for copy in copies:
        copy.wait()


def unpack(main, misc, hidden, table_turned):
    width = main.shape[1]
    shapes = ((hidden, width), (width, hidden), (width, width), (width, 3 * width), table_turned.shape)
    count = 5 + hidden // width + table_turned.shape[1] // width
    return pl.pallas_call(
        unpack_kernel,
        in_specs=[pl.BlockSpec(memory_space=pl.ANY)] * 2,
        out_specs=[pl.BlockSpec(memory_space=pl.ANY)] * 5,
        out_shape=tuple(jax.ShapeDtypeStruct(shape, F32) for shape in shapes),
        scratch_shapes=[pltpu.SemaphoreType.DMA((count,))],
        compiler_params=PARAMS,
        name="unpack",
    )(main, misc)


def sum_over_dp(main, misc):
    chips = lax.axis_size("dp") // 2
    width = main.shape[1]
    sizes = (main.shape[0] // (4 * chips), misc.shape[0] // (4 * chips))
    slots = lambda which: pltpu.VMEM((2, chips, sizes[which], width), F32)
    sems = lambda *shape: pltpu.SemaphoreType.DMA(shape)
    return pl.pallas_call(
        functools.partial(sum_kernel, chips),
        in_specs=[pl.BlockSpec(memory_space=pl.ANY)] * 2,
        out_specs=[pl.BlockSpec(memory_space=pl.ANY)] * 2,
        out_shape=(jax.ShapeDtypeStruct(main.shape, F32), jax.ShapeDtypeStruct(misc.shape, F32)),
        scratch_shapes=[slots(0), slots(1)] * 3
        + [pltpu.VMEM((2, sizes[1], width), F32)]
        + [sems(2, 2, chips)] * 5
        + [sems(2)] * 2
        + [sems(2, 2)]
        + [sems(2, 2, chips)] * 4,
        compiler_params=pltpu.CompilerParams(
            collective_id=0, has_side_effects=True, vmem_limit_bytes=48 << 20
        ),
        name="sum_over_dp",
    )(main, misc)


def nothing_kernel(*refs):
    pass


def unwritten(shapes):
    return pl.pallas_call(
        nothing_kernel,
        out_specs=[pl.BlockSpec(memory_space=pl.ANY)] * len(shapes),
        out_shape=tuple(shapes),
        name="unwritten",
    )()


KEPT = ("n1", "query", "key", "value", "context", "marks", "mid", "n2", "active", "slope", "result", "latent")
BACK = (
    "out_low", "preact_low", "mid_grad", "branch_low", "query_grad", "key_grad", "value_grad",
    "entry", "latent_out", "sums_late", "sums_early", "head_late", "head_early",
)


class Rows:
    def __init__(self, side, edges, wide, unit, windows, query_mark, key_mark, weights, head):
        self.side, self.edges, self.wide, self.unit = side, edges, wide, unit
        self.windows, self.query_mark, self.key_mark = windows, query_mark, key_mark
        (
            self.attention_in, self.attention_out, self.hidden_in, self.hidden_out,
            self.gains, self.biases, self.hidden_bias,
        ) = weights
        (
            self.output_gain, self.head_bias, self.down, self.down_bias, self.up,
        ) = head
        self.rows, self.count, self.width = edges.shape
        self.hidden = self.hidden_in.shape[1]
        self.narrow = unit.shape[1]

    def kept_shapes(self):
        n, d, f = self.count, self.width, self.hidden
        table = dict(
            n1=(d, BF), query=(d, BF), key=(d, BF), value=(d, BF), context=(d, BF), marks=(d, BF),
            mid=(d, F32), n2=(d, BF), active=(f, BF), slope=(f, BF), latent=(self.narrow, F32),
        )
        shapes = {name: jax.ShapeDtypeStruct((n, size), kind) for name, (size, kind) in table.items()}
        shapes["result"] = jax.ShapeDtypeStruct((self.rows, n, d), F32)
        return shapes

    def back_shapes(self):
        n, d, f = self.count, self.width, self.hidden
        table = dict(
            out_low=(n, d, BF), preact_low=(n, f, BF), mid_grad=(n, d, F32), branch_low=(n, d, BF),
            query_grad=(n, d, BF), key_grad=(n, d, BF), value_grad=(n, d, BF),
            latent_out=(self.narrow, n, F32), sums_late=(16, d, F32), sums_early=(16, d, F32),
            head_late=(self.narrow, d, F32), head_early=(self.narrow, d, F32),
        )
        shapes = {name: jax.ShapeDtypeStruct((a, b), kind) for name, (a, b, kind) in table.items()}
        shapes["entry"] = jax.ShapeDtypeStruct((self.rows, n, d), F32)
        return shapes

    def turned(self, array):
        return pl.BlockSpec((array.shape[0], TOKENS), lambda step: (0, step))

    def side_spec(self):
        return pl.BlockSpec(memory_space=pltpu.SMEM)

    def tokens(self, array):
        return pl.BlockSpec((TOKENS, array.shape[1]), lambda step: (step, 0))

    def whole(self, array):
        return pl.BlockSpec(array.shape, lambda step: (0,) * len(array.shape))

    def entry_specs(self, row):
        steps = self.count // TOKENS
        return [
            pl.BlockSpec((None, TOKENS, self.width), lambda step: (row, step, 0)),
            pl.BlockSpec((TOKENS, self.wide.shape[1]), lambda step: (row * steps + step, 0)),
            self.whole(self.up),
            self.whole(self.head_bias),
        ]

    def row_spec(self, row):
        return pl.BlockSpec((None, TOKENS, self.width), lambda step: (row, step, 0))

    def unit_spec(self, row):
        steps = self.count // TOKENS
        return pl.BlockSpec((TOKENS, self.narrow), lambda step: (row * steps + step, 0))

    def call(self, kernel, in_specs, operands, outs, out_specs, name, scratch=(), rest=None, place=0):
        aliases = {}
        if rest is not None:
            inner, number = kernel, len(operands)

            def kernel(*refs):
                inner(*refs[:number], *refs[number + 1 :])

            in_specs, operands = in_specs + [pl.BlockSpec(memory_space=pl.ANY)], operands + (rest,)
            aliases = {number: place}
        return pl.pallas_call(
            kernel,
            input_output_aliases=aliases,
            grid=(self.count // TOKENS,),
            in_specs=in_specs,
            out_specs=out_specs,
            out_shape=tuple(outs),
            scratch_shapes=list(scratch),
            compiler_params=PARAMS,
            name=name,
        )(*operands)

    def attention_call(self, kernel, row, operands, outs, name, scratch=()):
        half = self.width // 2

        def spec(array):
            if array.ndim == 3:
                return pl.BlockSpec((None, self.count, array.shape[2]), lambda step, info: (row, 0, 0))
            return pl.BlockSpec((self.count, half), lambda step, info: (0, step))

        return pl.pallas_call(
            functools.partial(kernel, row=row),
            grid_spec=pltpu.PrefetchScalarGridSpec(
                num_scalar_prefetch=1,
                grid=(2,),
                in_specs=[spec(array) for array in operands],
                out_specs=[spec(array) for array in outs],
                scratch_shapes=list(scratch),
            ),
            out_shape=tuple(outs),
            compiler_params=PARAMS,
            name=name,
        )(self.windows, *operands)

    def forward(self, row, rest=None):
        shapes = self.kept_shapes()
        entry = (self.edges, self.wide, self.up, self.head_bias)
        kept = {}
        names = ("n1", "query", "key", "value")
        outs = self.call(
            project_kernel,
            [self.side_spec()] + self.entry_specs(row)
            + [self.whole(self.gains), self.whole(self.biases), self.whole(self.attention_in)],
            (self.side,) + entry + (self.gains, self.biases, self.attention_in),
            [shapes[name] for name in names],
            [self.tokens(shapes[name]) for name in names],
            "project",
        )
        kept.update(zip(names, outs))
        names = ("context", "marks")
        outs = self.attention_call(
            attend_kernel, row,
            (kept["query"], kept["key"], kept["value"], self.query_mark, self.key_mark),
            [shapes[name] for name in names],
            "attend",
        )
        kept.update(zip(names, outs))
        names = ("mid", "n2", "active", "slope", "result", "latent")
        consts = (
            self.attention_out, self.gains, self.biases, self.hidden_in, self.hidden_bias, self.hidden_out,
            self.output_gain, self.down, self.down_bias,
        )
        outs = self.call(
            hidden_kernel,
            [self.side_spec()] + self.entry_specs(row) + [self.tokens(kept["context"])]
            + [self.whole(array) for array in consts],
            (self.side,) + entry + (kept["context"],) + consts,
            [shapes[name] for name in names],
            [self.row_spec(row) if name == "result" else self.tokens(shapes[name]) for name in names],
            "hidden",
            rest=rest,
            place=names.index("result"),
        )
        kept.update(zip(names, outs))
        return kept

    def backward(self, row, kept, latent_in, former=None, rest=None):
        shapes = self.back_shapes()
        prior = () if former is None else (former["sums_late"], former["head_late"])
        adding = int(former is not None)
        back = {}
        names = ("out_low", "preact_low", "mid_grad", "branch_low", "context_grad", "sums_late", "head_late")
        shapes["context_grad"] = shapes["out_low"]
        consts = (self.output_gain, self.head_bias, self.down, self.down_bias, self.hidden_out)
        late = (self.gains, self.biases, self.attention_out)
        outs = self.call(
            functools.partial(tail_back_kernel, adding=adding),
            [self.side_spec(), self.row_spec(row), self.entry_specs(row)[0], self.unit_spec(row),
             self.turned(latent_in)]
            + [self.whole(array) for array in consts]
            + [self.tokens(kept["slope"]), self.whole(self.hidden_in), self.tokens(kept["mid"])]
            + [self.whole(array) for array in late + prior],
            (self.side, kept["result"], self.edges, self.unit, latent_in) + consts
            + (kept["slope"], self.hidden_in, kept["mid"]) + late + prior,
            [shapes[name] for name in names],
            [self.tokens(shapes[name]) for name in names[:5]] + [self.whole(shapes[name]) for name in names[5:]],
            "tail_back",
            scratch=[pltpu.VMEM((TOKENS, self.width), F32)],
        )
        back.update(zip(names, outs))
        names = ("query_grad", "key_grad", "value_grad")
        half = self.width // 2
        outs = self.attention_call(
            attend_back_kernel, row,
            (kept["query"], kept["marks"], kept["key"], kept["value"], back.pop("context_grad"), kept["context"],
             self.key_mark),
            [shapes[name] for name in names],
            "attend_back",
            scratch=[
                pltpu.VMEM((self.count, half), BF),
                pltpu.VMEM((self.count, half), F32),
                pltpu.VMEM((self.count, half), F32),
            ],
        )
        back.update(zip(names, outs))
        names = ("entry", "latent_out", "sums_early", "head_early")
        prior = () if former is None else (former["sums_early"], former["head_early"])
        grads = (back["query_grad"], back["key_grad"], back["value_grad"])
        outs = self.call(
            functools.partial(entry_back_kernel, adding=adding),
            [self.side_spec()] + self.entry_specs(row) + [self.unit_spec(row)]
            + [self.tokens(array) for array in grads]
            + [self.whole(self.attention_in), self.whole(self.gains), self.whole(self.biases),
               self.tokens(back["mid_grad"])] + [self.whole(array) for array in prior],
            (self.side, self.edges, self.wide, self.up, self.head_bias, self.unit) + grads
            + (self.attention_in, self.gains, self.biases, back["mid_grad"]) + prior,
            [shapes[name] for name in names],
            [self.row_spec(row), self.turned(shapes["latent_out"])] + [self.whole(shapes[name]) for name in names[2:]],
            "entry_back",
            rest=rest,
        )
        back.update(zip(names, outs))
        return back


def as_list(table, names):
    return [table[name] for name in names]


def windows_of(segments):
    rows, count = segments.shape
    steps = count // WINDOW
    blocks = segments.reshape(rows, steps, WINDOW)
    least, most = blocks[:, :, 0], blocks[:, :, -1]
    meets = (most[:, :, None] >= least[:, None, :]) & (least[:, :, None] <= most[:, None, :])
    place = jnp.arange(steps)
    start = jnp.min(jnp.where(meets, place, steps), -1)
    stop = jnp.max(jnp.where(meets, place, -1), -1) + 1
    return jnp.stack([start, stop - start], -1).reshape(-1).astype(jnp.int32)


def on_device(
    boundary, segments, code_index, attention_in, attention_out, hidden_in, hidden_out, block_gains,
    block_biases, hidden_bias, output_gain, head_bias, down_weight, down_bias, up_weight, codebook,
):
    section = lax.axis_index("section")
    encoder = section == 0
    side = section.astype(jnp.int32)[None]
    edges = boundary[0]
    rows, count, width = edges.shape
    hidden = hidden_in.shape[2]
    index = code_index.reshape(-1)
    table_turned = codebook.T
    unit, wide, query_mark, key_mark = gather_codes(index, table_turned, segments)
    work = Rows(
        side, edges, wide, unit, windows_of(segments), query_mark, key_mark,
        (
            attention_in[0], attention_out[0], hidden_in[0], hidden_out[0], block_gains[0], block_biases[0],
            hidden_bias,
        ),
        (
            output_gain[None], head_bias, down_weight.T, down_bias[None], up_weight,
        ),
    )
    kept_shapes = as_list(work.kept_shapes(), KEPT)
    back_shapes = as_list(work.back_shapes(), BACK)
    book_out = book_shape(table_turned, width)
    weight_out = jax.ShapeDtypeStruct((2 * hidden + 4 * width, width), F32)
    quiet = jnp.zeros((unit.shape[1], count), F32)
    first_kept = work.forward(0)

    def encoder_second():
        return as_list(work.forward(1), KEPT), list(unwritten(back_shapes))

    def decoder_first():
        return list(unwritten(kept_shapes)), as_list(work.backward(0, first_kept, quiet), BACK)

    kept_a, back_a = lax.cond(encoder, encoder_second, decoder_first)
    back_a = dict(zip(BACK, back_a))
    kept_a = dict(zip(KEPT, kept_a))
    latent_in = lax.ppermute(back_a["latent_out"], "section", [(1, 0)])

    def encoder_third():
        return list(unwritten(kept_shapes)), as_list(work.backward(0, first_kept, latent_in), BACK)

    def decoder_third():
        return as_list(work.forward(1, first_kept["result"]), KEPT), list(unwritten(back_shapes))

    kept_b, back_b = lax.cond(encoder, encoder_third, decoder_third)
    kept_b, back_b = dict(zip(KEPT, kept_b)), dict(zip(BACK, back_b))

    def encoder_fourth():
        book = scatter_codes(index, unit, (first_kept["latent"], kept_a["latent"]), table_turned, width)
        return list(unwritten(back_shapes)), weight_grads(first_kept, back_b), book

    def decoder_fourth():
        weights, book = unwritten([weight_out, book_out])
        return as_list(work.backward(1, kept_b, quiet, back_a), BACK), weights, book

    back_c, weights_c, book = lax.cond(encoder, encoder_fourth, decoder_fourth)
    back_c = dict(zip(BACK, back_c))
    latent_in_second = lax.ppermute(back_c["latent_out"], "section", [(1, 0)])

    def encoder_fifth():
        back = work.backward(1, kept_a, latent_in_second, back_b, back_b["entry"])
        total = weight_grads(kept_a, back, weights_c)
        return total, as_list(back, BACK[-4:]), back["entry"]

    def decoder_fifth():
        total = weight_grads(first_kept, back_a)
        total = weight_grads(kept_b, back_c, total)
        return total, as_list(back_c, BACK[-4:]), kept_b["result"]

    totals, (late, early, down, up), edge = lax.cond(encoder, encoder_fifth, decoder_fifth)
    totals, misc = sum_all(totals, gather_head(side, book, down, up, late, early))
    hidden_out_grad, hidden_in_grad, attention_out_grad, attention_in_grad, book = unpack(
        totals, misc, hidden, table_turned
    )
    narrow = unit.shape[1]
    pieces, at = [], book_out.shape[0]
    for size in (narrow, narrow, 16, 16, 16, 16):
        pieces.append(misc[at : at + size])
        at += size
    down_grad, up_grad, first_late, first_early, second_late, second_early = pieces
    late = jnp.where(encoder, first_late, second_late)
    early = jnp.where(encoder, first_early, second_early)
    return (
        edge[None],
        attention_in_grad[None],
        attention_out_grad[None],
        hidden_in_grad[None],
        hidden_out_grad[None],
        jnp.stack([early[2], late[6]])[None],
        jnp.stack([early[0], early[1], late[5], early[3], late[7], late[4]])[None],
        late[: hidden // width].reshape(1, hidden),
        first_late[8],
        jnp.stack([first_late[9], second_early[4]]),
        down_grad.T,
        first_late[10, :narrow],
        up_grad,
        book.T,
    )


def sum_all(main, misc):
    if lax.axis_size("dp") < 4:
        return main, lax.psum(misc, "section")
    return sum_over_dp(main, misc)


def solution(mesh):
    return jax.shard_map(
        on_device,
        mesh=mesh,
        in_specs=(
            P("section", "dp", None, None), P("dp", None), P("dp", None),
            P("section", None, None), P("section", None, None), P("section", None, None),
            P("section", None, None), P("section", None, None), P("section", None, None),
            P("section", None), P(), P(), P(), P(), P(), P(),
        ),
        out_specs=(
            P("section", "dp", None, None), P("section", None, None), P("section", None, None),
            P("section", None, None), P("section", None, None), P("section", None, None),
            P("section", None, None), P("section", None), P(), P(), P(), P(), P(), P(),
        ),
        check_vma=False,
    )
```

```python
import functools
import math

import jax
import jax.numpy as jnp
from jax import lax
from jax.experimental import pallas as pl
from jax.experimental.pallas import tpu as pltpu
from jax.sharding import PartitionSpec as P

HEAD = 64
BF = jnp.bfloat16
F32 = jnp.float32
LOG2E = math.log2(math.e)
NORM_EPS = 1e-06
MASKED = -1e30
GELU = 0.7978845608028654
CUBIC = 0.044715
NN = (((1,), (0,)), ((), ()))
NT = (((1,), (1,)), ((), ()))
TN = (((0,), (0,)), ((), ()))
TOKENS = 256
WINDOW = 256
PARAMS = pltpu.CompilerParams(vmem_limit_bytes=56 << 20)


def dot(a, b, dims):
    return lax.dot_general(a, b, dims, preferred_element_type=F32)


def lanes(shape):
    return lax.broadcasted_iota(jnp.int32, shape, 1)


def split(values):
    high = values.astype(BF)
    return high, (values - high.astype(F32)).astype(BF)


def dot3(left, right, dims):
    return dot(left[0], right[0], dims) + dot(left[0], right[1], dims) + dot(left[1], right[0], dims)


def norm_parts(values):
    center = values - jnp.mean(values, -1, keepdims=True)
    inverse = lax.rsqrt(jnp.mean(center * center, -1, keepdims=True) + NORM_EPS)
    return center * inverse, inverse


def norm_back(grad, gain, hat, inverse):
    scaled = grad * gain
    return inverse * (
        scaled
        - jnp.mean(scaled, -1, keepdims=True)
        - hat * jnp.mean(scaled * hat, -1, keepdims=True)
    )


def column_sum(values):
    return jnp.sum(values, 0, keepdims=True)


def code_kernel(index, table_turned, segments, unit, wide, query_mark, key_mark, table, raw):
    count = raw.shape[0]
    block = 512

    def turn(step, carry):
        start = pl.multiple_of(step * block, block)
        table[pl.ds(start, block), :] = table_turned[:, pl.ds(start, block)].T
        return carry

    lax.fori_loop(0, table.shape[0] // block, turn, 0)

    def some(step, carry):
        for inner in range(16):
            token = step * 16 + inner
            raw[pl.ds(token, 1), :] = table[pl.ds(index[token], 1), :]
        return carry

    lax.fori_loop(0, count // 16, some, 0)
    values = raw[...]
    values = values * lax.rsqrt(jnp.sum(values * values, -1, keepdims=True) + NORM_EPS)
    unit[...] = values
    high, low = split(values)
    wide[...] = jnp.concatenate([high, low, high, jnp.zeros_like(high)], 1)
    length = segments.shape[1]
    lane = lanes((length, 128)) & 63
    for row in range(segments.shape[0]):
        owner = jnp.broadcast_to(segments[row : row + 1, :], (128, length)).T
        same = owner == lane
        query_mark[row] = jnp.where((lane < 4) & jnp.logical_not(same), MASKED, 0.0).astype(BF)
        key_mark[row] = jnp.where(((lane < 4) & same) | ((lane > 3) & (lane < 7)), 1.0, 0.0).astype(BF)


def gather_codes(index, table_turned, segments):
    count, width = index.shape[0], table_turned.shape[0]
    vmem = pl.BlockSpec(memory_space=pltpu.VMEM)
    mark = jax.ShapeDtypeStruct(segments.shape + (128,), BF)
    return pl.pallas_call(
        code_kernel,
        in_specs=[pl.BlockSpec(memory_space=pltpu.SMEM), vmem, vmem],
        out_specs=[vmem] * 4,
        out_shape=(
            jax.ShapeDtypeStruct((count, width), F32),
            jax.ShapeDtypeStruct((count, 4 * width), BF),
            mark,
            mark,
        ),
        scratch_shapes=[pltpu.VMEM(table_turned.shape[::-1], F32), pltpu.VMEM((count, width), F32)],
        compiler_params=PARAMS,
        name="gather_codes",
    )(index, table_turned, segments)


def scatter_kernel(index, unit, latent_first, latent_second, table_turned, out, total, rows):
    count = rows.shape[0]
    width = unit.shape[1]
    half = count // 2
    total[...] = jnp.zeros_like(total)
    rows[:half, :] = 2.0 * (unit[:half, :] - latent_first[...])
    rows[half:, :] = 2.0 * (unit[half:, :] - latent_second[...])

    def some(step, carry):
        for inner in range(8):
            token = step * 8 + inner
            here = pl.ds(index[token], 1)
            total[here, :] = total[here, :] + rows[pl.ds(token, 1), :]
        return carry

    lax.fori_loop(0, count // 8, some, 0)
    block = out.shape[1]

    def back(step, carry):
        start = pl.multiple_of(step * block, block)
        values = table_turned[:, pl.ds(start, block)]
        grad = total[pl.ds(start, block), :].T
        inverse = lax.rsqrt(jnp.sum(values * values, 0, keepdims=True) + NORM_EPS)
        book = values * inverse
        out[pl.ds(pl.multiple_of(step * width, width), width), :] = inverse * (
            grad - book * jnp.sum(book * grad, 0, keepdims=True)
        )
        return carry

    lax.fori_loop(0, total.shape[0] // block, back, 0)


def book_shape(table_turned, width):
    return jax.ShapeDtypeStruct((table_turned.size // width, width), F32)


def scatter_codes(index, unit, latents, table_turned, width):
    return pl.pallas_call(
        scatter_kernel,
        in_specs=[pl.BlockSpec(memory_space=pltpu.SMEM)] + [pl.BlockSpec(memory_space=pltpu.VMEM)] * 4,
        out_specs=pl.BlockSpec(memory_space=pltpu.VMEM),
        out_shape=book_shape(table_turned, width),
        scratch_shapes=[pltpu.VMEM(table_turned.shape[::-1], F32), pltpu.VMEM(unit.shape, F32)],
        compiler_params=PARAMS,
        name="scatter_codes",
    )(index, unit, *latents, table_turned)


def entry_values(encoder, edge, wide, up, head_bias):
    high, low = split(up)
    parts = jnp.concatenate([high, high, low, jnp.zeros_like(low)], 0)
    return jnp.where(encoder, edge.astype(F32), dot(wide, parts, NN) + head_bias[1:2, :])


def project_kernel(side, edge, wide, up, head_bias, gains, biases, weight, n1, query, key, value):
    width = edge.shape[1]
    encoder = side[0] == 0
    values = entry_values(encoder, edge[...], wide[...], up[...], head_bias[...])
    hat, unused = norm_parts(values)
    normed = (hat * gains[0:1, :] + biases[3:4, :]).astype(BF)
    n1[...] = normed
    query[...] = (
        (dot(normed, weight[:, :width], NN) + biases[0:1, :]) * (LOG2E * HEAD ** (-0.5))
    ).astype(BF)
    key[...] = dot(normed, weight[:, width : 2 * width], NN).astype(BF)
    value[...] = (dot(normed, weight[:, 2 * width :], NN) + biases[1:2, :]).astype(BF)


def merge(low_half, left, right):
    return jnp.where(low_half, left, right)


def attend_kernel(windows, query, key, value, query_mark, key_mark, context, marks, *, row):
    count = query.shape[0]
    size = TOKENS
    pairs = query.shape[1] // 128
    low_query = lanes((size, 128)) < 64
    mark_lane = lanes((size, 128)) & 63

    def block(number, start, extent):
        rows = pl.ds(pl.multiple_of(number * size, size), size)
        keys = pl.ds(pl.multiple_of(start, WINDOW), extent)
        low_key = lanes((extent, 128)) < 64
        query_aug, key_aug = query_mark[rows, :], key_mark[keys, :]
        ones = jnp.ones((extent, 128), BF)
        scores = []
        for pair in range(pairs):
            here = slice(pair * 128, pair * 128 + 128)
            query_pair, key_pair = query[rows, here], key[keys, here]
            scores.append(
                dot(merge(low_query, query_pair, query_aug), merge(low_key, key_pair, key_aug), NT)
            )
            scores.append(
                dot(merge(low_query, query_aug, query_pair), merge(low_key, key_aug, key_pair), NT)
            )
        tops = [jnp.max(score, -1, keepdims=True) for score in scores]
        raised = [jnp.exp2(score - top).astype(BF) for score, top in zip(scores, tops)]
        for pair in range(pairs):
            here = slice(pair * 128, pair * 128 + 128)
            value_pair = value[keys, here]
            even = dot(raised[2 * pair], merge(low_key, value_pair, ones), NN)
            odd = dot(raised[2 * pair + 1], merge(low_key, ones, value_pair), NN)
            total = merge(low_query, odd, even)
            context[rows, here] = (
                merge(low_query, even, odd) / pltpu.roll(total, 64, 1)
            ).astype(BF)
            level = -(merge(low_query, tops[2 * pair + 1], tops[2 * pair]) + jnp.log2(total))
            first = level.astype(BF)
            rest = level - first.astype(F32)
            second, third = split(rest)
            marks[rows, here] = merge(
                mark_lane == 4, first, merge(mark_lane == 5, second, merge(mark_lane == 6, third, query_aug))
            )

    def one(number, carry):
        base = (row * (count // size) + number) * 2
        for_windows(windows[base], windows[base + 1], count, functools.partial(block, number))
        return carry

    lax.fori_loop(0, count // size, one, 0)


def for_windows(start, steps, count, run):
    extents = list(range(2 * WINDOW, count + 1, WINDOW))
    for position, extent in enumerate(extents):
        take = steps * WINDOW <= extent
        if position:
            take = take & (steps * WINDOW > extents[position - 1])

        @pl.when(take)
        def _():
            run(jnp.minimum(start * WINDOW, count - extent), extent)


def gelu_parts(values):
    square = values * values
    half = 0.5 + 0.5 * jnp.tanh(values * (GELU + (GELU * CUBIC) * square))
    active = values * half
    slope = half + active * (1.0 - half) * (2.0 * GELU + (6.0 * GELU * CUBIC) * square)
    return active, slope


def hidden_kernel(
    side, edge, wide, up, head_bias, context, weight_out, gains, biases, weight_in, hidden_bias,
    weight_last, output_gain, down, down_bias,
    mid, n2, active_out, slope_out, result, latent_out,
):
    encoder = side[0] == 0
    width = edge.shape[1]
    values = entry_values(encoder, edge[...], wide[...], up[...], head_bias[...])
    midway = values + (dot(context[...], weight_out[...], NN) + biases[2:3, :])
    mid[...] = midway
    hat, unused = norm_parts(midway)
    normed = (hat * gains[1:2, :] + biases[4:5, :]).astype(BF)
    n2[...] = normed
    total = midway + biases[5:6, :]
    chunk = 256
    for start in range(0, weight_in.shape[1], chunk):
        here = slice(start, start + chunk)
        active, slope = gelu_parts(dot(normed, weight_in[:, here], NN) + hidden_bias[0:1, here])
        active = active.astype(BF)
        active_out[:, here] = active
        slope_out[:, here] = slope.astype(BF)
        total = total + dot(active, weight_last[here, :], NN)
    result[...] = total

    @pl.when(encoder)
    def _():
        last_hat, unused = norm_parts(total)
        code = last_hat * output_gain[0:1, :] + head_bias[0:1, :]
        latent = code_product(code, down[...]) + down_bias[0:1, :]
        scale = lax.rsqrt(jnp.sum(latent * latent, -1, keepdims=True) + NORM_EPS)
        latent_out[...] = latent * scale


def code_product(values, weight):
    return dot3(split(values), split(weight), NT)


def tail_back_kernel(
    side, result, cotangent, unit, latent_in, output_gain, head_bias, down, down_bias,
    weight_last, slope, weight_in, mid, gains, biases, weight_out, *refs, adding
):
    before, refs = refs[: 2 * adding], refs[2 * adding :]
    out_low, preact_low, mid_grad, branch_low, context_grad, sums, head_weight, upstream = refs
    encoder = side[0] == 0
    width = result.shape[1]
    narrow = unit.shape[1]

    @pl.when(pl.program_id(0) == 0)
    def _():
        sums[...] = before[0][...] if adding else jnp.zeros_like(sums)
        head_weight[...] = before[1][...] if adding else jnp.zeros_like(head_weight)

    @pl.when(encoder)
    def _():
        hat, inverse = norm_parts(result[...])
        normed = hat * output_gain[0:1, :] + head_bias[0:1, :]
        latent = code_product(normed, down[...]) + down_bias[0:1, :]
        scale = lax.rsqrt(jnp.sum(latent * latent, -1, keepdims=True) + NORM_EPS)
        code = latent * scale
        code_grad = latent_in[...].T + 0.5 * (code - unit[...])
        latent_grad = scale * (code_grad - code * jnp.sum(code * code_grad, -1, keepdims=True))
        pieces = split(latent_grad)
        normed_grad = dot3(pieces, split(down[...]), NN)
        head_weight[...] += dot3(pieces, split(normed), TN)
        sums[8:9, :] += column_sum(normed_grad * hat)
        sums[9:10, :] += column_sum(normed_grad)
        sums[10:11, :narrow] += column_sum(latent_grad)
        upstream[...] = norm_back(normed_grad, output_gain[0:1, :], hat, inverse)

    @pl.when(jnp.logical_not(encoder))
    def _():
        upstream[...] = cotangent[...].astype(F32)

    above = upstream[...]
    low = above.astype(BF)
    out_low[...] = low
    sums[4:5, :] += column_sum(low.astype(F32))
    normed_grad = None
    chunk = 1024
    for start in range(0, weight_in.shape[1], chunk):
        here = slice(start, start + chunk)
        active_grad = dot(low, weight_last[here, :], NT)
        inner = (active_grad * slope[:, here].astype(F32)).astype(BF)
        preact_low[:, here] = inner
        part = column_sum(inner.astype(F32))
        for at in range(0, chunk, min(chunk, width)):
            row, lane = (start + at) // width, (start + at) % width
            size = min(chunk, width)
            sums[row : row + 1, lane : lane + size] += part[:, at : at + size]
        term = dot(inner, weight_in[:, here], NT)
        normed_grad = term if normed_grad is None else normed_grad + term
    hat, inverse = norm_parts(mid[...])
    sums[6:7, :] += column_sum(normed_grad * hat)
    sums[7:8, :] += column_sum(normed_grad)
    middle = above + norm_back(normed_grad, gains[1:2, :], hat, inverse)
    mid_grad[...] = middle
    branch = middle.astype(BF)
    branch_low[...] = branch
    sums[5:6, :] += column_sum(branch.astype(F32))
    context_grad[...] = dot(branch, weight_out[...], NT).astype(BF)


def mark_grads(context_grad, context, grad_mark):
    count = context_grad.shape[0]
    lane_all = lanes((count, 128)) & 63
    across = (
        lax.broadcasted_iota(jnp.int32, (128, 128), 0) // 64 != lanes((128, 128)) // 64
    ).astype(BF)
    zero = jnp.zeros((count, 128), BF)
    for pair in range(context_grad.shape[1] // 128):
        here = slice(pair * 128, pair * 128 + 128)
        product = split(context_grad[:, here].astype(F32) * context[:, here].astype(F32))
        level = -(dot(product[0], across, NN) + dot(product[1], across, NN))
        first = level.astype(BF)
        second, third = split(level - first.astype(F32))
        grad_mark[:, here] = merge(
            lane_all == 0, first, merge(lane_all == 1, second, merge(lane_all == 2, third, zero))
        )


def attend_back_block(
    number, start, extent, base, pairs,
    query, marks, key, value, context_grad, key_mark, grad_mark, query_grad, key_total, value_total,
):
    size = TOKENS
    low_query = lanes((size, 128)) < 64
    rows = pl.ds(pl.multiple_of(number * size, size), size)
    keys = pl.ds(pl.multiple_of(start, WINDOW), extent)
    low_key = lanes((extent, 128)) < 64
    key_aug = key_mark[keys, :]
    ones = jnp.where((lanes((extent, 128)) & 63) < 3, 1.0, 0.0).astype(BF)
    none = jnp.zeros((extent, 128), BF)
    for pair in range(pairs):
        here = pl.ds(pl.multiple_of(base + pair * 128, 128), 128)
        query_pair, key_pair, value_pair = query[rows, here], key[keys, here], value[keys, here]
        grad_pair, query_aug, grad_aug = context_grad[rows, here], marks[rows, here], grad_mark[rows, here]
        found = []
        for swap in (False, True):

            def both(low, left, right):
                return merge(low, right, left) if swap else merge(low, left, right)

            scores = dot(both(low_key, key_pair, key_aug), both(low_query, query_pair, query_aug), NT)
            rise = dot(both(low_key, value_pair, ones), both(low_query, grad_pair, grad_aug), NT)
            chance = jnp.exp2(scores)
            score_grad = (chance * rise).astype(BF)
            found.append(
                (
                    dot(score_grad, query_pair, NN),
                    dot(chance.astype(BF), grad_pair, NN),
                    dot(score_grad, both(low_key, key_pair, none), TN),
                )
            )
        key_total[keys, here] += merge(low_key, found[0][0], found[1][0])
        value_total[keys, here] += merge(low_key, found[0][1], found[1][1])
        query_grad[rows, here] = ((found[0][2] + found[1][2]) * HEAD ** (-0.5)).astype(BF)


def attend_back_kernel(
    windows, query, marks, key, value, context_grad, context, key_mark,
    query_grad, key_grad, value_grad, grad_mark, key_total, value_total, *, row
):
    count = query.shape[0]
    steps = count // TOKENS
    pairs = query.shape[1] // 128
    mark_grads(context_grad, context, grad_mark)
    key_total[...] = jnp.zeros_like(key_total)
    value_total[...] = jnp.zeros_like(value_total)

    def one(turn, carry):
        number, pair = turn // pairs, turn % pairs
        at = (row * steps + number) * 2

        def run(start, extent):
            attend_back_block(
                number, start, extent, pair * 128, 1,
                query, marks, key, value, context_grad, key_mark, grad_mark, query_grad, key_total, value_total,
            )

        for_windows(windows[at], windows[at + 1], count, run)
        return carry

    lax.fori_loop(0, steps * pairs, one, 0)
    key_grad[...] = (key_total[...] * (1.0 / LOG2E)).astype(BF)
    value_grad[...] = value_total[...].astype(BF)


def entry_back_kernel(
    side, edge, wide, up, head_bias, unit, query_grad, key_grad, value_grad, weight, gains, biases,
    mid_grad, *refs, adding
):
    before, refs = refs[: 2 * adding], refs[2 * adding :]
    entry, latent_out, sums, head_weight = refs
    encoder = side[0] == 0
    width = edge.shape[1]
    narrow = unit.shape[1]

    @pl.when(pl.program_id(0) == 0)
    def _():
        sums[...] = before[0][...] if adding else jnp.zeros_like(sums)
        head_weight[...] = before[1][...] if adding else jnp.zeros_like(head_weight)

    values = entry_values(encoder, edge[...], wide[...], up[...], head_bias[...])
    normed_grad = (
        dot(query_grad[...], weight[:, :width], NT)
        + dot(key_grad[...], weight[:, width : 2 * width], NT)
        + dot(value_grad[...], weight[:, 2 * width :], NT)
    )
    hat, inverse = norm_parts(values)
    sums[0:1, :] += column_sum(query_grad[...].astype(F32))
    sums[1:2, :] += column_sum(value_grad[...].astype(F32))
    sums[2:3, :] += column_sum(normed_grad * hat)
    sums[3:4, :] += column_sum(normed_grad)
    total = mid_grad[...] + norm_back(normed_grad, gains[0:1, :], hat, inverse)
    entry[...] = total

    @pl.when(jnp.logical_not(encoder))
    def _():
        sums[4:5, :] += column_sum(total)
        latent_out[...] = code_product(total, up[...]).T
        head_weight[...] += dot3(split(unit[...]), split(total), TN)


def hidden_weight_kernel(active, out_low, n2, preact_low, *refs):
    out = refs[-1]
    before = refs[0] if len(refs) > 1 else None
    step = pl.program_id(0)
    first = pl.num_programs(0) // 2
    width = n2.shape[1]

    def put(value, rows):
        out[rows, :] = value if before is None else value + before[rows, :]

    @pl.when(step < first)
    def _():
        put(dot(active[...], out_low[...], TN), slice(0, 2 * width))

    @pl.when(step >= first)
    def _():
        value = dot(n2[...], preact_low[...], TN)
        put(value[:, :width], slice(0, width))
        put(value[:, width:], slice(width, 2 * width))


def attention_weight_kernel(context, branch_low, n1, query_grad, key_grad, value_grad, *refs):
    out = refs[-1]
    before = refs[0] if len(refs) > 1 else None
    step = pl.program_id(0)
    width = n1.shape[1]

    def put(value, number):
        rows = slice(number * width, (number + 1) * width)
        out[rows, :] = value if before is None else value + before[rows, :]

    @pl.when(step == 0)
    def _():
        put(dot(context[...], branch_low[...], TN), 0)
        put(dot(n1[...], query_grad[...], TN), 1)

    @pl.when(step == 1)
    def _():
        put(dot(n1[...], key_grad[...], TN), 0)
        put(dot(n1[...], value_grad[...], TN), 1)


def weight_call(kernel, operands, in_specs, steps, before, name):
    width = operands[1].shape[1]
    out_spec = pl.BlockSpec((2 * width, width), lambda step: (step, 0))
    aliases = {}
    if before is not None:
        aliases = {len(operands): 0}
        operands, in_specs = operands + [before], in_specs + [out_spec]
    return pl.pallas_call(
        kernel,
        grid=(steps,),
        in_specs=in_specs,
        out_specs=out_spec,
        out_shape=jax.ShapeDtypeStruct((2 * steps * width, width), F32),
        input_output_aliases=aliases,
        compiler_params=PARAMS,
        name=name,
    )(*operands)


def hidden_weights(kept, back, before=None):
    operands = [kept["active"], back["out_low"], kept["n2"], back["preact_low"]]
    count, width = kept["n2"].shape
    first = kept["active"].shape[1] // (2 * width)
    full = pl.BlockSpec((count, width), lambda step: (0, 0))
    in_specs = [
        pl.BlockSpec((count, 2 * width), lambda step: (0, jnp.minimum(step, first - 1))),
        full,
        full,
        pl.BlockSpec((count, 2 * width), lambda step: (0, jnp.maximum(step - first, 0))),
    ]
    return weight_call(hidden_weight_kernel, operands, in_specs, 2 * first, before, "hidden_weights")


def attention_weights(kept, back, before=None):
    operands = [kept["context"], back["branch_low"], kept["n1"]]
    operands += [back["query_grad"], back["key_grad"], back["value_grad"]]
    full = pl.BlockSpec(kept["n1"].shape, lambda step: (0, 0))
    return weight_call(attention_weight_kernel, operands, [full] * 6, 2, before, "attention_weights")


MESH = pl.DeviceIdType.MESH
LEAST_DEVICES = 4


def ring_chip(position, chips):
    odd = position // (chips // 2)
    return (1 - odd) * (2 * position) + odd * (2 * (chips - 1 - position) + 1)


class Ring:
    @staticmethod
    def scratch(arrays, ways, crossing):
        chips = lax.axis_size("dp") // 2
        sizes = [array.shape[0] // (2 * count * chips) for array, count in zip(arrays, ways)]
        shapes = [(count, chips, size, array.shape[1]) for array, count, size in zip(arrays, ways, sizes)]
        buffers = [pltpu.VMEM(shape, F32) for shape in shapes] * 3
        sems = [pltpu.SemaphoreType.DMA(shape[:2]) for shape in shapes] * 10
        far = []
        if crossing is not None:
            count, unused, size, width = shapes[crossing]
            far = [pltpu.VMEM((count, size, width), F32)] + [pltpu.SemaphoreType.DMA((count,))] * 2
        return buffers + sems + far

    def __init__(self, sources, results, ways, crossing, scratch):
        number = len(sources)
        take = lambda at: scratch[at * number : (at + 1) * number]
        self.chips = lax.axis_size("dp") // 2
        self.sources, self.results, self.ways, self.crossing = sources, results, ways, crossing
        self.own, self.pair, self.run = take(0), take(1), take(2)
        (
            self.load_sems, self.pair_send, self.pair_recv, self.run_send, self.run_recv,
            self.keep_sems, self.spread_send, self.spread_recv, self.side_send, self.side_recv,
        ) = (take(at) for at in range(3, 13))
        self.far = scratch[13 * number :]
        self.sizes = [run.shape[2] for run in self.run]
        self.lanes = [(which, way) for way in range(max(ways)) for which in range(number) if way < ways[which]]
        place = lax.axis_index("dp")
        chip, self.core = place // 2, place % 2
        column, odd = chip // 2, chip % 2
        chips = self.chips
        self.position = (1 - odd) * column + odd * (chips - 1 - column)
        self.other = {"dp": chip * 2 + (1 - self.core)}
        self.across = {"section": 1 - lax.axis_index("section")}
        self.targets = (
            {"dp": ring_chip((self.position + 1) % chips, chips) * 2 + self.core},
            {"dp": ring_chip((self.position + chips - 1) % chips, chips) * 2 + self.core},
        )

    def greet(self):
        self.barrier = pltpu.get_barrier_semaphore()
        devices = (self.other,) + self.targets + (() if self.crossing is None else (self.across,))
        for device in devices:
            pl.semaphore_signal(self.barrier, inc=1, device_id=device, device_id_type=MESH)
        self.greeted = len(devices)

    def piece(self, step, way):
        return (self.position + (2 * self.chips - step if way % 2 == 0 else step)) % self.chips

    def rows(self, which, half, way, number):
        size = self.sizes[which]
        return pl.ds(pl.multiple_of(((half * self.ways[which] + way) * self.chips + number) * size, 8), size)

    def final(self, which, half, way, step):
        return self.results[which].at[self.rows(which, half, way, self.piece(step + self.chips - 1, way))]

    def load(self, which, way, step):
        return pltpu.make_async_copy(
            self.sources[which].at[self.rows(which, self.core, way, self.piece(step, way))],
            self.own[which].at[way, step],
            self.load_sems[which].at[way, step],
        )

    def remote(self, source, target, send, recv, device):
        return pltpu.make_async_remote_copy(
            src_ref=source, dst_ref=target, send_sem=send, recv_sem=recv, device_id=device, device_id_type=MESH
        )

    def swap(self, which, way, step):
        return self.remote(
            self.sources[which].at[self.rows(which, 1 - self.core, way, self.piece(step, way))],
            self.pair[which].at[way, step],
            self.pair_send[which].at[way, step],
            self.pair_recv[which].at[way, step],
            self.other,
        )

    def pass_on(self, which, way, step):
        return self.remote(
            self.run[which].at[way, step],
            self.run[which].at[way, step + 1],
            self.run_send[which].at[way, step],
            self.run_recv[which].at[way, step + 1],
            self.targets[way % 2],
        )

    def cross(self, way):
        return self.remote(
            self.run[self.crossing].at[way, self.chips - 1],
            self.far[0].at[way],
            self.far[1].at[way],
            self.far[2].at[way],
            self.across,
        )

    def keep(self, which, way):
        return pltpu.make_async_copy(
            self.run[which].at[way, self.chips - 1], self.final(which, self.core, way, 0), self.keep_sems[which].at[way, 0]
        )

    def spread(self, which, way, step, first=False):
        here = self.final(which, self.core, way, step)
        return self.remote(
            self.run[which].at[way, self.chips - 1] if first else here,
            here,
            self.spread_send[which].at[way, step],
            self.spread_recv[which].at[way, step],
            self.targets[way % 2],
        )

    def incoming(self, which, way, step):
        here = self.final(which, self.core, way, step)
        return self.remote(
            here, here, self.spread_send[which].at[way, step], self.spread_recv[which].at[way, step - 1],
            self.targets[way % 2],
        )

    def aside(self, which, way, step, first=False):
        here = self.final(which, self.core, way, step)
        return self.remote(
            self.run[which].at[way, self.chips - 1] if first else here,
            here,
            self.side_send[which].at[way, step],
            self.side_recv[which].at[way, step],
            self.other,
        )

    def beside(self, which, way, step):
        here = self.final(which, 1 - self.core, way, step)
        return self.remote(
            here, here, self.side_send[which].at[way, step], self.side_recv[which].at[way, step], self.other
        )

    def begin(self):
        def load(step, carry):
            for which, way in self.lanes:
                self.load(which, way, step).start()
            return carry

        def swap(step, carry):
            for which, way in self.lanes:
                self.swap(which, way, step).start()
            return carry

        lax.fori_loop(0, self.chips, load, 0)
        pl.semaphore_wait(self.barrier, self.greeted)
        lax.fori_loop(0, self.chips, swap, 0)
        for which, way in self.lanes:
            self.load(which, way, 0).wait()
            self.swap(which, way, 0).wait_recv()
            self.run[which][way, 0] = self.own[which][way, 0] + self.pair[which][way, 0]
            self.pass_on(which, way, 0).start()

    def gather(self, step):
        for which, way in self.lanes:
            run, own, pair = self.run[which], self.own[which], self.pair[which]
            self.load(which, way, step).wait()
            self.swap(which, way, step).wait_recv()
            self.pass_on(which, way, step - 1).wait_recv()
            run[way, step] = run[way, step] + own[way, step] + pair[way, step]

            @pl.when(step < self.chips - 1)
            def _():
                self.pass_on(which, way, step).start()

    def turn(self):
        for which, way in self.lanes:
            if which == self.crossing:
                self.cross(way).start()
        for which, way in self.lanes:
            if which != self.crossing:
                self.hand_out(which, way)
        for which, way in self.lanes:
            if which == self.crossing:
                run = self.run[which]
                self.cross(way).wait()
                run[way, self.chips - 1] = run[way, self.chips - 1] + self.far[0][way]
                self.hand_out(which, way)

    def hand_out(self, which, way):
        self.spread(which, way, 0, True).start()
        self.aside(which, way, 0, True).start()
        self.keep(which, way).start()

    def pass_out(self, step):
        for which, way in self.lanes:
            self.incoming(which, way, step).wait_recv()

            @pl.when(step < self.chips - 1)
            def _():
                self.spread(which, way, step).start()

            self.aside(which, way, step).start()

    def finish(self):
        def one(step, carry):
            for which, way in self.lanes:
                self.swap(which, way, step).wait_send()
                self.beside(which, way, step).wait_recv()
                self.aside(which, way, step).wait_send()

                @pl.when(step < self.chips - 1)
                def _():
                    self.pass_on(which, way, step).wait_send()
                    self.spread(which, way, step).wait_send()

            return carry

        lax.fori_loop(0, self.chips, one, 0)
        for which, way in self.lanes:
            self.keep(which, way).wait()


def loop(start, stop, run):
    def one(step, carry):
        run(step)
        return carry

    lax.fori_loop(start, stop, one, 0)


SUM_WAYS = (4, 2)


def sum_kernel(main, misc, main_out, misc_out, *scratch):
    ring = Ring((main, misc), (main_out, misc_out), SUM_WAYS, 1, scratch)
    ring.greet()
    ring.begin()
    loop(1, ring.chips, ring.gather)
    ring.turn()
    loop(1, ring.chips, ring.pass_out)
    ring.finish()


def sum_all(main, misc):
    if lax.axis_size("dp") < LEAST_DEVICES:
        return main, lax.psum(misc, "section")
    arrays = (main, misc)
    return pl.pallas_call(
        sum_kernel,
        in_specs=[pl.BlockSpec(memory_space=pl.ANY)] * 2,
        out_specs=[pl.BlockSpec(memory_space=pl.ANY)] * 2,
        out_shape=tuple(jax.ShapeDtypeStruct(array.shape, F32) for array in arrays),
        scratch_shapes=Ring.scratch(arrays, SUM_WAYS, 1),
        compiler_params=pltpu.CompilerParams(collective_id=0, has_side_effects=True, vmem_limit_bytes=40 << 20),
        name="sum_all",
    )(*arrays)


FINISH_WAYS = (4,)


def finish_kernel(
    hidden, attention, query, marks, key, value, context_grad, context, key_mark, edges, mid_grad, weight, branch_low, n1,
    gains, book, down, up, late, early,
    hidden_out, attention_out, misc, entry,
    query_in, marks_in, key_in, value_in, grad_in, context_in, key_mark_in, edge_in, mid_in, weight_in, branch_in, n1_in,
    part, grad_mark, query_grad, key_total, value_total, key_grad, value_grad, in_sems, part_sem, out_sems,
    *scratch,
):
    encoder = lax.axis_index("section") == 0
    ring = Ring((hidden,), (hidden_out,), FINISH_WAYS, None, scratch) if scratch else None
    count, width = query.shape
    narrow = down.shape[0]
    steps = count // TOKENS
    pairs = width // 128
    row = edges.shape[0] - 1
    at = book.shape[0] + 2 * narrow
    inputs = (
        (query, query_in), (marks, marks_in), (key, key_in), (value, value_in), (context_grad, grad_in),
        (context, context_in), (key_mark.at[row], key_mark_in), (edges.at[row], edge_in), (mid_grad, mid_in),
        (weight, weight_in), (branch_low, branch_in), (n1, n1_in),
    )
    loads = [pltpu.make_async_copy(*pair, in_sems.at[number]) for number, pair in enumerate(inputs)]
    part_load = pltpu.make_async_copy(attention, part, part_sem)

    if ring:
        ring.greet()

    @pl.when(encoder)
    def _():
        for load in loads:
            load.start()
        part_load.start()

    if ring:
        ring.begin()
    misc[...] = jnp.zeros_like(misc)

    @pl.when(encoder)
    def _():
        misc[: book.shape[0], :] = book[...]
        misc[book.shape[0] : book.shape[0] + narrow, :] = down[...]
        misc[at : at + 16, :] = late[...]
        misc[at + 16 : at + 32, :] = early[...]
        for load in loads:
            load.wait()
        part_load.wait()
        mark_grads(grad_in, context_in, grad_mark)
        key_total[...] = jnp.zeros_like(key_total)
        value_total[...] = jnp.zeros_like(value_total)

    @pl.when(jnp.logical_not(encoder))
    def _():
        misc[book.shape[0] + narrow : at, :] = up[...]
        misc[at + 32 : at + 48, :] = late[...]
        misc[at + 48 : at + 64, :] = early[...]

    def attention_piece(turn):
        attend_back_block(
            turn // 2, 0, count, (turn % 2) * (width // 2), pairs // 2,
            query_in, marks_in, key_in, value_in, grad_in, key_mark_in, grad_mark, query_grad, key_total, value_total,
        )

    def entry_piece(number):
        rows = pl.ds(pl.multiple_of(number * TOKENS, TOKENS), TOKENS)
        normed_grad = (
            dot(query_grad[rows, :], weight_in[:, :width], NT)
            + dot(key_grad[rows, :], weight_in[:, width : 2 * width], NT)
            + dot(value_grad[rows, :], weight_in[:, 2 * width :], NT)
        )
        hat, inverse = norm_parts(edge_in[rows, :].astype(F32))
        misc[at + 16 : at + 17, :] += column_sum(query_grad[rows, :].astype(F32))
        misc[at + 17 : at + 18, :] += column_sum(value_grad[rows, :].astype(F32))
        misc[at + 18 : at + 19, :] += column_sum(normed_grad * hat)
        misc[at + 19 : at + 20, :] += column_sum(normed_grad)
        mid_in[rows, :] = mid_in[rows, :] + norm_back(normed_grad, gains[0:1, :], hat, inverse)

    def weight_piece(number):
        def put(left, right):
            rows = pl.ds(pl.multiple_of(number * width, width), width)
            part[rows, :] = part[rows, :] + dot(left[...], right[...], TN)

        for choice, (left, right) in enumerate(
            ((context_in, branch_in), (n1_in, query_grad), (n1_in, key_grad), (n1_in, value_grad))
        ):
            pl.when(number == choice)(functools.partial(put, left, right))

    def summing(step):
        if ring:
            ring.gather(step)

        @pl.when(encoder)
        def _():
            attention_piece(step - 1)

    chips = ring.chips if ring else 8
    pieces = 2 * steps
    inside = min(chips - 1, pieces)
    loop(1, inside + 1, summing)
    if ring:
        loop(inside + 1, chips, ring.gather)
        ring.turn()

    @pl.when(encoder)
    def _():
        loop(inside, pieces, attention_piece)
        key_grad[...] = (key_total[...] * (1.0 / LOG2E)).astype(BF)
        value_grad[...] = value_total[...].astype(BF)

    def spreading(step):
        if ring:
            ring.pass_out(step)

        @pl.when(encoder)
        def _():
            entry_piece(step - 1)
            weight_piece(step - 1)

    loop(1, steps + 1, spreading)
    stores = [
        pltpu.make_async_copy(mid_in, entry, out_sems.at[0]),
        pltpu.make_async_copy(part, attention_out, out_sems.at[1]),
    ]

    @pl.when(encoder)
    def _():
        for store in stores:
            store.start()

    if ring:
        loop(steps + 1, chips, ring.pass_out)
        ring.finish()

    @pl.when(encoder)
    def _():
        for store in stores:
            store.wait()


def finish_row(work, kept, late, early, up, book, hidden, attention):
    count, width = kept["n1"].shape
    alone = lax.axis_size("dp") < LEAST_DEVICES
    operands = [
        hidden, attention, kept["query"], kept["marks"], kept["key"], kept["value"], late["context_grad"],
        kept["context"], work.key_mark, work.edges, late["mid_grad"], work.attention_in, late["branch_low"], kept["n1"],
        work.gains, book, late["head_late"], up, late["sums_late"], early,
    ]
    hbm, vmem = pl.BlockSpec(memory_space=pl.ANY), pl.BlockSpec(memory_space=pltpu.VMEM)
    rows = book.shape[0] + 2 * work.narrow + 64
    unit = 16 * lax.axis_size("dp")
    low = pltpu.VMEM((count, width), BF)
    wide = pltpu.VMEM((count, width), F32)
    scratch = [low] * 6 + [pltpu.VMEM((count, 128), BF), low, wide, pltpu.VMEM(work.attention_in.shape, BF), low, low]
    scratch += [pltpu.VMEM(attention.shape, F32), low, low, wide, wide, low, low]
    scratch += [pltpu.SemaphoreType.DMA((12,)), pltpu.SemaphoreType.DMA, pltpu.SemaphoreType.DMA((2,))]
    settings = {}
    if not alone:
        scratch += Ring.scratch((hidden,), FINISH_WAYS, None)
        settings = dict(collective_id=1, has_side_effects=True)
    outs = pl.pallas_call(
        finish_kernel,
        in_specs=[hbm] * 14 + [vmem] * 6,
        out_specs=[hbm, hbm, vmem, hbm],
        out_shape=(
            jax.ShapeDtypeStruct(hidden.shape, F32),
            jax.ShapeDtypeStruct(attention.shape, F32),
            jax.ShapeDtypeStruct((rows + (-rows % unit), width), F32),
            jax.ShapeDtypeStruct((count, width), F32),
        ),
        scratch_shapes=scratch,
        input_output_aliases={1: 1},
        compiler_params=pltpu.CompilerParams(vmem_limit_bytes=58 << 20, **settings),
        name="finish_row",
    )(*operands)
    return (hidden,) + tuple(outs[1:]) if alone else outs


def unpack_kernel(
    side, hidden, attention, misc, first_entry, second_entry, first_result, second_result,
    hidden_out, hidden_in, attention_out, attention_in, book, edge, held, head, rows, ins, outs, row_ins, row_outs,
):
    width = hidden.shape[1]
    narrow = book.shape[0]
    steps = hidden_out.shape[0] // width
    targets = [hidden_out.at[pl.ds(number * width, width), :] for number in range(steps)]
    targets += [hidden_in.at[:, pl.ds(number * width, width)] for number in range(steps)]
    targets += [attention_out]
    targets += [attention_in.at[:, pl.ds(number * width, width)] for number in range(3)]
    sources = [hidden.at[pl.ds(number * width, width), :] for number in range(2 * steps)]
    sources += [attention.at[pl.ds(number * width, width), :] for number in range(4)]
    tiles = range(len(targets))
    for mine, pair in ((0, (first_entry, second_entry)), (1, (first_result, second_result))):

        @pl.when(side[0] == mine)
        def _():
            for row in range(2):
                pltpu.make_async_copy(pair[row], rows.at[row], row_ins.at[row]).start()

    loads = [pltpu.make_async_copy(sources[number], held.at[number], ins.at[number]) for number in tiles]
    loads.append(pltpu.make_async_copy(misc.at[pl.ds(0, head.shape[0]), :], head, ins.at[len(targets)]))
    for load in loads:
        load.start()
    stores = []
    for row in range(2):
        pltpu.make_async_copy(first_entry, rows.at[row], row_ins.at[row]).wait()
        stores.append(pltpu.make_async_copy(rows.at[row], edge.at[row], row_outs.at[row]))
        stores[-1].start()
    for number in tiles:
        loads[number].wait()
        stores.append(pltpu.make_async_copy(held.at[number], targets[number], outs.at[number]))
        stores[-1].start()
    loads[-1].wait()
    for number in range(book.shape[1] // width):
        book[:, number * width : (number + 1) * width] = head[number * narrow : (number + 1) * narrow, :]
    for store in stores:
        store.wait()


def unpack(side, hidden, attention, misc, ends, table_turned):
    width = hidden.shape[1]
    features = hidden.shape[0] // 2
    tiles = (hidden.shape[0] + attention.shape[0]) // width
    shapes = (
        (features, width), (width, features), (width, width), (width, 3 * width), table_turned.shape,
        (2,) + ends[0].shape,
    )
    hbm, vmem = pl.BlockSpec(memory_space=pl.ANY), pl.BlockSpec(memory_space=pltpu.VMEM)
    return pl.pallas_call(
        unpack_kernel,
        in_specs=[pl.BlockSpec(memory_space=pltpu.SMEM)] + [hbm] * 7,
        out_specs=[hbm] * 4 + [vmem, hbm],
        out_shape=tuple(jax.ShapeDtypeStruct(shape, F32) for shape in shapes),
        scratch_shapes=[
            pltpu.VMEM((tiles, width, width), F32),
            pltpu.VMEM((table_turned.size // width, width), F32),
            pltpu.VMEM((2,) + ends[0].shape, F32),
            pltpu.SemaphoreType.DMA((tiles + 1,)),
            pltpu.SemaphoreType.DMA((tiles,)),
            pltpu.SemaphoreType.DMA((2,)),
            pltpu.SemaphoreType.DMA((2,)),
        ],
        compiler_params=PARAMS,
        name="unpack",
    )(side, hidden, attention, misc, *ends)


def nothing_kernel(*refs):
    pass


def unwritten(shapes):
    return pl.pallas_call(
        nothing_kernel,
        out_specs=[pl.BlockSpec(memory_space=pl.ANY)] * len(shapes),
        out_shape=tuple(shapes),
        name="unwritten",
    )()


KEPT = ("n1", "query", "key", "value", "context", "marks", "mid", "n2", "active", "slope", "result", "latent")
BACK = (
    "out_low", "preact_low", "mid_grad", "branch_low", "context_grad", "query_grad", "key_grad", "value_grad",
    "entry", "latent_out", "sums_late", "sums_early", "head_late", "head_early",
)


class Rows:
    def __init__(self, side, edges, wide, unit, windows, query_mark, key_mark, weights, head):
        self.side, self.edges, self.wide, self.unit = side, edges, wide, unit
        self.windows, self.query_mark, self.key_mark = windows, query_mark, key_mark
        (
            self.attention_in, self.attention_out, self.hidden_in, self.hidden_out,
            self.gains, self.biases, self.hidden_bias,
        ) = weights
        (
            self.output_gain, self.head_bias, self.down, self.down_bias, self.up,
        ) = head
        self.rows, self.count, self.width = edges.shape
        self.hidden = self.hidden_in.shape[1]
        self.narrow = unit.shape[1]

    def kept_shapes(self):
        n, d, f = self.count, self.width, self.hidden
        table = dict(
            n1=(d, BF), query=(d, BF), key=(d, BF), value=(d, BF), context=(d, BF), marks=(d, BF),
            mid=(d, F32), n2=(d, BF), active=(f, BF), slope=(f, BF), latent=(self.narrow, F32),
        )
        table["result"] = (d, F32)
        return {name: jax.ShapeDtypeStruct((n, size), kind) for name, (size, kind) in table.items()}

    def back_shapes(self):
        n, d, f = self.count, self.width, self.hidden
        table = dict(
            out_low=(n, d, BF), preact_low=(n, f, BF), mid_grad=(n, d, F32), branch_low=(n, d, BF),
            query_grad=(n, d, BF), key_grad=(n, d, BF), value_grad=(n, d, BF),
            latent_out=(self.narrow, n, F32), sums_late=(16, d, F32), sums_early=(16, d, F32),
            head_late=(self.narrow, d, F32), head_early=(self.narrow, d, F32),
        )
        table["entry"] = table["mid_grad"]
        table["context_grad"] = table["out_low"]
        return {name: jax.ShapeDtypeStruct((a, b), kind) for name, (a, b, kind) in table.items()}

    def turned(self, array):
        return pl.BlockSpec((array.shape[0], TOKENS), lambda step: (0, step))

    def side_spec(self):
        return pl.BlockSpec(memory_space=pltpu.SMEM)

    def tokens(self, array):
        return pl.BlockSpec((TOKENS, array.shape[1]), lambda step: (step, 0))

    def whole(self, array):
        return pl.BlockSpec(array.shape, lambda step: (0,) * len(array.shape))

    def entry_specs(self, row):
        steps = self.count // TOKENS
        return [
            pl.BlockSpec((None, TOKENS, self.width), lambda step: (row, step, 0)),
            pl.BlockSpec((TOKENS, self.wide.shape[1]), lambda step: (row * steps + step, 0)),
            self.whole(self.up),
            self.whole(self.head_bias),
        ]

    def unit_spec(self, row):
        steps = self.count // TOKENS
        return pl.BlockSpec((TOKENS, self.narrow), lambda step: (row * steps + step, 0))

    def call(self, kernel, in_specs, operands, outs, out_specs, name, scratch=()):
        return pl.pallas_call(
            kernel,
            grid=(self.count // TOKENS,),
            in_specs=in_specs,
            out_specs=out_specs,
            out_shape=tuple(outs),
            scratch_shapes=list(scratch),
            compiler_params=PARAMS,
            name=name,
        )(*operands)

    def attention_call(self, kernel, row, operands, outs, name, scratch=()):
        half = self.width // 2

        def spec(array):
            if array.ndim == 3:
                return pl.BlockSpec((None, self.count, array.shape[2]), lambda step, info: (row, 0, 0))
            return pl.BlockSpec((self.count, half), lambda step, info: (0, step))

        return pl.pallas_call(
            functools.partial(kernel, row=row),
            grid_spec=pltpu.PrefetchScalarGridSpec(
                num_scalar_prefetch=1,
                grid=(2,),
                in_specs=[spec(array) for array in operands],
                out_specs=[spec(array) for array in outs],
                scratch_shapes=list(scratch),
            ),
            out_shape=tuple(outs),
            compiler_params=PARAMS,
            name=name,
        )(self.windows, *operands)

    def forward(self, row):
        shapes = self.kept_shapes()
        entry = (self.edges, self.wide, self.up, self.head_bias)
        kept = {}
        names = ("n1", "query", "key", "value")
        outs = self.call(
            project_kernel,
            [self.side_spec()] + self.entry_specs(row)
            + [self.whole(self.gains), self.whole(self.biases), self.whole(self.attention_in)],
            (self.side,) + entry + (self.gains, self.biases, self.attention_in),
            [shapes[name] for name in names],
            [self.tokens(shapes[name]) for name in names],
            "project",
        )
        kept.update(zip(names, outs))
        names = ("context", "marks")
        outs = self.attention_call(
            attend_kernel, row,
            (kept["query"], kept["key"], kept["value"], self.query_mark, self.key_mark),
            [shapes[name] for name in names],
            "attend",
        )
        kept.update(zip(names, outs))
        names = ("mid", "n2", "active", "slope", "result", "latent")
        consts = (
            self.attention_out, self.gains, self.biases, self.hidden_in, self.hidden_bias, self.hidden_out,
            self.output_gain, self.down, self.down_bias,
        )
        outs = self.call(
            hidden_kernel,
            [self.side_spec()] + self.entry_specs(row) + [self.tokens(kept["context"])]
            + [self.whole(array) for array in consts],
            (self.side,) + entry + (kept["context"],) + consts,
            [shapes[name] for name in names],
            [self.tokens(shapes[name]) for name in names],
            "hidden",
        )
        kept.update(zip(names, outs))
        return kept

    def backward(self, row, kept, latent_in, former=None):
        back = self.backward_late(row, kept, latent_in, former)
        back.update(self.backward_early(row, kept, back, former))
        return back

    def backward_late(self, row, kept, latent_in, former=None):
        shapes = self.back_shapes()
        prior = () if former is None else (former["sums_late"], former["head_late"])
        adding = int(former is not None)
        names = ("out_low", "preact_low", "mid_grad", "branch_low", "context_grad", "sums_late", "head_late")
        consts = (self.output_gain, self.head_bias, self.down, self.down_bias, self.hidden_out)
        late = (self.gains, self.biases, self.attention_out)
        outs = self.call(
            functools.partial(tail_back_kernel, adding=adding),
            [self.side_spec(), self.tokens(kept["result"]), self.entry_specs(row)[0], self.unit_spec(row),
             self.turned(latent_in)]
            + [self.whole(array) for array in consts]
            + [self.tokens(kept["slope"]), self.whole(self.hidden_in), self.tokens(kept["mid"])]
            + [self.whole(array) for array in late + prior],
            (self.side, kept["result"], self.edges, self.unit, latent_in) + consts
            + (kept["slope"], self.hidden_in, kept["mid"]) + late + prior,
            [shapes[name] for name in names],
            [self.tokens(shapes[name]) for name in names[:5]] + [self.whole(shapes[name]) for name in names[5:]],
            "tail_back",
            scratch=[pltpu.VMEM((TOKENS, self.width), F32)],
        )
        return dict(zip(names, outs))

    def backward_early(self, row, kept, late, former=None):
        shapes = self.back_shapes()
        adding = int(former is not None)
        back = {}
        names = ("query_grad", "key_grad", "value_grad")
        half = self.width // 2
        outs = self.attention_call(
            attend_back_kernel, row,
            (kept["query"], kept["marks"], kept["key"], kept["value"], late["context_grad"], kept["context"],
             self.key_mark),
            [shapes[name] for name in names],
            "attend_back",
            scratch=[
                pltpu.VMEM((self.count, half), BF),
                pltpu.VMEM((self.count, half), F32),
                pltpu.VMEM((self.count, half), F32),
            ],
        )
        back.update(zip(names, outs))
        names = ("entry", "latent_out", "sums_early", "head_early")
        prior = () if former is None else (former["sums_early"], former["head_early"])
        grads = (back["query_grad"], back["key_grad"], back["value_grad"])
        outs = self.call(
            functools.partial(entry_back_kernel, adding=adding),
            [self.side_spec()] + self.entry_specs(row) + [self.unit_spec(row)]
            + [self.tokens(array) for array in grads]
            + [self.whole(self.attention_in), self.whole(self.gains), self.whole(self.biases),
               self.tokens(late["mid_grad"])] + [self.whole(array) for array in prior],
            (self.side, self.edges, self.wide, self.up, self.head_bias, self.unit) + grads
            + (self.attention_in, self.gains, self.biases, late["mid_grad"]) + prior,
            [shapes[name] for name in names],
            [self.tokens(shapes["entry"]), self.turned(shapes["latent_out"])] + [self.whole(shapes[name]) for name in names[2:]],
            "entry_back",
        )
        back.update(zip(names, outs))
        return back


def as_list(table, names):
    return [table[name] for name in names]


def windows_of(segments):
    rows, count = segments.shape
    steps = count // WINDOW
    blocks = segments.reshape(rows, steps, WINDOW)
    least, most = blocks[:, :, 0], blocks[:, :, -1]
    meets = (most[:, :, None] >= least[:, None, :]) & (least[:, :, None] <= most[:, None, :])
    place = jnp.arange(steps)
    start = jnp.min(jnp.where(meets, place, steps), -1)
    stop = jnp.max(jnp.where(meets, place, -1), -1) + 1
    return jnp.stack([start, stop - start], -1).reshape(-1).astype(jnp.int32)


def on_device(
    boundary, segments, code_index, attention_in, attention_out, hidden_in, hidden_out, block_gains,
    block_biases, hidden_bias, output_gain, head_bias, down_weight, down_bias, up_weight, codebook,
):
    section = lax.axis_index("section")
    encoder = section == 0
    side = section.astype(jnp.int32)[None]
    edges = boundary[0]
    rows, count, width = edges.shape
    hidden = hidden_in.shape[2]
    index = code_index.reshape(-1)
    table_turned = codebook.T
    unit, wide, query_mark, key_mark = gather_codes(index, table_turned, segments)
    work = Rows(
        side, edges, wide, unit, windows_of(segments), query_mark, key_mark,
        (
            attention_in[0], attention_out[0], hidden_in[0], hidden_out[0], block_gains[0], block_biases[0],
            hidden_bias,
        ),
        (
            output_gain[None], head_bias, down_weight.T, down_bias[None], up_weight,
        ),
    )
    kept_shapes = as_list(work.kept_shapes(), KEPT)
    back_shapes = as_list(work.back_shapes(), BACK)
    book_out = book_shape(table_turned, width)
    hidden_out_shape = jax.ShapeDtypeStruct((2 * hidden, width), F32)
    attention_shape = jax.ShapeDtypeStruct((4 * width, width), F32)
    quiet = jnp.zeros((unit.shape[1], count), F32)
    first_kept = work.forward(0)

    def encoder_second():
        return as_list(work.forward(1), KEPT), list(unwritten(back_shapes))

    def decoder_first():
        return list(unwritten(kept_shapes)), as_list(work.backward(0, first_kept, quiet), BACK)

    kept_a, back_a = lax.cond(encoder, encoder_second, decoder_first)
    back_a = dict(zip(BACK, back_a))
    kept_a = dict(zip(KEPT, kept_a))
    latent_in = lax.ppermute(back_a["latent_out"], "section", [(1, 0)])

    def encoder_third():
        return list(unwritten(kept_shapes)), as_list(work.backward(0, first_kept, latent_in), BACK)

    def decoder_third():
        return as_list(work.forward(1), KEPT), list(unwritten(back_shapes))

    kept_b, back_b = lax.cond(encoder, encoder_third, decoder_third)
    kept_b, back_b = dict(zip(KEPT, kept_b)), dict(zip(BACK, back_b))

    def encoder_fourth():
        book = scatter_codes(index, unit, (first_kept["latent"], kept_a["latent"]), table_turned, width)
        weights = hidden_weights(first_kept, back_b), attention_weights(first_kept, back_b)
        return list(unwritten(back_shapes)), weights, book

    def decoder_fourth():
        *weights, book = unwritten([hidden_out_shape, attention_shape, book_out])
        return as_list(work.backward(1, kept_b, quiet, back_a), BACK), tuple(weights), book

    back_c, weights_c, book = lax.cond(encoder, encoder_fourth, decoder_fourth)
    back_c = dict(zip(BACK, back_c))
    latent_in_second = lax.ppermute(back_c["latent_out"], "section", [(1, 0)])
    late_names = ("branch_low", "mid_grad", "context_grad", "sums_late", "head_late")

    def encoder_fifth():
        late = work.backward_late(1, kept_a, latent_in_second, back_b)
        total = hidden_weights(kept_a, late, weights_c[0])
        return total, weights_c[1], as_list(late, late_names), back_b["sums_early"]

    def decoder_fifth():
        total = hidden_weights(kept_b, back_c, hidden_weights(first_kept, back_a))
        attention = attention_weights(kept_b, back_c, attention_weights(first_kept, back_a))
        return total, attention, as_list(back_c, late_names), back_c["sums_early"]

    hidden_total, attention_total, late, early = lax.cond(encoder, encoder_fifth, decoder_fifth)
    late = dict(zip(late_names, late))
    hidden_total, attention_total, misc, second_entry = finish_row(
        work, kept_a, late, early, back_c["head_early"], book, hidden_total, attention_total
    )
    attention_total, misc = sum_all(attention_total, misc)
    hidden_out_grad, hidden_in_grad, attention_out_grad, attention_in_grad, book, edge = unpack(
        side, hidden_total, attention_total, misc,
        (back_b["entry"], second_entry, first_kept["result"], kept_b["result"]), table_turned,
    )
    narrow = unit.shape[1]
    pieces, at = [], book_out.shape[0]
    for size in (narrow, narrow, 16, 16, 16, 16):
        pieces.append(misc[at : at + size])
        at += size
    down_grad, up_grad, first_late, first_early, second_late, second_early = pieces
    late = jnp.where(encoder, first_late, second_late)
    early = jnp.where(encoder, first_early, second_early)
    return (
        edge[None],
        attention_in_grad[None],
        attention_out_grad[None],
        hidden_in_grad[None],
        hidden_out_grad[None],
        jnp.stack([early[2], late[6]])[None],
        jnp.stack([early[0], early[1], late[5], early[3], late[7], late[4]])[None],
        late[: hidden // width].reshape(1, hidden),
        first_late[8],
        jnp.stack([first_late[9], second_early[4]]),
        down_grad.T,
        first_late[10, :narrow],
        up_grad,
        book.T,
    )


def solution(mesh):
    return jax.shard_map(
        on_device,
        mesh=mesh,
        in_specs=(
            P("section", "dp", None, None), P("dp", None), P("dp", None),
            P("section", None, None), P("section", None, None), P("section", None, None),
            P("section", None, None), P("section", None, None), P("section", None, None),
            P("section", None), P(), P(), P(), P(), P(), P(),
        ),
        out_specs=(
            P("section", "dp", None, None), P("section", None, None), P("section", None, None),
            P("section", None, None), P("section", None, None), P("section", None, None),
            P("section", None, None), P("section", None), P(), P(), P(), P(), P(), P(),
        ),
        check_vma=False,
    )
```

```python
import functools
import math
from typing import Any, NamedTuple

import jax
import jax.numpy as jnp
from jax import lax
from jax.experimental import pallas as pl
from jax.experimental.pallas import tpu as pltpu
from jax.sharding import PartitionSpec as P

HEAD = 64
SECTION, DP = "section", "dp"
BF = jnp.bfloat16
F32 = jnp.float32
LOG2E = math.log2(math.e)
NORM_EPS = 1e-06
MASKED = -1e30
GELU = 0.7978845608028654
CUBIC = 0.044715
NN = (((1,), (0,)), ((), ()))
NT = (((1,), (1,)), ((), ()))
TN = (((0,), (0,)), ((), ()))
TOKENS = 256
WINDOW = 256
PARAMS = pltpu.CompilerParams(vmem_limit_bytes=56 << 20)


def dot(a, b, dims):
    return lax.dot_general(a, b, dims, preferred_element_type=F32)


def lanes(shape):
    return lax.broadcasted_iota(jnp.int32, shape, 1)


def split(values):
    high = values.astype(BF)
    return high, (values - high.astype(F32)).astype(BF)


def dot3(left, right, dims):
    return dot(left[0], right[0], dims) + dot(left[0], right[1], dims) + dot(left[1], right[0], dims)


def unit_of(values):
    scale = lax.rsqrt(jnp.sum(values * values, -1, keepdims=True) + NORM_EPS)
    return values * scale, scale


def norm_parts(values):
    center = values - jnp.mean(values, -1, keepdims=True)
    inverse = lax.rsqrt(jnp.mean(center * center, -1, keepdims=True) + NORM_EPS)
    return center * inverse, inverse


def norm_back(grad, gain, hat, inverse):
    scaled = grad * gain
    return inverse * (
        scaled
        - jnp.mean(scaled, -1, keepdims=True)
        - hat * jnp.mean(scaled * hat, -1, keepdims=True)
    )


def column_sum(values):
    return jnp.sum(values, 0, keepdims=True)


def code_kernel(index, table_turned, segments, unit, wide, query_mark, key_mark, table, raw):
    count = raw.shape[0]
    block = 512

    def turn(step, carry):
        start = pl.multiple_of(step * block, block)
        table[pl.ds(start, block), :] = table_turned[:, pl.ds(start, block)].T
        return carry

    lax.fori_loop(0, table.shape[0] // block, turn, 0)

    length = segments.shape[1]
    for row in range(index.shape[0]):

        def some(step, carry):
            for inner in range(16):
                token = step * 16 + inner
                raw[pl.ds(row * length + token, 1), :] = table[pl.ds(index[row, token], 1), :]
            return carry

        lax.fori_loop(0, length // 16, some, 0)

    values = raw[...]
    values = values * lax.rsqrt(jnp.sum(values * values, -1, keepdims=True) + NORM_EPS)
    unit[...] = values
    high, low = split(values)
    wide[...] = jnp.concatenate([high, low, high, jnp.zeros_like(high)], 1)
    lane = lanes((length, 128)) & 63
    for row in range(segments.shape[0]):
        owner = jnp.broadcast_to(segments[row : row + 1, :], (128, length)).T
        same = owner == lane
        query_mark[row] = jnp.where((lane < 4) & jnp.logical_not(same), MASKED, 0.0).astype(BF)
        key_mark[row] = jnp.where(((lane < 4) & same) | ((lane > 3) & (lane < 7)), 1.0, 0.0).astype(BF)


def gather_codes(index, table_turned, segments):
    count, width = index.size, table_turned.shape[0]
    vmem = pl.BlockSpec(memory_space=pltpu.VMEM)
    mark = jax.ShapeDtypeStruct(segments.shape + (128,), BF)
    return pl.pallas_call(
        code_kernel,
        in_specs=[pl.BlockSpec(memory_space=pltpu.SMEM), vmem, vmem],
        out_specs=[vmem] * 4,
        out_shape=(
            jax.ShapeDtypeStruct((count, width), F32),
            jax.ShapeDtypeStruct((count, 4 * width), BF),
            mark,
            mark,
        ),
        scratch_shapes=[pltpu.VMEM(table_turned.shape[::-1], F32), pltpu.VMEM((count, width), F32)],
        compiler_params=PARAMS,
    )(index, table_turned, segments)


def scatter_kernel(index, unit, latent_first, latent_second, table_turned, out, total, rows):
    count = rows.shape[0]
    width = unit.shape[1]
    half = count // 2
    total[...] = jnp.zeros_like(total)
    for row, latent in enumerate((latent_first, latent_second)):
        here = slice(row * half, (row + 1) * half)
        code, unused = unit_of(latent[...])
        rows[here, :] = 2.0 * (unit[here, :] - code)

        def some(step, carry):
            for inner in range(8):
                token = step * 8 + inner
                place = pl.ds(index[row, token], 1)
                total[place, :] = total[place, :] + rows[pl.ds(row * half + token, 1), :]
            return carry

        lax.fori_loop(0, half // 8, some, 0)
    block = out.shape[1]

    def back(step, carry):
        start = pl.multiple_of(step * block, block)
        values = table_turned[:, pl.ds(start, block)]
        grad = total[pl.ds(start, block), :].T
        inverse = lax.rsqrt(jnp.sum(values * values, 0, keepdims=True) + NORM_EPS)
        book = values * inverse
        out[pl.ds(pl.multiple_of(step * width, width), width), :] = inverse * (
            grad - book * jnp.sum(book * grad, 0, keepdims=True)
        )
        return carry

    lax.fori_loop(0, total.shape[0] // block, back, 0)


def book_shape(table_turned, width):
    return jax.ShapeDtypeStruct((table_turned.size // width, width), F32)


def scatter_codes(index, unit, latents, table_turned, width):
    return pl.pallas_call(
        scatter_kernel,
        in_specs=[pl.BlockSpec(memory_space=pltpu.SMEM)] + [pl.BlockSpec(memory_space=pltpu.VMEM)] * 4,
        out_specs=pl.BlockSpec(memory_space=pltpu.VMEM),
        out_shape=book_shape(table_turned, width),
        scratch_shapes=[pltpu.VMEM(table_turned.shape[::-1], F32), pltpu.VMEM(unit.shape, F32)],
        compiler_params=PARAMS,
    )(index, unit, *latents, table_turned)


def entry_values(encoder, edge, wide, up, head_bias):
    high, low = split(up)
    parts = jnp.concatenate([high, high, low, jnp.zeros_like(low)], 0)
    return jnp.where(encoder, edge.astype(F32), dot(wide, parts, NN) + head_bias[1:2, :])


def project_kernel(side, edge, wide, up, head_bias, gains, biases, weight, n1, query, key, value):
    width = edge.shape[1]
    encoder = side[0] == 0
    values = entry_values(encoder, edge[...], wide[...], up[...], head_bias[...])
    hat, unused = norm_parts(values)
    normed = (hat * gains[0:1, :] + biases[3:4, :]).astype(BF)
    n1[...] = normed
    query[...] = (
        (dot(normed, weight[:, :width], NN) + biases[0:1, :]) * (LOG2E * HEAD ** (-0.5))
    ).astype(BF)
    key[...] = dot(normed, weight[:, width : 2 * width], NN).astype(BF)
    value[...] = (dot(normed, weight[:, 2 * width :], NN) + biases[1:2, :]).astype(BF)


def merge(low_half, left, right):
    return jnp.where(low_half, left, right)


def attend_kernel(windows, query, key, value, query_mark, key_mark, context, marks, *, row):
    count = query.shape[0]
    size = TOKENS
    pairs = query.shape[1] // 128
    low_query = lanes((size, 128)) < 64
    mark_lane = lanes((size, 128)) & 63

    def block(number, start, extent):
        rows = pl.ds(pl.multiple_of(number * size, size), size)
        keys = pl.ds(pl.multiple_of(start, WINDOW), extent)
        low_key = lanes((extent, 128)) < 64
        query_aug, key_aug = query_mark[rows, :], key_mark[keys, :]
        ones = jnp.ones((extent, 128), BF)
        scores = []
        for pair in range(pairs):
            here = slice(pair * 128, pair * 128 + 128)
            query_pair, key_pair = query[rows, here], key[keys, here]
            scores.append(
                dot(merge(low_query, query_pair, query_aug), merge(low_key, key_pair, key_aug), NT)
            )
            scores.append(
                dot(merge(low_query, query_aug, query_pair), merge(low_key, key_aug, key_pair), NT)
            )
        tops = [jnp.max(score, -1, keepdims=True) for score in scores]
        raised = [jnp.exp2(score - top).astype(BF) for score, top in zip(scores, tops)]
        for pair in range(pairs):
            here = slice(pair * 128, pair * 128 + 128)
            value_pair = value[keys, here]
            even = dot(raised[2 * pair], merge(low_key, value_pair, ones), NN)
            odd = dot(raised[2 * pair + 1], merge(low_key, ones, value_pair), NN)
            total = merge(low_query, odd, even)
            context[rows, here] = (
                merge(low_query, even, odd) / pltpu.roll(total, 64, 1)
            ).astype(BF)
            level = -(merge(low_query, tops[2 * pair + 1], tops[2 * pair]) + jnp.log2(total))
            first = level.astype(BF)
            rest = level - first.astype(F32)
            second, third = split(rest)
            marks[rows, here] = merge(
                mark_lane == 4, first, merge(mark_lane == 5, second, merge(mark_lane == 6, third, query_aug))
            )

    def one(number, carry):
        base = (row * (count // size) + number) * 2
        for_windows(windows[base], windows[base + 1], count, functools.partial(block, number))
        return carry

    lax.fori_loop(0, count // size, one, 0)


def for_windows(start, steps, count, run):
    extents = list(range(2 * WINDOW, count + 1, WINDOW))
    for position, extent in enumerate(extents):
        take = steps * WINDOW <= extent
        if position:
            take = take & (steps * WINDOW > extents[position - 1])

        @pl.when(take)
        def _():
            run(jnp.minimum(start * WINDOW, count - extent), extent)


def gelu_parts(values):
    square = values * values
    half = 0.5 + 0.5 * jnp.tanh(values * (GELU + (GELU * CUBIC) * square))
    active = values * half
    slope = half + active * (1.0 - half) * (2.0 * GELU + (6.0 * GELU * CUBIC) * square)
    return active, slope


def hidden_kernel(
    side, edge, wide, up, head_bias, context, weight_out, gains, biases, weight_in, hidden_bias,
    weight_last, output_gain, down, down_bias,
    mid, n2, active_out, slope_out, result, latent_out,
):
    encoder = side[0] == 0
    width = edge.shape[1]
    values = entry_values(encoder, edge[...], wide[...], up[...], head_bias[...])
    midway = values + (dot(context[...], weight_out[...], NN) + biases[2:3, :])
    mid[...] = midway
    hat, unused = norm_parts(midway)
    normed = (hat * gains[1:2, :] + biases[4:5, :]).astype(BF)
    n2[...] = normed
    total = midway + biases[5:6, :]
    chunk = 256
    for start in range(0, weight_in.shape[1], chunk):
        here = slice(start, start + chunk)
        active, slope = gelu_parts(dot(normed, weight_in[:, here], NN) + hidden_bias[0:1, here])
        active = active.astype(BF)
        active_out[:, here] = active
        slope_out[:, here] = slope.astype(BF)
        total = total + dot(active, weight_last[here, :], NN)
    result[...] = total

    @pl.when(encoder)
    def _():
        last_hat, unused = norm_parts(total)
        code = last_hat * output_gain[0:1, :] + head_bias[0:1, :]
        latent_out[...] = code_product(code, down[...]) + down_bias[0:1, :]


def code_product(values, weight):
    return dot3(split(values), split(weight), NT)


def tail_back_kernel(
    side, result, cotangent, unit, latent_in, latent, output_gain, head_bias, down,
    weight_last, slope, weight_in, mid, gains, biases, weight_out, *refs, adding
):
    before, refs = refs[: 2 * adding], refs[2 * adding :]
    out_low, preact_low, mid_grad, branch_low, context_grad, sums, head_weight, upstream = refs
    encoder = side[0] == 0
    width = result.shape[1]
    narrow = unit.shape[1]

    @pl.when(pl.program_id(0) == 0)
    def _():
        sums[...] = before[0][...] if adding else jnp.zeros_like(sums)
        head_weight[...] = before[1][...] if adding else jnp.zeros_like(head_weight)

    @pl.when(encoder)
    def _():
        hat, inverse = norm_parts(result[...])
        normed = hat * output_gain[0:1, :] + head_bias[0:1, :]
        code, scale = unit_of(latent[...])
        code_grad = latent_in[...].T + 0.5 * (code - unit[...])
        latent_grad = scale * (code_grad - code * jnp.sum(code * code_grad, -1, keepdims=True))
        pieces = split(latent_grad)
        normed_grad = dot3(pieces, split(down[...]), NN)
        head_weight[...] += dot3(pieces, split(normed), TN)
        sums[8:9, :] += column_sum(normed_grad * hat)
        sums[9:10, :] += column_sum(normed_grad)
        sums[10:11, :narrow] += column_sum(latent_grad)
        upstream[...] = norm_back(normed_grad, output_gain[0:1, :], hat, inverse)

    @pl.when(jnp.logical_not(encoder))
    def _():
        upstream[...] = cotangent[...].astype(F32)

    above = upstream[...]
    low = above.astype(BF)
    out_low[...] = low
    sums[4:5, :] += column_sum(low.astype(F32))
    normed_grad = None
    chunk = 1024
    for start in range(0, weight_in.shape[1], chunk):
        here = slice(start, start + chunk)
        active_grad = dot(low, weight_last[here, :], NT)
        inner = (active_grad * slope[:, here].astype(F32)).astype(BF)
        preact_low[:, here] = inner
        part = column_sum(inner.astype(F32))
        for at in range(0, chunk, min(chunk, width)):
            row, lane = (start + at) // width, (start + at) % width
            size = min(chunk, width)
            sums[row : row + 1, lane : lane + size] += part[:, at : at + size]
        term = dot(inner, weight_in[:, here], NT)
        normed_grad = term if normed_grad is None else normed_grad + term
    hat, inverse = norm_parts(mid[...])
    sums[6:7, :] += column_sum(normed_grad * hat)
    sums[7:8, :] += column_sum(normed_grad)
    middle = above + norm_back(normed_grad, gains[1:2, :], hat, inverse)
    mid_grad[...] = middle
    branch = middle.astype(BF)
    branch_low[...] = branch
    sums[5:6, :] += column_sum(branch.astype(F32))
    context_grad[...] = dot(branch, weight_out[...], NT).astype(BF)


def mark_grads(context_grad, context, grad_mark):
    count = context_grad.shape[0]
    lane_all = lanes((count, 128)) & 63
    across = (
        lax.broadcasted_iota(jnp.int32, (128, 128), 0) // 64 != lanes((128, 128)) // 64
    ).astype(BF)
    zero = jnp.zeros((count, 128), BF)
    for pair in range(context_grad.shape[1] // 128):
        here = slice(pair * 128, pair * 128 + 128)
        product = split(context_grad[:, here].astype(F32) * context[:, here].astype(F32))
        level = -(dot(product[0], across, NN) + dot(product[1], across, NN))
        first = level.astype(BF)
        second, third = split(level - first.astype(F32))
        grad_mark[:, here] = merge(
            lane_all == 0, first, merge(lane_all == 1, second, merge(lane_all == 2, third, zero))
        )


def attend_back_block(
    number, start, extent, base, pairs,
    query, marks, key, value, context_grad, key_mark, grad_mark, query_grad, key_total, value_total,
):
    size = TOKENS
    low_query = lanes((size, 128)) < 64
    rows = pl.ds(pl.multiple_of(number * size, size), size)
    keys = pl.ds(pl.multiple_of(start, WINDOW), extent)
    low_key = lanes((extent, 128)) < 64
    key_aug = key_mark[keys, :]
    ones = jnp.where((lanes((extent, 128)) & 63) < 3, 1.0, 0.0).astype(BF)
    none = jnp.zeros((extent, 128), BF)
    for pair in range(pairs):
        here = pl.ds(pl.multiple_of(base + pair * 128, 128), 128)
        query_pair, key_pair, value_pair = query[rows, here], key[keys, here], value[keys, here]
        grad_pair, query_aug, grad_aug = context_grad[rows, here], marks[rows, here], grad_mark[rows, here]
        found = []
        for swap in (False, True):

            def both(low, left, right):
                return merge(low, right, left) if swap else merge(low, left, right)

            scores = dot(both(low_key, key_pair, key_aug), both(low_query, query_pair, query_aug), NT)
            rise = dot(both(low_key, value_pair, ones), both(low_query, grad_pair, grad_aug), NT)
            chance = jnp.exp2(scores)
            score_grad = (chance * rise).astype(BF)
            found.append(
                (
                    dot(score_grad, query_pair, NN),
                    dot(chance.astype(BF), grad_pair, NN),
                    dot(score_grad, both(low_key, key_pair, none), TN),
                )
            )
        key_total[keys, here] += merge(low_key, found[0][0], found[1][0])
        value_total[keys, here] += merge(low_key, found[0][1], found[1][1])
        query_grad[rows, here] = ((found[0][2] + found[1][2]) * HEAD ** (-0.5)).astype(BF)


def attend_back_kernel(
    windows, query, marks, key, value, context_grad, context, key_mark,
    query_grad, key_grad, value_grad, grad_mark, key_total, value_total, *, row
):
    count = query.shape[0]
    steps = count // TOKENS
    pairs = query.shape[1] // 128
    mark_grads(context_grad, context, grad_mark)
    key_total[...] = jnp.zeros_like(key_total)
    value_total[...] = jnp.zeros_like(value_total)

    def one(turn, carry):
        number = turn
        at = (row * steps + number) * 2

        def run(start, extent):
            attend_back_block(
                number, start, extent, 0, pairs,
                query, marks, key, value, context_grad, key_mark, grad_mark, query_grad, key_total, value_total,
            )

        for_windows(windows[at], windows[at + 1], count, run)
        return carry

    lax.fori_loop(0, steps, one, 0)
    key_grad[...] = (key_total[...] * (1.0 / LOG2E)).astype(BF)
    value_grad[...] = value_total[...].astype(BF)


def entry_back_kernel(
    side, edge, wide, up, head_bias, unit, query_grad, key_grad, value_grad, weight, gains, biases,
    mid_grad, *refs, adding
):
    before, refs = refs[: 2 * adding], refs[2 * adding :]
    entry, latent_out, sums, head_weight = refs
    encoder = side[0] == 0
    width = edge.shape[1]
    narrow = unit.shape[1]

    @pl.when(pl.program_id(0) == 0)
    def _():
        sums[...] = before[0][...] if adding else jnp.zeros_like(sums)
        head_weight[...] = before[1][...] if adding else jnp.zeros_like(head_weight)

    values = entry_values(encoder, edge[...], wide[...], up[...], head_bias[...])
    normed_grad = (
        dot(query_grad[...], weight[:, :width], NT)
        + dot(key_grad[...], weight[:, width : 2 * width], NT)
        + dot(value_grad[...], weight[:, 2 * width :], NT)
    )
    hat, inverse = norm_parts(values)
    sums[0:1, :] += column_sum(query_grad[...].astype(F32))
    sums[1:2, :] += column_sum(value_grad[...].astype(F32))
    sums[2:3, :] += column_sum(normed_grad * hat)
    sums[3:4, :] += column_sum(normed_grad)
    total = mid_grad[...] + norm_back(normed_grad, gains[0:1, :], hat, inverse)
    entry[...] = total

    @pl.when(jnp.logical_not(encoder))
    def _():
        sums[4:5, :] += column_sum(total)
        latent_out[...] = code_product(total, up[...]).T
        head_weight[...] += dot3(split(unit[...]), split(total), TN)


def hidden_weight_kernel(active, out_low, n2, preact_low, *refs):
    out = refs[-1]
    before = refs[0] if len(refs) > 1 else None
    step = pl.program_id(0)
    first = pl.num_programs(0) // 2
    width = n2.shape[1]

    def put(value, rows):
        out[rows, :] = value if before is None else value + before[rows, :]

    @pl.when(step < first)
    def _():
        put(dot(active[...], out_low[...], TN), slice(0, 2 * width))

    @pl.when(step >= first)
    def _():
        value = dot(n2[...], preact_low[...], TN)
        put(value[:, :width], slice(0, width))
        put(value[:, width:], slice(width, 2 * width))


def attention_weight_kernel(context, branch_low, n1, query_grad, key_grad, value_grad, *refs):
    out = refs[-1]
    before = refs[0] if len(refs) > 1 else None
    step = pl.program_id(0)
    width = n1.shape[1]

    def put(value, number):
        rows = slice(number * width, (number + 1) * width)
        out[rows, :] = value if before is None else value + before[rows, :]

    @pl.when(step == 0)
    def _():
        put(dot(context[...], branch_low[...], TN), 0)
        put(dot(n1[...], query_grad[...], TN), 1)

    @pl.when(step == 1)
    def _():
        put(dot(n1[...], key_grad[...], TN), 0)
        put(dot(n1[...], value_grad[...], TN), 1)


def weight_call(kernel, operands, in_specs, steps, before):
    width = operands[1].shape[1]
    out_spec = pl.BlockSpec((2 * width, width), lambda step: (step, 0))
    aliases = {}
    if before is not None:
        aliases = {len(operands): 0}
        operands, in_specs = operands + [before], in_specs + [out_spec]
    return pl.pallas_call(
        kernel,
        grid=(steps,),
        in_specs=in_specs,
        out_specs=out_spec,
        out_shape=jax.ShapeDtypeStruct((2 * steps * width, width), F32),
        input_output_aliases=aliases,
        compiler_params=PARAMS,
    )(*operands)


def hidden_weights(kept, late, before=None):
    operands = [kept.active, late.out_low, kept.n2, late.preact_low]
    count, width = kept.n2.shape
    first = kept.active.shape[1] // (2 * width)
    full = pl.BlockSpec((count, width), lambda step: (0, 0))
    in_specs = [
        pl.BlockSpec((count, 2 * width), lambda step: (0, jnp.minimum(step, first - 1))),
        full,
        full,
        pl.BlockSpec((count, 2 * width), lambda step: (0, jnp.maximum(step - first, 0))),
    ]
    return weight_call(hidden_weight_kernel, operands, in_specs, 2 * first, before)


def attention_weights(kept, late, early, before=None):
    operands = [kept.context, late.branch_low, kept.n1]
    operands += list(early[:3])
    full = pl.BlockSpec(kept.n1.shape, lambda step: (0, 0))
    return weight_call(attention_weight_kernel, operands, [full] * 6, 2, before)


MESH = pl.DeviceIdType.MESH
LEAST_DEVICES = 4


def ring_chip(position, chips):
    odd = position // (chips // 2)
    return (1 - odd) * (2 * position) + odd * (2 * (chips - 1 - position) + 1)


class Ring:
    @staticmethod
    def scratch(arrays, ways, crossing):
        chips = lax.axis_size(DP) // 2
        sizes = [array.shape[0] // (2 * count * chips) for array, count in zip(arrays, ways)]
        shapes = [(count, chips, size, array.shape[1]) for array, count, size in zip(arrays, ways, sizes)]
        buffers = [pltpu.VMEM(shape, F32) for shape in shapes] * 3
        sems = [pltpu.SemaphoreType.DMA(shape[:2]) for shape in shapes] * 10
        far = []
        if crossing is not None:
            count, unused, size, width = shapes[crossing]
            far = [pltpu.VMEM((count, size, width), F32)] + [pltpu.SemaphoreType.DMA((count,))] * 2
        return buffers + sems + far

    def __init__(self, sources, results, ways, crossing, scratch):
        number = len(sources)
        take = lambda at: scratch[at * number : (at + 1) * number]
        self.chips = lax.axis_size(DP) // 2
        self.sources, self.results, self.ways, self.crossing = sources, results, ways, crossing
        self.own, self.pair, self.run = take(0), take(1), take(2)
        (
            self.load_sems, self.pair_send, self.pair_recv, self.run_send, self.run_recv,
            self.keep_sems, self.spread_send, self.spread_recv, self.side_send, self.side_recv,
        ) = (take(at) for at in range(3, 13))
        self.far = scratch[13 * number :]
        self.sizes = [run.shape[2] for run in self.run]
        self.lanes = [(which, way) for way in range(max(ways)) for which in range(number) if way < ways[which]]
        place = lax.axis_index(DP)
        chip, self.core = place // 2, place % 2
        column, odd = chip // 2, chip % 2
        chips = self.chips
        self.position = (1 - odd) * column + odd * (chips - 1 - column)
        self.other = {DP: chip * 2 + (1 - self.core)}
        self.across = {SECTION: 1 - lax.axis_index(SECTION)}
        self.targets = (
            {DP: ring_chip((self.position + 1) % chips, chips) * 2 + self.core},
            {DP: ring_chip((self.position + chips - 1) % chips, chips) * 2 + self.core},
        )

    def greet(self):
        self.barrier = pltpu.get_barrier_semaphore()
        devices = (self.other,) + self.targets + (() if self.crossing is None else (self.across,))
        for device in devices:
            pl.semaphore_signal(self.barrier, inc=1, device_id=device, device_id_type=MESH)
        self.greeted = len(devices)

    def piece(self, step, way):
        return (self.position + (2 * self.chips - step if way % 2 == 0 else step)) % self.chips

    def rows(self, which, half, way, number):
        size = self.sizes[which]
        return pl.ds(pl.multiple_of(((half * self.ways[which] + way) * self.chips + number) * size, 8), size)

    def final(self, which, half, way, step):
        return self.results[which].at[self.rows(which, half, way, self.piece(step + self.chips - 1, way))]

    def load(self, which, way, step):
        return pltpu.make_async_copy(
            self.sources[which].at[self.rows(which, self.core, way, self.piece(step, way))],
            self.own[which].at[way, step],
            self.load_sems[which].at[way, step],
        )

    def remote(self, source, target, send, recv, device):
        return pltpu.make_async_remote_copy(
            src_ref=source, dst_ref=target, send_sem=send, recv_sem=recv, device_id=device, device_id_type=MESH
        )

    def swap(self, which, way, step):
        return self.remote(
            self.sources[which].at[self.rows(which, 1 - self.core, way, self.piece(step, way))],
            self.pair[which].at[way, step],
            self.pair_send[which].at[way, step],
            self.pair_recv[which].at[way, step],
            self.other,
        )

    def pass_on(self, which, way, step):
        return self.remote(
            self.run[which].at[way, step],
            self.run[which].at[way, step + 1],
            self.run_send[which].at[way, step],
            self.run_recv[which].at[way, step + 1],
            self.targets[way % 2],
        )

    def cross(self, way):
        return self.remote(
            self.run[self.crossing].at[way, self.chips - 1],
            self.far[0].at[way],
            self.far[1].at[way],
            self.far[2].at[way],
            self.across,
        )

    def keep(self, which, way):
        return pltpu.make_async_copy(
            self.run[which].at[way, self.chips - 1], self.final(which, self.core, way, 0), self.keep_sems[which].at[way, 0]
        )

    def spread(self, which, way, step, first=False):
        here = self.final(which, self.core, way, step)
        return self.remote(
            self.run[which].at[way, self.chips - 1] if first else here,
            here,
            self.spread_send[which].at[way, step],
            self.spread_recv[which].at[way, step],
            self.targets[way % 2],
        )

    def incoming(self, which, way, step):
        here = self.final(which, self.core, way, step)
        return self.remote(
            here, here, self.spread_send[which].at[way, step], self.spread_recv[which].at[way, step - 1],
            self.targets[way % 2],
        )

    def aside(self, which, way, step, first=False):
        here = self.final(which, self.core, way, step)
        return self.remote(
            self.run[which].at[way, self.chips - 1] if first else here,
            here,
            self.side_send[which].at[way, step],
            self.side_recv[which].at[way, step],
            self.other,
        )

    def beside(self, which, way, step):
        here = self.final(which, 1 - self.core, way, step)
        return self.remote(
            here, here, self.side_send[which].at[way, step], self.side_recv[which].at[way, step], self.other
        )

    def begin(self):
        def load(step, carry):
            for which, way in self.lanes:
                self.load(which, way, step).start()
            return carry

        def swap(step, carry):
            for which, way in self.lanes:
                self.swap(which, way, step).start()
            return carry

        lax.fori_loop(0, self.chips, load, 0)
        pl.semaphore_wait(self.barrier, self.greeted)
        lax.fori_loop(0, self.chips, swap, 0)
        for which, way in self.lanes:
            self.load(which, way, 0).wait()
            self.swap(which, way, 0).wait_recv()
            self.run[which][way, 0] = self.own[which][way, 0] + self.pair[which][way, 0]
            self.pass_on(which, way, 0).start()

    def gather(self, step, lanes=None):
        for which, way in self.lanes if lanes is None else lanes:
            run, own, pair = self.run[which], self.own[which], self.pair[which]
            self.load(which, way, step).wait()
            self.swap(which, way, step).wait_recv()
            self.pass_on(which, way, step - 1).wait_recv()
            run[way, step] = run[way, step] + own[way, step] + pair[way, step]

            @pl.when(step < self.chips - 1)
            def _():
                self.pass_on(which, way, step).start()

    def turn(self):
        for which, way in self.lanes:
            if which == self.crossing:
                self.cross(way).start()
        for which, way in self.lanes:
            if which != self.crossing:
                self.hand_out(which, way)
        for which, way in self.lanes:
            if which == self.crossing:
                run = self.run[which]
                self.cross(way).wait()
                run[way, self.chips - 1] = run[way, self.chips - 1] + self.far[0][way]
                self.hand_out(which, way)

    def hand_out(self, which, way):
        self.spread(which, way, 0, True).start()
        self.aside(which, way, 0, True).start()
        self.keep(which, way).start()

    def pass_out(self, step, lanes=None):
        for which, way in self.lanes if lanes is None else lanes:
            self.incoming(which, way, step).wait_recv()

            @pl.when(step < self.chips - 1)
            def _():
                self.spread(which, way, step).start()

            self.aside(which, way, step).start()

    def finish(self):
        def one(step, carry):
            for which, way in self.lanes:
                self.swap(which, way, step).wait_send()
                self.beside(which, way, step).wait_recv()
                self.aside(which, way, step).wait_send()

                @pl.when(step < self.chips - 1)
                def _():
                    self.pass_on(which, way, step).wait_send()
                    self.spread(which, way, step).wait_send()

            return carry

        lax.fori_loop(0, self.chips, one, 0)
        for which, way in self.lanes:
            self.keep(which, way).wait()


def loop(start, stop, run):
    def one(step, carry):
        run(step)
        return carry

    lax.fori_loop(start, stop, one, 0)


SUM_WAYS = (4, 2)


def sum_kernel(main, misc, main_out, misc_out, *scratch):
    ring = Ring((main, misc), (main_out, misc_out), SUM_WAYS, 1, scratch)
    ring.greet()
    ring.begin()
    loop(1, ring.chips, ring.gather)
    ring.turn()
    loop(1, ring.chips, ring.pass_out)
    ring.finish()


def sum_all(main, misc):
    if lax.axis_size(DP) < LEAST_DEVICES:
        return main, lax.psum(misc, SECTION)
    arrays = (main, misc)
    return pl.pallas_call(
        sum_kernel,
        in_specs=[pl.BlockSpec(memory_space=pl.ANY)] * 2,
        out_specs=[pl.BlockSpec(memory_space=pl.ANY)] * 2,
        out_shape=tuple(jax.ShapeDtypeStruct(array.shape, F32) for array in arrays),
        scratch_shapes=Ring.scratch(arrays, SUM_WAYS, 1),
        compiler_params=pltpu.CompilerParams(collective_id=0, has_side_effects=True, vmem_limit_bytes=40 << 20),
    )(*arrays)


FINISH_WAYS = (4,)


def finish_kernel(
    hidden, attention, query, marks, key, value, context_grad, context, key_mark, edges, mid_grad, weight, branch_low, n1,
    gains, book, down, up, late, early,
    hidden_out, attention_out, misc, entry,
    query_in, marks_in, key_in, value_in, grad_in, context_in, key_mark_in, edge_in, mid_in, weight_in, branch_in, n1_in,
    part, grad_mark, query_grad, key_total, value_total, key_grad, value_grad, in_sems, part_sem, out_sems,
    *scratch,
):
    encoder = lax.axis_index(SECTION) == 0
    ring = Ring((hidden,), (hidden_out,), FINISH_WAYS, None, scratch) if scratch else None
    count, width = query.shape
    narrow = down.shape[0]
    steps = count // TOKENS
    pairs = width // 128
    row = edges.shape[0] - 1
    at = book.shape[0] + 2 * narrow
    inputs = (
        (query, query_in), (marks, marks_in), (key, key_in), (value, value_in), (context_grad, grad_in),
        (context, context_in), (key_mark.at[row], key_mark_in), (edges.at[row], edge_in), (mid_grad, mid_in),
        (weight, weight_in), (branch_low, branch_in), (n1, n1_in),
    )
    loads = [pltpu.make_async_copy(*pair, in_sems.at[number]) for number, pair in enumerate(inputs)]
    part_load = pltpu.make_async_copy(attention, part, part_sem)

    if ring:
        ring.greet()

    @pl.when(encoder)
    def _():
        for load in loads:
            load.start()
        part_load.start()

    if ring:
        ring.begin()
    misc[...] = jnp.zeros_like(misc)

    @pl.when(encoder)
    def _():
        misc[: book.shape[0], :] = book[...]
        misc[book.shape[0] : book.shape[0] + narrow, :] = down[...]
        misc[at : at + 16, :] = late[...]
        misc[at + 16 : at + 32, :] = early[...]
        for load in loads:
            load.wait()
        part_load.wait()
        mark_grads(grad_in, context_in, grad_mark)
        key_total[...] = jnp.zeros_like(key_total)
        value_total[...] = jnp.zeros_like(value_total)

    @pl.when(jnp.logical_not(encoder))
    def _():
        misc[book.shape[0] + narrow : at, :] = up[...]
        misc[at + 32 : at + 48, :] = late[...]
        misc[at + 48 : at + 64, :] = early[...]

    def attention_piece(turn):
        attend_back_block(
            turn // pairs, 0, count, (turn % pairs) * 128, 1,
            query_in, marks_in, key_in, value_in, grad_in, key_mark_in, grad_mark, query_grad, key_total, value_total,
        )

    def entry_piece(number):
        rows = pl.ds(pl.multiple_of(number * TOKENS, TOKENS), TOKENS)
        normed_grad = (
            dot(query_grad[rows, :], weight_in[:, :width], NT)
            + dot(key_grad[rows, :], weight_in[:, width : 2 * width], NT)
            + dot(value_grad[rows, :], weight_in[:, 2 * width :], NT)
        )
        hat, inverse = norm_parts(edge_in[rows, :].astype(F32))
        misc[at + 16 : at + 17, :] += column_sum(query_grad[rows, :].astype(F32))
        misc[at + 17 : at + 18, :] += column_sum(value_grad[rows, :].astype(F32))
        misc[at + 18 : at + 19, :] += column_sum(normed_grad * hat)
        misc[at + 19 : at + 20, :] += column_sum(normed_grad)
        mid_in[rows, :] = mid_in[rows, :] + norm_back(normed_grad, gains[0:1, :], hat, inverse)

    def weight_piece(number):
        def put(left, right):
            rows = pl.ds(pl.multiple_of(number * width, width), width)
            part[rows, :] = part[rows, :] + dot(left[...], right[...], TN)

        for choice, (left, right) in enumerate(
            ((context_in, branch_in), (n1_in, query_grad), (n1_in, key_grad), (n1_in, value_grad))
        ):
            pl.when(number == choice)(functools.partial(put, left, right))

    halves = (ring.lanes[:2], ring.lanes[2:]) if ring else (None, None)
    chips = ring.chips if ring else 8
    pieces = steps * pairs

    def summing(step):
        for half in range(2):
            if ring:
                ring.gather(step, halves[half])

            @pl.when(encoder)
            def _():
                attention_piece(2 * (step - 1) + half)

    inside = min(chips - 1, pieces // 2)
    loop(1, inside + 1, summing)
    if ring:
        loop(inside + 1, chips, ring.gather)
        ring.turn()

    @pl.when(encoder)
    def _():
        loop(2 * inside, pieces, attention_piece)
        key_grad[...] = (key_total[...] * (1.0 / LOG2E)).astype(BF)
        value_grad[...] = value_total[...].astype(BF)

    def spreading(step):
        for half, work in enumerate((entry_piece, weight_piece)):
            if ring:
                ring.pass_out(step, halves[half])

            @pl.when(encoder)
            def _():
                work(step - 1)

    loop(1, steps + 1, spreading)
    stores = [
        pltpu.make_async_copy(mid_in, entry, out_sems.at[0]),
        pltpu.make_async_copy(part, attention_out, out_sems.at[1]),
    ]

    @pl.when(encoder)
    def _():
        for store in stores:
            store.start()

    if ring:
        loop(steps + 1, chips, ring.pass_out)
        ring.finish()

    @pl.when(encoder)
    def _():
        for store in stores:
            store.wait()


def finish_row(work, kept, late, early, book, hidden, attention):
    count, width = kept.n1.shape
    alone = lax.axis_size(DP) < LEAST_DEVICES
    operands = [
        hidden, attention, kept.query, kept.marks, kept.key, kept.value, late.context_grad,
        kept.context, work.key_mark, work.edges, late.mid_grad, work.attention_in, late.branch_low, kept.n1,
        work.gains, book, late.head, early.head, late.sums, early.sums,
    ]
    hbm, vmem = pl.BlockSpec(memory_space=pl.ANY), pl.BlockSpec(memory_space=pltpu.VMEM)
    rows = book.shape[0] + 2 * work.narrow + 64
    unit = 16 * lax.axis_size(DP)
    low = pltpu.VMEM((count, width), BF)
    wide = pltpu.VMEM((count, width), F32)
    scratch = [low] * 6 + [pltpu.VMEM((count, 128), BF), low, wide, pltpu.VMEM(work.attention_in.shape, BF), low, low]
    scratch += [pltpu.VMEM(attention.shape, F32), low, low, wide, wide, low, low]
    scratch += [pltpu.SemaphoreType.DMA((12,)), pltpu.SemaphoreType.DMA, pltpu.SemaphoreType.DMA((2,))]
    settings = {}
    if not alone:
        scratch += Ring.scratch((hidden,), FINISH_WAYS, None)
        settings = dict(collective_id=1, has_side_effects=True)
    outs = pl.pallas_call(
        finish_kernel,
        in_specs=[hbm] * 14 + [vmem] * 6,
        out_specs=[hbm, hbm, vmem, hbm],
        out_shape=(
            jax.ShapeDtypeStruct(hidden.shape, F32),
            jax.ShapeDtypeStruct(attention.shape, F32),
            jax.ShapeDtypeStruct((rows + (-rows % unit), width), F32),
            jax.ShapeDtypeStruct((count, width), F32),
        ),
        scratch_shapes=scratch,
        input_output_aliases={1: 1},
        compiler_params=pltpu.CompilerParams(vmem_limit_bytes=58 << 20, **settings),
    )(*operands)
    return (hidden,) + tuple(outs[1:]) if alone else outs


def unpack_kernel(
    side, hidden, attention, misc, first_entry, second_entry, first_result, second_result,
    hidden_out, hidden_in, attention_out, attention_in, edge, book, gains, biases, bias, last_gain, head_bias, down, down_last,
    up, held, head, rows, ins, outs, row_ins, row_outs,
):
    width = hidden.shape[1]
    narrow = book.shape[0]
    steps = hidden_out.shape[0] // width
    targets = [hidden_out.at[pl.ds(number * width, width), :] for number in range(steps)]
    targets += [hidden_in.at[:, pl.ds(number * width, width)] for number in range(steps)]
    targets += [attention_out]
    targets += [attention_in.at[:, pl.ds(number * width, width)] for number in range(3)]
    sources = [hidden.at[pl.ds(number * width, width), :] for number in range(2 * steps)]
    sources += [attention.at[pl.ds(number * width, width), :] for number in range(4)]
    tiles = range(len(targets))
    for mine, pair in ((0, (first_entry, second_entry)), (1, (first_result, second_result))):

        @pl.when(side[0] == mine)
        def _():
            for row in range(2):
                pltpu.make_async_copy(pair[row], rows.at[row], row_ins.at[row]).start()

    loads = [pltpu.make_async_copy(sources[number], held.at[number], ins.at[number]) for number in tiles]
    loads.append(pltpu.make_async_copy(misc.at[pl.ds(0, head.shape[0]), :], head, ins.at[len(targets)]))
    for load in loads:
        load.start()
    stores = []
    for row in range(2):
        pltpu.make_async_copy(first_entry, rows.at[row], row_ins.at[row]).wait()
        stores.append(pltpu.make_async_copy(rows.at[row], edge.at[row], row_outs.at[row]))
        stores[-1].start()
    for number in tiles:
        loads[number].wait()
        stores.append(pltpu.make_async_copy(held.at[number], targets[number], outs.at[number]))
        stores[-1].start()
    loads[-1].wait()
    for number in range(book.shape[1] // width):
        book[:, number * width : (number + 1) * width] = head[number * narrow : (number + 1) * narrow, :]
    at = book.shape[0] * book.shape[1] // width
    down[...] = head[at : at + narrow, :]
    up[...] = head[at + narrow : at + 2 * narrow, :]
    at += 2 * narrow
    last_gain[...] = head[at + 8 : at + 9, :]
    head_bias[0:1, :] = head[at + 9 : at + 10, :]
    head_bias[1:2, :] = head[at + 52 : at + 53, :]
    down_last[...] = head[at + 10 : at + 11, :narrow]
    mine = jnp.where(side[0] == 0, head[at : at + 32, :], head[at + 32 : at + 64, :])
    bias[...] = mine[:steps, :]
    for out, places in ((gains, (18, 6)), (biases, (16, 17, 5, 19, 7, 4))):
        for number, place in enumerate(places):
            out[number : number + 1, :] = mine[place : place + 1, :]
    for store in stores:
        store.wait()


def unpack(side, hidden, attention, misc, ends, table_turned):
    width = hidden.shape[1]
    features = hidden.shape[0] // 2
    tiles = (hidden.shape[0] + attention.shape[0]) // width
    narrow = table_turned.shape[0]
    rows = table_turned.size // width + 2 * narrow + 64
    shapes = (
        (features, width), (width, features), (width, width), (width, 3 * width), (2,) + ends[0].shape,
        table_turned.shape, (2, width), (6, width), (features // width, width), (1, width), (2, width),
        (narrow, width), (1, narrow), (narrow, width),
    )
    hbm, vmem = pl.BlockSpec(memory_space=pl.ANY), pl.BlockSpec(memory_space=pltpu.VMEM)
    return pl.pallas_call(
        unpack_kernel,
        in_specs=[pl.BlockSpec(memory_space=pltpu.SMEM)] + [hbm] * 7,
        out_specs=[hbm] * 5 + [vmem] * 9,
        out_shape=tuple(jax.ShapeDtypeStruct(shape, F32) for shape in shapes),
        scratch_shapes=[
            pltpu.VMEM((tiles, width, width), F32),
            pltpu.VMEM((rows, width), F32),
            pltpu.VMEM((2,) + ends[0].shape, F32),
            pltpu.SemaphoreType.DMA((tiles + 1,)),
            pltpu.SemaphoreType.DMA((tiles,)),
            pltpu.SemaphoreType.DMA((2,)),
            pltpu.SemaphoreType.DMA((2,)),
        ],
        compiler_params=PARAMS,
    )(side, hidden, attention, misc, *ends)


def nothing_kernel(*refs):
    pass


def unwritten(shapes):
    leaves, tree = jax.tree.flatten(shapes)
    arrays = pl.pallas_call(
        nothing_kernel,
        out_specs=[pl.BlockSpec(memory_space=pl.ANY)] * len(leaves),
        out_shape=tuple(leaves),
    )()
    return jax.tree.unflatten(tree, arrays)


class Kept(NamedTuple):
    n1: Any
    query: Any
    key: Any
    value: Any
    context: Any
    marks: Any
    mid: Any
    n2: Any
    active: Any
    slope: Any
    result: Any
    latent: Any


class Late(NamedTuple):
    out_low: Any
    preact_low: Any
    mid_grad: Any
    branch_low: Any
    context_grad: Any
    sums: Any
    head: Any


class Early(NamedTuple):
    query_grad: Any
    key_grad: Any
    value_grad: Any
    entry: Any
    latent_out: Any
    sums: Any
    head: Any


class Rows:
    def __init__(self, side, edges, wide, unit, windows, query_mark, key_mark, weights, head):
        self.side, self.edges, self.wide, self.unit = side, edges, wide, unit
        self.windows, self.query_mark, self.key_mark = windows, query_mark, key_mark
        (
            self.attention_in, self.attention_out, self.hidden_in, self.hidden_out,
            self.gains, self.biases, self.hidden_bias,
        ) = weights
        (
            self.output_gain, self.head_bias, self.down, self.down_bias, self.up,
        ) = head
        self.rows, self.count, self.width = edges.shape
        self.hidden = self.hidden_in.shape[1]
        self.narrow = unit.shape[1]
        n, d, f = self.count, self.width, self.hidden
        shape = jax.ShapeDtypeStruct
        low, tall, wide = shape((n, d), BF), shape((n, f), BF), shape((n, d), F32)
        sums, head = shape((16, d), F32), shape((self.narrow, d), F32)
        self.kept = Kept(low, low, low, low, low, low, wide, low, tall, tall, wide, shape((n, self.narrow), F32))
        self.late = Late(low, tall, wide, low, low, sums, head)
        self.early = Early(low, low, low, wide, shape((self.narrow, n), F32), sums, head)

    def side_spec(self):
        return pl.BlockSpec(memory_space=pltpu.SMEM)

    def tokens(self, array):
        return pl.BlockSpec((TOKENS, array.shape[1]), lambda step: (step, 0))

    def turned(self, array):
        return pl.BlockSpec((array.shape[0], TOKENS), lambda step: (0, step))

    def whole(self, array):
        return pl.BlockSpec(array.shape, lambda step: (0,) * len(array.shape))

    def entry_specs(self, row):
        steps = self.count // TOKENS
        return [
            pl.BlockSpec((None, TOKENS, self.width), lambda step: (row, step, 0)),
            pl.BlockSpec((TOKENS, self.wide.shape[1]), lambda step: (row * steps + step, 0)),
            self.whole(self.up),
            self.whole(self.head_bias),
        ]

    def unit_spec(self, row):
        steps = self.count // TOKENS
        return pl.BlockSpec((TOKENS, self.narrow), lambda step: (row * steps + step, 0))

    def call(self, kernel, in_specs, operands, outs, out_specs, scratch=()):
        return pl.pallas_call(
            kernel,
            grid=(self.count // TOKENS,),
            in_specs=in_specs,
            out_specs=out_specs,
            out_shape=tuple(outs),
            scratch_shapes=list(scratch),
            compiler_params=PARAMS,
        )(*operands)

    def attention_call(self, kernel, row, operands, outs, scratch=()):
        half = self.width // 2

        def spec(array):
            if array.ndim == 3:
                return pl.BlockSpec((None, self.count, array.shape[2]), lambda step, info: (row, 0, 0))
            return pl.BlockSpec((self.count, half), lambda step, info: (0, step))

        return pl.pallas_call(
            functools.partial(kernel, row=row),
            grid_spec=pltpu.PrefetchScalarGridSpec(
                num_scalar_prefetch=1,
                grid=(2,),
                in_specs=[spec(array) for array in operands],
                out_specs=[spec(array) for array in outs],
                scratch_shapes=list(scratch),
            ),
            out_shape=tuple(outs),
            compiler_params=PARAMS,
        )(self.windows, *operands)

    def forward(self, row):
        shapes = self.kept
        entry = (self.edges, self.wide, self.up, self.head_bias)
        outs = shapes[:4]
        n1, query, key, value = self.call(
            project_kernel,
            [self.side_spec()] + self.entry_specs(row)
            + [self.whole(self.gains), self.whole(self.biases), self.whole(self.attention_in)],
            (self.side,) + entry + (self.gains, self.biases, self.attention_in),
            outs,
            [self.tokens(array) for array in outs],
        )
        context, marks = self.attention_call(
            attend_kernel, row, (query, key, value, self.query_mark, self.key_mark), shapes[4:6]
        )
        consts = (
            self.attention_out, self.gains, self.biases, self.hidden_in, self.hidden_bias, self.hidden_out,
            self.output_gain, self.down, self.down_bias,
        )
        outs = shapes[6:]
        outs = self.call(
            hidden_kernel,
            [self.side_spec()] + self.entry_specs(row) + [self.tokens(context)]
            + [self.whole(array) for array in consts],
            (self.side,) + entry + (context,) + consts,
            outs,
            [self.tokens(array) for array in outs],
        )
        return Kept(n1, query, key, value, context, marks, *outs)

    def backward(self, row, kept, latent_in, former=(None, None)):
        late = self.backward_late(row, kept, latent_in, former[0])
        return late, self.backward_early(row, kept, late, former[1])

    def backward_late(self, row, kept, latent_in, former=None):
        prior = () if former is None else (former.sums, former.head)
        adding = int(former is not None)
        consts = (self.output_gain, self.head_bias, self.down, self.hidden_out)
        late = (self.gains, self.biases, self.attention_out)
        outs = self.late
        return Late(*self.call(
            functools.partial(tail_back_kernel, adding=adding),
            [self.side_spec(), self.tokens(kept.result), self.entry_specs(row)[0], self.unit_spec(row),
             self.turned(latent_in), self.tokens(kept.latent)]
            + [self.whole(array) for array in consts]
            + [self.tokens(kept.slope), self.whole(self.hidden_in), self.tokens(kept.mid)]
            + [self.whole(array) for array in late + prior],
            (self.side, kept.result, self.edges, self.unit, latent_in, kept.latent) + consts
            + (kept.slope, self.hidden_in, kept.mid) + late + prior,
            outs,
            [self.tokens(array) for array in outs[:5]] + [self.whole(array) for array in outs[5:]],
            scratch=[pltpu.VMEM((TOKENS, self.width), F32)],
        ))

    def backward_early(self, row, kept, late, former=None):
        adding = int(former is not None)
        half = self.width // 2
        grads = tuple(self.attention_call(
            attend_back_kernel, row,
            (kept.query, kept.marks, kept.key, kept.value, late.context_grad, kept.context, self.key_mark),
            self.early[:3],
            scratch=[
                pltpu.VMEM((self.count, half), BF),
                pltpu.VMEM((self.count, half), F32),
                pltpu.VMEM((self.count, half), F32),
            ],
        ))
        prior = () if former is None else (former.sums, former.head)
        outs = self.early[3:]
        outs = self.call(
            functools.partial(entry_back_kernel, adding=adding),
            [self.side_spec()] + self.entry_specs(row) + [self.unit_spec(row)]
            + [self.tokens(array) for array in grads]
            + [self.whole(self.attention_in), self.whole(self.gains), self.whole(self.biases),
               self.tokens(late.mid_grad)] + [self.whole(array) for array in prior],
            (self.side, self.edges, self.wide, self.up, self.head_bias, self.unit) + grads
            + (self.attention_in, self.gains, self.biases, late.mid_grad) + prior,
            outs,
            [self.tokens(outs[0]), self.turned(outs[1])] + [self.whole(array) for array in outs[2:]],
        )
        return Early(*grads, *outs)


def windows_of(segments):
    rows, count = segments.shape
    steps = count // WINDOW
    blocks = segments.reshape(rows, steps, WINDOW)
    least, most = blocks[:, :, 0], blocks[:, :, -1]
    meets = (most[:, :, None] >= least[:, None, :]) & (least[:, :, None] <= most[:, None, :])
    place = jnp.arange(steps)
    start = jnp.min(jnp.where(meets, place, steps), -1)
    stop = jnp.max(jnp.where(meets, place, -1), -1) + 1
    return jnp.stack([start, stop - start], -1).reshape(-1).astype(jnp.int32)


def on_device(
    boundary, segments, code_index, attention_in, attention_out, hidden_in, hidden_out, block_gains,
    block_biases, hidden_bias, output_gain, head_bias, down_weight, down_bias, up_weight, codebook,
):
    section = lax.axis_index(SECTION)
    encoder = section == 0
    side = section.astype(jnp.int32)[None]
    edges = boundary[0]
    rows, count, width = edges.shape
    hidden = hidden_in.shape[2]
    table_turned = codebook.T
    unit, wide, query_mark, key_mark = gather_codes(code_index, table_turned, segments)
    work = Rows(
        side, edges, wide, unit, windows_of(segments), query_mark, key_mark,
        (
            attention_in[0], attention_out[0], hidden_in[0], hidden_out[0], block_gains[0], block_biases[0],
            hidden_bias,
        ),
        (output_gain[None], head_bias, down_weight.T, down_bias[None], up_weight),
    )
    book_out = book_shape(table_turned, width)
    hidden_shape = jax.ShapeDtypeStruct((2 * hidden, width), F32)
    attention_shape = jax.ShapeDtypeStruct((4 * width, width), F32)
    quiet = jnp.zeros((unit.shape[1], count), F32)
    first_kept = work.forward(0)

    def encoder_second():
        kept = work.forward(1)
        book = scatter_codes(code_index, unit, (first_kept.latent, kept.latent), table_turned, width)
        return (kept, *unwritten((work.late, work.early)), book)

    def decoder_first():
        kept, book = unwritten((work.kept, book_out))
        return (kept, *work.backward(0, first_kept, quiet), book)

    kept_a, late_a, early_a, book = lax.cond(encoder, encoder_second, decoder_first)
    latent_in = lax.ppermute(early_a.latent_out, SECTION, [(1, 0)])

    def encoder_third():
        late, early = work.backward(0, first_kept, latent_in)
        weights = hidden_weights(first_kept, late), attention_weights(first_kept, late, early)
        return unwritten(work.kept), late, early, weights

    def decoder_third():
        kept = work.forward(1)
        return (kept, *work.backward(1, kept, quiet, (late_a, early_a)), unwritten((hidden_shape, attention_shape)))

    kept_b, late_b, early_b, weights_b = lax.cond(encoder, encoder_third, decoder_third)
    latent_in_second = lax.ppermute(early_b.latent_out, SECTION, [(1, 0)])

    def encoder_fifth():
        late = work.backward_late(1, kept_a, latent_in_second, late_b)
        return hidden_weights(kept_a, late, weights_b[0]), weights_b[1], late[2:]

    def decoder_fifth():
        total = hidden_weights(kept_b, late_b, hidden_weights(first_kept, late_a))
        attention = attention_weights(kept_b, late_b, early_b, attention_weights(first_kept, late_a, early_a))
        return total, attention, (*unwritten(work.late[2:5]), late_b.sums, late_b.head)

    hidden_total, attention_total, late = lax.cond(encoder, encoder_fifth, decoder_fifth)
    late = Late(None, None, *late)
    hidden_total, attention_total, misc, second_entry = finish_row(
        work, kept_a, late, early_b, book, hidden_total, attention_total
    )
    attention_total, misc = sum_all(attention_total, misc)
    (
        hidden_out_grad, hidden_in_grad, attention_out_grad, attention_in_grad, edge, book, gains, biases, bias,
        last_gain, head, down_grad, down_last, up_grad,
    ) = unpack(
        side, hidden_total, attention_total, misc,
        (early_b.entry, second_entry, first_kept.result, kept_b.result), table_turned,
    )
    return (
        edge[None],
        attention_in_grad[None],
        attention_out_grad[None],
        hidden_in_grad[None],
        hidden_out_grad[None],
        gains[None],
        biases[None],
        bias.reshape(1, hidden),
        last_gain[0],
        head,
        down_grad.T,
        down_last[0],
        up_grad,
        book.T,
    )


def solution(mesh):
    wide, split_last, flat = P(SECTION, DP, None, None), P(SECTION, None, None), P(SECTION, None)
    blocks = (split_last,) * 6 + (flat,)
    return jax.shard_map(
        on_device,
        mesh=mesh,
        in_specs=(wide, P(DP, None), P(DP, None)) + blocks + (P(),) * 6,
        out_specs=(wide,) + blocks + (P(),) * 6,
        check_vma=False,
    )
```

```python
import functools
import math
from typing import Any, NamedTuple

import jax
import jax.numpy as jnp
from jax import lax
from jax.experimental import pallas as pl
from jax.experimental.pallas import tpu as pltpu
from jax.sharding import PartitionSpec as P

HEAD = 64
SECTION, DP = "section", "dp"
BF = jnp.bfloat16
F32 = jnp.float32
LOG2E = math.log2(math.e)
NORM_EPS = 1e-06
MASKED = -1e30
GELU = 0.7978845608028654
CUBIC = 0.044715
NN = (((1,), (0,)), ((), ()))
NT = (((1,), (1,)), ((), ()))
TN = (((0,), (0,)), ((), ()))
TOKENS = 256
WINDOW = 256
PARAMS = pltpu.CompilerParams(vmem_limit_bytes=56 << 20)


def dot(a, b, dims):
    return lax.dot_general(a, b, dims, preferred_element_type=F32)


def lanes(shape):
    return lax.broadcasted_iota(jnp.int32, shape, 1)


def split(values):
    high = values.astype(BF)
    return high, (values - high.astype(F32)).astype(BF)


def dot3(left, right, dims):
    return dot(left[0], right[0], dims) + dot(left[0], right[1], dims) + dot(left[1], right[0], dims)


def unit_of(values):
    scale = lax.rsqrt(jnp.sum(values * values, -1, keepdims=True) + NORM_EPS)
    return values * scale, scale


def norm_parts(values):
    center = values - jnp.mean(values, -1, keepdims=True)
    inverse = lax.rsqrt(jnp.mean(center * center, -1, keepdims=True) + NORM_EPS)
    return center * inverse, inverse


def norm_back(grad, gain, hat, inverse):
    scaled = grad * gain
    return inverse * (
        scaled
        - jnp.mean(scaled, -1, keepdims=True)
        - hat * jnp.mean(scaled * hat, -1, keepdims=True)
    )


def column_sum(values):
    return jnp.sum(values, 0, keepdims=True)


def code_kernel(index, table_turned, segments, unit, wide, query_mark, key_mark, table, raw):
    count = raw.shape[0]
    block = 512

    def turn(step, carry):
        start = pl.multiple_of(step * block, block)
        table[pl.ds(start, block), :] = table_turned[:, pl.ds(start, block)].T
        return carry

    lax.fori_loop(0, table.shape[0] // block, turn, 0)

    length = segments.shape[1]

    def some(step, carry):
        for inner in range(16):
            token = step * 16 + inner
            raw[pl.ds(token, 1), :] = table[pl.ds(index[token], 1), :]
        return carry

    lax.fori_loop(0, count // 16, some, 0)

    values = raw[...]
    values = values * lax.rsqrt(jnp.sum(values * values, -1, keepdims=True) + NORM_EPS)
    unit[...] = values
    high, low = split(values)
    wide[...] = jnp.concatenate([high, low, high, jnp.zeros_like(high)], 1)
    lane = lanes((length, 128)) & 63
    for row in range(segments.shape[0]):
        owner = jnp.broadcast_to(segments[row : row + 1, :], (128, length)).T
        same = owner == lane
        query_mark[row] = jnp.where((lane < 4) & jnp.logical_not(same), MASKED, 0.0).astype(BF)
        key_mark[row] = jnp.where(((lane < 4) & same) | ((lane > 3) & (lane < 7)), 1.0, 0.0).astype(BF)


def gather_codes(index, table_turned, segments):
    count, width = index.shape[0], table_turned.shape[0]
    vmem = pl.BlockSpec(memory_space=pltpu.VMEM)
    mark = jax.ShapeDtypeStruct(segments.shape + (128,), BF)
    return pl.pallas_call(
        code_kernel,
        in_specs=[pl.BlockSpec(memory_space=pltpu.SMEM), vmem, vmem],
        out_specs=[vmem] * 4,
        out_shape=(
            jax.ShapeDtypeStruct((count, width), F32),
            jax.ShapeDtypeStruct((count, 4 * width), BF),
            mark,
            mark,
        ),
        scratch_shapes=[pltpu.VMEM(table_turned.shape[::-1], F32), pltpu.VMEM((count, width), F32)],
        compiler_params=PARAMS,
    )(index, table_turned, segments)


def scatter_kernel(index, unit, latent_first, latent_second, table_turned, out, total, rows):
    count = rows.shape[0]
    width = unit.shape[1]
    half = count // 2
    total[...] = jnp.zeros_like(total)
    for row, latent in enumerate((latent_first, latent_second)):
        here = slice(row * half, (row + 1) * half)
        code, unused = unit_of(latent[...])
        rows[here, :] = 2.0 * (unit[here, :] - code)

    def some(step, carry):
        for inner in range(8):
            token = step * 8 + inner
            place = pl.ds(index[token], 1)
            total[place, :] = total[place, :] + rows[pl.ds(token, 1), :]
        return carry

    lax.fori_loop(0, count // 8, some, 0)
    block = out.shape[1]

    def back(step, carry):
        start = pl.multiple_of(step * block, block)
        values = table_turned[:, pl.ds(start, block)]
        grad = total[pl.ds(start, block), :].T
        inverse = lax.rsqrt(jnp.sum(values * values, 0, keepdims=True) + NORM_EPS)
        book = values * inverse
        out[pl.ds(pl.multiple_of(step * width, width), width), :] = inverse * (
            grad - book * jnp.sum(book * grad, 0, keepdims=True)
        )
        return carry

    lax.fori_loop(0, total.shape[0] // block, back, 0)


def book_shape(table_turned, width):
    return jax.ShapeDtypeStruct((table_turned.size // width, width), F32)


def scatter_codes(index, unit, latents, table_turned, width):
    return pl.pallas_call(
        scatter_kernel,
        in_specs=[pl.BlockSpec(memory_space=pltpu.SMEM)] + [pl.BlockSpec(memory_space=pltpu.VMEM)] * 4,
        out_specs=pl.BlockSpec(memory_space=pltpu.VMEM),
        out_shape=book_shape(table_turned, width),
        scratch_shapes=[pltpu.VMEM(table_turned.shape[::-1], F32), pltpu.VMEM(unit.shape, F32)],
        compiler_params=PARAMS,
    )(index, unit, *latents, table_turned)


def entry_values(encoder, edge, wide, up, head_bias):
    high, low = split(up)
    parts = jnp.concatenate([high, high, low, jnp.zeros_like(low)], 0)
    return jnp.where(encoder, edge.astype(F32), dot(wide, parts, NN) + head_bias[1:2, :])


def project_kernel(side, edge, wide, up, head_bias, gains, biases, weight, n1, query, key, value):
    width = edge.shape[1]
    encoder = side[0] == 0
    values = entry_values(encoder, edge[...], wide[...], up[...], head_bias[...])
    hat, unused = norm_parts(values)
    normed = (hat * gains[0:1, :] + biases[3:4, :]).astype(BF)
    n1[...] = normed
    query[...] = (
        (dot(normed, weight[:, :width], NN) + biases[0:1, :]) * (LOG2E * HEAD ** (-0.5))
    ).astype(BF)
    key[...] = dot(normed, weight[:, width : 2 * width], NN).astype(BF)
    value[...] = (dot(normed, weight[:, 2 * width :], NN) + biases[1:2, :]).astype(BF)


def merge(low_half, left, right):
    return jnp.where(low_half, left, right)


def attend_kernel(windows, query, key, value, query_mark, key_mark, context, marks, *, row):
    count = query.shape[0]
    size = TOKENS
    pairs = query.shape[1] // 128
    low_query = lanes((size, 128)) < 64
    mark_lane = lanes((size, 128)) & 63

    def block(number, start, extent):
        rows = pl.ds(pl.multiple_of(number * size, size), size)
        keys = pl.ds(pl.multiple_of(start, WINDOW), extent)
        low_key = lanes((extent, 128)) < 64
        query_aug, key_aug = query_mark[rows, :], key_mark[keys, :]
        ones = jnp.ones((extent, 128), BF)
        scores = []
        for pair in range(pairs):
            here = slice(pair * 128, pair * 128 + 128)
            query_pair, key_pair = query[rows, here], key[keys, here]
            scores.append(
                dot(merge(low_query, query_pair, query_aug), merge(low_key, key_pair, key_aug), NT)
            )
            scores.append(
                dot(merge(low_query, query_aug, query_pair), merge(low_key, key_aug, key_pair), NT)
            )
        tops = [jnp.max(score, -1, keepdims=True) for score in scores]
        raised = [jnp.exp2(score - top).astype(BF) for score, top in zip(scores, tops)]
        for pair in range(pairs):
            here = slice(pair * 128, pair * 128 + 128)
            value_pair = value[keys, here]
            even = dot(raised[2 * pair], merge(low_key, value_pair, ones), NN)
            odd = dot(raised[2 * pair + 1], merge(low_key, ones, value_pair), NN)
            total = merge(low_query, odd, even)
            context[rows, here] = (
                merge(low_query, even, odd) / pltpu.roll(total, 64, 1)
            ).astype(BF)
            level = -(merge(low_query, tops[2 * pair + 1], tops[2 * pair]) + jnp.log2(total))
            first = level.astype(BF)
            rest = level - first.astype(F32)
            second, third = split(rest)
            marks[rows, here] = merge(
                mark_lane == 4, first, merge(mark_lane == 5, second, merge(mark_lane == 6, third, query_aug))
            )

    def one(number, carry):
        base = (row * (count // size) + number) * 2
        for_windows(windows[base], windows[base + 1], count, functools.partial(block, number))
        return carry

    lax.fori_loop(0, count // size, one, 0)


def for_windows(start, steps, count, run):
    extents = list(range(2 * WINDOW, count + 1, WINDOW))
    for position, extent in enumerate(extents):
        take = steps * WINDOW <= extent
        if position:
            take = take & (steps * WINDOW > extents[position - 1])

        @pl.when(take)
        def _():
            run(jnp.minimum(start * WINDOW, count - extent), extent)


def gelu_parts(values):
    square = values * values
    half = 0.5 + 0.5 * jnp.tanh(values * (GELU + (GELU * CUBIC) * square))
    active = values * half
    slope = half + active * (1.0 - half) * (2.0 * GELU + (6.0 * GELU * CUBIC) * square)
    return active, slope


def hidden_kernel(
    side, edge, wide, up, head_bias, context, weight_out, gains, biases, weight_in, hidden_bias,
    weight_last, output_gain, down, down_bias,
    mid, n2, active_out, slope_out, result, latent_out,
):
    encoder = side[0] == 0
    width = edge.shape[1]
    values = entry_values(encoder, edge[...], wide[...], up[...], head_bias[...])
    midway = values + (dot(context[...], weight_out[...], NN) + biases[2:3, :])
    mid[...] = midway
    hat, unused = norm_parts(midway)
    normed = (hat * gains[1:2, :] + biases[4:5, :]).astype(BF)
    n2[...] = normed
    total = midway + biases[5:6, :]
    chunk = 256
    for start in range(0, weight_in.shape[1], chunk):
        here = slice(start, start + chunk)
        active, slope = gelu_parts(dot(normed, weight_in[:, here], NN) + hidden_bias[0:1, here])
        active = active.astype(BF)
        active_out[:, here] = active
        slope_out[:, here] = slope.astype(BF)
        total = total + dot(active, weight_last[here, :], NN)
    result[...] = total

    @pl.when(encoder)
    def _():
        last_hat, unused = norm_parts(total)
        code = last_hat * output_gain[0:1, :] + head_bias[0:1, :]
        latent_out[...] = code_product(code, down[...]) + down_bias[0:1, :]


def code_product(values, weight):
    return dot3(split(values), split(weight), NT)


def tail_back_kernel(
    side, result, cotangent, unit, latent_in, latent, output_gain, head_bias, down,
    weight_last, slope, weight_in, mid, gains, biases, weight_out, *refs, adding
):
    before, refs = refs[: 2 * adding], refs[2 * adding :]
    out_low, preact_low, mid_grad, branch_low, context_grad, sums, head_weight, upstream = refs
    encoder = side[0] == 0
    width = result.shape[1]
    narrow = unit.shape[1]

    @pl.when(pl.program_id(0) == 0)
    def _():
        sums[...] = before[0][...] if adding else jnp.zeros_like(sums)
        head_weight[...] = before[1][...] if adding else jnp.zeros_like(head_weight)

    @pl.when(encoder)
    def _():
        hat, inverse = norm_parts(result[...])
        normed = hat * output_gain[0:1, :] + head_bias[0:1, :]
        code, scale = unit_of(latent[...])
        code_grad = latent_in[...].T + 0.5 * (code - unit[...])
        latent_grad = scale * (code_grad - code * jnp.sum(code * code_grad, -1, keepdims=True))
        pieces = split(latent_grad)
        normed_grad = dot3(pieces, split(down[...]), NN)
        head_weight[...] += dot(pieces[0], normed.astype(BF), TN) + dot(pieces[1], normed.astype(BF), TN)
        sums[8:9, :] += column_sum(normed_grad * hat)
        sums[9:10, :] += column_sum(normed_grad)
        sums[10:11, :narrow] += column_sum(latent_grad)
        upstream[...] = norm_back(normed_grad, output_gain[0:1, :], hat, inverse)

    @pl.when(jnp.logical_not(encoder))
    def _():
        upstream[...] = cotangent[...].astype(F32)

    above = upstream[...]
    low = above.astype(BF)
    out_low[...] = low
    sums[4:5, :] += column_sum(low.astype(F32))
    normed_grad = None
    chunk = 1024
    for start in range(0, weight_in.shape[1], chunk):
        here = slice(start, start + chunk)
        active_grad = dot(low, weight_last[here, :], NT)
        inner = (active_grad * slope[:, here].astype(F32)).astype(BF)
        preact_low[:, here] = inner
        part = column_sum(inner.astype(F32))
        for at in range(0, chunk, min(chunk, width)):
            row, lane = (start + at) // width, (start + at) % width
            size = min(chunk, width)
            sums[row : row + 1, lane : lane + size] += part[:, at : at + size]
        term = dot(inner, weight_in[:, here], NT)
        normed_grad = term if normed_grad is None else normed_grad + term
    hat, inverse = norm_parts(mid[...])
    sums[6:7, :] += column_sum(normed_grad * hat)
    sums[7:8, :] += column_sum(normed_grad)
    middle = above + norm_back(normed_grad, gains[1:2, :], hat, inverse)
    mid_grad[...] = middle
    branch = middle.astype(BF)
    branch_low[...] = branch
    sums[5:6, :] += column_sum(branch.astype(F32))
    context_grad[...] = dot(branch, weight_out[...], NT).astype(BF)


def mark_grads(context_grad, context, grad_mark):
    count = context_grad.shape[0]
    lane_all = lanes((count, 128)) & 63
    across = (
        lax.broadcasted_iota(jnp.int32, (128, 128), 0) // 64 != lanes((128, 128)) // 64
    ).astype(BF)
    zero = jnp.zeros((count, 128), BF)
    for pair in range(context_grad.shape[1] // 128):
        here = slice(pair * 128, pair * 128 + 128)
        product = split(context_grad[:, here].astype(F32) * context[:, here].astype(F32))
        level = -(dot(product[0], across, NN) + dot(product[1], across, NN))
        first = level.astype(BF)
        second, third = split(level - first.astype(F32))
        grad_mark[:, here] = merge(
            lane_all == 0, first, merge(lane_all == 1, second, merge(lane_all == 2, third, zero))
        )


def attend_back_block(
    number, start, extent, base, pairs,
    query, marks, key, value, context_grad, key_mark, grad_mark, query_grad, key_total, value_total,
):
    size = TOKENS
    low_query = lanes((size, 128)) < 64
    rows = pl.ds(pl.multiple_of(number * size, size), size)
    keys = pl.ds(pl.multiple_of(start, WINDOW), extent)
    low_key = lanes((extent, 128)) < 64
    key_aug = key_mark[keys, :]
    ones = jnp.where((lanes((extent, 128)) & 63) < 3, 1.0, 0.0).astype(BF)
    none = jnp.zeros((extent, 128), BF)
    for pair in range(pairs):
        here = pl.ds(pl.multiple_of(base + pair * 128, 128), 128)
        query_pair, key_pair, value_pair = query[rows, here], key[keys, here], value[keys, here]
        grad_pair, query_aug, grad_aug = context_grad[rows, here], marks[rows, here], grad_mark[rows, here]
        found = []
        for swap in (False, True):

            def both(low, left, right):
                return merge(low, right, left) if swap else merge(low, left, right)

            scores = dot(both(low_key, key_pair, key_aug), both(low_query, query_pair, query_aug), NT)
            rise = dot(both(low_key, value_pair, ones), both(low_query, grad_pair, grad_aug), NT)
            chance = jnp.exp2(scores)
            score_grad = (chance * rise).astype(BF)
            found.append(
                (
                    dot(score_grad, query_pair, NN),
                    dot(chance.astype(BF), grad_pair, NN),
                    dot(score_grad, both(low_key, key_pair, none), TN),
                )
            )
        key_total[keys, here] += merge(low_key, found[0][0], found[1][0])
        value_total[keys, here] += merge(low_key, found[0][1], found[1][1])
        query_grad[rows, here] = ((found[0][2] + found[1][2]) * HEAD ** (-0.5)).astype(BF)


def attend_back_kernel(
    windows, query, marks, key, value, context_grad, context, key_mark,
    query_grad, key_grad, value_grad, grad_mark, key_total, value_total, *, row
):
    count = query.shape[0]
    steps = count // TOKENS
    pairs = query.shape[1] // 128
    mark_grads(context_grad, context, grad_mark)
    key_total[...] = jnp.zeros_like(key_total)
    value_total[...] = jnp.zeros_like(value_total)

    def one(turn, carry):
        number = turn
        at = (row * steps + number) * 2

        def run(start, extent):
            attend_back_block(
                number, start, extent, 0, pairs,
                query, marks, key, value, context_grad, key_mark, grad_mark, query_grad, key_total, value_total,
            )

        for_windows(windows[at], windows[at + 1], count, run)
        return carry

    lax.fori_loop(0, steps, one, 0)
    key_grad[...] = (key_total[...] * (1.0 / LOG2E)).astype(BF)
    value_grad[...] = value_total[...].astype(BF)


def entry_back_kernel(
    side, edge, wide, up, head_bias, unit, query_grad, key_grad, value_grad, weight, gains, biases,
    mid_grad, *refs, adding
):
    before, refs = refs[: 2 * adding], refs[2 * adding :]
    entry, latent_out, sums, head_weight = refs
    encoder = side[0] == 0
    width = edge.shape[1]
    narrow = unit.shape[1]

    @pl.when(pl.program_id(0) == 0)
    def _():
        sums[...] = before[0][...] if adding else jnp.zeros_like(sums)
        head_weight[...] = before[1][...] if adding else jnp.zeros_like(head_weight)

    values = entry_values(encoder, edge[...], wide[...], up[...], head_bias[...])
    normed_grad = (
        dot(query_grad[...], weight[:, :width], NT)
        + dot(key_grad[...], weight[:, width : 2 * width], NT)
        + dot(value_grad[...], weight[:, 2 * width :], NT)
    )
    hat, inverse = norm_parts(values)
    sums[0:1, :] += column_sum(query_grad[...].astype(F32))
    sums[1:2, :] += column_sum(value_grad[...].astype(F32))
    sums[2:3, :] += column_sum(normed_grad * hat)
    sums[3:4, :] += column_sum(normed_grad)
    total = mid_grad[...] + norm_back(normed_grad, gains[0:1, :], hat, inverse)
    entry[...] = total

    @pl.when(jnp.logical_not(encoder))
    def _():
        sums[4:5, :] += column_sum(total)
        latent_out[...] = code_product(total, up[...]).T
        head_weight[...] += dot3(split(unit[...]), split(total), TN)


def hidden_weight_kernel(active, out_low, n2, preact_low, *refs):
    out = refs[-1]
    before = refs[0] if len(refs) > 1 else None
    step = pl.program_id(0)
    first = pl.num_programs(0) // 2
    width = n2.shape[1]

    def put(value, rows):
        out[rows, :] = value if before is None else value + before[rows, :]

    @pl.when(step < first)
    def _():
        put(dot(active[...], out_low[...], TN), slice(0, 2 * width))

    @pl.when(step >= first)
    def _():
        value = dot(n2[...], preact_low[...], TN)
        put(value[:, :width], slice(0, width))
        put(value[:, width:], slice(width, 2 * width))


def attention_weight_kernel(context, branch_low, n1, query_grad, key_grad, value_grad, *refs):
    out = refs[-1]
    before = refs[0] if len(refs) > 1 else None
    step = pl.program_id(0)
    width = n1.shape[1]

    def put(value, number):
        rows = slice(number * width, (number + 1) * width)
        out[rows, :] = value if before is None else value + before[rows, :]

    @pl.when(step == 0)
    def _():
        put(dot(context[...], branch_low[...], TN), 0)
        put(dot(n1[...], query_grad[...], TN), 1)

    @pl.when(step == 1)
    def _():
        put(dot(n1[...], key_grad[...], TN), 0)
        put(dot(n1[...], value_grad[...], TN), 1)


def weight_call(kernel, operands, in_specs, steps, before):
    width = operands[1].shape[1]
    out_spec = pl.BlockSpec((2 * width, width), lambda step: (step, 0))
    aliases = {}
    if before is not None:
        aliases = {len(operands): 0}
        operands, in_specs = operands + [before], in_specs + [out_spec]
    return pl.pallas_call(
        kernel,
        grid=(steps,),
        in_specs=in_specs,
        out_specs=out_spec,
        out_shape=jax.ShapeDtypeStruct((2 * steps * width, width), F32),
        input_output_aliases=aliases,
        compiler_params=PARAMS,
    )(*operands)


def hidden_weights(kept, late, before=None):
    operands = [kept.active, late.out_low, kept.n2, late.preact_low]
    count, width = kept.n2.shape
    first = kept.active.shape[1] // (2 * width)
    full = pl.BlockSpec((count, width), lambda step: (0, 0))
    in_specs = [
        pl.BlockSpec((count, 2 * width), lambda step: (0, jnp.minimum(step, first - 1))),
        full,
        full,
        pl.BlockSpec((count, 2 * width), lambda step: (0, jnp.maximum(step - first, 0))),
    ]
    return weight_call(hidden_weight_kernel, operands, in_specs, 2 * first, before)


def attention_weights(kept, late, early, before=None):
    operands = [kept.context, late.branch_low, kept.n1]
    operands += list(early[:3])
    full = pl.BlockSpec(kept.n1.shape, lambda step: (0, 0))
    return weight_call(attention_weight_kernel, operands, [full] * 6, 2, before)


MESH = pl.DeviceIdType.MESH
LEAST_DEVICES = 4


def ring_chip(position, chips):
    odd = position // (chips // 2)
    return (1 - odd) * (2 * position) + odd * (2 * (chips - 1 - position) + 1)


class Ring:
    @staticmethod
    def scratch(arrays, ways, crossing):
        chips = lax.axis_size(DP) // 2
        sizes = [array.shape[0] // (2 * count * chips) for array, count in zip(arrays, ways)]
        shapes = [(count, chips, size, array.shape[1]) for array, count, size in zip(arrays, ways, sizes)]
        buffers = [pltpu.VMEM(shape, F32) for shape in shapes] * 3
        sems = [pltpu.SemaphoreType.DMA(shape[:2]) for shape in shapes] * 10
        far = []
        if crossing is not None:
            count, unused, size, width = shapes[crossing]
            far = [pltpu.VMEM((count, size, width), F32)] + [pltpu.SemaphoreType.DMA((count,))] * 2
        return buffers + sems + far

    def __init__(self, sources, results, ways, crossing, scratch):
        number = len(sources)
        take = lambda at: scratch[at * number : (at + 1) * number]
        self.chips = lax.axis_size(DP) // 2
        self.sources, self.results, self.ways, self.crossing = sources, results, ways, crossing
        self.own, self.pair, self.run = take(0), take(1), take(2)
        (
            self.load_sems, self.pair_send, self.pair_recv, self.run_send, self.run_recv,
            self.keep_sems, self.spread_send, self.spread_recv, self.side_send, self.side_recv,
        ) = (take(at) for at in range(3, 13))
        self.far = scratch[13 * number :]
        self.sizes = [run.shape[2] for run in self.run]
        self.lanes = [(which, way) for way in range(max(ways)) for which in range(number) if way < ways[which]]
        place = lax.axis_index(DP)
        chip, self.core = place // 2, place % 2
        column, odd = chip // 2, chip % 2
        chips = self.chips
        self.position = (1 - odd) * column + odd * (chips - 1 - column)
        self.other = {DP: chip * 2 + (1 - self.core)}
        self.across = {SECTION: 1 - lax.axis_index(SECTION)}
        self.targets = (
            {DP: ring_chip((self.position + 1) % chips, chips) * 2 + self.core},
            {DP: ring_chip((self.position + chips - 1) % chips, chips) * 2 + self.core},
        )

    def greet(self):
        self.barrier = pltpu.get_barrier_semaphore()
        devices = (self.other,) + self.targets + (() if self.crossing is None else (self.across,))
        for device in devices:
            pl.semaphore_signal(self.barrier, inc=1, device_id=device, device_id_type=MESH)
        self.greeted = len(devices)

    def piece(self, step, way):
        return (self.position + (2 * self.chips - step if way % 2 == 0 else step)) % self.chips

    def rows(self, which, half, way, number):
        size = self.sizes[which]
        return pl.ds(pl.multiple_of(((half * self.ways[which] + way) * self.chips + number) * size, 8), size)

    def final(self, which, half, way, step):
        return self.results[which].at[self.rows(which, half, way, self.piece(step + self.chips - 1, way))]

    def load(self, which, way, step):
        return pltpu.make_async_copy(
            self.sources[which].at[self.rows(which, self.core, way, self.piece(step, way))],
            self.own[which].at[way, step],
            self.load_sems[which].at[way, step],
        )

    def remote(self, source, target, send, recv, device):
        return pltpu.make_async_remote_copy(
            src_ref=source, dst_ref=target, send_sem=send, recv_sem=recv, device_id=device, device_id_type=MESH
        )

    def swap(self, which, way, step):
        return self.remote(
            self.sources[which].at[self.rows(which, 1 - self.core, way, self.piece(step, way))],
            self.pair[which].at[way, step],
            self.pair_send[which].at[way, step],
            self.pair_recv[which].at[way, step],
            self.other,
        )

    def pass_on(self, which, way, step):
        return self.remote(
            self.run[which].at[way, step],
            self.run[which].at[way, step + 1],
            self.run_send[which].at[way, step],
            self.run_recv[which].at[way, step + 1],
            self.targets[way % 2],
        )

    def cross(self, way):
        return self.remote(
            self.run[self.crossing].at[way, self.chips - 1],
            self.far[0].at[way],
            self.far[1].at[way],
            self.far[2].at[way],
            self.across,
        )

    def keep(self, which, way):
        return pltpu.make_async_copy(
            self.run[which].at[way, self.chips - 1], self.final(which, self.core, way, 0), self.keep_sems[which].at[way, 0]
        )

    def spread(self, which, way, step, first=False):
        here = self.final(which, self.core, way, step)
        return self.remote(
            self.run[which].at[way, self.chips - 1] if first else here,
            here,
            self.spread_send[which].at[way, step],
            self.spread_recv[which].at[way, step],
            self.targets[way % 2],
        )

    def incoming(self, which, way, step):
        here = self.final(which, self.core, way, step)
        return self.remote(
            here, here, self.spread_send[which].at[way, step], self.spread_recv[which].at[way, step - 1],
            self.targets[way % 2],
        )

    def aside(self, which, way, step, first=False):
        here = self.final(which, self.core, way, step)
        return self.remote(
            self.run[which].at[way, self.chips - 1] if first else here,
            here,
            self.side_send[which].at[way, step],
            self.side_recv[which].at[way, step],
            self.other,
        )

    def beside(self, which, way, step):
        here = self.final(which, 1 - self.core, way, step)
        return self.remote(
            here, here, self.side_send[which].at[way, step], self.side_recv[which].at[way, step], self.other
        )

    def begin(self):
        def load(step, carry):
            for which, way in self.lanes:
                self.load(which, way, step).start()
            return carry

        def swap(step, carry):
            for which, way in self.lanes:
                self.swap(which, way, step).start()
            return carry

        lax.fori_loop(0, self.chips, load, 0)
        pl.semaphore_wait(self.barrier, self.greeted)
        lax.fori_loop(0, self.chips, swap, 0)
        for which, way in self.lanes:
            self.load(which, way, 0).wait()
            self.swap(which, way, 0).wait_recv()
            self.run[which][way, 0] = self.own[which][way, 0] + self.pair[which][way, 0]
            self.pass_on(which, way, 0).start()

    def gather(self, step, lanes=None):
        for which, way in self.lanes if lanes is None else lanes:
            run, own, pair = self.run[which], self.own[which], self.pair[which]
            self.load(which, way, step).wait()
            self.swap(which, way, step).wait_recv()
            self.pass_on(which, way, step - 1).wait_recv()
            run[way, step] = run[way, step] + own[way, step] + pair[way, step]

            @pl.when(step < self.chips - 1)
            def _():
                self.pass_on(which, way, step).start()

    def turn(self):
        for which, way in self.lanes:
            if which == self.crossing:
                self.cross(way).start()
        for which, way in self.lanes:
            if which != self.crossing:
                self.hand_out(which, way)
        for which, way in self.lanes:
            if which == self.crossing:
                run = self.run[which]
                self.cross(way).wait()
                run[way, self.chips - 1] = run[way, self.chips - 1] + self.far[0][way]
                self.hand_out(which, way)

    def hand_out(self, which, way):
        self.spread(which, way, 0, True).start()
        self.aside(which, way, 0, True).start()
        self.keep(which, way).start()

    def pass_out(self, step, lanes=None):
        for which, way in self.lanes if lanes is None else lanes:
            self.incoming(which, way, step).wait_recv()

            @pl.when(step < self.chips - 1)
            def _():
                self.spread(which, way, step).start()

            self.aside(which, way, step).start()

    def finish(self):
        def one(step, carry):
            for which, way in self.lanes:
                self.swap(which, way, step).wait_send()
                self.beside(which, way, step).wait_recv()
                self.aside(which, way, step).wait_send()

                @pl.when(step < self.chips - 1)
                def _():
                    self.pass_on(which, way, step).wait_send()
                    self.spread(which, way, step).wait_send()

            return carry

        lax.fori_loop(0, self.chips, one, 0)
        for which, way in self.lanes:
            self.keep(which, way).wait()


def loop(start, stop, run):
    def one(step, carry):
        run(step)
        return carry

    lax.fori_loop(start, stop, one, 0)


SUM_WAYS = (4, 2)


def sum_kernel(main, misc, main_out, misc_out, *scratch):
    ring = Ring((main, misc), (main_out, misc_out), SUM_WAYS, 1, scratch)
    ring.greet()
    ring.begin()
    loop(1, ring.chips, ring.gather)
    ring.turn()
    loop(1, ring.chips, ring.pass_out)
    ring.finish()


def sum_all(main, misc):
    if lax.axis_size(DP) < LEAST_DEVICES:
        return main, lax.psum(misc, SECTION)
    arrays = (main, misc)
    return pl.pallas_call(
        sum_kernel,
        in_specs=[pl.BlockSpec(memory_space=pl.ANY)] * 2,
        out_specs=[pl.BlockSpec(memory_space=pl.ANY)] * 2,
        out_shape=tuple(jax.ShapeDtypeStruct(array.shape, F32) for array in arrays),
        scratch_shapes=Ring.scratch(arrays, SUM_WAYS, 1),
        compiler_params=pltpu.CompilerParams(collective_id=0, has_side_effects=True, vmem_limit_bytes=40 << 20),
    )(*arrays)


FINISH_WAYS = (4,)


def finish_kernel(
    hidden, attention, query, marks, key, value, context_grad, context, key_mark, edges, mid_grad, weight, branch_low, n1,
    *refs,
):
    others, refs = refs[:12], refs[12:]
    (
        gains, book, down, up, late, early,
        hidden_out, attention_out, misc, entry,
        query_in, marks_in, key_in, value_in, grad_in, context_in, key_mark_in, edge_in, mid_in, weight_in, branch_in,
        n1_in, part, grad_mark, query_grad, key_total, value_total, key_grad, value_grad, in_sems, part_sem, out_sems,
    ), scratch = refs[:32], refs[32:]
    encoder = lax.axis_index(SECTION) == 0
    ring = Ring((hidden,), (hidden_out,), FINISH_WAYS, None, scratch) if scratch else None
    count, width = query.shape
    narrow = down.shape[0]
    steps = count // TOKENS
    pairs = width // 128
    row = edges.shape[0] - 1
    at = book.shape[0] + 2 * narrow
    inputs = (
        (query, query_in), (marks, marks_in), (key, key_in), (value, value_in), (context_grad, grad_in),
        (context, context_in), (key_mark.at[row], key_mark_in), (edges.at[row], edge_in), (mid_grad, mid_in),
        (weight, weight_in), (branch_low, branch_in), (n1, n1_in),
    )
    loads = [pltpu.make_async_copy(*pair, in_sems.at[number]) for number, pair in enumerate(inputs)]
    part_load = pltpu.make_async_copy(attention, part, part_sem)
    first_held = (query_in, marks_in, key_in, value_in, grad_in, grad_mark)
    second_held = (context_in, branch_in, n1_in, query_grad, key_grad, value_grad)
    other_loads = [
        pltpu.make_async_copy(*pair, in_sems.at[number])
        for number, pair in enumerate(zip(others, first_held + second_held))
    ]

    if ring:
        ring.greet()

    @pl.when(encoder)
    def _():
        for load in loads:
            load.start()
        part_load.start()

    @pl.when(jnp.logical_not(encoder))
    def _():
        for load in other_loads:
            load.start()

    if ring:
        ring.begin()
    misc[...] = jnp.zeros_like(misc)

    @pl.when(encoder)
    def _():
        misc[: book.shape[0], :] = book[...]
        misc[book.shape[0] : book.shape[0] + narrow, :] = down[...]
        misc[at : at + 16, :] = late[...]
        misc[at + 16 : at + 32, :] = early[...]
        for load in loads:
            load.wait()
        part_load.wait()
        mark_grads(grad_in, context_in, grad_mark)
        key_total[...] = jnp.zeros_like(key_total)
        value_total[...] = jnp.zeros_like(value_total)

    @pl.when(jnp.logical_not(encoder))
    def _():
        misc[book.shape[0] + narrow : at, :] = up[...]
        misc[at + 32 : at + 48, :] = late[...]
        misc[at + 48 : at + 64, :] = early[...]
        for load in other_loads:
            load.wait()

    def attention_piece(turn):
        attend_back_block(
            turn // pairs, 0, count, (turn % pairs) * 128, 1,
            query_in, marks_in, key_in, value_in, grad_in, key_mark_in, grad_mark, query_grad, key_total, value_total,
        )

    def entry_piece(number):
        rows = pl.ds(pl.multiple_of(number * TOKENS, TOKENS), TOKENS)
        normed_grad = (
            dot(query_grad[rows, :], weight_in[:, :width], NT)
            + dot(key_grad[rows, :], weight_in[:, width : 2 * width], NT)
            + dot(value_grad[rows, :], weight_in[:, 2 * width :], NT)
        )
        hat, inverse = norm_parts(edge_in[rows, :].astype(F32))
        misc[at + 16 : at + 17, :] += column_sum(query_grad[rows, :].astype(F32))
        misc[at + 17 : at + 18, :] += column_sum(value_grad[rows, :].astype(F32))
        misc[at + 18 : at + 19, :] += column_sum(normed_grad * hat)
        misc[at + 19 : at + 20, :] += column_sum(normed_grad)
        mid_in[rows, :] = mid_in[rows, :] + norm_back(normed_grad, gains[0:1, :], hat, inverse)

    def both_piece(number):
        def put(first, second):
            rows = pl.ds(pl.multiple_of(number * width, width), width)
            part[rows, :] = dot(first[0][...], first[1][...], TN) + dot(second[0][...], second[1][...], TN)

        for choice, places in enumerate(((0, 1), (2, 3), (2, 4), (2, 5))):
            pairs_of = [[held[place] for place in places] for held in (first_held, second_held)]
            pl.when(number == choice)(functools.partial(put, *pairs_of))

    def weight_piece(number):
        def put(left, right):
            rows = pl.ds(pl.multiple_of(number * width, width), width)
            part[rows, :] = part[rows, :] + dot(left[...], right[...], TN)

        for choice, (left, right) in enumerate(
            ((context_in, branch_in), (n1_in, query_grad), (n1_in, key_grad), (n1_in, value_grad))
        ):
            pl.when(number == choice)(functools.partial(put, left, right))

    halves = (ring.lanes[:2], ring.lanes[2:]) if ring else (None, None)
    chips = ring.chips if ring else 8
    pieces = steps * pairs

    def summing(step):
        for half in range(2):
            if ring:
                ring.gather(step, halves[half])

            @pl.when(encoder)
            def _():
                attention_piece(2 * (step - 1) + half)

        @pl.when(jnp.logical_not(encoder) & (step <= 4))
        def _():
            both_piece(step - 1)

    inside = min(chips - 1, pieces // 2)
    loop(1, inside + 1, summing)
    if ring:
        loop(inside + 1, chips, ring.gather)
        ring.turn()

    @pl.when(encoder)
    def _():
        loop(2 * inside, pieces, attention_piece)
        key_grad[...] = (key_total[...] * (1.0 / LOG2E)).astype(BF)
        value_grad[...] = value_total[...].astype(BF)

    def spreading(step):
        for half, work in enumerate((entry_piece, weight_piece)):
            if ring:
                ring.pass_out(step, halves[half])

            @pl.when(encoder)
            def _():
                work(step - 1)

    loop(1, steps + 1, spreading)
    stores = [
        pltpu.make_async_copy(mid_in, entry, out_sems.at[0]),
        pltpu.make_async_copy(part, attention_out, out_sems.at[1]),
    ]

    @pl.when(encoder)
    def _():
        stores[0].start()

    stores[1].start()
    if ring:
        loop(steps + 1, chips, ring.pass_out)
        ring.finish()

    @pl.when(encoder)
    def _():
        stores[0].wait()

    stores[1].wait()


def finish_row(work, kept, late, early, book, hidden, attention, others):
    count, width = kept.n1.shape
    alone = lax.axis_size(DP) < LEAST_DEVICES
    operands = [
        hidden, attention, kept.query, kept.marks, kept.key, kept.value, late.context_grad,
        kept.context, work.key_mark, work.edges, late.mid_grad, work.attention_in, late.branch_low, kept.n1,
    ]
    for its_kept, its_late, its_early in others:
        operands += [its_kept.context, its_late.branch_low, its_kept.n1, *its_early[:3]]
    operands += [work.gains, book, late.head, early.head, late.sums, early.sums]
    hbm, vmem = pl.BlockSpec(memory_space=pl.ANY), pl.BlockSpec(memory_space=pltpu.VMEM)
    rows = book.shape[0] + 2 * work.narrow + 64
    unit = 16 * lax.axis_size(DP)
    low = pltpu.VMEM((count, width), BF)
    wide = pltpu.VMEM((count, width), F32)
    scratch = [low] * 6 + [pltpu.VMEM((count, 128), BF), low, wide, pltpu.VMEM(work.attention_in.shape, BF), low, low]
    scratch += [pltpu.VMEM(attention.shape, F32), low, low, wide, wide, low, low]
    scratch += [pltpu.SemaphoreType.DMA((12,)), pltpu.SemaphoreType.DMA, pltpu.SemaphoreType.DMA((2,))]
    settings = {}
    if not alone:
        scratch += Ring.scratch((hidden,), FINISH_WAYS, None)
        settings = dict(collective_id=1, has_side_effects=True)
    outs = pl.pallas_call(
        finish_kernel,
        in_specs=[hbm] * 26 + [vmem] * 6,
        out_specs=[hbm, hbm, vmem, hbm],
        out_shape=(
            jax.ShapeDtypeStruct(hidden.shape, F32),
            jax.ShapeDtypeStruct(attention.shape, F32),
            jax.ShapeDtypeStruct((rows + (-rows % unit), width), F32),
            jax.ShapeDtypeStruct((count, width), F32),
        ),
        scratch_shapes=scratch,
        input_output_aliases={1: 1},
        compiler_params=pltpu.CompilerParams(vmem_limit_bytes=58 << 20, **settings),
    )(*operands)
    return (hidden,) + tuple(outs[1:]) if alone else outs


def unpack_kernel(
    side, hidden, attention, misc, first_entry, second_entry, first_result, second_result,
    hidden_out, hidden_in, attention_out, attention_in, edge, book, gains, biases, bias, last_gain, head_bias, down, down_last,
    up, held, head, rows, ins, outs, row_ins, row_outs,
):
    width = hidden.shape[1]
    narrow = book.shape[0]
    steps = hidden_out.shape[0] // width
    targets = [hidden_out.at[pl.ds(number * width, width), :] for number in range(steps)]
    targets += [hidden_in.at[:, pl.ds(number * width, width)] for number in range(steps)]
    targets += [attention_out]
    targets += [attention_in.at[:, pl.ds(number * width, width)] for number in range(3)]
    sources = [hidden.at[pl.ds(number * width, width), :] for number in range(2 * steps)]
    sources += [attention.at[pl.ds(number * width, width), :] for number in range(4)]
    tiles = range(len(targets))
    for mine, pair in ((0, (first_entry, second_entry)), (1, (first_result, second_result))):

        @pl.when(side[0] == mine)
        def _():
            for row in range(2):
                pltpu.make_async_copy(pair[row], rows.at[row], row_ins.at[row]).start()

    loads = [pltpu.make_async_copy(sources[number], held.at[number], ins.at[number]) for number in tiles]
    loads.append(pltpu.make_async_copy(misc.at[pl.ds(0, head.shape[0]), :], head, ins.at[len(targets)]))
    for load in loads:
        load.start()
    stores = []
    for row in range(2):
        pltpu.make_async_copy(first_entry, rows.at[row], row_ins.at[row]).wait()
        stores.append(pltpu.make_async_copy(rows.at[row], edge.at[row], row_outs.at[row]))
        stores[-1].start()
    for number in tiles:
        loads[number].wait()
        stores.append(pltpu.make_async_copy(held.at[number], targets[number], outs.at[number]))
        stores[-1].start()
    loads[-1].wait()
    for number in range(book.shape[1] // width):
        book[:, number * width : (number + 1) * width] = head[number * narrow : (number + 1) * narrow, :]
    at = book.shape[0] * book.shape[1] // width
    down[...] = head[at : at + narrow, :]
    up[...] = head[at + narrow : at + 2 * narrow, :]
    at += 2 * narrow
    last_gain[...] = head[at + 8 : at + 9, :]
    head_bias[0:1, :] = head[at + 9 : at + 10, :]
    head_bias[1:2, :] = head[at + 52 : at + 53, :]
    down_last[...] = head[at + 10 : at + 11, :narrow]
    mine = jnp.where(side[0] == 0, head[at : at + 32, :], head[at + 32 : at + 64, :])
    bias[...] = mine[:steps, :]
    for out, places in ((gains, (18, 6)), (biases, (16, 17, 5, 19, 7, 4))):
        for number, place in enumerate(places):
            out[number : number + 1, :] = mine[place : place + 1, :]
    for store in stores:
        store.wait()


def unpack(side, hidden, attention, misc, ends, table_turned):
    width = hidden.shape[1]
    features = hidden.shape[0] // 2
    tiles = (hidden.shape[0] + attention.shape[0]) // width
    narrow = table_turned.shape[0]
    rows = table_turned.size // width + 2 * narrow + 64
    shapes = (
        (features, width), (width, features), (width, width), (width, 3 * width), (2,) + ends[0].shape,
        table_turned.shape, (2, width), (6, width), (features // width, width), (1, width), (2, width),
        (narrow, width), (1, narrow), (narrow, width),
    )
    hbm, vmem = pl.BlockSpec(memory_space=pl.ANY), pl.BlockSpec(memory_space=pltpu.VMEM)
    return pl.pallas_call(
        unpack_kernel,
        in_specs=[pl.BlockSpec(memory_space=pltpu.SMEM)] + [hbm] * 7,
        out_specs=[hbm] * 5 + [vmem] * 9,
        out_shape=tuple(jax.ShapeDtypeStruct(shape, F32) for shape in shapes),
        scratch_shapes=[
            pltpu.VMEM((tiles, width, width), F32),
            pltpu.VMEM((rows, width), F32),
            pltpu.VMEM((2,) + ends[0].shape, F32),
            pltpu.SemaphoreType.DMA((tiles + 1,)),
            pltpu.SemaphoreType.DMA((tiles,)),
            pltpu.SemaphoreType.DMA((2,)),
            pltpu.SemaphoreType.DMA((2,)),
        ],
        compiler_params=PARAMS,
    )(side, hidden, attention, misc, *ends)


def nothing_kernel(*refs):
    pass


def unwritten(shapes):
    leaves, tree = jax.tree.flatten(shapes)
    arrays = pl.pallas_call(
        nothing_kernel,
        out_specs=[pl.BlockSpec(memory_space=pl.ANY)] * len(leaves),
        out_shape=tuple(leaves),
    )()
    return jax.tree.unflatten(tree, arrays)


class Kept(NamedTuple):
    n1: Any
    query: Any
    key: Any
    value: Any
    context: Any
    marks: Any
    mid: Any
    n2: Any
    active: Any
    slope: Any
    result: Any
    latent: Any


class Late(NamedTuple):
    out_low: Any
    preact_low: Any
    mid_grad: Any
    branch_low: Any
    context_grad: Any
    sums: Any
    head: Any


class Early(NamedTuple):
    query_grad: Any
    key_grad: Any
    value_grad: Any
    entry: Any
    latent_out: Any
    sums: Any
    head: Any


class Rows:
    def __init__(self, side, edges, wide, unit, windows, query_mark, key_mark, weights, head):
        self.side, self.edges, self.wide, self.unit = side, edges, wide, unit
        self.windows, self.query_mark, self.key_mark = windows, query_mark, key_mark
        (
            self.attention_in, self.attention_out, self.hidden_in, self.hidden_out,
            self.gains, self.biases, self.hidden_bias,
        ) = weights
        (
            self.output_gain, self.head_bias, self.down, self.down_bias, self.up,
        ) = head
        self.rows, self.count, self.width = edges.shape
        self.hidden = self.hidden_in.shape[1]
        self.narrow = unit.shape[1]
        self.size = TOKENS
        n, d, f = self.count, self.width, self.hidden
        shape = jax.ShapeDtypeStruct
        low, tall, wide = shape((n, d), BF), shape((n, f), BF), shape((n, d), F32)
        sums, head = shape((16, d), F32), shape((self.narrow, d), F32)
        self.kept = Kept(low, low, low, low, low, low, wide, low, tall, tall, wide, shape((n, self.narrow), F32))
        self.late = Late(low, tall, wide, low, low, sums, head)
        self.early = Early(low, low, low, wide, shape((self.narrow, n), F32), sums, head)

    def side_spec(self):
        return pl.BlockSpec(memory_space=pltpu.SMEM)

    def tokens(self, array):
        return pl.BlockSpec((self.size, array.shape[1]), lambda step: (step, 0))

    def turned(self, array):
        return pl.BlockSpec((array.shape[0], self.size), lambda step: (0, step))

    def whole(self, array):
        return pl.BlockSpec(array.shape, lambda step: (0,) * len(array.shape))

    def entry_specs(self, row):
        steps = self.count // self.size
        return [
            pl.BlockSpec((None, self.size, self.width), lambda step: (row, step, 0)),
            pl.BlockSpec((self.size, self.wide.shape[1]), lambda step: (row * steps + step, 0)),
            self.whole(self.up),
            self.whole(self.head_bias),
        ]

    def unit_spec(self, row):
        steps = self.count // self.size
        return pl.BlockSpec((self.size, self.narrow), lambda step: (row * steps + step, 0))

    def call(self, kernel, in_specs, operands, outs, out_specs, scratch=()):
        return pl.pallas_call(
            kernel,
            grid=(self.count // self.size,),
            in_specs=in_specs,
            out_specs=out_specs,
            out_shape=tuple(outs),
            scratch_shapes=list(scratch),
            compiler_params=PARAMS,
        )(*operands)

    def attention_call(self, kernel, row, operands, outs, scratch=()):
        half = self.width // 2

        def spec(array):
            if array.ndim == 3:
                return pl.BlockSpec((None, self.count, array.shape[2]), lambda step, info: (row, 0, 0))
            return pl.BlockSpec((self.count, half), lambda step, info: (0, step))

        return pl.pallas_call(
            functools.partial(kernel, row=row),
            grid_spec=pltpu.PrefetchScalarGridSpec(
                num_scalar_prefetch=1,
                grid=(2,),
                in_specs=[spec(array) for array in operands],
                out_specs=[spec(array) for array in outs],
                scratch_shapes=list(scratch),
            ),
            out_shape=tuple(outs),
            compiler_params=PARAMS,
        )(self.windows, *operands)

    def forward(self, row):
        shapes = self.kept
        entry = (self.edges, self.wide, self.up, self.head_bias)
        outs = shapes[:4]
        self.size = 2 * TOKENS
        n1, query, key, value = self.call(
            project_kernel,
            [self.side_spec()] + self.entry_specs(row)
            + [self.whole(self.gains), self.whole(self.biases), self.whole(self.attention_in)],
            (self.side,) + entry + (self.gains, self.biases, self.attention_in),
            outs,
            [self.tokens(array) for array in outs],
        )
        self.size = TOKENS
        context, marks = self.attention_call(
            attend_kernel, row, (query, key, value, self.query_mark, self.key_mark), shapes[4:6]
        )
        consts = (
            self.attention_out, self.gains, self.biases, self.hidden_in, self.hidden_bias, self.hidden_out,
            self.output_gain, self.down, self.down_bias,
        )
        outs = shapes[6:]
        outs = self.call(
            hidden_kernel,
            [self.side_spec()] + self.entry_specs(row) + [self.tokens(context)]
            + [self.whole(array) for array in consts],
            (self.side,) + entry + (context,) + consts,
            outs,
            [self.tokens(array) for array in outs],
        )
        return Kept(n1, query, key, value, context, marks, *outs)

    def backward(self, row, kept, latent_in, former=(None, None)):
        late = self.backward_late(row, kept, latent_in, former[0])
        return late, self.backward_early(row, kept, late, former[1])

    def backward_late(self, row, kept, latent_in, former=None):
        prior = () if former is None else (former.sums, former.head)
        adding = int(former is not None)
        consts = (self.output_gain, self.head_bias, self.down, self.hidden_out)
        late = (self.gains, self.biases, self.attention_out)
        outs = self.late
        return Late(*self.call(
            functools.partial(tail_back_kernel, adding=adding),
            [self.side_spec(), self.tokens(kept.result), self.entry_specs(row)[0], self.unit_spec(row),
             self.turned(latent_in), self.tokens(kept.latent)]
            + [self.whole(array) for array in consts]
            + [self.tokens(kept.slope), self.whole(self.hidden_in), self.tokens(kept.mid)]
            + [self.whole(array) for array in late + prior],
            (self.side, kept.result, self.edges, self.unit, latent_in, kept.latent) + consts
            + (kept.slope, self.hidden_in, kept.mid) + late + prior,
            outs,
            [self.tokens(array) for array in outs[:5]] + [self.whole(array) for array in outs[5:]],
            scratch=[pltpu.VMEM((self.size, self.width), F32)],
        ))

    def backward_early(self, row, kept, late, former=None):
        adding = int(former is not None)
        half = self.width // 2
        grads = tuple(self.attention_call(
            attend_back_kernel, row,
            (kept.query, kept.marks, kept.key, kept.value, late.context_grad, kept.context, self.key_mark),
            self.early[:3],
            scratch=[
                pltpu.VMEM((self.count, half), BF),
                pltpu.VMEM((self.count, half), F32),
                pltpu.VMEM((self.count, half), F32),
            ],
        ))
        prior = () if former is None else (former.sums, former.head)
        outs = self.early[3:]
        outs = self.call(
            functools.partial(entry_back_kernel, adding=adding),
            [self.side_spec()] + self.entry_specs(row) + [self.unit_spec(row)]
            + [self.tokens(array) for array in grads]
            + [self.whole(self.attention_in), self.whole(self.gains), self.whole(self.biases),
               self.tokens(late.mid_grad)] + [self.whole(array) for array in prior],
            (self.side, self.edges, self.wide, self.up, self.head_bias, self.unit) + grads
            + (self.attention_in, self.gains, self.biases, late.mid_grad) + prior,
            outs,
            [self.tokens(outs[0]), self.turned(outs[1])] + [self.whole(array) for array in outs[2:]],
        )
        return Early(*grads, *outs)


def windows_of(segments):
    rows, count = segments.shape
    steps = count // WINDOW
    blocks = segments.reshape(rows, steps, WINDOW)
    least, most = blocks[:, :, 0], blocks[:, :, -1]
    meets = (most[:, :, None] >= least[:, None, :]) & (least[:, :, None] <= most[:, None, :])
    place = jnp.arange(steps)
    start = jnp.min(jnp.where(meets, place, steps), -1)
    stop = jnp.max(jnp.where(meets, place, -1), -1) + 1
    return jnp.stack([start, stop - start], -1).reshape(-1).astype(jnp.int32)


def on_device(
    boundary, segments, code_index, attention_in, attention_out, hidden_in, hidden_out, block_gains,
    block_biases, hidden_bias, output_gain, head_bias, down_weight, down_bias, up_weight, codebook,
):
    section = lax.axis_index(SECTION)
    encoder = section == 0
    side = section.astype(jnp.int32)[None]
    edges = boundary[0]
    rows, count, width = edges.shape
    hidden = hidden_in.shape[2]
    table_turned = codebook.T
    code_index = code_index.reshape(-1)
    unit, wide, query_mark, key_mark = gather_codes(code_index, table_turned, segments)
    work = Rows(
        side, edges, wide, unit, windows_of(segments), query_mark, key_mark,
        (
            attention_in[0], attention_out[0], hidden_in[0], hidden_out[0], block_gains[0], block_biases[0],
            hidden_bias,
        ),
        (output_gain[None], head_bias, down_weight.T, down_bias[None], up_weight),
    )
    book_out = book_shape(table_turned, width)
    hidden_shape = jax.ShapeDtypeStruct((2 * hidden, width), F32)
    attention_shape = jax.ShapeDtypeStruct((4 * width, width), F32)
    quiet = jnp.zeros((unit.shape[1], count), F32)
    first_kept = work.forward(0)

    def encoder_second():
        return (work.forward(1), *unwritten((work.late, work.early)))

    def decoder_first():
        return (unwritten(work.kept), *work.backward(0, first_kept, quiet))

    kept_a, late_a, early_a = lax.cond(encoder, encoder_second, decoder_first)
    latent_in = lax.ppermute(early_a.latent_out, SECTION, [(1, 0)])

    def encoder_third():
        late, early = work.backward(0, first_kept, latent_in)
        weights = hidden_weights(first_kept, late), attention_weights(first_kept, late, early)
        book = scatter_codes(code_index, unit, (first_kept.latent, kept_a.latent), table_turned, width)
        return unwritten(work.kept), late, early, weights, book

    def decoder_third():
        kept = work.forward(1)
        weights, book = unwritten(((hidden_shape, attention_shape), book_out))
        return (kept, *work.backward(1, kept, quiet, (late_a, early_a)), weights, book)

    kept_b, late_b, early_b, weights_b, book = lax.cond(section == 1, decoder_third, encoder_third)
    latent_in_second = lax.ppermute(early_b.latent_out, SECTION, [(1, 0)])

    def encoder_fifth():
        late = work.backward_late(1, kept_a, latent_in_second, late_b)
        return hidden_weights(kept_a, late, weights_b[0]), late[2:]

    def decoder_fifth():
        total = hidden_weights(kept_b, late_b, hidden_weights(first_kept, late_a))
        return total, (*unwritten(work.late[2:5]), late_b.sums, late_b.head)

    hidden_total, late = lax.cond(encoder, encoder_fifth, decoder_fifth)
    late = Late(None, None, *late)
    hidden_total, attention_total, misc, second_entry = finish_row(
        work, kept_a, late, early_b, book, hidden_total, weights_b[1],
        ((first_kept, late_a, early_a), (kept_b, late_b, early_b)),
    )
    attention_total, misc = sum_all(attention_total, misc)
    (
        hidden_out_grad, hidden_in_grad, attention_out_grad, attention_in_grad, edge, book, gains, biases, bias,
        last_gain, head, down_grad, down_last, up_grad,
    ) = unpack(
        side, hidden_total, attention_total, misc,
        (early_b.entry, second_entry, first_kept.result, kept_b.result), table_turned,
    )
    return (
        edge[None],
        attention_in_grad[None],
        attention_out_grad[None],
        hidden_in_grad[None],
        hidden_out_grad[None],
        gains[None],
        biases[None],
        bias.reshape(1, hidden),
        last_gain[0],
        head,
        down_grad.T,
        down_last[0],
        up_grad,
        book.T,
    )


def solution(mesh):
    wide, split_last, flat = P(SECTION, DP, None, None), P(SECTION, None, None), P(SECTION, None)
    blocks = (split_last,) * 6 + (flat,)
    return jax.shard_map(
        on_device,
        mesh=mesh,
        in_specs=(wide, P(DP, None), P(DP, None)) + blocks + (P(),) * 6,
        out_specs=(wide,) + blocks + (P(),) * 6,
        check_vma=False,
    )
```

```python
import functools
import math
from typing import Any, NamedTuple

import jax
import jax.numpy as jnp
from jax import lax
from jax.experimental import pallas as pl
from jax.experimental.pallas import tpu as pltpu
from jax.sharding import PartitionSpec as P

HEAD = 64
SECTION, DP = "section", "dp"
BF = jnp.bfloat16
F32 = jnp.float32
LOG2E = math.log2(math.e)
NORM_EPS = 1e-06
MASKED = -1e30
GELU = 0.7978845608028654
CUBIC = 0.044715
NN = (((1,), (0,)), ((), ()))
NT = (((1,), (1,)), ((), ()))
TN = (((0,), (0,)), ((), ()))
TOKENS = 256
WINDOW = 256
PARAMS = pltpu.CompilerParams(vmem_limit_bytes=56 << 20)


def dot(a, b, dims):
    return lax.dot_general(a, b, dims, preferred_element_type=F32)


def lanes(shape):
    return lax.broadcasted_iota(jnp.int32, shape, 1)


def split(values):
    high = values.astype(BF)
    return high, (values - high.astype(F32)).astype(BF)


def dot3(left, right, dims):
    return dot(left[0], right[0], dims) + dot(left[0], right[1], dims) + dot(left[1], right[0], dims)


def unit_of(values):
    scale = lax.rsqrt(jnp.sum(values * values, -1, keepdims=True) + NORM_EPS)
    return values * scale, scale


def norm_parts(values):
    center = values - jnp.mean(values, -1, keepdims=True)
    inverse = lax.rsqrt(jnp.mean(center * center, -1, keepdims=True) + NORM_EPS)
    return center * inverse, inverse


def norm_back(grad, gain, hat, inverse):
    scaled = grad * gain
    return inverse * (
        scaled
        - jnp.mean(scaled, -1, keepdims=True)
        - hat * jnp.mean(scaled * hat, -1, keepdims=True)
    )


def column_sum(values):
    return jnp.sum(values, 0, keepdims=True)


def code_kernel(index, table_turned, segments, unit, wide, query_mark, key_mark, table, raw):
    count = raw.shape[0]
    block = 512

    def turn(step, carry):
        start = pl.multiple_of(step * block, block)
        table[pl.ds(start, block), :] = table_turned[:, pl.ds(start, block)].T
        return carry

    lax.fori_loop(0, table.shape[0] // block, turn, 0)

    length = segments.shape[1]

    def some(step, carry):
        for inner in range(16):
            token = step * 16 + inner
            raw[pl.ds(token, 1), :] = table[pl.ds(index[token], 1), :]
        return carry

    lax.fori_loop(0, count // 16, some, 0)

    values = raw[...]
    values = values * lax.rsqrt(jnp.sum(values * values, -1, keepdims=True) + NORM_EPS)
    unit[...] = values
    high, low = split(values)
    wide[...] = jnp.concatenate([high, low, high, jnp.zeros_like(high)], 1)
    lane = lanes((length, 128)) & 63
    for row in range(segments.shape[0]):
        owner = jnp.broadcast_to(segments[row : row + 1, :], (128, length)).T
        same = owner == lane
        query_mark[row] = jnp.where((lane < 4) & jnp.logical_not(same), MASKED, 0.0).astype(BF)
        key_mark[row] = jnp.where(((lane < 4) & same) | ((lane > 3) & (lane < 7)), 1.0, 0.0).astype(BF)


def gather_codes(index, table_turned, segments):
    count, width = index.shape[0], table_turned.shape[0]
    vmem = pl.BlockSpec(memory_space=pltpu.VMEM)
    mark = jax.ShapeDtypeStruct(segments.shape + (128,), BF)
    return pl.pallas_call(
        code_kernel,
        in_specs=[pl.BlockSpec(memory_space=pltpu.SMEM), vmem, vmem],
        out_specs=[vmem] * 4,
        out_shape=(
            jax.ShapeDtypeStruct((count, width), F32),
            jax.ShapeDtypeStruct((count, 4 * width), BF),
            mark,
            mark,
        ),
        scratch_shapes=[pltpu.VMEM(table_turned.shape[::-1], F32), pltpu.VMEM((count, width), F32)],
        compiler_params=PARAMS,
    )(index, table_turned, segments)


def scatter_kernel(index, unit, latent_first, latent_second, table_turned, out, total, rows):
    count = rows.shape[0]
    width = unit.shape[1]
    half = count // 2
    total[...] = jnp.zeros_like(total)
    for row, latent in enumerate((latent_first, latent_second)):
        here = slice(row * half, (row + 1) * half)
        code, unused = unit_of(latent[...])
        rows[here, :] = 2.0 * (unit[here, :] - code)

    def some(step, carry):
        for inner in range(8):
            token = step * 8 + inner
            place = pl.ds(index[token], 1)
            total[place, :] = total[place, :] + rows[pl.ds(token, 1), :]
        return carry

    lax.fori_loop(0, count // 8, some, 0)
    block = out.shape[1]

    def back(step, carry):
        start = pl.multiple_of(step * block, block)
        values = table_turned[:, pl.ds(start, block)]
        grad = total[pl.ds(start, block), :].T
        inverse = lax.rsqrt(jnp.sum(values * values, 0, keepdims=True) + NORM_EPS)
        book = values * inverse
        out[pl.ds(pl.multiple_of(step * width, width), width), :] = inverse * (
            grad - book * jnp.sum(book * grad, 0, keepdims=True)
        )
        return carry

    lax.fori_loop(0, total.shape[0] // block, back, 0)


def book_shape(table_turned, width):
    return jax.ShapeDtypeStruct((table_turned.size // width, width), F32)


def scatter_codes(index, unit, latents, table_turned, width):
    return pl.pallas_call(
        scatter_kernel,
        in_specs=[pl.BlockSpec(memory_space=pltpu.SMEM)] + [pl.BlockSpec(memory_space=pltpu.VMEM)] * 4,
        out_specs=pl.BlockSpec(memory_space=pltpu.VMEM),
        out_shape=book_shape(table_turned, width),
        scratch_shapes=[pltpu.VMEM(table_turned.shape[::-1], F32), pltpu.VMEM(unit.shape, F32)],
        compiler_params=PARAMS,
    )(index, unit, *latents, table_turned)


def entry_values(encoder, edge, wide, up, head_bias):
    high, low = split(up)
    parts = jnp.concatenate([high, high, low, jnp.zeros_like(low)], 0)
    return jnp.where(encoder, edge.astype(F32), dot(wide, parts, NN) + head_bias[1:2, :])


def project_kernel(side, edge, wide, up, head_bias, gains, biases, weight, n1, query, key, value):
    width = edge.shape[1]
    encoder = side[0] == 0
    values = entry_values(encoder, edge[...], wide[...], up[...], head_bias[...])
    hat, unused = norm_parts(values)
    normed = (hat * gains[0:1, :] + biases[3:4, :]).astype(BF)
    n1[...] = normed
    query[...] = (
        (dot(normed, weight[:, :width], NN) + biases[0:1, :]) * (LOG2E * HEAD ** (-0.5))
    ).astype(BF)
    key[...] = dot(normed, weight[:, width : 2 * width], NN).astype(BF)
    value[...] = (dot(normed, weight[:, 2 * width :], NN) + biases[1:2, :]).astype(BF)


def merge(low_half, left, right):
    return jnp.where(low_half, left, right)


def attend_kernel(windows, query, key, value, query_mark, key_mark, context, marks, *, row):
    count = query.shape[0]
    size = TOKENS
    pairs = query.shape[1] // 128
    low_query = lanes((size, 128)) < 64
    mark_lane = lanes((size, 128)) & 63

    def block(number, start, extent):
        rows = pl.ds(pl.multiple_of(number * size, size), size)
        keys = pl.ds(pl.multiple_of(start, WINDOW), extent)
        low_key = lanes((extent, 128)) < 64
        query_aug, key_aug = query_mark[rows, :], key_mark[keys, :]
        ones = jnp.ones((extent, 128), BF)
        scores = []
        for pair in range(pairs):
            here = slice(pair * 128, pair * 128 + 128)
            query_pair, key_pair = query[rows, here], key[keys, here]
            scores.append(
                dot(merge(low_query, query_pair, query_aug), merge(low_key, key_pair, key_aug), NT)
            )
            scores.append(
                dot(merge(low_query, query_aug, query_pair), merge(low_key, key_aug, key_pair), NT)
            )
        tops = [jnp.max(score, -1, keepdims=True) for score in scores]
        raised = [jnp.exp2(score - top).astype(BF) for score, top in zip(scores, tops)]
        for pair in range(pairs):
            here = slice(pair * 128, pair * 128 + 128)
            value_pair = value[keys, here]
            even = dot(raised[2 * pair], merge(low_key, value_pair, ones), NN)
            odd = dot(raised[2 * pair + 1], merge(low_key, ones, value_pair), NN)
            total = merge(low_query, odd, even)
            context[rows, here] = (
                merge(low_query, even, odd) / pltpu.roll(total, 64, 1)
            ).astype(BF)
            level = -(merge(low_query, tops[2 * pair + 1], tops[2 * pair]) + jnp.log2(total))
            first = level.astype(BF)
            rest = level - first.astype(F32)
            second, third = split(rest)
            marks[rows, here] = merge(
                mark_lane == 4, first, merge(mark_lane == 5, second, merge(mark_lane == 6, third, query_aug))
            )

    def one(number, carry):
        base = (row * (count // size) + number) * 2
        for_windows(windows[base], windows[base + 1], count, functools.partial(block, number))
        return carry

    lax.fori_loop(0, count // size, one, 0)


def for_windows(start, steps, count, run):
    extents = list(range(2 * WINDOW, count + 1, WINDOW))
    for position, extent in enumerate(extents):
        take = steps * WINDOW <= extent
        if position:
            take = take & (steps * WINDOW > extents[position - 1])

        @pl.when(take)
        def _():
            run(jnp.minimum(start * WINDOW, count - extent), extent)


def gelu_parts(values):
    square = values * values
    half = 0.5 + 0.5 * jnp.tanh(values * (GELU + (GELU * CUBIC) * square))
    active = values * half
    slope = half + active * (1.0 - half) * (2.0 * GELU + (6.0 * GELU * CUBIC) * square)
    return active, slope


def hidden_kernel(
    side, edge, wide, up, head_bias, context, weight_out, gains, biases, weight_in, hidden_bias,
    weight_last, output_gain, down, down_bias,
    mid, n2, active_out, slope_out, result, latent_out,
):
    encoder = side[0] == 0
    width = edge.shape[1]
    values = entry_values(encoder, edge[...], wide[...], up[...], head_bias[...])
    midway = values + (dot(context[...], weight_out[...], NN) + biases[2:3, :])
    mid[...] = midway
    hat, unused = norm_parts(midway)
    normed = (hat * gains[1:2, :] + biases[4:5, :]).astype(BF)
    n2[...] = normed
    total = midway + biases[5:6, :]
    chunk = 256
    for start in range(0, weight_in.shape[1], chunk):
        here = slice(start, start + chunk)
        active, slope = gelu_parts(dot(normed, weight_in[:, here], NN) + hidden_bias[0:1, here])
        active = active.astype(BF)
        active_out[:, here] = active
        slope_out[:, here] = slope.astype(BF)
        total = total + dot(active, weight_last[here, :], NN)
    result[...] = total

    @pl.when(encoder)
    def _():
        last_hat, unused = norm_parts(total)
        code = last_hat * output_gain[0:1, :] + head_bias[0:1, :]
        latent_out[...] = code_product(code, down[...]) + down_bias[0:1, :]


def code_product(values, weight):
    return dot3(split(values), split(weight), NT)


def tail_back_kernel(
    side, result, cotangent, unit, latent_in, latent, output_gain, head_bias, down,
    weight_last, slope, weight_in, mid, gains, biases, weight_out, *refs, adding
):
    before, refs = refs[: 2 * adding], refs[2 * adding :]
    out_low, preact_low, mid_grad, branch_low, context_grad, sums, head_weight, upstream = refs
    encoder = side[0] == 0
    width = result.shape[1]
    narrow = unit.shape[1]

    @pl.when(pl.program_id(0) == 0)
    def _():
        sums[...] = before[0][...] if adding else jnp.zeros_like(sums)
        head_weight[...] = before[1][...] if adding else jnp.zeros_like(head_weight)

    @pl.when(encoder)
    def _():
        hat, inverse = norm_parts(result[...])
        normed = hat * output_gain[0:1, :] + head_bias[0:1, :]
        code, scale = unit_of(latent[...])
        code_grad = latent_in[...].T + 0.5 * (code - unit[...])
        latent_grad = scale * (code_grad - code * jnp.sum(code * code_grad, -1, keepdims=True))
        pieces = split(latent_grad)
        normed_grad = dot3(pieces, split(down[...]), NN)
        head_weight[...] += dot(pieces[0], normed.astype(BF), TN) + dot(pieces[1], normed.astype(BF), TN)
        sums[8:9, :] += column_sum(normed_grad * hat)
        sums[9:10, :] += column_sum(normed_grad)
        sums[10:11, :narrow] += column_sum(latent_grad)
        upstream[...] = norm_back(normed_grad, output_gain[0:1, :], hat, inverse)

    @pl.when(jnp.logical_not(encoder))
    def _():
        upstream[...] = cotangent[...].astype(F32)

    above = upstream[...]
    low = above.astype(BF)
    out_low[...] = low
    sums[4:5, :] += column_sum(low.astype(F32))
    normed_grad = None
    chunk = 1024
    for start in range(0, weight_in.shape[1], chunk):
        here = slice(start, start + chunk)
        active_grad = dot(low, weight_last[here, :], NT)
        inner = (active_grad * slope[:, here].astype(F32)).astype(BF)
        preact_low[:, here] = inner
        part = column_sum(inner.astype(F32))
        for at in range(0, chunk, min(chunk, width)):
            row, lane = (start + at) // width, (start + at) % width
            size = min(chunk, width)
            sums[row : row + 1, lane : lane + size] += part[:, at : at + size]
        term = dot(inner, weight_in[:, here], NT)
        normed_grad = term if normed_grad is None else normed_grad + term
    hat, inverse = norm_parts(mid[...])
    sums[6:7, :] += column_sum(normed_grad * hat)
    sums[7:8, :] += column_sum(normed_grad)
    middle = above + norm_back(normed_grad, gains[1:2, :], hat, inverse)
    mid_grad[...] = middle
    branch = middle.astype(BF)
    branch_low[...] = branch
    sums[5:6, :] += column_sum(branch.astype(F32))
    context_grad[...] = dot(branch, weight_out[...], NT).astype(BF)


def mark_grads(context_grad, context, grad_mark):
    count = context_grad.shape[0]
    lane_all = lanes((count, 128)) & 63
    across = (
        lax.broadcasted_iota(jnp.int32, (128, 128), 0) // 64 != lanes((128, 128)) // 64
    ).astype(BF)
    zero = jnp.zeros((count, 128), BF)
    for pair in range(context_grad.shape[1] // 128):
        here = slice(pair * 128, pair * 128 + 128)
        product = split(context_grad[:, here].astype(F32) * context[:, here].astype(F32))
        level = -(dot(product[0], across, NN) + dot(product[1], across, NN))
        first = level.astype(BF)
        second, third = split(level - first.astype(F32))
        grad_mark[:, here] = merge(
            lane_all == 0, first, merge(lane_all == 1, second, merge(lane_all == 2, third, zero))
        )


def attend_back_block(
    number, start, extent, base, pairs,
    query, marks, key, value, context_grad, key_mark, grad_mark, query_grad, key_total, value_total,
):
    size = TOKENS
    low_query = lanes((size, 128)) < 64
    rows = pl.ds(pl.multiple_of(number * size, size), size)
    keys = pl.ds(pl.multiple_of(start, WINDOW), extent)
    low_key = lanes((extent, 128)) < 64
    key_aug = key_mark[keys, :]
    ones = jnp.where((lanes((extent, 128)) & 63) < 3, 1.0, 0.0).astype(BF)
    none = jnp.zeros((extent, 128), BF)
    for pair in range(pairs):
        here = pl.ds(pl.multiple_of(base + pair * 128, 128), 128)
        query_pair, key_pair, value_pair = query[rows, here], key[keys, here], value[keys, here]
        grad_pair, query_aug, grad_aug = context_grad[rows, here], marks[rows, here], grad_mark[rows, here]
        found = []
        for swap in (False, True):

            def both(low, left, right):
                return merge(low, right, left) if swap else merge(low, left, right)

            scores = dot(both(low_key, key_pair, key_aug), both(low_query, query_pair, query_aug), NT)
            rise = dot(both(low_key, value_pair, ones), both(low_query, grad_pair, grad_aug), NT)
            chance = jnp.exp2(scores)
            score_grad = (chance * rise).astype(BF)
            found.append(
                (
                    dot(score_grad, query_pair, NN),
                    dot(chance.astype(BF), grad_pair, NN),
                    dot(score_grad, both(low_key, key_pair, none), TN),
                )
            )
        key_total[keys, here] += merge(low_key, found[0][0], found[1][0])
        value_total[keys, here] += merge(low_key, found[0][1], found[1][1])
        query_grad[rows, here] = ((found[0][2] + found[1][2]) * HEAD ** (-0.5)).astype(BF)


def attend_back_kernel(
    windows, query, marks, key, value, context_grad, context, key_mark,
    query_grad, key_grad, value_grad, grad_mark, key_total, value_total, *, row
):
    count = query.shape[0]
    steps = count // TOKENS
    pairs = query.shape[1] // 128
    mark_grads(context_grad, context, grad_mark)
    key_total[...] = jnp.zeros_like(key_total)
    value_total[...] = jnp.zeros_like(value_total)

    def one(turn, carry):
        number = turn
        at = (row * steps + number) * 2

        def run(start, extent):
            attend_back_block(
                number, start, extent, 0, pairs,
                query, marks, key, value, context_grad, key_mark, grad_mark, query_grad, key_total, value_total,
            )

        for_windows(windows[at], windows[at + 1], count, run)
        return carry

    lax.fori_loop(0, steps, one, 0)
    key_grad[...] = (key_total[...] * (1.0 / LOG2E)).astype(BF)
    value_grad[...] = value_total[...].astype(BF)


def entry_back_kernel(
    side, edge, wide, up, head_bias, unit, query_grad, key_grad, value_grad, weight, gains, biases,
    mid_grad, *refs, adding
):
    before, refs = refs[: 2 * adding], refs[2 * adding :]
    entry, latent_out, sums, head_weight = refs
    encoder = side[0] == 0
    width = edge.shape[1]
    narrow = unit.shape[1]

    @pl.when(pl.program_id(0) == 0)
    def _():
        sums[...] = before[0][...] if adding else jnp.zeros_like(sums)
        head_weight[...] = before[1][...] if adding else jnp.zeros_like(head_weight)

    values = entry_values(encoder, edge[...], wide[...], up[...], head_bias[...])
    normed_grad = (
        dot(query_grad[...], weight[:, :width], NT)
        + dot(key_grad[...], weight[:, width : 2 * width], NT)
        + dot(value_grad[...], weight[:, 2 * width :], NT)
    )
    hat, inverse = norm_parts(values)
    sums[0:1, :] += column_sum(query_grad[...].astype(F32))
    sums[1:2, :] += column_sum(value_grad[...].astype(F32))
    sums[2:3, :] += column_sum(normed_grad * hat)
    sums[3:4, :] += column_sum(normed_grad)
    total = mid_grad[...] + norm_back(normed_grad, gains[0:1, :], hat, inverse)
    entry[...] = total

    @pl.when(jnp.logical_not(encoder))
    def _():
        sums[4:5, :] += column_sum(total)
        latent_out[...] = code_product(total, up[...]).T
        head_weight[...] += dot3(split(unit[...]), split(total), TN)


def hidden_weight_kernel(active, out_low, n2, preact_low, *refs):
    out = refs[-1]
    before = refs[0] if len(refs) > 1 else None
    step = pl.program_id(0)
    first = pl.num_programs(0) // 2
    width = n2.shape[1]

    def put(value, rows):
        out[rows, :] = value if before is None else value + before[rows, :]

    @pl.when(step < first)
    def _():
        put(dot(active[...], out_low[...], TN), slice(0, 2 * width))

    @pl.when(step >= first)
    def _():
        value = dot(n2[...], preact_low[...], TN)
        put(value[:, :width], slice(0, width))
        put(value[:, width:], slice(width, 2 * width))


def weight_call(kernel, operands, in_specs, steps, before):
    width = operands[1].shape[1]
    out_spec = pl.BlockSpec((2 * width, width), lambda step: (step, 0))
    aliases = {}
    if before is not None:
        aliases = {len(operands): 0}
        operands, in_specs = operands + [before], in_specs + [out_spec]
    return pl.pallas_call(
        kernel,
        grid=(steps,),
        in_specs=in_specs,
        out_specs=out_spec,
        out_shape=jax.ShapeDtypeStruct((2 * steps * width, width), F32),
        input_output_aliases=aliases,
        compiler_params=PARAMS,
    )(*operands)


def hidden_weights(kept, late, before=None):
    operands = [kept.active, late.out_low, kept.n2, late.preact_low]
    count, width = kept.n2.shape
    first = kept.active.shape[1] // (2 * width)
    full = pl.BlockSpec((count, width), lambda step: (0, 0))
    in_specs = [
        pl.BlockSpec((count, 2 * width), lambda step: (0, jnp.minimum(step, first - 1))),
        full,
        full,
        pl.BlockSpec((count, 2 * width), lambda step: (0, jnp.maximum(step - first, 0))),
    ]
    return weight_call(hidden_weight_kernel, operands, in_specs, 2 * first, before)


MESH = pl.DeviceIdType.MESH
LEAST_DEVICES = 4


def ring_chip(position, chips):
    odd = position // (chips // 2)
    return (1 - odd) * (2 * position) + odd * (2 * (chips - 1 - position) + 1)


class Ring:
    @staticmethod
    def scratch(arrays, ways, crossing):
        chips = lax.axis_size(DP) // 2
        sizes = [array.shape[0] // (2 * count * chips) for array, count in zip(arrays, ways)]
        shapes = [(count, chips, size, array.shape[1]) for array, count, size in zip(arrays, ways, sizes)]
        buffers = [pltpu.VMEM(shape, F32) for shape in shapes] * 3
        sems = [pltpu.SemaphoreType.DMA(shape[:2]) for shape in shapes] * 10
        far = []
        if crossing is not None:
            count, unused, size, width = shapes[crossing]
            far = [pltpu.VMEM((count, size, width), F32)] + [pltpu.SemaphoreType.DMA((count,))] * 2
        return buffers + sems + far

    def __init__(self, sources, results, ways, crossing, scratch):
        number = len(sources)
        take = lambda at: scratch[at * number : (at + 1) * number]
        self.chips = lax.axis_size(DP) // 2
        self.sources, self.results, self.ways, self.crossing = sources, results, ways, crossing
        self.own, self.pair, self.run = take(0), take(1), take(2)
        (
            self.load_sems, self.pair_send, self.pair_recv, self.run_send, self.run_recv,
            self.keep_sems, self.spread_send, self.spread_recv, self.side_send, self.side_recv,
        ) = (take(at) for at in range(3, 13))
        self.far = scratch[13 * number :]
        self.sizes = [run.shape[2] for run in self.run]
        self.lanes = [(which, way) for way in range(max(ways)) for which in range(number) if way < ways[which]]
        place = lax.axis_index(DP)
        chip, self.core = place // 2, place % 2
        column, odd = chip // 2, chip % 2
        chips = self.chips
        self.position = (1 - odd) * column + odd * (chips - 1 - column)
        self.other = {DP: chip * 2 + (1 - self.core)}
        self.across = {SECTION: 1 - lax.axis_index(SECTION)}
        self.targets = (
            {DP: ring_chip((self.position + 1) % chips, chips) * 2 + self.core},
            {DP: ring_chip((self.position + chips - 1) % chips, chips) * 2 + self.core},
        )

    def greet(self):
        self.barrier = pltpu.get_barrier_semaphore()
        devices = (self.other, self.across) + self.targets
        for device in devices:
            pl.semaphore_signal(self.barrier, inc=1, device_id=device, device_id_type=MESH)
        self.greeted = len(devices)

    def piece(self, step, way):
        return (self.position + (2 * self.chips - step if way % 2 == 0 else step)) % self.chips

    def rows(self, which, half, way, number):
        size = self.sizes[which]
        return pl.ds(pl.multiple_of(((half * self.ways[which] + way) * self.chips + number) * size, 8), size)

    def final(self, which, half, way, step):
        return self.results[which].at[self.rows(which, half, way, self.piece(step + self.chips - 1, way))]

    def load(self, which, way, step):
        return pltpu.make_async_copy(
            self.sources[which].at[self.rows(which, self.core, way, self.piece(step, way))],
            self.own[which].at[way, step],
            self.load_sems[which].at[way, step],
        )

    def remote(self, source, target, send, recv, device):
        return pltpu.make_async_remote_copy(
            src_ref=source, dst_ref=target, send_sem=send, recv_sem=recv, device_id=device, device_id_type=MESH
        )

    def swap(self, which, way, step):
        return self.remote(
            self.sources[which].at[self.rows(which, 1 - self.core, way, self.piece(step, way))],
            self.pair[which].at[way, step],
            self.pair_send[which].at[way, step],
            self.pair_recv[which].at[way, step],
            self.other,
        )

    def pass_on(self, which, way, step):
        return self.remote(
            self.run[which].at[way, step],
            self.run[which].at[way, step + 1],
            self.run_send[which].at[way, step],
            self.run_recv[which].at[way, step + 1],
            self.targets[way % 2],
        )

    def cross(self, way):
        return self.remote(
            self.run[self.crossing].at[way, self.chips - 1],
            self.far[0].at[way],
            self.far[1].at[way],
            self.far[2].at[way],
            self.across,
        )

    def keep(self, which, way):
        return pltpu.make_async_copy(
            self.run[which].at[way, self.chips - 1], self.final(which, self.core, way, 0), self.keep_sems[which].at[way, 0]
        )

    def spread(self, which, way, step, first=False):
        here = self.final(which, self.core, way, step)
        return self.remote(
            self.run[which].at[way, self.chips - 1] if first else here,
            here,
            self.spread_send[which].at[way, step],
            self.spread_recv[which].at[way, step],
            self.targets[way % 2],
        )

    def incoming(self, which, way, step):
        here = self.final(which, self.core, way, step)
        return self.remote(
            here, here, self.spread_send[which].at[way, step], self.spread_recv[which].at[way, step - 1],
            self.targets[way % 2],
        )

    def aside(self, which, way, step, first=False):
        here = self.final(which, self.core, way, step)
        return self.remote(
            self.run[which].at[way, self.chips - 1] if first else here,
            here,
            self.side_send[which].at[way, step],
            self.side_recv[which].at[way, step],
            self.other,
        )

    def beside(self, which, way, step):
        here = self.final(which, 1 - self.core, way, step)
        return self.remote(
            here, here, self.side_send[which].at[way, step], self.side_recv[which].at[way, step], self.other
        )

    def begin(self, waiting=True):
        def load(step, carry):
            for which, way in self.lanes:
                self.load(which, way, step).start()
            return carry

        def swap(step, carry):
            for which, way in self.lanes:
                self.swap(which, way, step).start()
            return carry

        lax.fori_loop(0, self.chips, load, 0)
        if waiting:
            pl.semaphore_wait(self.barrier, self.greeted)
        lax.fori_loop(0, self.chips, swap, 0)
        for which, way in self.lanes:
            self.load(which, way, 0).wait()
            self.swap(which, way, 0).wait_recv()
            self.run[which][way, 0] = self.own[which][way, 0] + self.pair[which][way, 0]
            self.pass_on(which, way, 0).start()

    def gather(self, step, lanes=None):
        for which, way in self.lanes if lanes is None else lanes:
            run, own, pair = self.run[which], self.own[which], self.pair[which]
            self.load(which, way, step).wait()
            self.swap(which, way, step).wait_recv()
            self.pass_on(which, way, step - 1).wait_recv()
            run[way, step] = run[way, step] + own[way, step] + pair[way, step]

            @pl.when(step < self.chips - 1)
            def _():
                self.pass_on(which, way, step).start()

    def turn(self):
        for which, way in self.lanes:
            if which == self.crossing:
                self.cross(way).start()
        for which, way in self.lanes:
            if which != self.crossing:
                self.hand_out(which, way)
        for which, way in self.lanes:
            if which == self.crossing:
                run = self.run[which]
                self.cross(way).wait()
                run[way, self.chips - 1] = run[way, self.chips - 1] + self.far[0][way]
                self.hand_out(which, way)

    def hand_out(self, which, way):
        self.spread(which, way, 0, True).start()
        self.aside(which, way, 0, True).start()
        self.keep(which, way).start()

    def pass_out(self, step, lanes=None):
        for which, way in self.lanes if lanes is None else lanes:
            self.incoming(which, way, step).wait_recv()

            @pl.when(step < self.chips - 1)
            def _():
                self.spread(which, way, step).start()

            self.aside(which, way, step).start()

    def finish(self):
        def one(step, carry):
            for which, way in self.lanes:
                self.swap(which, way, step).wait_send()
                self.beside(which, way, step).wait_recv()
                self.aside(which, way, step).wait_send()

                @pl.when(step < self.chips - 1)
                def _():
                    self.pass_on(which, way, step).wait_send()
                    self.spread(which, way, step).wait_send()

            return carry

        lax.fori_loop(0, self.chips, one, 0)
        for which, way in self.lanes:
            self.keep(which, way).wait()


def loop(start, stop, run):
    def one(step, carry):
        run(step)
        return carry

    lax.fori_loop(start, stop, one, 0)


HIDDEN_WAYS = (4,)
OTHER_WAYS = (4, 2)


def finish_kernel(*refs, held):
    (
        hidden, query, marks, key, value, context_grad, context, key_mark, edges, mid_grad, weight, branch_low, n1,
    ), refs = refs[:13], refs[13:]
    mine, others, refs = refs[:6], refs[6:18], refs[18:]
    (
        gains, book, down, up, late, early,
        hidden_out, attention_out, misc_out, entry,
        query_in, marks_in, key_in, value_in, grad_in, context_in, key_mark_in, edge_in, mid_in, weight_in, branch_in,
        n1_in, part, misc, grad_mark, query_grad, key_total, value_total, key_grad, value_grad, in_sems, out_sems,
    ), scratch = refs[:32], refs[32:]
    encoder = lax.axis_index(SECTION) == 0
    decoder = jnp.logical_not(encoder)
    ring = Ring((hidden,), (hidden_out,), HIDDEN_WAYS, None, scratch[:held]) if scratch else None
    last = Ring((part, misc), (attention_out, misc_out), OTHER_WAYS, 1, scratch[held:]) if scratch else None
    count, width = query.shape
    narrow = down.shape[0]
    steps = count // TOKENS
    pairs = width // 128
    row = edges.shape[0] - 1
    at = book.shape[0] + 2 * narrow
    inputs = (
        (query, query_in), (marks, marks_in), (key, key_in), (value, value_in), (context_grad, grad_in),
        (context, context_in), (key_mark.at[row], key_mark_in), (edges.at[row], edge_in), (mid_grad, mid_in),
        (weight, weight_in), (branch_low, branch_in), (n1, n1_in),
    )
    first_held = (query_in, marks_in, key_in, value_in, grad_in, grad_mark)
    second_held = (context_in, branch_in, n1_in, query_grad, key_grad, value_grad)

    def copies(pairs):
        return [pltpu.make_async_copy(*pair, in_sems.at[number]) for number, pair in enumerate(pairs)]

    loads = copies(inputs)
    other_loads = copies(zip(others, first_held + second_held))
    first_loads = copies(zip(mine, first_held))

    def start(copies):
        for copy in copies:
            copy.start()

    def wait(copies):
        for copy in copies:
            copy.wait()

    if ring:
        ring.greet()
    pl.when(encoder)(functools.partial(start, loads))
    pl.when(decoder)(functools.partial(start, other_loads))
    if ring:
        ring.begin()
    misc[...] = jnp.zeros_like(misc)

    @pl.when(encoder)
    def _():
        misc[: book.shape[0], :] = book[...]
        misc[book.shape[0] : book.shape[0] + narrow, :] = down[...]
        misc[at : at + 16, :] = late[...]
        misc[at + 16 : at + 32, :] = early[...]
        wait(loads)
        mark_grads(grad_in, context_in, grad_mark)
        key_total[...] = jnp.zeros_like(key_total)
        value_total[...] = jnp.zeros_like(value_total)

    @pl.when(decoder)
    def _():
        misc[book.shape[0] + narrow : at, :] = up[...]
        misc[at + 32 : at + 48, :] = late[...]
        misc[at + 48 : at + 64, :] = early[...]
        wait(other_loads)

    def attention_piece(turn):
        attend_back_block(
            turn // pairs, 0, count, (turn % pairs) * 128, 1,
            query_in, marks_in, key_in, value_in, grad_in, key_mark_in, grad_mark, query_grad, key_total, value_total,
        )

    def entry_piece(number):
        rows = pl.ds(pl.multiple_of(number * TOKENS, TOKENS), TOKENS)
        normed_grad = (
            dot(query_grad[rows, :], weight_in[:, :width], NT)
            + dot(key_grad[rows, :], weight_in[:, width : 2 * width], NT)
            + dot(value_grad[rows, :], weight_in[:, 2 * width :], NT)
        )
        hat, inverse = norm_parts(edge_in[rows, :].astype(F32))
        misc[at + 16 : at + 17, :] += column_sum(query_grad[rows, :].astype(F32))
        misc[at + 17 : at + 18, :] += column_sum(value_grad[rows, :].astype(F32))
        misc[at + 18 : at + 19, :] += column_sum(normed_grad * hat)
        misc[at + 19 : at + 20, :] += column_sum(normed_grad)
        mid_in[rows, :] = mid_in[rows, :] + norm_back(normed_grad, gains[0:1, :], hat, inverse)

    def weight_piece(number):
        def put(first, second):
            rows = pl.ds(pl.multiple_of(number * width, width), width)
            part[rows, :] = dot(first[0][...], first[1][...], TN) + dot(second[0][...], second[1][...], TN)

        for choice, places in enumerate(((0, 1), (2, 3), (2, 4), (2, 5))):
            both = [[held[place] for place in places] for held in (first_held, second_held)]
            pl.when(number == choice)(functools.partial(put, *both))

    halves = (ring.lanes[:2], ring.lanes[2:]) if ring else (None, None)
    chips = ring.chips if ring else 8
    pieces = steps * pairs

    def summing(step):
        for half in range(2):
            if ring:
                ring.gather(step, halves[half])

            @pl.when(encoder)
            def _():
                attention_piece(2 * (step - 1) + half)

    inside = min(chips - 1, pieces // 2)
    loop(1, inside + 1, summing)
    if ring:
        loop(inside + 1, chips, ring.gather)
        ring.turn()

    @pl.when(encoder)
    def _():
        loop(2 * inside, pieces, attention_piece)
        start(first_loads)
        key_grad[...] = (key_total[...] * (1.0 / LOG2E)).astype(BF)
        value_grad[...] = value_total[...].astype(BF)
        wait(first_loads)

    def spreading(step):
        if ring:
            ring.pass_out(step, halves[0])

        @pl.when(encoder)
        def _():
            entry_piece(step - 1)

        if ring:
            ring.pass_out(step, halves[1])
        weight_piece(step - 1)

    loop(1, steps + 1, spreading)
    store = pltpu.make_async_copy(mid_in, entry, out_sems.at[0])

    @pl.when(encoder)
    def _():
        store.start()

    if ring:
        last.begin(False)

        def both(step):
            ring.pass_out(step)
            last.gather(step - steps)

        loop(steps + 1, chips, both)
        loop(chips - steps, chips, last.gather)
        last.turn()
        loop(1, chips, last.pass_out)
        ring.finish()
        last.finish()
    else:
        stores = [
            pltpu.make_async_copy(part, attention_out, out_sems.at[1]),
            pltpu.make_async_copy(misc, misc_out, out_sems.at[2]),
        ]
        start(stores)
        wait(stores)

    @pl.when(encoder)
    def _():
        store.wait()


def finish_row(work, first_kept, kept, late, mine, book, others, hidden):
    count, width = kept.n1.shape
    alone = lax.axis_size(DP) < LEAST_DEVICES
    its_late, its_early = mine
    operands = [
        hidden, kept.query, kept.marks, kept.key, kept.value, late.context_grad,
        kept.context, work.key_mark, work.edges, late.mid_grad, work.attention_in, late.branch_low, kept.n1,
    ]
    for a_kept, a_late, a_early in ((first_kept, its_late, its_early),) + others:
        operands += [a_kept.context, a_late.branch_low, a_kept.n1, *a_early[:3]]
    operands += [work.gains, book, late.head, its_early.head, late.sums, its_early.sums]
    hbm, vmem = pl.BlockSpec(memory_space=pl.ANY), pl.BlockSpec(memory_space=pltpu.VMEM)
    rows = book.shape[0] + 2 * work.narrow + 64
    unit = 16 * lax.axis_size(DP)
    attention = jax.ShapeDtypeStruct((4 * width, width), F32)
    misc = jax.ShapeDtypeStruct((rows + (-rows % unit), width), F32)
    low = pltpu.VMEM((count, width), BF)
    wide = pltpu.VMEM((count, width), F32)
    scratch = [low] * 6 + [pltpu.VMEM((count, 128), BF), low, wide, pltpu.VMEM(work.attention_in.shape, BF), low, low]
    scratch += [pltpu.VMEM(attention.shape, F32), pltpu.VMEM(misc.shape, F32), low, low, wide, wide, low, low]
    scratch += [pltpu.SemaphoreType.DMA((12,)), pltpu.SemaphoreType.DMA((3,))]
    settings = {}
    held = 0
    if not alone:
        rings = Ring.scratch((hidden,), HIDDEN_WAYS, None)
        held = len(rings)
        scratch += rings + Ring.scratch((attention, misc), OTHER_WAYS, 1)
        settings = dict(collective_id=0, has_side_effects=True)
    outs = pl.pallas_call(
        functools.partial(finish_kernel, held=held),
        in_specs=[hbm] * 31 + [vmem] * 6,
        out_specs=[hbm] * 4,
        out_shape=(
            jax.ShapeDtypeStruct(hidden.shape, F32), attention, misc, jax.ShapeDtypeStruct((count, width), F32),
        ),
        scratch_shapes=scratch,
        compiler_params=pltpu.CompilerParams(vmem_limit_bytes=60 << 20, **settings),
    )(*operands)
    if alone:
        return hidden, outs[1], lax.psum(outs[2], SECTION), outs[3]
    return outs


def unpack_kernel(
    side, hidden, attention, misc, first_entry, second_entry, first_result, second_result,
    hidden_out, hidden_in, attention_out, attention_in, edge, book, gains, biases, bias, last_gain, head_bias, down, down_last,
    up, held, head, rows, ins, outs, row_ins, row_outs,
):
    width = hidden.shape[1]
    narrow = book.shape[0]
    steps = hidden_out.shape[0] // width
    targets = [hidden_out.at[pl.ds(number * width, width), :] for number in range(steps)]
    targets += [hidden_in.at[:, pl.ds(number * width, width)] for number in range(steps)]
    targets += [attention_out]
    targets += [attention_in.at[:, pl.ds(number * width, width)] for number in range(3)]
    sources = [hidden.at[pl.ds(number * width, width), :] for number in range(2 * steps)]
    sources += [attention.at[pl.ds(number * width, width), :] for number in range(4)]
    tiles = range(len(targets))
    for mine, pair in ((0, (first_entry, second_entry)), (1, (first_result, second_result))):

        @pl.when(side[0] == mine)
        def _():
            for row in range(2):
                pltpu.make_async_copy(pair[row], rows.at[row], row_ins.at[row]).start()

    loads = [pltpu.make_async_copy(sources[number], held.at[number], ins.at[number]) for number in tiles]
    loads.append(pltpu.make_async_copy(misc.at[pl.ds(0, head.shape[0]), :], head, ins.at[len(targets)]))
    for load in loads:
        load.start()
    stores = []
    for row in range(2):
        pltpu.make_async_copy(first_entry, rows.at[row], row_ins.at[row]).wait()
        stores.append(pltpu.make_async_copy(rows.at[row], edge.at[row], row_outs.at[row]))
        stores[-1].start()
    for number in tiles:
        loads[number].wait()
        stores.append(pltpu.make_async_copy(held.at[number], targets[number], outs.at[number]))
        stores[-1].start()
    loads[-1].wait()
    for number in range(book.shape[1] // width):
        book[:, number * width : (number + 1) * width] = head[number * narrow : (number + 1) * narrow, :]
    at = book.shape[0] * book.shape[1] // width
    down[...] = head[at : at + narrow, :]
    up[...] = head[at + narrow : at + 2 * narrow, :]
    at += 2 * narrow
    last_gain[...] = head[at + 8 : at + 9, :]
    head_bias[0:1, :] = head[at + 9 : at + 10, :]
    head_bias[1:2, :] = head[at + 52 : at + 53, :]
    down_last[...] = head[at + 10 : at + 11, :narrow]
    mine = jnp.where(side[0] == 0, head[at : at + 32, :], head[at + 32 : at + 64, :])
    bias[...] = mine[:steps, :]
    for out, places in ((gains, (18, 6)), (biases, (16, 17, 5, 19, 7, 4))):
        for number, place in enumerate(places):
            out[number : number + 1, :] = mine[place : place + 1, :]
    for store in stores:
        store.wait()


def unpack(side, hidden, attention, misc, ends, table_turned):
    width = hidden.shape[1]
    features = hidden.shape[0] // 2
    tiles = (hidden.shape[0] + attention.shape[0]) // width
    narrow = table_turned.shape[0]
    rows = table_turned.size // width + 2 * narrow + 64
    shapes = (
        (features, width), (width, features), (width, width), (width, 3 * width), (2,) + ends[0].shape,
        table_turned.shape, (2, width), (6, width), (features // width, width), (1, width), (2, width),
        (narrow, width), (1, narrow), (narrow, width),
    )
    hbm, vmem = pl.BlockSpec(memory_space=pl.ANY), pl.BlockSpec(memory_space=pltpu.VMEM)
    return pl.pallas_call(
        unpack_kernel,
        in_specs=[pl.BlockSpec(memory_space=pltpu.SMEM)] + [hbm] * 7,
        out_specs=[hbm] * 5 + [vmem] * 9,
        out_shape=tuple(jax.ShapeDtypeStruct(shape, F32) for shape in shapes),
        scratch_shapes=[
            pltpu.VMEM((tiles, width, width), F32),
            pltpu.VMEM((rows, width), F32),
            pltpu.VMEM((2,) + ends[0].shape, F32),
            pltpu.SemaphoreType.DMA((tiles + 1,)),
            pltpu.SemaphoreType.DMA((tiles,)),
            pltpu.SemaphoreType.DMA((2,)),
            pltpu.SemaphoreType.DMA((2,)),
        ],
        compiler_params=PARAMS,
    )(side, hidden, attention, misc, *ends)


def nothing_kernel(*refs):
    pass


def unwritten(shapes):
    leaves, tree = jax.tree.flatten(shapes)
    arrays = pl.pallas_call(
        nothing_kernel,
        out_specs=[pl.BlockSpec(memory_space=pl.ANY)] * len(leaves),
        out_shape=tuple(leaves),
    )()
    return jax.tree.unflatten(tree, arrays)


class Kept(NamedTuple):
    n1: Any
    query: Any
    key: Any
    value: Any
    context: Any
    marks: Any
    mid: Any
    n2: Any
    active: Any
    slope: Any
    result: Any
    latent: Any


class Late(NamedTuple):
    out_low: Any
    preact_low: Any
    mid_grad: Any
    branch_low: Any
    context_grad: Any
    sums: Any
    head: Any


class Early(NamedTuple):
    query_grad: Any
    key_grad: Any
    value_grad: Any
    entry: Any
    latent_out: Any
    sums: Any
    head: Any


class Rows:
    def __init__(self, side, edges, wide, unit, windows, query_mark, key_mark, weights, head):
        self.side, self.edges, self.wide, self.unit = side, edges, wide, unit
        self.windows, self.query_mark, self.key_mark = windows, query_mark, key_mark
        (
            self.attention_in, self.attention_out, self.hidden_in, self.hidden_out,
            self.gains, self.biases, self.hidden_bias,
        ) = weights
        (
            self.output_gain, self.head_bias, self.down, self.down_bias, self.up,
        ) = head
        self.rows, self.count, self.width = edges.shape
        self.hidden = self.hidden_in.shape[1]
        self.narrow = unit.shape[1]
        self.size = TOKENS
        n, d, f = self.count, self.width, self.hidden
        shape = jax.ShapeDtypeStruct
        low, tall, wide = shape((n, d), BF), shape((n, f), BF), shape((n, d), F32)
        sums, head = shape((16, d), F32), shape((self.narrow, d), F32)
        self.kept = Kept(low, low, low, low, low, low, wide, low, tall, tall, wide, shape((n, self.narrow), F32))
        self.late = Late(low, tall, wide, low, low, sums, head)
        self.early = Early(low, low, low, wide, shape((self.narrow, n), F32), sums, head)

    def side_spec(self):
        return pl.BlockSpec(memory_space=pltpu.SMEM)

    def tokens(self, array):
        return pl.BlockSpec((self.size, array.shape[1]), lambda step: (step, 0))

    def turned(self, array):
        return pl.BlockSpec((array.shape[0], self.size), lambda step: (0, step))

    def whole(self, array):
        return pl.BlockSpec(array.shape, lambda step: (0,) * len(array.shape))

    def entry_specs(self, row):
        steps = self.count // self.size
        return [
            pl.BlockSpec((None, self.size, self.width), lambda step: (row, step, 0)),
            pl.BlockSpec((self.size, self.wide.shape[1]), lambda step: (row * steps + step, 0)),
            self.whole(self.up),
            self.whole(self.head_bias),
        ]

    def unit_spec(self, row):
        steps = self.count // self.size
        return pl.BlockSpec((self.size, self.narrow), lambda step: (row * steps + step, 0))

    def call(self, kernel, in_specs, operands, outs, out_specs, scratch=()):
        return pl.pallas_call(
            kernel,
            grid=(self.count // self.size,),
            in_specs=in_specs,
            out_specs=out_specs,
            out_shape=tuple(outs),
            scratch_shapes=list(scratch),
            compiler_params=PARAMS,
        )(*operands)

    def attention_call(self, kernel, row, operands, outs, scratch=()):
        half = self.width // 2

        def spec(array):
            if array.ndim == 3:
                return pl.BlockSpec((None, self.count, array.shape[2]), lambda step, info: (row, 0, 0))
            return pl.BlockSpec((self.count, half), lambda step, info: (0, step))

        return pl.pallas_call(
            functools.partial(kernel, row=row),
            grid_spec=pltpu.PrefetchScalarGridSpec(
                num_scalar_prefetch=1,
                grid=(2,),
                in_specs=[spec(array) for array in operands],
                out_specs=[spec(array) for array in outs],
                scratch_shapes=list(scratch),
            ),
            out_shape=tuple(outs),
            compiler_params=PARAMS,
        )(self.windows, *operands)

    def forward(self, row):
        shapes = self.kept
        entry = (self.edges, self.wide, self.up, self.head_bias)
        outs = shapes[:4]
        self.size = 2 * TOKENS
        n1, query, key, value = self.call(
            project_kernel,
            [self.side_spec()] + self.entry_specs(row)
            + [self.whole(self.gains), self.whole(self.biases), self.whole(self.attention_in)],
            (self.side,) + entry + (self.gains, self.biases, self.attention_in),
            outs,
            [self.tokens(array) for array in outs],
        )
        self.size = TOKENS
        context, marks = self.attention_call(
            attend_kernel, row, (query, key, value, self.query_mark, self.key_mark), shapes[4:6]
        )
        consts = (
            self.attention_out, self.gains, self.biases, self.hidden_in, self.hidden_bias, self.hidden_out,
            self.output_gain, self.down, self.down_bias,
        )
        outs = shapes[6:]
        outs = self.call(
            hidden_kernel,
            [self.side_spec()] + self.entry_specs(row) + [self.tokens(context)]
            + [self.whole(array) for array in consts],
            (self.side,) + entry + (context,) + consts,
            outs,
            [self.tokens(array) for array in outs],
        )
        return Kept(n1, query, key, value, context, marks, *outs)

    def backward(self, row, kept, latent_in, former=(None, None)):
        late = self.backward_late(row, kept, latent_in, former[0])
        return late, self.backward_early(row, kept, late, former[1])

    def backward_late(self, row, kept, latent_in, former=None):
        prior = () if former is None else (former.sums, former.head)
        adding = int(former is not None)
        consts = (self.output_gain, self.head_bias, self.down, self.hidden_out)
        late = (self.gains, self.biases, self.attention_out)
        outs = self.late
        return Late(*self.call(
            functools.partial(tail_back_kernel, adding=adding),
            [self.side_spec(), self.tokens(kept.result), self.entry_specs(row)[0], self.unit_spec(row),
             self.turned(latent_in), self.tokens(kept.latent)]
            + [self.whole(array) for array in consts]
            + [self.tokens(kept.slope), self.whole(self.hidden_in), self.tokens(kept.mid)]
            + [self.whole(array) for array in late + prior],
            (self.side, kept.result, self.edges, self.unit, latent_in, kept.latent) + consts
            + (kept.slope, self.hidden_in, kept.mid) + late + prior,
            outs,
            [self.tokens(array) for array in outs[:5]] + [self.whole(array) for array in outs[5:]],
            scratch=[pltpu.VMEM((self.size, self.width), F32)],
        ))

    def backward_early(self, row, kept, late, former=None):
        adding = int(former is not None)
        half = self.width // 2
        grads = tuple(self.attention_call(
            attend_back_kernel, row,
            (kept.query, kept.marks, kept.key, kept.value, late.context_grad, kept.context, self.key_mark),
            self.early[:3],
            scratch=[
                pltpu.VMEM((self.count, half), BF),
                pltpu.VMEM((self.count, half), F32),
                pltpu.VMEM((self.count, half), F32),
            ],
        ))
        prior = () if former is None else (former.sums, former.head)
        outs = self.early[3:]
        outs = self.call(
            functools.partial(entry_back_kernel, adding=adding),
            [self.side_spec()] + self.entry_specs(row) + [self.unit_spec(row)]
            + [self.tokens(array) for array in grads]
            + [self.whole(self.attention_in), self.whole(self.gains), self.whole(self.biases),
               self.tokens(late.mid_grad)] + [self.whole(array) for array in prior],
            (self.side, self.edges, self.wide, self.up, self.head_bias, self.unit) + grads
            + (self.attention_in, self.gains, self.biases, late.mid_grad) + prior,
            outs,
            [self.tokens(outs[0]), self.turned(outs[1])] + [self.whole(array) for array in outs[2:]],
        )
        return Early(*grads, *outs)


def windows_of(segments):
    rows, count = segments.shape
    steps = count // WINDOW
    blocks = segments.reshape(rows, steps, WINDOW)
    least, most = blocks[:, :, 0], blocks[:, :, -1]
    meets = (most[:, :, None] >= least[:, None, :]) & (least[:, :, None] <= most[:, None, :])
    place = jnp.arange(steps)
    start = jnp.min(jnp.where(meets, place, steps), -1)
    stop = jnp.max(jnp.where(meets, place, -1), -1) + 1
    return jnp.stack([start, stop - start], -1).reshape(-1).astype(jnp.int32)


def on_device(
    boundary, segments, code_index, attention_in, attention_out, hidden_in, hidden_out, block_gains,
    block_biases, hidden_bias, output_gain, head_bias, down_weight, down_bias, up_weight, codebook,
):
    section = lax.axis_index(SECTION)
    encoder = section == 0
    side = section.astype(jnp.int32)[None]
    edges = boundary[0]
    rows, count, width = edges.shape
    hidden = hidden_in.shape[2]
    table_turned = codebook.T
    code_index = code_index.reshape(-1)
    unit, wide, query_mark, key_mark = gather_codes(code_index, table_turned, segments)
    work = Rows(
        side, edges, wide, unit, windows_of(segments), query_mark, key_mark,
        (
            attention_in[0], attention_out[0], hidden_in[0], hidden_out[0], block_gains[0], block_biases[0],
            hidden_bias,
        ),
        (output_gain[None], head_bias, down_weight.T, down_bias[None], up_weight),
    )
    book_out = book_shape(table_turned, width)
    hidden_shape = jax.ShapeDtypeStruct((2 * hidden, width), F32)
    quiet = jnp.zeros((unit.shape[1], count), F32)
    first_kept = work.forward(0)

    def encoder_first():
        return (work.forward(1), *unwritten((work.late, work.early)))

    def decoder_first():
        return (unwritten(work.kept), *work.backward(0, first_kept, quiet))

    kept_a, late_a, early_a = lax.cond(encoder, encoder_first, decoder_first)
    latent_in = lax.ppermute(early_a.latent_out, SECTION, [(1, 0)])

    def encoder_second():
        late, early = work.backward(0, first_kept, latent_in)
        book = scatter_codes(code_index, unit, (first_kept.latent, kept_a.latent), table_turned, width)
        return unwritten(work.kept), late, early, hidden_weights(first_kept, late), book

    def decoder_second():
        kept = work.forward(1)
        weights, book = unwritten((hidden_shape, book_out))
        return (kept, *work.backward(1, kept, quiet, (late_a, early_a)), weights, book)

    kept_b, late_b, early_b, weights_b, book = lax.cond(encoder, encoder_second, decoder_second)
    latent_in_second = lax.ppermute(early_b.latent_out, SECTION, [(1, 0)])

    def decoder_fourth():
        total = hidden_weights(kept_b, late_b, hidden_weights(first_kept, late_a))
        return total, (*unwritten(work.late[2:5]), late_b.sums, late_b.head)

    def encoder_fourth():
        late = work.backward_late(1, kept_a, latent_in_second, late_b)
        return hidden_weights(kept_a, late, weights_b), late[2:]

    hidden_total, late = lax.cond(encoder, encoder_fourth, decoder_fourth)
    late = Late(None, None, *late)
    hidden_total, attention_total, misc, second_entry = finish_row(
        work, first_kept, kept_a, late, (late_b, early_b), book,
        ((first_kept, late_a, early_a), (kept_b, late_b, early_b)), hidden_total,
    )
    (
        hidden_out_grad, hidden_in_grad, attention_out_grad, attention_in_grad, edge, book, gains, biases, bias,
        last_gain, head, down_grad, down_last, up_grad,
    ) = unpack(
        side, hidden_total, attention_total, misc,
        (early_b.entry, second_entry, first_kept.result, kept_b.result), table_turned,
    )
    return (
        edge[None],
        attention_in_grad[None],
        attention_out_grad[None],
        hidden_in_grad[None],
        hidden_out_grad[None],
        gains[None],
        biases[None],
        bias.reshape(1, hidden),
        last_gain[0],
        head,
        down_grad.T,
        down_last[0],
        up_grad,
        book.T,
    )


def solution(mesh):
    wide, split_last, flat = P(SECTION, DP, None, None), P(SECTION, None, None), P(SECTION, None)
    blocks = (split_last,) * 6 + (flat,)
    return jax.shard_map(
        on_device,
        mesh=mesh,
        in_specs=(wide, P(DP, None), P(DP, None)) + blocks + (P(),) * 6,
        out_specs=(wide,) + blocks + (P(),) * 6,
        check_vma=False,
    )
```

```python
import functools
import math
from typing import Any, NamedTuple

import jax
import jax.numpy as jnp
from jax import lax
from jax.experimental import pallas as pl
from jax.experimental.pallas import tpu as pltpu
from jax.sharding import PartitionSpec as P

HEAD = 64
SECTION, DP = "section", "dp"
BF = jnp.bfloat16
F32 = jnp.float32
LOG2E = math.log2(math.e)
NORM_EPS = 1e-06
MASKED = -1e30
GELU = 0.7978845608028654
CUBIC = 0.044715
NN = (((1,), (0,)), ((), ()))
NT = (((1,), (1,)), ((), ()))
TN = (((0,), (0,)), ((), ()))
TOKENS = 256
WINDOW = 256
PARAMS = pltpu.CompilerParams(vmem_limit_bytes=56 << 20)


def dot(a, b, dims):
    return lax.dot_general(a, b, dims, preferred_element_type=F32)


def lanes(shape):
    return lax.broadcasted_iota(jnp.int32, shape, 1)


def split(values):
    high = values.astype(BF)
    return high, (values - high.astype(F32)).astype(BF)


def dot3(left, right, dims):
    return dot(left[0], right[0], dims) + dot(left[0], right[1], dims) + dot(left[1], right[0], dims)


def unit_of(values):
    scale = lax.rsqrt(jnp.sum(values * values, -1, keepdims=True) + NORM_EPS)
    return values * scale, scale


def norm_parts(values):
    center = values - jnp.mean(values, -1, keepdims=True)
    inverse = lax.rsqrt(jnp.mean(center * center, -1, keepdims=True) + NORM_EPS)
    return center * inverse, inverse


def norm_back(grad, gain, hat, inverse):
    scaled = grad * gain
    return inverse * (
        scaled
        - jnp.mean(scaled, -1, keepdims=True)
        - hat * jnp.mean(scaled * hat, -1, keepdims=True)
    )


def column_sum(values):
    return jnp.sum(values, 0, keepdims=True)


def code_kernel(index, table_turned, segments, unit, wide, query_mark, key_mark, table, raw):
    count = raw.shape[0]
    block = 512

    def turn(step, carry):
        start = pl.multiple_of(step * block, block)
        table[pl.ds(start, block), :] = table_turned[:, pl.ds(start, block)].T
        return carry

    lax.fori_loop(0, table.shape[0] // block, turn, 0)

    length = segments.shape[1]

    def some(step, carry):
        for inner in range(16):
            token = step * 16 + inner
            raw[pl.ds(token, 1), :] = table[pl.ds(index[token], 1), :]
        return carry

    lax.fori_loop(0, count // 16, some, 0)

    values = raw[...]
    values = values * lax.rsqrt(jnp.sum(values * values, -1, keepdims=True) + NORM_EPS)
    unit[...] = values
    high, low = split(values)
    wide[...] = jnp.concatenate([high, low, high, jnp.zeros_like(high)], 1)
    lane = lanes((length, 128)) & 63
    for row in range(segments.shape[0]):
        owner = jnp.broadcast_to(segments[row : row + 1, :], (128, length)).T
        same = owner == lane
        query_mark[row] = jnp.where((lane < 4) & jnp.logical_not(same), MASKED, 0.0).astype(BF)
        key_mark[row] = jnp.where(((lane < 4) & same) | ((lane > 3) & (lane < 7)), 1.0, 0.0).astype(BF)


def gather_codes(index, table_turned, segments):
    count, width = index.shape[0], table_turned.shape[0]
    vmem = pl.BlockSpec(memory_space=pltpu.VMEM)
    mark = jax.ShapeDtypeStruct(segments.shape + (128,), BF)
    return pl.pallas_call(
        code_kernel,
        in_specs=[pl.BlockSpec(memory_space=pltpu.SMEM), vmem, vmem],
        out_specs=[vmem] * 4,
        out_shape=(
            jax.ShapeDtypeStruct((count, width), F32),
            jax.ShapeDtypeStruct((count, 4 * width), BF),
            mark,
            mark,
        ),
        scratch_shapes=[pltpu.VMEM(table_turned.shape[::-1], F32), pltpu.VMEM((count, width), F32)],
        compiler_params=PARAMS,
    )(index, table_turned, segments)


def scatter_kernel(index, unit, latent_first, latent_second, table_turned, out, total, rows):
    count = rows.shape[0]
    width = unit.shape[1]
    half = count // 2
    total[...] = jnp.zeros_like(total)
    for row, latent in enumerate((latent_first, latent_second)):
        here = slice(row * half, (row + 1) * half)
        code, unused = unit_of(latent[...])
        rows[here, :] = 2.0 * (unit[here, :] - code)

    def some(step, carry):
        for inner in range(8):
            token = step * 8 + inner
            place = pl.ds(index[token], 1)
            total[place, :] = total[place, :] + rows[pl.ds(token, 1), :]
        return carry

    lax.fori_loop(0, count // 8, some, 0)
    block = out.shape[1]

    def back(step, carry):
        start = pl.multiple_of(step * block, block)
        values = table_turned[:, pl.ds(start, block)]
        grad = total[pl.ds(start, block), :].T
        inverse = lax.rsqrt(jnp.sum(values * values, 0, keepdims=True) + NORM_EPS)
        book = values * inverse
        out[pl.ds(pl.multiple_of(step * width, width), width), :] = inverse * (
            grad - book * jnp.sum(book * grad, 0, keepdims=True)
        )
        return carry

    lax.fori_loop(0, total.shape[0] // block, back, 0)


def book_shape(table_turned, width):
    return jax.ShapeDtypeStruct((table_turned.size // width, width), F32)


def scatter_codes(index, unit, latents, table_turned, width):
    return pl.pallas_call(
        scatter_kernel,
        in_specs=[pl.BlockSpec(memory_space=pltpu.SMEM)] + [pl.BlockSpec(memory_space=pltpu.VMEM)] * 4,
        out_specs=pl.BlockSpec(memory_space=pltpu.VMEM),
        out_shape=book_shape(table_turned, width),
        scratch_shapes=[pltpu.VMEM(table_turned.shape[::-1], F32), pltpu.VMEM(unit.shape, F32)],
        compiler_params=PARAMS,
    )(index, unit, *latents, table_turned)


def entry_values(encoder, edge, wide, up, head_bias):
    high, low = split(up)
    parts = jnp.concatenate([high, high, low, jnp.zeros_like(low)], 0)
    return jnp.where(encoder, edge.astype(F32), dot(wide, parts, NN) + head_bias[1:2, :])


def project_kernel(side, edge, wide, up, head_bias, gains, biases, weight, n1, query, key, value):
    width = edge.shape[1]
    encoder = side[0] == 0
    values = entry_values(encoder, edge[...], wide[...], up[...], head_bias[...])
    hat, unused = norm_parts(values)
    normed = (hat * gains[0:1, :] + biases[3]).astype(BF)
    n1[...] = normed
    query[...] = (
        (dot(normed, weight[:, :width], NN) + biases[0]) * (LOG2E * HEAD ** (-0.5))
    ).astype(BF)
    key[...] = dot(normed, weight[:, width : 2 * width], NN).astype(BF)
    value[...] = (dot(normed, weight[:, 2 * width :], NN) + biases[1]).astype(BF)


def merge(low_half, left, right):
    return jnp.where(low_half, left, right)


def attend_kernel(windows, query, key, value, query_mark, key_mark, context, marks, *, row):
    count = query.shape[0]
    size = TOKENS
    pairs = query.shape[1] // 128
    low_query = lanes((size, 128)) < 64
    mark_lane = lanes((size, 128)) & 63

    def block(number, start, extent):
        rows = pl.ds(pl.multiple_of(number * size, size), size)
        keys = pl.ds(pl.multiple_of(start, WINDOW), extent)
        low_key = lanes((extent, 128)) < 64
        query_aug, key_aug = query_mark[rows, :], key_mark[keys, :]
        ones = jnp.ones((extent, 128), BF)
        scores = []
        for pair in range(pairs):
            here = slice(pair * 128, pair * 128 + 128)
            query_pair, key_pair = query[rows, here], key[keys, here]
            scores.append(
                dot(merge(low_query, query_pair, query_aug), merge(low_key, key_pair, key_aug), NT)
            )
            scores.append(
                dot(merge(low_query, query_aug, query_pair), merge(low_key, key_aug, key_pair), NT)
            )
        tops = [jnp.max(score, -1, keepdims=True) for score in scores]
        raised = [jnp.exp2(score - top).astype(BF) for score, top in zip(scores, tops)]
        for pair in range(pairs):
            here = slice(pair * 128, pair * 128 + 128)
            value_pair = value[keys, here]
            even = dot(raised[2 * pair], merge(low_key, value_pair, ones), NN)
            odd = dot(raised[2 * pair + 1], merge(low_key, ones, value_pair), NN)
            total = merge(low_query, odd, even)
            context[rows, here] = (
                merge(low_query, even, odd) / pltpu.roll(total, 64, 1)
            ).astype(BF)
            level = -(merge(low_query, tops[2 * pair + 1], tops[2 * pair]) + jnp.log2(total))
            first = level.astype(BF)
            rest = level - first.astype(F32)
            second, third = split(rest)
            marks[rows, here] = merge(
                mark_lane == 4, first, merge(mark_lane == 5, second, merge(mark_lane == 6, third, query_aug))
            )

    def one(number, carry):
        base = (row * (count // size) + number) * 2
        for_windows(windows[base], windows[base + 1], count, functools.partial(block, number))
        return carry

    lax.fori_loop(0, count // size, one, 0)


def for_windows(start, steps, count, run):
    extents = list(range(2 * WINDOW, count + 1, WINDOW))
    for position, extent in enumerate(extents):
        take = steps * WINDOW <= extent
        if position:
            take = take & (steps * WINDOW > extents[position - 1])

        @pl.when(take)
        def _():
            run(jnp.minimum(start * WINDOW, count - extent), extent)


def gelu_parts(values):
    square = values * values
    half = 0.5 + 0.5 * jnp.tanh(values * (GELU + (GELU * CUBIC) * square))
    active = values * half
    slope = half + active * (1.0 - half) * (2.0 * GELU + (6.0 * GELU * CUBIC) * square)
    return active, slope


def hidden_kernel(
    side, edge, wide, up, head_bias, context, weight_out, gains, biases, weight_in, hidden_bias,
    weight_last, output_gain, down, down_bias,
    mid, n2, active_out, slope_out, result, latent_out,
):
    encoder = side[0] == 0
    width = edge.shape[1]
    values = entry_values(encoder, edge[...], wide[...], up[...], head_bias[...])
    midway = values + (dot(context[...], weight_out[...], NN) + biases[2])
    mid[...] = midway
    hat, unused = norm_parts(midway)
    normed = (hat * gains[1:2, :] + biases[4]).astype(BF)
    n2[...] = normed
    total = midway + biases[5]
    chunk = 256
    for start in range(0, weight_in.shape[1], chunk):
        here = slice(start, start + chunk)
        active, slope = gelu_parts(dot(normed, weight_in[:, here], NN) + hidden_bias[0:1, here])
        active = active.astype(BF)
        active_out[:, here] = active
        slope_out[:, here] = slope.astype(BF)
        total = total + dot(active, weight_last[here, :], NN)
    result[...] = total

    @pl.when(encoder)
    def _():
        last_hat, unused = norm_parts(total)
        code = last_hat * output_gain[0:1, :] + head_bias[0:1, :]
        latent_out[...] = code_product(code, down[...]) + down_bias[0:1, :]


def code_product(values, weight):
    return dot3(split(values), split(weight), NT)


def tail_back_kernel(
    side, result, cotangent, unit, latent_in, latent, output_gain, head_bias, down,
    weight_last, slope, weight_in, mid, gains, biases, weight_out, *refs, adding
):
    before, refs = refs[: 2 * adding], refs[2 * adding :]
    out_low, preact_low, mid_grad, branch_low, context_grad, sums, head_weight, upstream = refs
    encoder = side[0] == 0
    width = result.shape[1]
    narrow = unit.shape[1]

    @pl.when(pl.program_id(0) == 0)
    def _():
        sums[...] = before[0][...] if adding else jnp.zeros_like(sums)
        head_weight[...] = before[1][...] if adding else jnp.zeros_like(head_weight)

    @pl.when(encoder)
    def _():
        hat, inverse = norm_parts(result[...])
        normed = hat * output_gain[0:1, :] + head_bias[0:1, :]
        code, scale = unit_of(latent[...])
        code_grad = latent_in[...].T + 0.5 * (code - unit[...])
        latent_grad = scale * (code_grad - code * jnp.sum(code * code_grad, -1, keepdims=True))
        pieces = split(latent_grad)
        normed_grad = dot3(pieces, split(down[...]), NN)
        head_weight[...] += dot(pieces[0], normed.astype(BF), TN) + dot(pieces[1], normed.astype(BF), TN)
        sums[8:9, :] += column_sum(normed_grad * hat)
        sums[9:10, :] += column_sum(normed_grad)
        sums[10:11, :narrow] += column_sum(latent_grad)
        upstream[...] = norm_back(normed_grad, output_gain[0:1, :], hat, inverse)

    @pl.when(jnp.logical_not(encoder))
    def _():
        upstream[...] = cotangent[...].astype(F32)

    above = upstream[...]
    low = above.astype(BF)
    out_low[...] = low
    sums[4:5, :] += column_sum(low.astype(F32))
    normed_grad = None
    chunk = 1024
    for start in range(0, weight_in.shape[1], chunk):
        here = slice(start, start + chunk)
        active_grad = dot(low, weight_last[here, :], NT)
        inner = (active_grad * slope[:, here].astype(F32)).astype(BF)
        preact_low[:, here] = inner
        part = column_sum(inner.astype(F32))
        for at in range(0, chunk, min(chunk, width)):
            row, lane = (start + at) // width, (start + at) % width
            size = min(chunk, width)
            sums[row : row + 1, lane : lane + size] += part[:, at : at + size]
        term = dot(inner, weight_in[:, here], NT)
        normed_grad = term if normed_grad is None else normed_grad + term
    hat, inverse = norm_parts(mid[...])
    sums[6:7, :] += column_sum(normed_grad * hat)
    sums[7:8, :] += column_sum(normed_grad)
    middle = above + norm_back(normed_grad, gains[1:2, :], hat, inverse)
    mid_grad[...] = middle
    branch = middle.astype(BF)
    branch_low[...] = branch
    sums[5:6, :] += column_sum(branch.astype(F32))
    context_grad[...] = dot(branch, weight_out[...], NT).astype(BF)


def mark_grads(context_grad, context, grad_mark):
    count = context_grad.shape[0]
    lane_all = lanes((count, 128)) & 63
    across = (
        lax.broadcasted_iota(jnp.int32, (128, 128), 0) // 64 != lanes((128, 128)) // 64
    ).astype(BF)
    zero = jnp.zeros((count, 128), BF)
    for pair in range(context_grad.shape[1] // 128):
        here = slice(pair * 128, pair * 128 + 128)
        product = split(context_grad[:, here].astype(F32) * context[:, here].astype(F32))
        level = -(dot(product[0], across, NN) + dot(product[1], across, NN))
        first = level.astype(BF)
        second, third = split(level - first.astype(F32))
        grad_mark[:, here] = merge(
            lane_all == 0, first, merge(lane_all == 1, second, merge(lane_all == 2, third, zero))
        )


def attend_back_block(
    number, start, extent, base, pairs,
    query, marks, key, value, context_grad, key_mark, grad_mark, query_grad, key_total, value_total,
):
    size = TOKENS
    low_query = lanes((size, 128)) < 64
    rows = pl.ds(pl.multiple_of(number * size, size), size)
    keys = pl.ds(pl.multiple_of(start, WINDOW), extent)
    low_key = lanes((extent, 128)) < 64
    key_aug = key_mark[keys, :]
    ones = jnp.where((lanes((extent, 128)) & 63) < 3, 1.0, 0.0).astype(BF)
    none = jnp.zeros((extent, 128), BF)
    for pair in range(pairs):
        here = pl.ds(pl.multiple_of(base + pair * 128, 128), 128)
        query_pair, key_pair, value_pair = query[rows, here], key[keys, here], value[keys, here]
        grad_pair, query_aug, grad_aug = context_grad[rows, here], marks[rows, here], grad_mark[rows, here]
        found = []
        for swap in (False, True):

            def both(low, left, right):
                return merge(low, right, left) if swap else merge(low, left, right)

            scores = dot(both(low_key, key_pair, key_aug), both(low_query, query_pair, query_aug), NT)
            rise = dot(both(low_key, value_pair, ones), both(low_query, grad_pair, grad_aug), NT)
            chance = jnp.exp2(scores)
            score_grad = (chance * rise).astype(BF)
            found.append(
                (
                    dot(score_grad, query_pair, NN),
                    dot(chance.astype(BF), grad_pair, NN),
                    dot(score_grad, both(low_key, key_pair, none), TN),
                )
            )
        key_total[keys, here] += merge(low_key, found[0][0], found[1][0])
        value_total[keys, here] += merge(low_key, found[0][1], found[1][1])
        query_grad[rows, here] = ((found[0][2] + found[1][2]) * HEAD ** (-0.5)).astype(BF)


def attend_back_kernel(
    windows, query, marks, key, value, context_grad, context, key_mark,
    query_grad, key_grad, value_grad, grad_mark, key_total, value_total, *, row
):
    count = query.shape[0]
    steps = count // TOKENS
    pairs = query.shape[1] // 128
    mark_grads(context_grad, context, grad_mark)
    key_total[...] = jnp.zeros_like(key_total)
    value_total[...] = jnp.zeros_like(value_total)

    def one(turn, carry):
        number = turn
        at = (row * steps + number) * 2

        def run(start, extent):
            attend_back_block(
                number, start, extent, 0, pairs,
                query, marks, key, value, context_grad, key_mark, grad_mark, query_grad, key_total, value_total,
            )

        for_windows(windows[at], windows[at + 1], count, run)
        return carry

    lax.fori_loop(0, steps, one, 0)
    key_grad[...] = (key_total[...] * (1.0 / LOG2E)).astype(BF)
    value_grad[...] = value_total[...].astype(BF)


def entry_back_kernel(
    side, edge, wide, up, head_bias, unit, query_grad, key_grad, value_grad, weight, gains, biases,
    mid_grad, *refs, adding
):
    before, refs = refs[: 2 * adding], refs[2 * adding :]
    entry, latent_out, sums, head_weight = refs
    encoder = side[0] == 0
    width = edge.shape[1]
    narrow = unit.shape[1]

    @pl.when(pl.program_id(0) == 0)
    def _():
        sums[...] = before[0][...] if adding else jnp.zeros_like(sums)
        head_weight[...] = before[1][...] if adding else jnp.zeros_like(head_weight)

    values = entry_values(encoder, edge[...], wide[...], up[...], head_bias[...])
    normed_grad = (
        dot(query_grad[...], weight[:, :width], NT)
        + dot(key_grad[...], weight[:, width : 2 * width], NT)
        + dot(value_grad[...], weight[:, 2 * width :], NT)
    )
    hat, inverse = norm_parts(values)
    sums[0:1, :] += column_sum(query_grad[...].astype(F32))
    sums[1:2, :] += column_sum(value_grad[...].astype(F32))
    sums[2:3, :] += column_sum(normed_grad * hat)
    sums[3:4, :] += column_sum(normed_grad)
    total = mid_grad[...] + norm_back(normed_grad, gains[0:1, :], hat, inverse)
    entry[...] = total

    @pl.when(jnp.logical_not(encoder))
    def _():
        sums[4:5, :] += column_sum(total)
        latent_out[...] = code_product(total, up[...]).T
        head_weight[...] += dot3(split(unit[...]), split(total), TN)


def hidden_weight_kernel(active, out_low, n2, preact_low, *refs):
    out = refs[-1]
    before = refs[0] if len(refs) > 1 else None
    step = pl.program_id(0)
    first = pl.num_programs(0) // 2
    width = n2.shape[1]

    def put(value, rows):
        out[rows, :] = value if before is None else value + before[rows, :]

    @pl.when(step < first)
    def _():
        put(dot(active[...], out_low[...], TN), slice(0, 2 * width))

    @pl.when(step >= first)
    def _():
        value = dot(n2[...], preact_low[...], TN)
        put(value[:, :width], slice(0, width))
        put(value[:, width:], slice(width, 2 * width))


def weight_call(kernel, operands, in_specs, steps, before):
    width = operands[1].shape[1]
    out_spec = pl.BlockSpec((2 * width, width), lambda step: (step, 0))
    aliases = {}
    if before is not None:
        aliases = {len(operands): 0}
        operands, in_specs = operands + [before], in_specs + [out_spec]
    return pl.pallas_call(
        kernel,
        grid=(steps,),
        in_specs=in_specs,
        out_specs=out_spec,
        out_shape=jax.ShapeDtypeStruct((2 * steps * width, width), F32),
        input_output_aliases=aliases,
        compiler_params=PARAMS,
    )(*operands)


def hidden_weights(kept, late, before=None):
    operands = [kept.active, late.out_low, kept.n2, late.preact_low]
    count, width = kept.n2.shape
    first = kept.active.shape[1] // (2 * width)
    full = pl.BlockSpec((count, width), lambda step: (0, 0))
    in_specs = [
        pl.BlockSpec((count, 2 * width), lambda step: (0, jnp.minimum(step, first - 1))),
        full,
        full,
        pl.BlockSpec((count, 2 * width), lambda step: (0, jnp.maximum(step - first, 0))),
    ]
    return weight_call(hidden_weight_kernel, operands, in_specs, 2 * first, before)


MESH = pl.DeviceIdType.MESH
LEAST_DEVICES = 4


def ring_chip(position, chips):
    odd = position // (chips // 2)
    return (1 - odd) * (2 * position) + odd * (2 * (chips - 1 - position) + 1)


class Ring:
    @staticmethod
    def scratch(arrays, ways, crossing):
        chips = lax.axis_size(DP) // 2
        sizes = [array.shape[0] // (2 * count * chips) for array, count in zip(arrays, ways)]
        shapes = [(count, chips, size, array.shape[1]) for array, count, size in zip(arrays, ways, sizes)]
        buffers = [pltpu.VMEM(shape, F32) for shape in shapes] * 3
        sems = [pltpu.SemaphoreType.DMA(shape[:2]) for shape in shapes] * 10
        far = []
        if crossing is not None:
            count, unused, size, width = shapes[crossing]
            far = [pltpu.VMEM((count, size, width), F32)] + [pltpu.SemaphoreType.DMA((count,))] * 2
        return buffers + sems + far

    def __init__(self, sources, results, ways, crossing, scratch):
        number = len(sources)
        take = lambda at: scratch[at * number : (at + 1) * number]
        self.chips = lax.axis_size(DP) // 2
        self.sources, self.results, self.ways, self.crossing = sources, results, ways, crossing
        self.own, self.pair, self.run = take(0), take(1), take(2)
        (
            self.load_sems, self.pair_send, self.pair_recv, self.run_send, self.run_recv,
            self.keep_sems, self.spread_send, self.spread_recv, self.side_send, self.side_recv,
        ) = (take(at) for at in range(3, 13))
        self.far = scratch[13 * number :]
        self.sizes = [run.shape[2] for run in self.run]
        self.lanes = [(which, way) for way in range(max(ways)) for which in range(number) if way < ways[which]]
        place = lax.axis_index(DP)
        chip, self.core = place // 2, place % 2
        column, odd = chip // 2, chip % 2
        chips = self.chips
        self.position = (1 - odd) * column + odd * (chips - 1 - column)
        self.other = {DP: chip * 2 + (1 - self.core)}
        self.across = {SECTION: 1 - lax.axis_index(SECTION)}
        self.targets = (
            {DP: ring_chip((self.position + 1) % chips, chips) * 2 + self.core},
            {DP: ring_chip((self.position + chips - 1) % chips, chips) * 2 + self.core},
        )

    def greet(self):
        self.barrier = pltpu.get_barrier_semaphore()
        devices = (self.other, self.across) + self.targets
        for device in devices:
            pl.semaphore_signal(self.barrier, inc=1, device_id=device, device_id_type=MESH)
        self.greeted = len(devices)

    def piece(self, step, way):
        return (self.position + (2 * self.chips - step if way % 2 == 0 else step)) % self.chips

    def rows(self, which, half, way, number):
        size = self.sizes[which]
        return pl.ds(pl.multiple_of(((half * self.ways[which] + way) * self.chips + number) * size, 8), size)

    def final(self, which, half, way, step):
        return self.results[which].at[self.rows(which, half, way, self.piece(step + self.chips - 1, way))]

    def load(self, which, way, step):
        return pltpu.make_async_copy(
            self.sources[which].at[self.rows(which, self.core, way, self.piece(step, way))],
            self.own[which].at[way, step],
            self.load_sems[which].at[way, step],
        )

    def remote(self, source, target, send, recv, device):
        return pltpu.make_async_remote_copy(
            src_ref=source, dst_ref=target, send_sem=send, recv_sem=recv, device_id=device, device_id_type=MESH
        )

    def swap(self, which, way, step):
        return self.remote(
            self.sources[which].at[self.rows(which, 1 - self.core, way, self.piece(step, way))],
            self.pair[which].at[way, step],
            self.pair_send[which].at[way, step],
            self.pair_recv[which].at[way, step],
            self.other,
        )

    def pass_on(self, which, way, step):
        return self.remote(
            self.run[which].at[way, step],
            self.run[which].at[way, step + 1],
            self.run_send[which].at[way, step],
            self.run_recv[which].at[way, step + 1],
            self.targets[way % 2],
        )

    def cross(self, way):
        return self.remote(
            self.run[self.crossing].at[way, self.chips - 1],
            self.far[0].at[way],
            self.far[1].at[way],
            self.far[2].at[way],
            self.across,
        )

    def keep(self, which, way):
        return pltpu.make_async_copy(
            self.run[which].at[way, self.chips - 1], self.final(which, self.core, way, 0), self.keep_sems[which].at[way, 0]
        )

    def spread(self, which, way, step, first=False):
        here = self.final(which, self.core, way, step)
        return self.remote(
            self.run[which].at[way, self.chips - 1] if first else here,
            here,
            self.spread_send[which].at[way, step],
            self.spread_recv[which].at[way, step],
            self.targets[way % 2],
        )

    def incoming(self, which, way, step):
        here = self.final(which, self.core, way, step)
        return self.remote(
            here, here, self.spread_send[which].at[way, step], self.spread_recv[which].at[way, step - 1],
            self.targets[way % 2],
        )

    def aside(self, which, way, step, first=False):
        here = self.final(which, self.core, way, step)
        return self.remote(
            self.run[which].at[way, self.chips - 1] if first else here,
            here,
            self.side_send[which].at[way, step],
            self.side_recv[which].at[way, step],
            self.other,
        )

    def beside(self, which, way, step):
        here = self.final(which, 1 - self.core, way, step)
        return self.remote(
            here, here, self.side_send[which].at[way, step], self.side_recv[which].at[way, step], self.other
        )

    def begin(self, waiting=True):
        def load(step, carry):
            for which, way in self.lanes:
                self.load(which, way, step).start()
            return carry

        def swap(step, carry):
            for which, way in self.lanes:
                self.swap(which, way, step).start()
            return carry

        lax.fori_loop(0, self.chips, load, 0)
        if waiting:
            pl.semaphore_wait(self.barrier, self.greeted)
        lax.fori_loop(0, self.chips, swap, 0)
        for which, way in self.lanes:
            self.load(which, way, 0).wait()
            self.swap(which, way, 0).wait_recv()
            self.run[which][way, 0] = self.own[which][way, 0] + self.pair[which][way, 0]
            self.pass_on(which, way, 0).start()

    def gather(self, step, lanes=None):
        for which, way in self.lanes if lanes is None else lanes:
            run, own, pair = self.run[which], self.own[which], self.pair[which]
            self.load(which, way, step).wait()
            self.swap(which, way, step).wait_recv()
            self.pass_on(which, way, step - 1).wait_recv()
            run[way, step] = run[way, step] + own[way, step] + pair[way, step]

            @pl.when(step < self.chips - 1)
            def _():
                self.pass_on(which, way, step).start()

    def turn(self):
        for which, way in self.lanes:
            if which == self.crossing:
                self.cross(way).start()
        for which, way in self.lanes:
            if which != self.crossing:
                self.hand_out(which, way)
        for which, way in self.lanes:
            if which == self.crossing:
                run = self.run[which]
                self.cross(way).wait()
                run[way, self.chips - 1] = run[way, self.chips - 1] + self.far[0][way]
                self.hand_out(which, way)

    def hand_out(self, which, way):
        self.spread(which, way, 0, True).start()
        self.aside(which, way, 0, True).start()
        self.keep(which, way).start()

    def pass_out(self, step, lanes=None):
        for which, way in self.lanes if lanes is None else lanes:
            self.incoming(which, way, step).wait_recv()

            @pl.when(step < self.chips - 1)
            def _():
                self.spread(which, way, step).start()

            self.aside(which, way, step).start()

    def finish(self):
        def one(step, carry):
            for which, way in self.lanes:
                self.swap(which, way, step).wait_send()
                self.beside(which, way, step).wait_recv()
                self.aside(which, way, step).wait_send()

                @pl.when(step < self.chips - 1)
                def _():
                    self.pass_on(which, way, step).wait_send()
                    self.spread(which, way, step).wait_send()

            return carry

        lax.fori_loop(0, self.chips, one, 0)
        for which, way in self.lanes:
            self.keep(which, way).wait()


def loop(start, stop, run):
    def one(step, carry):
        run(step)
        return carry

    lax.fori_loop(start, stop, one, 0)


HIDDEN_WAYS = (4,)
OTHER_WAYS = (4, 2)


def finish_kernel(*refs, held):
    (
        hidden, query, marks, key, value, context_grad, context, key_mark, edges, mid_grad, weight, branch_low, n1,
    ), refs = refs[:13], refs[13:]
    mine, others, refs = refs[:6], refs[6:18], refs[18:]
    (
        gains, book, down, up, late, early,
        hidden_out, attention_out, misc_out, entry,
        query_in, marks_in, key_in, value_in, grad_in, context_in, key_mark_in, edge_in, mid_in, weight_in, branch_in,
        n1_in, part, misc, grad_mark, query_grad, key_total, value_total, key_grad, value_grad, in_sems, out_sems,
    ), scratch = refs[:32], refs[32:]
    encoder = lax.axis_index(SECTION) == 0
    decoder = jnp.logical_not(encoder)
    ring = Ring((hidden,), (hidden_out,), HIDDEN_WAYS, None, scratch[:held]) if scratch else None
    last = Ring((part, misc), (attention_out, misc_out), OTHER_WAYS, 1, scratch[held:]) if scratch else None
    count, width = query.shape
    narrow = down.shape[0]
    steps = count // TOKENS
    pairs = width // 128
    row = edges.shape[0] - 1
    at = book.shape[0] + 2 * narrow
    inputs = (
        (query, query_in), (marks, marks_in), (key, key_in), (value, value_in), (context_grad, grad_in),
        (context, context_in), (key_mark.at[row], key_mark_in), (edges.at[row], edge_in), (mid_grad, mid_in),
        (weight, weight_in), (branch_low, branch_in), (n1, n1_in),
    )
    first_held = (query_in, marks_in, key_in, value_in, grad_in, grad_mark)
    second_held = (context_in, branch_in, n1_in, query_grad, key_grad, value_grad)

    def copies(pairs):
        return [pltpu.make_async_copy(*pair, in_sems.at[number]) for number, pair in enumerate(pairs)]

    loads = copies(inputs)
    other_loads = copies(zip(others, first_held + second_held))
    first_loads = copies(zip(mine, first_held))

    def start(copies):
        for copy in copies:
            copy.start()

    def wait(copies):
        for copy in copies:
            copy.wait()

    if ring:
        ring.greet()
    pl.when(encoder)(functools.partial(start, loads))
    pl.when(decoder)(functools.partial(start, other_loads))
    if ring:
        ring.begin()
    misc[...] = jnp.zeros_like(misc)

    def attention_piece(turn):
        attend_back_block(
            turn // pairs, 0, count, (turn % pairs) * 128, 1,
            query_in, marks_in, key_in, value_in, grad_in, key_mark_in, grad_mark, query_grad, key_total, value_total,
        )

    @pl.when(encoder)
    def _():
        misc[: book.shape[0], :] = book[...]
        misc[book.shape[0] : book.shape[0] + narrow, :] = down[...]
        misc[at : at + 16, :] = late[...]
        misc[at + 16 : at + 32, :] = early[...]
        wait(loads)
        mark_grads(grad_in, context_in, grad_mark)
        key_total[...] = jnp.zeros_like(key_total)
        value_total[...] = jnp.zeros_like(value_total)
        loop(0, 2, attention_piece)

    @pl.when(decoder)
    def _():
        misc[book.shape[0] + narrow : at, :] = up[...]
        misc[at + 32 : at + 48, :] = late[...]
        misc[at + 48 : at + 64, :] = early[...]
        wait(other_loads)

    def entry_piece(number):
        rows = pl.ds(pl.multiple_of(number * TOKENS, TOKENS), TOKENS)
        normed_grad = (
            dot(query_grad[rows, :], weight_in[:, :width], NT)
            + dot(key_grad[rows, :], weight_in[:, width : 2 * width], NT)
            + dot(value_grad[rows, :], weight_in[:, 2 * width :], NT)
        )
        hat, inverse = norm_parts(edge_in[rows, :].astype(F32))
        misc[at + 16 : at + 17, :] += column_sum(query_grad[rows, :].astype(F32))
        misc[at + 17 : at + 18, :] += column_sum(value_grad[rows, :].astype(F32))
        misc[at + 18 : at + 19, :] += column_sum(normed_grad * hat)
        misc[at + 19 : at + 20, :] += column_sum(normed_grad)
        mid_in[rows, :] = mid_in[rows, :] + norm_back(normed_grad, gains[0:1, :], hat, inverse)

    def weight_piece(number):
        def put(first, second):
            rows = pl.ds(pl.multiple_of(number * width, width), width)
            part[rows, :] = dot(first[0][...], first[1][...], TN) + dot(second[0][...], second[1][...], TN)

        for choice, places in enumerate(((0, 1), (2, 3), (2, 4), (2, 5))):
            both = [[held[place] for place in places] for held in (first_held, second_held)]
            pl.when(number == choice)(functools.partial(put, *both))

    halves = (ring.lanes[:2], ring.lanes[2:]) if ring else (None, None)
    chips = ring.chips if ring else 8
    pieces = steps * pairs

    def summing(step):
        for half in range(2):
            if ring:
                ring.gather(step, halves[half])

            @pl.when(encoder)
            def _():
                attention_piece(2 * step + half)

    inside = min(chips - 1, pieces // 2 - 1)
    loop(1, inside + 1, summing)
    if ring:
        loop(inside + 1, chips, ring.gather)
        ring.turn()

    @pl.when(encoder)
    def _():
        loop(2 * inside + 2, pieces, attention_piece)
        start(first_loads)
        key_grad[...] = (key_total[...] * (1.0 / LOG2E)).astype(BF)
        value_grad[...] = value_total[...].astype(BF)

    def spreading(step):
        if ring:
            ring.pass_out(step, halves[0])

        @pl.when(encoder)
        def _():
            entry_piece(step - 1)

        if ring:
            ring.pass_out(step, halves[1])
        pl.when(encoder & (step == 1))(functools.partial(wait, first_loads))
        weight_piece(step - 1)

    loop(1, steps + 1, spreading)
    store = pltpu.make_async_copy(mid_in, entry, out_sems.at[0])

    @pl.when(encoder)
    def _():
        store.start()

    if ring:
        last.begin(False)

        def both(step):
            ring.pass_out(step)
            last.gather(step - steps)

        loop(steps + 1, chips, both)
        loop(chips - steps, chips, last.gather)
        last.turn()
        loop(1, chips, last.pass_out)
        ring.finish()
        last.finish()
    else:
        stores = [
            pltpu.make_async_copy(part, attention_out, out_sems.at[1]),
            pltpu.make_async_copy(misc, misc_out, out_sems.at[2]),
        ]
        start(stores)
        wait(stores)

    @pl.when(encoder)
    def _():
        store.wait()


def finish_row(work, first_kept, kept, late, mine, book, others, hidden):
    count, width = kept.n1.shape
    alone = lax.axis_size(DP) < LEAST_DEVICES
    its_late, its_early = mine
    operands = [
        hidden, kept.query, kept.marks, kept.key, kept.value, late.context_grad,
        kept.context, work.key_mark, work.edges, late.mid_grad, work.attention_in, late.branch_low, kept.n1,
    ]
    for a_kept, a_late, a_early in ((first_kept, its_late, its_early),) + others:
        operands += [a_kept.context, a_late.branch_low, a_kept.n1, *a_early[:3]]
    operands += [work.gains, book, late.head, its_early.head, late.sums, its_early.sums]
    hbm, vmem = pl.BlockSpec(memory_space=pl.ANY), pl.BlockSpec(memory_space=pltpu.VMEM)
    rows = book.shape[0] + 2 * work.narrow + 64
    unit = 16 * lax.axis_size(DP)
    attention = jax.ShapeDtypeStruct((4 * width, width), F32)
    misc = jax.ShapeDtypeStruct((rows + (-rows % unit), width), F32)
    low = pltpu.VMEM((count, width), BF)
    wide = pltpu.VMEM((count, width), F32)
    scratch = [low] * 6 + [pltpu.VMEM((count, 128), BF), low, wide, pltpu.VMEM(work.attention_in.shape, BF), low, low]
    scratch += [pltpu.VMEM(attention.shape, F32), pltpu.VMEM(misc.shape, F32), low, low, wide, wide, low, low]
    scratch += [pltpu.SemaphoreType.DMA((12,)), pltpu.SemaphoreType.DMA((3,))]
    settings = {}
    held = 0
    if not alone:
        rings = Ring.scratch((hidden,), HIDDEN_WAYS, None)
        held = len(rings)
        scratch += rings + Ring.scratch((attention, misc), OTHER_WAYS, 1)
        settings = dict(collective_id=0, has_side_effects=True)
    outs = pl.pallas_call(
        functools.partial(finish_kernel, held=held),
        in_specs=[hbm] * 31 + [vmem] * 6,
        out_specs=[hbm] * 4,
        out_shape=(
            jax.ShapeDtypeStruct(hidden.shape, F32), attention, misc, jax.ShapeDtypeStruct((count, width), F32),
        ),
        scratch_shapes=scratch,
        compiler_params=pltpu.CompilerParams(vmem_limit_bytes=60 << 20, **settings),
    )(*operands)
    if alone:
        return hidden, outs[1], lax.psum(outs[2], SECTION), outs[3]
    return outs


def unpack_kernel(
    side, hidden, attention, misc, first_entry, second_entry, first_result, second_result,
    hidden_out, hidden_in, attention_out, attention_in, edge, book, gains, biases, bias, last_gain, head_bias, down, down_last,
    up, held, head, rows, ins, outs, row_ins, row_outs,
):
    width = hidden.shape[1]
    narrow = book.shape[0]
    steps = hidden_out.shape[0] // width
    targets = [hidden_out.at[pl.ds(number * width, width), :] for number in range(steps)]
    targets += [hidden_in.at[:, pl.ds(number * width, width)] for number in range(steps)]
    targets += [attention_out]
    targets += [attention_in.at[:, pl.ds(number * width, width)] for number in range(3)]
    sources = [hidden.at[pl.ds(number * width, width), :] for number in range(2 * steps)]
    sources += [attention.at[pl.ds(number * width, width), :] for number in range(4)]
    tiles = range(len(targets))
    for mine, pair in ((0, (first_entry, second_entry)), (1, (first_result, second_result))):

        @pl.when(side[0] == mine)
        def _():
            for row in range(2):
                pltpu.make_async_copy(pair[row], rows.at[row], row_ins.at[row]).start()

    loads = [pltpu.make_async_copy(sources[number], held.at[number], ins.at[number]) for number in tiles]
    loads.append(pltpu.make_async_copy(misc.at[pl.ds(0, head.shape[0]), :], head, ins.at[len(targets)]))
    for load in loads:
        load.start()
    stores = []
    for row in range(2):
        pltpu.make_async_copy(first_entry, rows.at[row], row_ins.at[row]).wait()
        stores.append(pltpu.make_async_copy(rows.at[row], edge.at[row], row_outs.at[row]))
        stores[-1].start()
    for number in tiles:
        loads[number].wait()
        stores.append(pltpu.make_async_copy(held.at[number], targets[number], outs.at[number]))
        stores[-1].start()
    loads[-1].wait()
    for number in range(book.shape[1] // width):
        book[:, number * width : (number + 1) * width] = head[number * narrow : (number + 1) * narrow, :]
    at = book.shape[0] * book.shape[1] // width
    down[...] = head[at : at + narrow, :]
    up[...] = head[at + narrow : at + 2 * narrow, :]
    at += 2 * narrow
    last_gain[...] = head[at + 8 : at + 9, :]
    head_bias[0:1, :] = head[at + 9 : at + 10, :]
    head_bias[1:2, :] = head[at + 52 : at + 53, :]
    down_last[...] = head[at + 10 : at + 11, :narrow]
    mine = jnp.where(side[0] == 0, head[at : at + 32, :], head[at + 32 : at + 64, :])
    for number in range(steps):
        bias[:, number * width : (number + 1) * width] = mine[number : number + 1, :]
    for number, place in enumerate((18, 6)):
        gains[number : number + 1, :] = mine[place : place + 1, :]
    for number, place in enumerate((16, 17, 5, 19, 7, 4)):
        biases[number] = mine[place : place + 1, :]
    for store in stores:
        store.wait()


def unpack(side, hidden, attention, misc, ends, table_turned):
    width = hidden.shape[1]
    features = hidden.shape[0] // 2
    tiles = (hidden.shape[0] + attention.shape[0]) // width
    narrow = table_turned.shape[0]
    rows = table_turned.size // width + 2 * narrow + 64
    shapes = (
        (features, width), (width, features), (width, width), (width, 3 * width), (2,) + ends[0].shape,
        table_turned.shape, (2, width), (6, 1, width), (1, features), (1, width), (2, width),
        (narrow, width), (1, narrow), (narrow, width),
    )
    hbm, vmem = pl.BlockSpec(memory_space=pl.ANY), pl.BlockSpec(memory_space=pltpu.VMEM)
    return pl.pallas_call(
        unpack_kernel,
        in_specs=[pl.BlockSpec(memory_space=pltpu.SMEM)] + [hbm] * 7,
        out_specs=[hbm] * 5 + [vmem] * 9,
        out_shape=tuple(jax.ShapeDtypeStruct(shape, F32) for shape in shapes),
        scratch_shapes=[
            pltpu.VMEM((tiles, width, width), F32),
            pltpu.VMEM((rows, width), F32),
            pltpu.VMEM((2,) + ends[0].shape, F32),
            pltpu.SemaphoreType.DMA((tiles + 1,)),
            pltpu.SemaphoreType.DMA((tiles,)),
            pltpu.SemaphoreType.DMA((2,)),
            pltpu.SemaphoreType.DMA((2,)),
        ],
        compiler_params=PARAMS,
    )(side, hidden, attention, misc, *ends)


def nothing_kernel(*refs):
    pass


def unwritten(shapes):
    leaves, tree = jax.tree.flatten(shapes)
    arrays = pl.pallas_call(
        nothing_kernel,
        out_specs=[pl.BlockSpec(memory_space=pl.ANY)] * len(leaves),
        out_shape=tuple(leaves),
    )()
    return jax.tree.unflatten(tree, arrays)


class Kept(NamedTuple):
    n1: Any
    query: Any
    key: Any
    value: Any
    context: Any
    marks: Any
    mid: Any
    n2: Any
    active: Any
    slope: Any
    result: Any
    latent: Any


class Late(NamedTuple):
    out_low: Any
    preact_low: Any
    mid_grad: Any
    branch_low: Any
    context_grad: Any
    sums: Any
    head: Any


class Early(NamedTuple):
    query_grad: Any
    key_grad: Any
    value_grad: Any
    entry: Any
    latent_out: Any
    sums: Any
    head: Any


class Rows:
    def __init__(self, side, edges, wide, unit, windows, query_mark, key_mark, weights, head):
        self.side, self.edges, self.wide, self.unit = side, edges, wide, unit
        self.windows, self.query_mark, self.key_mark = windows, query_mark, key_mark
        (
            self.attention_in, self.attention_out, self.hidden_in, self.hidden_out,
            self.gains, self.biases, self.hidden_bias,
        ) = weights
        (
            self.output_gain, self.head_bias, self.down, self.down_bias, self.up,
        ) = head
        self.rows, self.count, self.width = edges.shape
        self.hidden = self.hidden_in.shape[1]
        self.narrow = unit.shape[1]
        self.size = TOKENS
        n, d, f = self.count, self.width, self.hidden
        shape = jax.ShapeDtypeStruct
        low, tall, wide = shape((n, d), BF), shape((n, f), BF), shape((n, d), F32)
        sums, head = shape((16, d), F32), shape((self.narrow, d), F32)
        self.kept = Kept(low, low, low, low, low, low, wide, low, tall, tall, wide, shape((n, self.narrow), F32))
        self.late = Late(low, tall, wide, low, low, sums, head)
        self.early = Early(low, low, low, wide, shape((self.narrow, n), F32), sums, head)

    def side_spec(self):
        return pl.BlockSpec(memory_space=pltpu.SMEM)

    def tokens(self, array):
        return pl.BlockSpec((self.size, array.shape[1]), lambda step: (step, 0))

    def turned(self, array):
        return pl.BlockSpec((array.shape[0], self.size), lambda step: (0, step))

    def whole(self, array):
        return pl.BlockSpec(array.shape, lambda step: (0,) * len(array.shape))

    def entry_specs(self, row):
        steps = self.count // self.size
        return [
            pl.BlockSpec((None, self.size, self.width), lambda step: (row, step, 0)),
            pl.BlockSpec((self.size, self.wide.shape[1]), lambda step: (row * steps + step, 0)),
            self.whole(self.up),
            self.whole(self.head_bias),
        ]

    def unit_spec(self, row):
        steps = self.count // self.size
        return pl.BlockSpec((self.size, self.narrow), lambda step: (row * steps + step, 0))

    def call(self, kernel, in_specs, operands, outs, out_specs, scratch=()):
        return pl.pallas_call(
            kernel,
            grid=(self.count // self.size,),
            in_specs=in_specs,
            out_specs=out_specs,
            out_shape=tuple(outs),
            scratch_shapes=list(scratch),
            compiler_params=PARAMS,
        )(*operands)

    def attention_call(self, kernel, row, operands, outs, scratch=()):
        half = self.width // 2

        def spec(array):
            if array.ndim == 3:
                return pl.BlockSpec((None, self.count, array.shape[2]), lambda step, info: (row, 0, 0))
            return pl.BlockSpec((self.count, half), lambda step, info: (0, step))

        return pl.pallas_call(
            functools.partial(kernel, row=row),
            grid_spec=pltpu.PrefetchScalarGridSpec(
                num_scalar_prefetch=1,
                grid=(2,),
                in_specs=[spec(array) for array in operands],
                out_specs=[spec(array) for array in outs],
                scratch_shapes=list(scratch),
            ),
            out_shape=tuple(outs),
            compiler_params=PARAMS,
        )(self.windows, *operands)

    def forward(self, row):
        shapes = self.kept
        entry = (self.edges, self.wide, self.up, self.head_bias)
        outs = shapes[:4]
        self.size = 2 * TOKENS
        n1, query, key, value = self.call(
            project_kernel,
            [self.side_spec()] + self.entry_specs(row)
            + [self.whole(self.gains), self.whole(self.biases), self.whole(self.attention_in)],
            (self.side,) + entry + (self.gains, self.biases, self.attention_in),
            outs,
            [self.tokens(array) for array in outs],
        )
        self.size = TOKENS
        context, marks = self.attention_call(
            attend_kernel, row, (query, key, value, self.query_mark, self.key_mark), shapes[4:6]
        )
        consts = (
            self.attention_out, self.gains, self.biases, self.hidden_in, self.hidden_bias, self.hidden_out,
            self.output_gain, self.down, self.down_bias,
        )
        outs = shapes[6:]
        outs = self.call(
            hidden_kernel,
            [self.side_spec()] + self.entry_specs(row) + [self.tokens(context)]
            + [self.whole(array) for array in consts],
            (self.side,) + entry + (context,) + consts,
            outs,
            [self.tokens(array) for array in outs],
        )
        return Kept(n1, query, key, value, context, marks, *outs)

    def backward(self, row, kept, latent_in, former=(None, None)):
        late = self.backward_late(row, kept, latent_in, former[0])
        return late, self.backward_early(row, kept, late, former[1])

    def backward_late(self, row, kept, latent_in, former=None):
        prior = () if former is None else (former.sums, former.head)
        adding = int(former is not None)
        consts = (self.output_gain, self.head_bias, self.down, self.hidden_out)
        late = (self.gains, self.biases, self.attention_out)
        outs = self.late
        return Late(*self.call(
            functools.partial(tail_back_kernel, adding=adding),
            [self.side_spec(), self.tokens(kept.result), self.entry_specs(row)[0], self.unit_spec(row),
             self.turned(latent_in), self.tokens(kept.latent)]
            + [self.whole(array) for array in consts]
            + [self.tokens(kept.slope), self.whole(self.hidden_in), self.tokens(kept.mid)]
            + [self.whole(array) for array in late + prior],
            (self.side, kept.result, self.edges, self.unit, latent_in, kept.latent) + consts
            + (kept.slope, self.hidden_in, kept.mid) + late + prior,
            outs,
            [self.tokens(array) for array in outs[:5]] + [self.whole(array) for array in outs[5:]],
            scratch=[pltpu.VMEM((self.size, self.width), F32)],
        ))

    def backward_early(self, row, kept, late, former=None):
        adding = int(former is not None)
        half = self.width // 2
        grads = tuple(self.attention_call(
            attend_back_kernel, row,
            (kept.query, kept.marks, kept.key, kept.value, late.context_grad, kept.context, self.key_mark),
            self.early[:3],
            scratch=[
                pltpu.VMEM((self.count, half), BF),
                pltpu.VMEM((self.count, half), F32),
                pltpu.VMEM((self.count, half), F32),
            ],
        ))
        prior = () if former is None else (former.sums, former.head)
        outs = self.early[3:]
        outs = self.call(
            functools.partial(entry_back_kernel, adding=adding),
            [self.side_spec()] + self.entry_specs(row) + [self.unit_spec(row)]
            + [self.tokens(array) for array in grads]
            + [self.whole(self.attention_in), self.whole(self.gains), self.whole(self.biases),
               self.tokens(late.mid_grad)] + [self.whole(array) for array in prior],
            (self.side, self.edges, self.wide, self.up, self.head_bias, self.unit) + grads
            + (self.attention_in, self.gains, self.biases, late.mid_grad) + prior,
            outs,
            [self.tokens(outs[0]), self.turned(outs[1])] + [self.whole(array) for array in outs[2:]],
        )
        return Early(*grads, *outs)


def windows_of(segments):
    rows, count = segments.shape
    steps = count // WINDOW
    blocks = segments.reshape(rows, steps, WINDOW)
    least, most = blocks[:, :, 0], blocks[:, :, -1]
    meets = (most[:, :, None] >= least[:, None, :]) & (least[:, :, None] <= most[:, None, :])
    place = jnp.arange(steps)
    start = jnp.min(jnp.where(meets, place, steps), -1)
    stop = jnp.max(jnp.where(meets, place, -1), -1) + 1
    return jnp.stack([start, stop - start], -1).reshape(-1).astype(jnp.int32)


def on_device(
    boundary, segments, code_index, attention_in, attention_out, hidden_in, hidden_out, block_gains,
    block_biases, hidden_bias, output_gain, head_bias, down_weight, down_bias, up_weight, codebook,
):
    section = lax.axis_index(SECTION)
    encoder = section == 0
    side = section.astype(jnp.int32)[None]
    edges = boundary[0]
    rows, count, width = edges.shape
    hidden = hidden_in.shape[2]
    table_turned = codebook.T
    code_index = code_index.reshape(-1)
    unit, wide, query_mark, key_mark = gather_codes(code_index, table_turned, segments)
    work = Rows(
        side, edges, wide, unit, windows_of(segments), query_mark, key_mark,
        (
            attention_in[0], attention_out[0], hidden_in[0], hidden_out[0], block_gains[0], block_biases.transpose(1, 0, 2),
            hidden_bias,
        ),
        (output_gain[None], head_bias, down_weight.T, down_bias[None], up_weight),
    )
    book_out = book_shape(table_turned, width)
    hidden_shape = jax.ShapeDtypeStruct((2 * hidden, width), F32)
    quiet = unwritten(work.early.latent_out)
    first_kept = work.forward(0)

    def encoder_first():
        return (work.forward(1), *unwritten((work.late, work.early)))

    def decoder_first():
        return (unwritten(work.kept), *work.backward(0, first_kept, quiet))

    kept_a, late_a, early_a = lax.cond(encoder, encoder_first, decoder_first)
    latent_in = lax.ppermute(early_a.latent_out, SECTION, [(1, 0)])

    def encoder_second():
        late, early = work.backward(0, first_kept, latent_in)
        book = scatter_codes(code_index, unit, (first_kept.latent, kept_a.latent), table_turned, width)
        return unwritten(work.kept), late, early, hidden_weights(first_kept, late), book

    def decoder_second():
        kept = work.forward(1)
        weights, book = unwritten((hidden_shape, book_out))
        return (kept, *work.backward(1, kept, quiet, (late_a, early_a)), weights, book)

    kept_b, late_b, early_b, weights_b, book = lax.cond(encoder, encoder_second, decoder_second)
    latent_in_second = lax.ppermute(early_b.latent_out, SECTION, [(1, 0)])

    def decoder_fourth():
        total = hidden_weights(kept_b, late_b, hidden_weights(first_kept, late_a))
        return total, (*unwritten(work.late[2:5]), late_b.sums, late_b.head)

    def encoder_fourth():
        late = work.backward_late(1, kept_a, latent_in_second, late_b)
        return hidden_weights(kept_a, late, weights_b), late[2:]

    hidden_total, late = lax.cond(encoder, encoder_fourth, decoder_fourth)
    late = Late(None, None, *late)
    hidden_total, attention_total, misc, second_entry = finish_row(
        work, first_kept, kept_a, late, (late_b, early_b), book,
        ((first_kept, late_a, early_a), (kept_b, late_b, early_b)), hidden_total,
    )
    (
        hidden_out_grad, hidden_in_grad, attention_out_grad, attention_in_grad, edge, book, gains, biases, bias,
        last_gain, head, down_grad, down_last, up_grad,
    ) = unpack(
        side, hidden_total, attention_total, misc,
        (early_b.entry, second_entry, first_kept.result, kept_b.result), table_turned,
    )
    return (
        edge[None],
        attention_in_grad[None],
        attention_out_grad[None],
        hidden_in_grad[None],
        hidden_out_grad[None],
        gains[None],
        biases.transpose(1, 0, 2),
        bias,
        last_gain[0],
        head,
        down_grad.T,
        down_last[0],
        up_grad,
        book.T,
    )


def solution(mesh):
    wide, split_last, flat = P(SECTION, DP, None, None), P(SECTION, None, None), P(SECTION, None)
    blocks = (split_last,) * 6 + (flat,)
    return jax.shard_map(
        on_device,
        mesh=mesh,
        in_specs=(wide, P(DP, None), P(DP, None)) + blocks + (P(),) * 6,
        out_specs=(wide,) + blocks + (P(),) * 6,
        check_vma=False,
    )
```

```python
import functools
import math
from typing import Any, NamedTuple

import jax
import jax.numpy as jnp
from jax import lax
from jax.experimental import pallas as pl
from jax.experimental.pallas import tpu as pltpu
from jax.sharding import PartitionSpec as P

HEAD = 64
SECTION, DP = "section", "dp"
BF = jnp.bfloat16
F32 = jnp.float32
LOG2E = math.log2(math.e)
NORM_EPS = 1e-06
MASKED = -1e30
GELU = 0.7978845608028654
CUBIC = 0.044715
NN = (((1,), (0,)), ((), ()))
NT = (((1,), (1,)), ((), ()))
TN = (((0,), (0,)), ((), ()))
TOKENS = 256
WINDOW = 128
PARAMS = pltpu.CompilerParams(vmem_limit_bytes=56 << 20)


def dot(a, b, dims):
    return lax.dot_general(a, b, dims, preferred_element_type=F32)


def lanes(shape):
    return lax.broadcasted_iota(jnp.int32, shape, 1)


def split(values):
    high = values.astype(BF)
    return high, (values - high.astype(F32)).astype(BF)


def dot3(left, right, dims):
    return dot(left[0], right[0], dims) + dot(left[0], right[1], dims) + dot(left[1], right[0], dims)


def unit_of(values):
    scale = lax.rsqrt(jnp.sum(values * values, -1, keepdims=True) + NORM_EPS)
    return values * scale, scale


def norm_parts(values):
    center = values - jnp.mean(values, -1, keepdims=True)
    inverse = lax.rsqrt(jnp.mean(center * center, -1, keepdims=True) + NORM_EPS)
    return center * inverse, inverse


def norm_back(grad, gain, hat, inverse):
    scaled = grad * gain
    return inverse * (
        scaled
        - jnp.mean(scaled, -1, keepdims=True)
        - hat * jnp.mean(scaled * hat, -1, keepdims=True)
    )


def column_sum(values):
    return jnp.sum(values, 0, keepdims=True)


def code_kernel(index, table_turned, segments, unit, wide, query_mark, key_mark, table, raw):
    count = raw.shape[0]
    block = 512

    def turn(step, carry):
        start = pl.multiple_of(step * block, block)
        table[pl.ds(start, block), :] = table_turned[:, pl.ds(start, block)].T
        return carry

    lax.fori_loop(0, table.shape[0] // block, turn, 0)

    length = segments.shape[1]

    def some(step, carry):
        for inner in range(16):
            token = step * 16 + inner
            raw[pl.ds(token, 1), :] = table[pl.ds(index[token], 1), :]
        return carry

    lax.fori_loop(0, count // 16, some, 0)

    values = raw[...]
    values = values * lax.rsqrt(jnp.sum(values * values, -1, keepdims=True) + NORM_EPS)
    unit[...] = values
    high, low = split(values)
    wide[...] = jnp.concatenate([high, low, high, jnp.zeros_like(high)], 1)
    lane = lanes((length, 128)) & 63
    for row in range(segments.shape[0]):
        owner = jnp.broadcast_to(segments[row : row + 1, :], (128, length)).T
        same = owner == lane
        query_mark[row] = jnp.where((lane < 4) & jnp.logical_not(same), MASKED, 0.0).astype(BF)
        key_mark[row] = jnp.where(((lane < 4) & same) | ((lane > 3) & (lane < 7)), 1.0, 0.0).astype(BF)


def gather_codes(index, table_turned, segments):
    count, width = index.shape[0], table_turned.shape[0]
    vmem = pl.BlockSpec(memory_space=pltpu.VMEM)
    mark = jax.ShapeDtypeStruct(segments.shape + (128,), BF)
    return pl.pallas_call(
        code_kernel,
        in_specs=[pl.BlockSpec(memory_space=pltpu.SMEM), vmem, vmem],
        out_specs=[vmem] * 4,
        out_shape=(
            jax.ShapeDtypeStruct((count, width), F32),
            jax.ShapeDtypeStruct((count, 4 * width), BF),
            mark,
            mark,
        ),
        scratch_shapes=[pltpu.VMEM(table_turned.shape[::-1], F32), pltpu.VMEM((count, width), F32)],
        compiler_params=PARAMS,
    )(index, table_turned, segments)


def scatter_kernel(index, unit, latent_first, latent_second, table_turned, out, total, rows):
    count = rows.shape[0]
    width = unit.shape[1]
    half = count // 2
    total[...] = jnp.zeros_like(total)
    for row, latent in enumerate((latent_first, latent_second)):
        here = slice(row * half, (row + 1) * half)
        code, unused = unit_of(latent[...])
        rows[here, :] = 2.0 * (unit[here, :] - code)

    def some(step, carry):
        for inner in range(8):
            token = step * 8 + inner
            place = pl.ds(index[token], 1)
            total[place, :] = total[place, :] + rows[pl.ds(token, 1), :]
        return carry

    lax.fori_loop(0, count // 8, some, 0)
    block = out.shape[1]

    def back(step, carry):
        start = pl.multiple_of(step * block, block)
        values = table_turned[:, pl.ds(start, block)]
        grad = total[pl.ds(start, block), :].T
        inverse = lax.rsqrt(jnp.sum(values * values, 0, keepdims=True) + NORM_EPS)
        book = values * inverse
        out[pl.ds(pl.multiple_of(step * width, width), width), :] = inverse * (
            grad - book * jnp.sum(book * grad, 0, keepdims=True)
        )
        return carry

    lax.fori_loop(0, total.shape[0] // block, back, 0)


def book_shape(table_turned, width):
    return jax.ShapeDtypeStruct((table_turned.size // width, width), F32)


def scatter_codes(index, unit, latents, table_turned, width):
    return pl.pallas_call(
        scatter_kernel,
        in_specs=[pl.BlockSpec(memory_space=pltpu.SMEM)] + [pl.BlockSpec(memory_space=pltpu.VMEM)] * 4,
        out_specs=pl.BlockSpec(memory_space=pltpu.VMEM),
        out_shape=book_shape(table_turned, width),
        scratch_shapes=[pltpu.VMEM(table_turned.shape[::-1], F32), pltpu.VMEM(unit.shape, F32)],
        compiler_params=PARAMS,
    )(index, unit, *latents, table_turned)


def entry_values(encoder, edge, wide, up, head_bias):
    high, low = split(up)
    parts = jnp.concatenate([high, high, low, jnp.zeros_like(low)], 0)
    return jnp.where(encoder, edge.astype(F32), dot(wide, parts, NN) + head_bias[1:2, :])


def project_kernel(side, edge, wide, up, head_bias, gains, biases, weight, n1, query, key, value):
    width = edge.shape[1]
    encoder = side[0] == 0
    values = entry_values(encoder, edge[...], wide[...], up[...], head_bias[...])
    hat, unused = norm_parts(values)
    normed = (hat * gains[0:1, :] + biases[3]).astype(BF)
    n1[...] = normed
    query[...] = (
        (dot(normed, weight[:, :width], NN) + biases[0]) * (LOG2E * HEAD ** (-0.5))
    ).astype(BF)
    key[...] = dot(normed, weight[:, width : 2 * width], NN).astype(BF)
    value[...] = (dot(normed, weight[:, 2 * width :], NN) + biases[1]).astype(BF)


def merge(low_half, left, right):
    return jnp.where(low_half, left, right)


def attend_kernel(windows, query, key, value, query_mark, key_mark, context, marks, *, row):
    count = query.shape[0]
    size = TOKENS
    pairs = query.shape[1] // 128
    low_query = lanes((size, 128)) < 64
    mark_lane = lanes((size, 128)) & 63

    def block(number, start, extent):
        rows = pl.ds(pl.multiple_of(number * size, size), size)
        keys = pl.ds(pl.multiple_of(start, WINDOW), extent)
        low_key = lanes((extent, 128)) < 64
        query_aug, key_aug = query_mark[rows, :], key_mark[keys, :]
        ones = jnp.ones((extent, 128), BF)
        scores = []
        for pair in range(pairs):
            here = slice(pair * 128, pair * 128 + 128)
            query_pair, key_pair = query[rows, here], key[keys, here]
            scores.append(
                dot(merge(low_query, query_pair, query_aug), merge(low_key, key_pair, key_aug), NT)
            )
            scores.append(
                dot(merge(low_query, query_aug, query_pair), merge(low_key, key_aug, key_pair), NT)
            )
        tops = [jnp.max(score, -1, keepdims=True) for score in scores]
        raised = [jnp.exp2(score - top).astype(BF) for score, top in zip(scores, tops)]
        for pair in range(pairs):
            here = slice(pair * 128, pair * 128 + 128)
            value_pair = value[keys, here]
            even = dot(raised[2 * pair], merge(low_key, value_pair, ones), NN)
            odd = dot(raised[2 * pair + 1], merge(low_key, ones, value_pair), NN)
            total = merge(low_query, odd, even)
            context[rows, here] = (
                merge(low_query, even, odd) / pltpu.roll(total, 64, 1)
            ).astype(BF)
            level = -(merge(low_query, tops[2 * pair + 1], tops[2 * pair]) + jnp.log2(total))
            first = level.astype(BF)
            rest = level - first.astype(F32)
            second, third = split(rest)
            marks[rows, here] = merge(
                mark_lane == 4, first, merge(mark_lane == 5, second, merge(mark_lane == 6, third, query_aug))
            )

    def one(number, carry):
        base = (row * (count // size) + number) * 2
        for_windows(windows[base], windows[base + 1], count, (768,), functools.partial(block, number))
        return carry

    lax.fori_loop(0, count // size, one, 0)


def for_windows(start, steps, count, extents, run):
    extents = [extent for extent in extents if extent < count] + [count]
    for position, extent in enumerate(extents):
        take = steps * WINDOW <= extent
        if position:
            take = take & (steps * WINDOW > extents[position - 1])

        @pl.when(take)
        def _():
            run(jnp.minimum(start * WINDOW, count - extent), extent)


def gelu_parts(values):
    square = values * values
    half = 0.5 + 0.5 * jnp.tanh(values * (GELU + (GELU * CUBIC) * square))
    active = values * half
    slope = half + active * (1.0 - half) * (2.0 * GELU + (6.0 * GELU * CUBIC) * square)
    return active, slope


def hidden_kernel(
    side, edge, wide, up, head_bias, context, weight_out, gains, biases, weight_in, hidden_bias,
    weight_last, output_gain, down, down_bias,
    mid, n2, active_out, slope_out, result, latent_out,
):
    encoder = side[0] == 0
    width = edge.shape[1]
    values = entry_values(encoder, edge[...], wide[...], up[...], head_bias[...])
    midway = values + (dot(context[...], weight_out[...], NN) + biases[2])
    mid[...] = midway
    hat, unused = norm_parts(midway)
    normed = (hat * gains[1:2, :] + biases[4]).astype(BF)
    n2[...] = normed
    total = midway + biases[5]
    chunk = 256
    for start in range(0, weight_in.shape[1], chunk):
        here = slice(start, start + chunk)
        active, slope = gelu_parts(dot(normed, weight_in[:, here], NN) + hidden_bias[0:1, here])
        active = active.astype(BF)
        active_out[:, here] = active
        slope_out[:, here] = slope.astype(BF)
        total = total + dot(active, weight_last[here, :], NN)
    result[...] = total

    @pl.when(encoder)
    def _():
        last_hat, unused = norm_parts(total)
        code = last_hat * output_gain[0:1, :] + head_bias[0:1, :]
        latent_out[...] = code_product(code, down[...]) + down_bias[0:1, :]


def code_product(values, weight):
    return dot3(split(values), split(weight), NT)


def tail_back_kernel(
    side, result, cotangent, unit, latent_in, latent, output_gain, head_bias, down,
    weight_last, slope, weight_in, mid, gains, biases, weight_out, *refs, adding
):
    before, refs = refs[: 2 * adding], refs[2 * adding :]
    out_low, preact_low, mid_grad, branch_low, context_grad, sums, head_weight, upstream = refs
    encoder = side[0] == 0
    width = result.shape[1]
    narrow = unit.shape[1]

    @pl.when(pl.program_id(0) == 0)
    def _():
        sums[...] = before[0][...] if adding else jnp.zeros_like(sums)
        head_weight[...] = before[1][...] if adding else jnp.zeros_like(head_weight)

    @pl.when(encoder)
    def _():
        hat, inverse = norm_parts(result[...])
        normed = hat * output_gain[0:1, :] + head_bias[0:1, :]
        code, scale = unit_of(latent[...])
        code_grad = latent_in[...].T + 0.5 * (code - unit[...])
        latent_grad = scale * (code_grad - code * jnp.sum(code * code_grad, -1, keepdims=True))
        pieces = split(latent_grad)
        normed_grad = dot3(pieces, split(down[...]), NN)
        head_weight[...] += dot(pieces[0], normed.astype(BF), TN) + dot(pieces[1], normed.astype(BF), TN)
        sums[8:9, :] += column_sum(normed_grad * hat)
        sums[9:10, :] += column_sum(normed_grad)
        sums[10:11, :narrow] += column_sum(latent_grad)
        upstream[...] = norm_back(normed_grad, output_gain[0:1, :], hat, inverse)

    @pl.when(jnp.logical_not(encoder))
    def _():
        upstream[...] = cotangent[...].astype(F32)

    above = upstream[...]
    low = above.astype(BF)
    out_low[...] = low
    sums[4:5, :] += column_sum(low.astype(F32))
    normed_grad = None
    chunk = 1024
    for start in range(0, weight_in.shape[1], chunk):
        here = slice(start, start + chunk)
        active_grad = dot(low, weight_last[here, :], NT)
        inner = (active_grad * slope[:, here].astype(F32)).astype(BF)
        preact_low[:, here] = inner
        part = column_sum(inner.astype(F32))
        for at in range(0, chunk, min(chunk, width)):
            row, lane = (start + at) // width, (start + at) % width
            size = min(chunk, width)
            sums[row : row + 1, lane : lane + size] += part[:, at : at + size]
        term = dot(inner, weight_in[:, here], NT)
        normed_grad = term if normed_grad is None else normed_grad + term
    hat, inverse = norm_parts(mid[...])
    sums[6:7, :] += column_sum(normed_grad * hat)
    sums[7:8, :] += column_sum(normed_grad)
    middle = above + norm_back(normed_grad, gains[1:2, :], hat, inverse)
    mid_grad[...] = middle
    branch = middle.astype(BF)
    branch_low[...] = branch
    sums[5:6, :] += column_sum(branch.astype(F32))
    context_grad[...] = dot(branch, weight_out[...], NT).astype(BF)


def mark_grads(context_grad, context, grad_mark):
    count = context_grad.shape[0]
    lane_all = lanes((count, 128)) & 63
    across = (
        lax.broadcasted_iota(jnp.int32, (128, 128), 0) // 64 != lanes((128, 128)) // 64
    ).astype(BF)
    zero = jnp.zeros((count, 128), BF)
    for pair in range(context_grad.shape[1] // 128):
        here = slice(pair * 128, pair * 128 + 128)
        product = split(context_grad[:, here].astype(F32) * context[:, here].astype(F32))
        level = -(dot(product[0], across, NN) + dot(product[1], across, NN))
        first = level.astype(BF)
        second, third = split(level - first.astype(F32))
        grad_mark[:, here] = merge(
            lane_all == 0, first, merge(lane_all == 1, second, merge(lane_all == 2, third, zero))
        )


def attend_back_block(
    number, start, extent, base, pairs,
    query, marks, key, value, context_grad, key_mark, grad_mark, query_grad, key_total, value_total,
):
    size = TOKENS
    low_query = lanes((size, 128)) < 64
    rows = pl.ds(pl.multiple_of(number * size, size), size)
    keys = pl.ds(pl.multiple_of(start, WINDOW), extent)
    low_key = lanes((extent, 128)) < 64
    key_aug = key_mark[keys, :]
    ones = jnp.where((lanes((extent, 128)) & 63) < 3, 1.0, 0.0).astype(BF)
    none = jnp.zeros((extent, 128), BF)
    for pair in range(pairs):
        here = pl.ds(pl.multiple_of(base + pair * 128, 128), 128)
        query_pair, key_pair, value_pair = query[rows, here], key[keys, here], value[keys, here]
        grad_pair, query_aug, grad_aug = context_grad[rows, here], marks[rows, here], grad_mark[rows, here]
        found = []
        for swap in (False, True):

            def both(low, left, right):
                return merge(low, right, left) if swap else merge(low, left, right)

            scores = dot(both(low_key, key_pair, key_aug), both(low_query, query_pair, query_aug), NT)
            rise = dot(both(low_key, value_pair, ones), both(low_query, grad_pair, grad_aug), NT)
            chance = jnp.exp2(scores)
            score_grad = (chance * rise).astype(BF)
            found.append(
                (
                    dot(score_grad, query_pair, NN),
                    dot(chance.astype(BF), grad_pair, NN),
                    dot(score_grad, both(low_key, key_pair, none), TN),
                )
            )
        key_total[keys, here] += merge(low_key, found[0][0], found[1][0])
        value_total[keys, here] += merge(low_key, found[0][1], found[1][1])
        query_grad[rows, here] = ((found[0][2] + found[1][2]) * HEAD ** (-0.5)).astype(BF)


def attend_back_kernel(
    windows, query, marks, key, value, context_grad, context, key_mark,
    query_grad, key_grad, value_grad, grad_mark, key_total, value_total, *, row
):
    count = query.shape[0]
    steps = count // TOKENS
    pairs = query.shape[1] // 128
    mark_grads(context_grad, context, grad_mark)
    key_total[...] = jnp.zeros_like(key_total)
    value_total[...] = jnp.zeros_like(value_total)

    def one(turn, carry):
        number = turn
        at = (row * steps + number) * 2

        def run(start, extent):
            attend_back_block(
                number, start, extent, 0, pairs,
                query, marks, key, value, context_grad, key_mark, grad_mark, query_grad, key_total, value_total,
            )

        for_windows(windows[at], windows[at + 1], count, (640, 768), run)
        return carry

    lax.fori_loop(0, steps, one, 0)
    key_grad[...] = (key_total[...] * (1.0 / LOG2E)).astype(BF)
    value_grad[...] = value_total[...].astype(BF)


def entry_back_kernel(
    side, edge, wide, up, head_bias, unit, query_grad, key_grad, value_grad, weight, gains, biases,
    mid_grad, *refs, adding
):
    before, refs = refs[: 2 * adding], refs[2 * adding :]
    entry, latent_out, sums, head_weight = refs
    encoder = side[0] == 0
    width = edge.shape[1]
    narrow = unit.shape[1]

    @pl.when(pl.program_id(0) == 0)
    def _():
        sums[...] = before[0][...] if adding else jnp.zeros_like(sums)
        head_weight[...] = before[1][...] if adding else jnp.zeros_like(head_weight)

    values = entry_values(encoder, edge[...], wide[...], up[...], head_bias[...])
    normed_grad = (
        dot(query_grad[...], weight[:, :width], NT)
        + dot(key_grad[...], weight[:, width : 2 * width], NT)
        + dot(value_grad[...], weight[:, 2 * width :], NT)
    )
    hat, inverse = norm_parts(values)
    sums[0:1, :] += column_sum(query_grad[...].astype(F32))
    sums[1:2, :] += column_sum(value_grad[...].astype(F32))
    sums[2:3, :] += column_sum(normed_grad * hat)
    sums[3:4, :] += column_sum(normed_grad)
    total = mid_grad[...] + norm_back(normed_grad, gains[0:1, :], hat, inverse)
    entry[...] = total

    @pl.when(jnp.logical_not(encoder))
    def _():
        sums[4:5, :] += column_sum(total)
        latent_out[...] = code_product(total, up[...]).T
        codes, low_total = split(unit[...]), total.astype(BF)
        head_weight[...] += dot(codes[0], low_total, TN) + dot(codes[1], low_total, TN)


def hidden_weight_kernel(active, out_low, n2, preact_low, *refs):
    out = refs[-1]
    before = refs[0] if len(refs) > 1 else None
    step = pl.program_id(0)
    first = pl.num_programs(0) // 2
    width = n2.shape[1]

    def put(value, rows):
        out[rows, :] = value if before is None else value + before[rows, :]

    @pl.when(step < first)
    def _():
        put(dot(active[...], out_low[...], TN), slice(0, 2 * width))

    @pl.when(step >= first)
    def _():
        value = dot(n2[...], preact_low[...], TN)
        put(value[:, :width], slice(0, width))
        put(value[:, width:], slice(width, 2 * width))


def weight_call(kernel, operands, in_specs, steps, before):
    width = operands[1].shape[1]
    out_spec = pl.BlockSpec((2 * width, width), lambda step: (step, 0))
    aliases = {}
    if before is not None:
        aliases = {len(operands): 0}
        operands, in_specs = operands + [before], in_specs + [out_spec]
    return pl.pallas_call(
        kernel,
        grid=(steps,),
        in_specs=in_specs,
        out_specs=out_spec,
        out_shape=jax.ShapeDtypeStruct((2 * steps * width, width), F32),
        input_output_aliases=aliases,
        compiler_params=PARAMS,
    )(*operands)


def hidden_weights(kept, late, before=None):
    operands = [kept.active, late.out_low, kept.n2, late.preact_low]
    count, width = kept.n2.shape
    first = kept.active.shape[1] // (2 * width)
    full = pl.BlockSpec((count, width), lambda step: (0, 0))
    in_specs = [
        pl.BlockSpec((count, 2 * width), lambda step: (0, jnp.minimum(step, first - 1))),
        full,
        full,
        pl.BlockSpec((count, 2 * width), lambda step: (0, jnp.maximum(step - first, 0))),
    ]
    return weight_call(hidden_weight_kernel, operands, in_specs, 2 * first, before)


MESH = pl.DeviceIdType.MESH
LEAST_DEVICES = 4


def ring_chip(position, chips):
    odd = position // (chips // 2)
    return (1 - odd) * (2 * position) + odd * (2 * (chips - 1 - position) + 1)


class Ring:
    @staticmethod
    def scratch(arrays, ways, crossing):
        chips = lax.axis_size(DP) // 2
        sizes = [array.shape[0] // (2 * count * chips) for array, count in zip(arrays, ways)]
        shapes = [(count, chips, size, array.shape[1]) for array, count, size in zip(arrays, ways, sizes)]
        buffers = [pltpu.VMEM(shape, F32) for shape in shapes] * 3
        sems = [pltpu.SemaphoreType.DMA(shape[:2]) for shape in shapes] * 10
        far = []
        if crossing is not None:
            count, unused, size, width = shapes[crossing]
            far = [pltpu.VMEM((count, size, width), F32)] + [pltpu.SemaphoreType.DMA((count,))] * 2
        return buffers + sems + far

    def __init__(self, sources, results, ways, crossing, scratch):
        number = len(sources)
        take = lambda at: scratch[at * number : (at + 1) * number]
        self.chips = lax.axis_size(DP) // 2
        self.sources, self.results, self.ways, self.crossing = sources, results, ways, crossing
        self.own, self.pair, self.run = take(0), take(1), take(2)
        (
            self.load_sems, self.pair_send, self.pair_recv, self.run_send, self.run_recv,
            self.keep_sems, self.spread_send, self.spread_recv, self.side_send, self.side_recv,
        ) = (take(at) for at in range(3, 13))
        self.far = scratch[13 * number :]
        self.sizes = [run.shape[2] for run in self.run]
        self.lanes = [(which, way) for way in range(max(ways)) for which in range(number) if way < ways[which]]
        place = lax.axis_index(DP)
        chip, self.core = place // 2, place % 2
        column, odd = chip // 2, chip % 2
        chips = self.chips
        self.position = (1 - odd) * column + odd * (chips - 1 - column)
        self.other = {DP: chip * 2 + (1 - self.core)}
        self.across = {SECTION: 1 - lax.axis_index(SECTION)}
        self.targets = (
            {DP: ring_chip((self.position + 1) % chips, chips) * 2 + self.core},
            {DP: ring_chip((self.position + chips - 1) % chips, chips) * 2 + self.core},
        )

    def greet(self):
        self.barrier = pltpu.get_barrier_semaphore()
        devices = (self.other, self.across) + self.targets
        for device in devices:
            pl.semaphore_signal(self.barrier, inc=1, device_id=device, device_id_type=MESH)
        self.greeted = len(devices)

    def piece(self, step, way):
        return (self.position + (2 * self.chips - step if way % 2 == 0 else step)) % self.chips

    def rows(self, which, half, way, number):
        size = self.sizes[which]
        return pl.ds(pl.multiple_of(((half * self.ways[which] + way) * self.chips + number) * size, 8), size)

    def final(self, which, half, way, step):
        return self.results[which].at[self.rows(which, half, way, self.piece(step + self.chips - 1, way))]

    def load(self, which, way, step):
        return pltpu.make_async_copy(
            self.sources[which].at[self.rows(which, self.core, way, self.piece(step, way))],
            self.own[which].at[way, step],
            self.load_sems[which].at[way, step],
        )

    def remote(self, source, target, send, recv, device):
        return pltpu.make_async_remote_copy(
            src_ref=source, dst_ref=target, send_sem=send, recv_sem=recv, device_id=device, device_id_type=MESH
        )

    def swap(self, which, way, step):
        return self.remote(
            self.sources[which].at[self.rows(which, 1 - self.core, way, self.piece(step, way))],
            self.pair[which].at[way, step],
            self.pair_send[which].at[way, step],
            self.pair_recv[which].at[way, step],
            self.other,
        )

    def pass_on(self, which, way, step):
        return self.remote(
            self.run[which].at[way, step],
            self.run[which].at[way, step + 1],
            self.run_send[which].at[way, step],
            self.run_recv[which].at[way, step + 1],
            self.targets[way % 2],
        )

    def cross(self, way):
        return self.remote(
            self.run[self.crossing].at[way, self.chips - 1],
            self.far[0].at[way],
            self.far[1].at[way],
            self.far[2].at[way],
            self.across,
        )

    def keep(self, which, way):
        return pltpu.make_async_copy(
            self.run[which].at[way, self.chips - 1], self.final(which, self.core, way, 0), self.keep_sems[which].at[way, 0]
        )

    def spread(self, which, way, step, first=False):
        here = self.final(which, self.core, way, step)
        return self.remote(
            self.run[which].at[way, self.chips - 1] if first else here,
            here,
            self.spread_send[which].at[way, step],
            self.spread_recv[which].at[way, step],
            self.targets[way % 2],
        )

    def incoming(self, which, way, step):
        here = self.final(which, self.core, way, step)
        return self.remote(
            here, here, self.spread_send[which].at[way, step], self.spread_recv[which].at[way, step - 1],
            self.targets[way % 2],
        )

    def aside(self, which, way, step, first=False):
        here = self.final(which, self.core, way, step)
        return self.remote(
            self.run[which].at[way, self.chips - 1] if first else here,
            here,
            self.side_send[which].at[way, step],
            self.side_recv[which].at[way, step],
            self.other,
        )

    def beside(self, which, way, step):
        here = self.final(which, 1 - self.core, way, step)
        return self.remote(
            here, here, self.side_send[which].at[way, step], self.side_recv[which].at[way, step], self.other
        )

    def begin(self, waiting=True):
        def load(step, carry):
            for which, way in self.lanes:
                self.load(which, way, step).start()
            return carry

        def swap(step, carry):
            for which, way in self.lanes:
                self.swap(which, way, step).start()
            return carry

        lax.fori_loop(0, self.chips, load, 0)
        if waiting:
            pl.semaphore_wait(self.barrier, self.greeted)
        lax.fori_loop(0, self.chips, swap, 0)
        for which, way in self.lanes:
            self.load(which, way, 0).wait()
            self.swap(which, way, 0).wait_recv()
            self.run[which][way, 0] = self.own[which][way, 0] + self.pair[which][way, 0]
            self.pass_on(which, way, 0).start()

    def gather(self, step, lanes=None):
        for which, way in self.lanes if lanes is None else lanes:
            run, own, pair = self.run[which], self.own[which], self.pair[which]
            self.load(which, way, step).wait()
            self.swap(which, way, step).wait_recv()
            self.pass_on(which, way, step - 1).wait_recv()
            run[way, step] = run[way, step] + own[way, step] + pair[way, step]

            @pl.when(step < self.chips - 1)
            def _():
                self.pass_on(which, way, step).start()

    def turn(self):
        for which, way in self.lanes:
            if which == self.crossing:
                self.cross(way).start()
        for which, way in self.lanes:
            if which != self.crossing:
                self.hand_out(which, way)
        for which, way in self.lanes:
            if which == self.crossing:
                run = self.run[which]
                self.cross(way).wait()
                run[way, self.chips - 1] = run[way, self.chips - 1] + self.far[0][way]
                self.hand_out(which, way)

    def hand_out(self, which, way):
        self.spread(which, way, 0, True).start()
        self.aside(which, way, 0, True).start()
        self.keep(which, way).start()

    def pass_out(self, step, lanes=None):
        for which, way in self.lanes if lanes is None else lanes:
            self.incoming(which, way, step).wait_recv()

            @pl.when(step < self.chips - 1)
            def _():
                self.spread(which, way, step).start()

            self.aside(which, way, step).start()

    def finish(self):
        def one(step, carry):
            for which, way in self.lanes:
                self.swap(which, way, step).wait_send()
                self.beside(which, way, step).wait_recv()
                self.aside(which, way, step).wait_send()

                @pl.when(step < self.chips - 1)
                def _():
                    self.pass_on(which, way, step).wait_send()
                    self.spread(which, way, step).wait_send()

            return carry

        lax.fori_loop(0, self.chips, one, 0)
        for which, way in self.lanes:
            self.keep(which, way).wait()


def loop(start, stop, run):
    def one(step, carry):
        run(step)
        return carry

    lax.fori_loop(start, stop, one, 0)


HIDDEN_WAYS = (4,)
OTHER_WAYS = (4, 2)


def finish_kernel(*refs, held):
    (
        hidden, query, marks, key, value, context_grad, context, key_mark, edges, mid_grad, weight, branch_low, n1,
    ), refs = refs[:13], refs[13:]
    mine, others, refs = refs[:6], refs[6:18], refs[18:]
    (
        gains, book, down, up, late, early,
        hidden_out, attention_out, misc_out, entry,
        query_in, marks_in, key_in, value_in, grad_in, context_in, key_mark_in, edge_in, mid_in, weight_in, branch_in,
        n1_in, part, misc, grad_mark, query_grad, key_total, value_total, key_grad, value_grad, in_sems, out_sems,
    ), scratch = refs[:32], refs[32:]
    encoder = lax.axis_index(SECTION) == 0
    decoder = jnp.logical_not(encoder)
    ring = Ring((hidden,), (hidden_out,), HIDDEN_WAYS, None, scratch[:held]) if scratch else None
    last = Ring((part, misc), (attention_out, misc_out), OTHER_WAYS, 1, scratch[held:]) if scratch else None
    count, width = query.shape
    narrow = down.shape[0]
    steps = count // TOKENS
    pairs = width // 128
    row = edges.shape[0] - 1
    at = book.shape[0] + 2 * narrow
    inputs = (
        (query, query_in), (marks, marks_in), (key, key_in), (value, value_in), (context_grad, grad_in),
        (context, context_in), (key_mark.at[row], key_mark_in), (edges.at[row], edge_in), (mid_grad, mid_in),
        (weight, weight_in), (branch_low, branch_in), (n1, n1_in),
    )
    first_held = (query_in, marks_in, key_in, value_in, grad_in, grad_mark)
    second_held = (context_in, branch_in, n1_in, query_grad, key_grad, value_grad)

    def copies(pairs):
        return [pltpu.make_async_copy(*pair, in_sems.at[number]) for number, pair in enumerate(pairs)]

    loads = copies(inputs)
    other_loads = copies(zip(others, first_held + second_held))
    first_loads = copies(zip(mine, first_held))

    def start(copies):
        for copy in copies:
            copy.start()

    def wait(copies):
        for copy in copies:
            copy.wait()

    if ring:
        ring.greet()
    pl.when(encoder)(functools.partial(start, loads))
    pl.when(decoder)(functools.partial(start, other_loads))
    if ring:
        ring.begin()
    misc[...] = jnp.zeros_like(misc)

    def attention_piece(turn):
        attend_back_block(
            turn // pairs, 0, count, (turn % pairs) * 128, 1,
            query_in, marks_in, key_in, value_in, grad_in, key_mark_in, grad_mark, query_grad, key_total, value_total,
        )

    @pl.when(encoder)
    def _():
        misc[: book.shape[0], :] = book[...]
        misc[book.shape[0] : book.shape[0] + narrow, :] = down[...]
        misc[at : at + 16, :] = late[...]
        misc[at + 16 : at + 32, :] = early[...]
        wait(loads)
        mark_grads(grad_in, context_in, grad_mark)
        key_total[...] = jnp.zeros_like(key_total)
        value_total[...] = jnp.zeros_like(value_total)
        loop(0, 2, attention_piece)

    @pl.when(decoder)
    def _():
        misc[book.shape[0] + narrow : at, :] = up[...]
        misc[at + 32 : at + 48, :] = late[...]
        misc[at + 48 : at + 64, :] = early[...]
        wait(other_loads)

    def entry_piece(number):
        rows = pl.ds(pl.multiple_of(number * TOKENS, TOKENS), TOKENS)
        normed_grad = (
            dot(query_grad[rows, :], weight_in[:, :width], NT)
            + dot(key_grad[rows, :], weight_in[:, width : 2 * width], NT)
            + dot(value_grad[rows, :], weight_in[:, 2 * width :], NT)
        )
        hat, inverse = norm_parts(edge_in[rows, :].astype(F32))
        misc[at + 16 : at + 17, :] += column_sum(query_grad[rows, :].astype(F32))
        misc[at + 17 : at + 18, :] += column_sum(value_grad[rows, :].astype(F32))
        misc[at + 18 : at + 19, :] += column_sum(normed_grad * hat)
        misc[at + 19 : at + 20, :] += column_sum(normed_grad)
        mid_in[rows, :] = mid_in[rows, :] + norm_back(normed_grad, gains[0:1, :], hat, inverse)

    def weight_piece(number):
        def put(first, second):
            rows = pl.ds(pl.multiple_of(number * width, width), width)
            part[rows, :] = dot(first[0][...], first[1][...], TN) + dot(second[0][...], second[1][...], TN)

        for choice, places in enumerate(((0, 1), (2, 3), (2, 4), (2, 5))):
            both = [[held[place] for place in places] for held in (first_held, second_held)]
            pl.when(number == choice)(functools.partial(put, *both))

    halves = (ring.lanes[:2], ring.lanes[2:]) if ring else (None, None)
    chips = ring.chips if ring else 8
    pieces = steps * pairs

    def summing(step):
        for half in range(2):
            if ring:
                ring.gather(step, halves[half])

            @pl.when(encoder)
            def _():
                attention_piece(2 * step + half)

    inside = min(chips - 1, pieces // 2 - 1)
    loop(1, inside + 1, summing)
    if ring:
        loop(inside + 1, chips, ring.gather)
        ring.turn()

    @pl.when(encoder)
    def _():
        loop(2 * inside + 2, pieces, attention_piece)
        start(first_loads)
        key_grad[...] = (key_total[...] * (1.0 / LOG2E)).astype(BF)
        value_grad[...] = value_total[...].astype(BF)

    def spreading(step):
        if ring:
            ring.pass_out(step, halves[0])

        @pl.when(encoder)
        def _():
            entry_piece(step - 1)

        if ring:
            ring.pass_out(step, halves[1])
        pl.when(encoder & (step == 1))(functools.partial(wait, first_loads))
        weight_piece(step - 1)

    loop(1, steps + 1, spreading)
    store = pltpu.make_async_copy(mid_in, entry, out_sems.at[0])

    @pl.when(encoder)
    def _():
        store.start()

    if ring:
        last.begin(False)

        def both(step):
            ring.pass_out(step)
            last.gather(step - steps)

        loop(steps + 1, chips, both)
        loop(chips - steps, chips, last.gather)
        last.turn()
        loop(1, chips, last.pass_out)
        ring.finish()
        last.finish()
    else:
        stores = [
            pltpu.make_async_copy(part, attention_out, out_sems.at[1]),
            pltpu.make_async_copy(misc, misc_out, out_sems.at[2]),
        ]
        start(stores)
        wait(stores)

    @pl.when(encoder)
    def _():
        store.wait()


def finish_row(work, first_kept, kept, late, mine, book, others, hidden):
    count, width = kept.n1.shape
    alone = lax.axis_size(DP) < LEAST_DEVICES
    its_late, its_early = mine
    operands = [
        hidden, kept.query, kept.marks, kept.key, kept.value, late.context_grad,
        kept.context, work.key_mark, work.edges, late.mid_grad, work.attention_in, late.branch_low, kept.n1,
    ]
    for a_kept, a_late, a_early in ((first_kept, its_late, its_early),) + others:
        operands += [a_kept.context, a_late.branch_low, a_kept.n1, *a_early[:3]]
    operands += [work.gains, book, late.head, its_early.head, late.sums, its_early.sums]
    hbm, vmem = pl.BlockSpec(memory_space=pl.ANY), pl.BlockSpec(memory_space=pltpu.VMEM)
    rows = book.shape[0] + 2 * work.narrow + 64
    unit = 16 * lax.axis_size(DP)
    attention = jax.ShapeDtypeStruct((4 * width, width), F32)
    misc = jax.ShapeDtypeStruct((rows + (-rows % unit), width), F32)
    low = pltpu.VMEM((count, width), BF)
    wide = pltpu.VMEM((count, width), F32)
    scratch = [low] * 6 + [pltpu.VMEM((count, 128), BF), low, wide, pltpu.VMEM(work.attention_in.shape, BF), low, low]
    scratch += [pltpu.VMEM(attention.shape, F32), pltpu.VMEM(misc.shape, F32), low, low, wide, wide, low, low]
    scratch += [pltpu.SemaphoreType.DMA((12,)), pltpu.SemaphoreType.DMA((3,))]
    settings = {}
    held = 0
    if not alone:
        rings = Ring.scratch((hidden,), HIDDEN_WAYS, None)
        held = len(rings)
        scratch += rings + Ring.scratch((attention, misc), OTHER_WAYS, 1)
        settings = dict(collective_id=0, has_side_effects=True)
    outs = pl.pallas_call(
        functools.partial(finish_kernel, held=held),
        in_specs=[hbm] * 31 + [vmem] * 6,
        out_specs=[hbm] * 4,
        out_shape=(
            jax.ShapeDtypeStruct(hidden.shape, F32), attention, misc, jax.ShapeDtypeStruct((count, width), F32),
        ),
        scratch_shapes=scratch,
        compiler_params=pltpu.CompilerParams(vmem_limit_bytes=60 << 20, **settings),
    )(*operands)
    if alone:
        return hidden, outs[1], lax.psum(outs[2], SECTION), outs[3]
    return outs


def unpack_kernel(
    side, hidden, attention, misc, first_entry, second_entry, first_result, second_result,
    hidden_out, hidden_in, attention_out, attention_in, edge, book, gains, biases, bias, last_gain, head_bias, down, down_last,
    up, held, head, rows, ins, outs, row_ins, row_outs,
):
    width = hidden.shape[1]
    narrow = book.shape[0]
    steps = hidden_out.shape[0] // width
    targets = [hidden_out.at[pl.ds(number * width, width), :] for number in range(steps)]
    targets += [hidden_in.at[:, pl.ds(number * width, width)] for number in range(steps)]
    targets += [attention_out]
    targets += [attention_in.at[:, pl.ds(number * width, width)] for number in range(3)]
    sources = [hidden.at[pl.ds(number * width, width), :] for number in range(2 * steps)]
    sources += [attention.at[pl.ds(number * width, width), :] for number in range(4)]
    tiles = range(len(targets))
    for mine, pair in ((0, (first_entry, second_entry)), (1, (first_result, second_result))):

        @pl.when(side[0] == mine)
        def _():
            for row in range(2):
                pltpu.make_async_copy(pair[row], rows.at[row], row_ins.at[row]).start()

    loads = [pltpu.make_async_copy(sources[number], held.at[number], ins.at[number]) for number in tiles]
    loads.append(pltpu.make_async_copy(misc.at[pl.ds(0, head.shape[0]), :], head, ins.at[len(targets)]))
    for load in loads:
        load.start()
    stores = []
    for row in range(2):
        pltpu.make_async_copy(first_entry, rows.at[row], row_ins.at[row]).wait()
        stores.append(pltpu.make_async_copy(rows.at[row], edge.at[row], row_outs.at[row]))
        stores[-1].start()
    for number in tiles:
        loads[number].wait()
        stores.append(pltpu.make_async_copy(held.at[number], targets[number], outs.at[number]))
        stores[-1].start()
    loads[-1].wait()
    for number in range(book.shape[1] // width):
        book[:, number * width : (number + 1) * width] = head[number * narrow : (number + 1) * narrow, :]
    at = book.shape[0] * book.shape[1] // width
    down[...] = head[at : at + narrow, :]
    up[...] = head[at + narrow : at + 2 * narrow, :]
    at += 2 * narrow
    last_gain[...] = head[at + 8 : at + 9, :]
    head_bias[0:1, :] = head[at + 9 : at + 10, :]
    head_bias[1:2, :] = head[at + 52 : at + 53, :]
    down_last[...] = head[at + 10 : at + 11, :narrow]
    mine = jnp.where(side[0] == 0, head[at : at + 32, :], head[at + 32 : at + 64, :])
    for number in range(steps):
        bias[:, number * width : (number + 1) * width] = mine[number : number + 1, :]
    for number, place in enumerate((18, 6)):
        gains[number : number + 1, :] = mine[place : place + 1, :]
    for number, place in enumerate((16, 17, 5, 19, 7, 4)):
        biases[number] = mine[place : place + 1, :]
    for store in stores:
        store.wait()


def unpack(side, hidden, attention, misc, ends, table_turned):
    width = hidden.shape[1]
    features = hidden.shape[0] // 2
    tiles = (hidden.shape[0] + attention.shape[0]) // width
    narrow = table_turned.shape[0]
    rows = table_turned.size // width + 2 * narrow + 64
    shapes = (
        (features, width), (width, features), (width, width), (width, 3 * width), (2,) + ends[0].shape,
        table_turned.shape, (2, width), (6, 1, width), (1, features), (1, width), (2, width),
        (narrow, width), (1, narrow), (narrow, width),
    )
    hbm, vmem = pl.BlockSpec(memory_space=pl.ANY), pl.BlockSpec(memory_space=pltpu.VMEM)
    return pl.pallas_call(
        unpack_kernel,
        in_specs=[pl.BlockSpec(memory_space=pltpu.SMEM)] + [hbm] * 7,
        out_specs=[hbm] * 5 + [vmem] * 9,
        out_shape=tuple(jax.ShapeDtypeStruct(shape, F32) for shape in shapes),
        scratch_shapes=[
            pltpu.VMEM((tiles, width, width), F32),
            pltpu.VMEM((rows, width), F32),
            pltpu.VMEM((2,) + ends[0].shape, F32),
            pltpu.SemaphoreType.DMA((tiles + 1,)),
            pltpu.SemaphoreType.DMA((tiles,)),
            pltpu.SemaphoreType.DMA((2,)),
            pltpu.SemaphoreType.DMA((2,)),
        ],
        compiler_params=PARAMS,
    )(side, hidden, attention, misc, *ends)


def nothing_kernel(*refs):
    pass


def unwritten(shapes):
    leaves, tree = jax.tree.flatten(shapes)
    arrays = pl.pallas_call(
        nothing_kernel,
        out_specs=[pl.BlockSpec(memory_space=pl.ANY)] * len(leaves),
        out_shape=tuple(leaves),
    )()
    return jax.tree.unflatten(tree, arrays)


class Kept(NamedTuple):
    n1: Any
    query: Any
    key: Any
    value: Any
    context: Any
    marks: Any
    mid: Any
    n2: Any
    active: Any
    slope: Any
    result: Any
    latent: Any


class Late(NamedTuple):
    out_low: Any
    preact_low: Any
    mid_grad: Any
    branch_low: Any
    context_grad: Any
    sums: Any
    head: Any


class Early(NamedTuple):
    query_grad: Any
    key_grad: Any
    value_grad: Any
    entry: Any
    latent_out: Any
    sums: Any
    head: Any


class Rows:
    def __init__(self, side, edges, wide, unit, windows, query_mark, key_mark, weights, head):
        self.side, self.edges, self.wide, self.unit = side, edges, wide, unit
        self.windows, self.query_mark, self.key_mark = windows, query_mark, key_mark
        (
            self.attention_in, self.attention_out, self.hidden_in, self.hidden_out,
            self.gains, self.biases, self.hidden_bias,
        ) = weights
        (
            self.output_gain, self.head_bias, self.down, self.down_bias, self.up,
        ) = head
        self.rows, self.count, self.width = edges.shape
        self.hidden = self.hidden_in.shape[1]
        self.narrow = unit.shape[1]
        self.size = TOKENS
        n, d, f = self.count, self.width, self.hidden
        shape = jax.ShapeDtypeStruct
        low, tall, wide = shape((n, d), BF), shape((n, f), BF), shape((n, d), F32)
        sums, head = shape((16, d), F32), shape((self.narrow, d), F32)
        self.kept = Kept(low, low, low, low, low, low, wide, low, tall, tall, wide, shape((n, self.narrow), F32))
        self.late = Late(low, tall, wide, low, low, sums, head)
        self.early = Early(low, low, low, wide, shape((self.narrow, n), F32), sums, head)

    def side_spec(self):
        return pl.BlockSpec(memory_space=pltpu.SMEM)

    def tokens(self, array):
        return pl.BlockSpec((self.size, array.shape[1]), lambda step: (step, 0))

    def turned(self, array):
        return pl.BlockSpec((array.shape[0], self.size), lambda step: (0, step))

    def whole(self, array):
        return pl.BlockSpec(array.shape, lambda step: (0,) * len(array.shape))

    def entry_specs(self, row):
        steps = self.count // self.size
        return [
            pl.BlockSpec((None, self.size, self.width), lambda step: (row, step, 0)),
            pl.BlockSpec((self.size, self.wide.shape[1]), lambda step: (row * steps + step, 0)),
            self.whole(self.up),
            self.whole(self.head_bias),
        ]

    def unit_spec(self, row):
        steps = self.count // self.size
        return pl.BlockSpec((self.size, self.narrow), lambda step: (row * steps + step, 0))

    def call(self, kernel, in_specs, operands, outs, out_specs, scratch=()):
        return pl.pallas_call(
            kernel,
            grid=(self.count // self.size,),
            in_specs=in_specs,
            out_specs=out_specs,
            out_shape=tuple(outs),
            scratch_shapes=list(scratch),
            compiler_params=PARAMS,
        )(*operands)

    def attention_call(self, kernel, row, operands, outs, scratch=()):
        half = self.width // 2

        def spec(array):
            if array.ndim == 3:
                return pl.BlockSpec((None, self.count, array.shape[2]), lambda step, info: (row, 0, 0))
            return pl.BlockSpec((self.count, half), lambda step, info: (0, step))

        return pl.pallas_call(
            functools.partial(kernel, row=row),
            grid_spec=pltpu.PrefetchScalarGridSpec(
                num_scalar_prefetch=1,
                grid=(2,),
                in_specs=[spec(array) for array in operands],
                out_specs=[spec(array) for array in outs],
                scratch_shapes=list(scratch),
            ),
            out_shape=tuple(outs),
            compiler_params=PARAMS,
        )(self.windows, *operands)

    def forward(self, row):
        shapes = self.kept
        entry = (self.edges, self.wide, self.up, self.head_bias)
        outs = shapes[:4]
        self.size = 2 * TOKENS
        n1, query, key, value = self.call(
            project_kernel,
            [self.side_spec()] + self.entry_specs(row)
            + [self.whole(self.gains), self.whole(self.biases), self.whole(self.attention_in)],
            (self.side,) + entry + (self.gains, self.biases, self.attention_in),
            outs,
            [self.tokens(array) for array in outs],
        )
        self.size = TOKENS
        context, marks = self.attention_call(
            attend_kernel, row, (query, key, value, self.query_mark, self.key_mark), shapes[4:6]
        )
        consts = (
            self.attention_out, self.gains, self.biases, self.hidden_in, self.hidden_bias, self.hidden_out,
            self.output_gain, self.down, self.down_bias,
        )
        outs = shapes[6:]
        outs = self.call(
            hidden_kernel,
            [self.side_spec()] + self.entry_specs(row) + [self.tokens(context)]
            + [self.whole(array) for array in consts],
            (self.side,) + entry + (context,) + consts,
            outs,
            [self.tokens(array) for array in outs],
        )
        return Kept(n1, query, key, value, context, marks, *outs)

    def backward(self, row, kept, latent_in, former=(None, None)):
        late = self.backward_late(row, kept, latent_in, former[0])
        return late, self.backward_early(row, kept, late, former[1])

    def backward_late(self, row, kept, latent_in, former=None):
        prior = () if former is None else (former.sums, former.head)
        adding = int(former is not None)
        consts = (self.output_gain, self.head_bias, self.down, self.hidden_out)
        late = (self.gains, self.biases, self.attention_out)
        outs = self.late
        return Late(*self.call(
            functools.partial(tail_back_kernel, adding=adding),
            [self.side_spec(), self.tokens(kept.result), self.entry_specs(row)[0], self.unit_spec(row),
             self.turned(latent_in), self.tokens(kept.latent)]
            + [self.whole(array) for array in consts]
            + [self.tokens(kept.slope), self.whole(self.hidden_in), self.tokens(kept.mid)]
            + [self.whole(array) for array in late + prior],
            (self.side, kept.result, self.edges, self.unit, latent_in, kept.latent) + consts
            + (kept.slope, self.hidden_in, kept.mid) + late + prior,
            outs,
            [self.tokens(array) for array in outs[:5]] + [self.whole(array) for array in outs[5:]],
            scratch=[pltpu.VMEM((self.size, self.width), F32)],
        ))

    def backward_early(self, row, kept, late, former=None):
        adding = int(former is not None)
        half = self.width // 2
        grads = tuple(self.attention_call(
            attend_back_kernel, row,
            (kept.query, kept.marks, kept.key, kept.value, late.context_grad, kept.context, self.key_mark),
            self.early[:3],
            scratch=[
                pltpu.VMEM((self.count, half), BF),
                pltpu.VMEM((self.count, half), F32),
                pltpu.VMEM((self.count, half), F32),
            ],
        ))
        prior = () if former is None else (former.sums, former.head)
        outs = self.early[3:]
        outs = self.call(
            functools.partial(entry_back_kernel, adding=adding),
            [self.side_spec()] + self.entry_specs(row) + [self.unit_spec(row)]
            + [self.tokens(array) for array in grads]
            + [self.whole(self.attention_in), self.whole(self.gains), self.whole(self.biases),
               self.tokens(late.mid_grad)] + [self.whole(array) for array in prior],
            (self.side, self.edges, self.wide, self.up, self.head_bias, self.unit) + grads
            + (self.attention_in, self.gains, self.biases, late.mid_grad) + prior,
            outs,
            [self.tokens(outs[0]), self.turned(outs[1])] + [self.whole(array) for array in outs[2:]],
        )
        return Early(*grads, *outs)


def windows_of(segments):
    rows, count = segments.shape
    steps = count // WINDOW
    wide, blocks = (segments.reshape(rows, -1, size) for size in (TOKENS, WINDOW))
    meets = (wide[:, :, None, -1] >= blocks[:, None, :, 0]) & (wide[:, :, None, 0] <= blocks[:, None, :, -1])
    place = jnp.arange(steps)
    start = jnp.min(jnp.where(meets, place, steps), -1)
    stop = jnp.max(jnp.where(meets, place, -1), -1) + 1
    return jnp.stack([start, stop - start], -1).reshape(-1).astype(jnp.int32)


def on_device(
    boundary, segments, code_index, attention_in, attention_out, hidden_in, hidden_out, block_gains,
    block_biases, hidden_bias, output_gain, head_bias, down_weight, down_bias, up_weight, codebook,
):
    section = lax.axis_index(SECTION)
    encoder = section == 0
    side = section.astype(jnp.int32)[None]
    edges = boundary[0]
    rows, count, width = edges.shape
    hidden = hidden_in.shape[2]
    table_turned = codebook.T
    code_index = code_index.reshape(-1)
    unit, wide, query_mark, key_mark = gather_codes(code_index, table_turned, segments)
    work = Rows(
        side, edges, wide, unit, windows_of(segments), query_mark, key_mark,
        (
            attention_in[0], attention_out[0], hidden_in[0], hidden_out[0], block_gains[0], block_biases.transpose(1, 0, 2),
            hidden_bias,
        ),
        (output_gain[None], head_bias, down_weight.T, down_bias[None], up_weight),
    )
    book_out = book_shape(table_turned, width)
    hidden_shape = jax.ShapeDtypeStruct((2 * hidden, width), F32)
    quiet = unwritten(work.early.latent_out)
    first_kept = work.forward(0)

    def encoder_first():
        return (work.forward(1), *unwritten((work.late, work.early)))

    def decoder_first():
        return (unwritten(work.kept), *work.backward(0, first_kept, quiet))

    kept_a, late_a, early_a = lax.cond(encoder, encoder_first, decoder_first)
    latent_in = lax.ppermute(early_a.latent_out, SECTION, [(1, 0)])

    def encoder_second():
        late, early = work.backward(0, first_kept, latent_in)
        book = scatter_codes(code_index, unit, (first_kept.latent, kept_a.latent), table_turned, width)
        return unwritten(work.kept), late, early, hidden_weights(first_kept, late), book

    def decoder_second():
        kept = work.forward(1)
        weights, book = unwritten((hidden_shape, book_out))
        return (kept, *work.backward(1, kept, quiet, (late_a, early_a)), weights, book)

    kept_b, late_b, early_b, weights_b, book = lax.cond(encoder, encoder_second, decoder_second)
    latent_in_second = lax.ppermute(early_b.latent_out, SECTION, [(1, 0)])

    def decoder_fourth():
        total = hidden_weights(kept_b, late_b, hidden_weights(first_kept, late_a))
        return total, (*unwritten(work.late[2:5]), late_b.sums, late_b.head)

    def encoder_fourth():
        late = work.backward_late(1, kept_a, latent_in_second, late_b)
        return hidden_weights(kept_a, late, weights_b), late[2:]

    hidden_total, late = lax.cond(encoder, encoder_fourth, decoder_fourth)
    late = Late(None, None, *late)
    hidden_total, attention_total, misc, second_entry = finish_row(
        work, first_kept, kept_a, late, (late_b, early_b), book,
        ((first_kept, late_a, early_a), (kept_b, late_b, early_b)), hidden_total,
    )
    (
        hidden_out_grad, hidden_in_grad, attention_out_grad, attention_in_grad, edge, book, gains, biases, bias,
        last_gain, head, down_grad, down_last, up_grad,
    ) = unpack(
        side, hidden_total, attention_total, misc,
        (early_b.entry, second_entry, first_kept.result, kept_b.result), table_turned,
    )
    return (
        edge[None],
        attention_in_grad[None],
        attention_out_grad[None],
        hidden_in_grad[None],
        hidden_out_grad[None],
        gains[None],
        biases.transpose(1, 0, 2),
        bias,
        last_gain[0],
        head,
        down_grad.T,
        down_last[0],
        up_grad,
        book.T,
    )


def solution(mesh):
    wide, split_last, flat = P(SECTION, DP, None, None), P(SECTION, None, None), P(SECTION, None)
    blocks = (split_last,) * 6 + (flat,)
    return jax.shard_map(
        on_device,
        mesh=mesh,
        in_specs=(wide, P(DP, None), P(DP, None)) + blocks + (P(),) * 6,
        out_specs=(wide,) + blocks + (P(),) * 6,
        check_vma=False,
    )
```

```python
import functools
import math
from typing import Any, NamedTuple

import jax
import jax.numpy as jnp
from jax import lax
from jax.experimental import pallas as pl
from jax.experimental.pallas import tpu as pltpu
from jax.sharding import PartitionSpec as P

HEAD = 64
SECTION, DP = "section", "dp"
BF = jnp.bfloat16
F32 = jnp.float32
LOG2E = math.log2(math.e)
NORM_EPS = 1e-06
MASKED = -1e30
GELU = 0.7978845608028654
CUBIC = 0.044715
NN = (((1,), (0,)), ((), ()))
NT = (((1,), (1,)), ((), ()))
TN = (((0,), (0,)), ((), ()))
TOKENS = 256
WINDOW = 128
PARAMS = pltpu.CompilerParams(vmem_limit_bytes=56 << 20)


def dot(a, b, dims):
    return lax.dot_general(a, b, dims, preferred_element_type=F32)


def lanes(shape):
    return lax.broadcasted_iota(jnp.int32, shape, 1)


def split(values):
    high = values.astype(BF)
    return high, (values - high.astype(F32)).astype(BF)


def dot3(left, right, dims):
    return dot(left[0], right[0], dims) + dot(left[0], right[1], dims) + dot(left[1], right[0], dims)


def unit_of(values):
    scale = lax.rsqrt(jnp.sum(values * values, -1, keepdims=True) + NORM_EPS)
    return values * scale, scale


def norm_parts(values):
    center = values - jnp.mean(values, -1, keepdims=True)
    inverse = lax.rsqrt(jnp.mean(center * center, -1, keepdims=True) + NORM_EPS)
    return center * inverse, inverse


def norm_back(grad, gain, hat, inverse):
    scaled = grad * gain
    return inverse * (
        scaled
        - jnp.mean(scaled, -1, keepdims=True)
        - hat * jnp.mean(scaled * hat, -1, keepdims=True)
    )


def column_sum(values):
    return jnp.sum(values, 0, keepdims=True)


def code_kernel(index, table_turned, segments, unit, wide, query_mark, key_mark, table, raw):
    count = raw.shape[0]
    block = 512

    def turn(step, carry):
        start = pl.multiple_of(step * block, block)
        table[pl.ds(start, block), :] = table_turned[:, pl.ds(start, block)].T
        return carry

    lax.fori_loop(0, table.shape[0] // block, turn, 0)

    length = segments.shape[1]

    def some(step, carry):
        for inner in range(16):
            token = step * 16 + inner
            raw[pl.ds(token, 1), :] = table[pl.ds(index[token], 1), :]
        return carry

    lax.fori_loop(0, count // 16, some, 0)

    values = raw[...]
    values = values * lax.rsqrt(jnp.sum(values * values, -1, keepdims=True) + NORM_EPS)
    unit[...] = values
    high, low = split(values)
    wide[...] = jnp.concatenate([high, low, high, jnp.zeros_like(high)], 1)
    lane = lanes((length, 128)) & 63
    for row in range(segments.shape[0]):
        owner = jnp.broadcast_to(segments[row : row + 1, :], (128, length)).T
        same = owner == lane
        query_mark[row] = jnp.where((lane < 4) & jnp.logical_not(same), MASKED, 0.0).astype(BF)
        key_mark[row] = jnp.where(((lane < 4) & same) | ((lane > 3) & (lane < 7)), 1.0, 0.0).astype(BF)


def gather_codes(index, table_turned, segments):
    count, width = index.shape[0], table_turned.shape[0]
    vmem = pl.BlockSpec(memory_space=pltpu.VMEM)
    mark = jax.ShapeDtypeStruct(segments.shape + (128,), BF)
    return pl.pallas_call(
        code_kernel,
        in_specs=[pl.BlockSpec(memory_space=pltpu.SMEM), vmem, vmem],
        out_specs=[vmem] * 4,
        out_shape=(
            jax.ShapeDtypeStruct((count, width), F32),
            jax.ShapeDtypeStruct((count, 4 * width), BF),
            mark,
            mark,
        ),
        scratch_shapes=[pltpu.VMEM(table_turned.shape[::-1], F32), pltpu.VMEM((count, width), F32)],
        compiler_params=PARAMS,
    )(index, table_turned, segments)


def scatter_kernel(index, unit, latent_first, latent_second, table_turned, out, total, rows):
    count = rows.shape[0]
    width = unit.shape[1]
    half = count // 2
    total[...] = jnp.zeros_like(total)
    for row, latent in enumerate((latent_first, latent_second)):
        here = slice(row * half, (row + 1) * half)
        code, unused = unit_of(latent[...])
        rows[here, :] = 2.0 * (unit[here, :] - code)

    def some(step, carry):
        for inner in range(8):
            token = step * 8 + inner
            place = pl.ds(index[token], 1)
            total[place, :] = total[place, :] + rows[pl.ds(token, 1), :]
        return carry

    lax.fori_loop(0, count // 8, some, 0)
    block = out.shape[1]

    def back(step, carry):
        start = pl.multiple_of(step * block, block)
        values = table_turned[:, pl.ds(start, block)]
        grad = total[pl.ds(start, block), :].T
        inverse = lax.rsqrt(jnp.sum(values * values, 0, keepdims=True) + NORM_EPS)
        book = values * inverse
        out[pl.ds(pl.multiple_of(step * width, width), width), :] = inverse * (
            grad - book * jnp.sum(book * grad, 0, keepdims=True)
        )
        return carry

    lax.fori_loop(0, total.shape[0] // block, back, 0)


def book_shape(table_turned, width):
    return jax.ShapeDtypeStruct((table_turned.size // width, width), F32)


def scatter_codes(index, unit, latents, table_turned, width):
    return pl.pallas_call(
        scatter_kernel,
        in_specs=[pl.BlockSpec(memory_space=pltpu.SMEM)] + [pl.BlockSpec(memory_space=pltpu.VMEM)] * 4,
        out_specs=pl.BlockSpec(memory_space=pltpu.VMEM),
        out_shape=book_shape(table_turned, width),
        scratch_shapes=[pltpu.VMEM(table_turned.shape[::-1], F32), pltpu.VMEM(unit.shape, F32)],
        compiler_params=PARAMS,
    )(index, unit, *latents, table_turned)


def entry_values(encoder, edge, wide, up, head_bias):
    high, low = split(up)
    parts = jnp.concatenate([high, high, low, jnp.zeros_like(low)], 0)
    return jnp.where(encoder, edge.astype(F32), dot(wide, parts, NN) + head_bias[1:2, :])


def project_kernel(side, edge, wide, up, head_bias, gains, biases, weight, n1, query, key, value):
    width = edge.shape[1]
    encoder = side[0] == 0
    values = entry_values(encoder, edge[...], wide[...], up[...], head_bias[...])
    hat, unused = norm_parts(values)
    normed = (hat * gains[0:1, :] + biases[3]).astype(BF)
    n1[...] = normed
    query[...] = (
        (dot(normed, weight[:, :width], NN) + biases[0]) * (LOG2E * HEAD ** (-0.5))
    ).astype(BF)
    key[...] = dot(normed, weight[:, width : 2 * width], NN).astype(BF)
    value[...] = (dot(normed, weight[:, 2 * width :], NN) + biases[1]).astype(BF)


def merge(low_half, left, right):
    return jnp.where(low_half, left, right)


def attend_kernel(windows, query, key, value, query_mark, key_mark, context, marks, *, row):
    count = query.shape[0]
    size = TOKENS
    pairs = query.shape[1] // 128
    low_query = lanes((size, 128)) < 64
    mark_lane = lanes((size, 128)) & 63

    def block(number, start, extent):
        rows = pl.ds(pl.multiple_of(number * size, size), size)
        keys = pl.ds(pl.multiple_of(start, WINDOW), extent)
        low_key = lanes((extent, 128)) < 64
        query_aug, key_aug = query_mark[rows, :], key_mark[keys, :]
        ones = jnp.ones((extent, 128), BF)
        scores = []
        for pair in range(pairs):
            here = slice(pair * 128, pair * 128 + 128)
            query_pair, key_pair = query[rows, here], key[keys, here]
            scores.append(
                dot(merge(low_query, query_pair, query_aug), merge(low_key, key_pair, key_aug), NT)
            )
            scores.append(
                dot(merge(low_query, query_aug, query_pair), merge(low_key, key_aug, key_pair), NT)
            )
        tops = [jnp.max(score, -1, keepdims=True) for score in scores]
        raised = [jnp.exp2(score - top).astype(BF) for score, top in zip(scores, tops)]
        for pair in range(pairs):
            here = slice(pair * 128, pair * 128 + 128)
            value_pair = value[keys, here]
            even = dot(raised[2 * pair], merge(low_key, value_pair, ones), NN)
            odd = dot(raised[2 * pair + 1], merge(low_key, ones, value_pair), NN)
            total = merge(low_query, odd, even)
            context[rows, here] = (
                merge(low_query, even, odd) / pltpu.roll(total, 64, 1)
            ).astype(BF)
            level = -(merge(low_query, tops[2 * pair + 1], tops[2 * pair]) + jnp.log2(total))
            first = level.astype(BF)
            rest = level - first.astype(F32)
            second, third = split(rest)
            marks[rows, here] = merge(
                mark_lane == 4, first, merge(mark_lane == 5, second, merge(mark_lane == 6, third, query_aug))
            )

    def one(number, carry):
        base = (row * (count // size) + number) * 2
        for_windows(windows[base], windows[base + 1], count, (768,), functools.partial(block, number))
        return carry

    lax.fori_loop(0, count // size, one, 0)


def for_windows(start, steps, count, extents, run):
    extents = [extent for extent in extents if extent < count] + [count]
    for position, extent in enumerate(extents):
        take = steps * WINDOW <= extent
        if position:
            take = take & (steps * WINDOW > extents[position - 1])

        @pl.when(take)
        def _():
            run(jnp.minimum(start * WINDOW, count - extent), extent)


def gelu_parts(values):
    square = values * values
    half = 0.5 + 0.5 * jnp.tanh(values * (GELU + (GELU * CUBIC) * square))
    active = values * half
    slope = half + active * (1.0 - half) * (2.0 * GELU + (6.0 * GELU * CUBIC) * square)
    return active, slope


def hidden_kernel(
    side, edge, wide, up, head_bias, context, weight_out, gains, biases, weight_in, hidden_bias,
    weight_last, output_gain, down, down_bias,
    mid, n2, active_out, slope_out, result, latent_out,
):
    encoder = side[0] == 0
    width = edge.shape[1]
    values = entry_values(encoder, edge[...], wide[...], up[...], head_bias[...])
    midway = values + (dot(context[...], weight_out[...], NN) + biases[2])
    mid[...] = midway
    hat, unused = norm_parts(midway)
    normed = (hat * gains[1:2, :] + biases[4]).astype(BF)
    n2[...] = normed
    total = midway + biases[5]
    chunk = 256
    for start in range(0, weight_in.shape[1], chunk):
        here = slice(start, start + chunk)
        active, slope = gelu_parts(dot(normed, weight_in[:, here], NN) + hidden_bias[0:1, here])
        active = active.astype(BF)
        active_out[:, here] = active
        slope_out[:, here] = slope.astype(BF)
        total = total + dot(active, weight_last[here, :], NN)
    result[...] = total

    @pl.when(encoder)
    def _():
        last_hat, unused = norm_parts(total)
        code = last_hat * output_gain[0:1, :] + head_bias[0:1, :]
        latent_out[...] = code_product(code, down[...]) + down_bias[0:1, :]


def code_product(values, weight):
    return dot3(split(values), split(weight), NT)


def tail_back_kernel(
    side, result, cotangent, unit, latent_in, latent, output_gain, head_bias, down,
    weight_last, slope, weight_in, mid, gains, biases, weight_out, *refs, adding
):
    before, refs = refs[: 2 * adding], refs[2 * adding :]
    out_low, preact_low, mid_grad, branch_low, context_grad, sums, head_weight, upstream = refs
    encoder = side[0] == 0
    width = result.shape[1]
    narrow = unit.shape[1]

    @pl.when(pl.program_id(0) == 0)
    def _():
        sums[...] = before[0][...] if adding else jnp.zeros_like(sums)
        head_weight[...] = before[1][...] if adding else jnp.zeros_like(head_weight)

    @pl.when(encoder)
    def _():
        hat, inverse = norm_parts(result[...])
        normed = hat * output_gain[0:1, :] + head_bias[0:1, :]
        code, scale = unit_of(latent[...])
        code_grad = latent_in[...].T + 0.5 * (code - unit[...])
        latent_grad = scale * (code_grad - code * jnp.sum(code * code_grad, -1, keepdims=True))
        pieces = split(latent_grad)
        low_down = down[...].astype(BF)
        normed_grad = dot(pieces[0], low_down, NN) + dot(pieces[1], low_down, NN)
        head_weight[...] += dot(pieces[0], normed.astype(BF), TN) + dot(pieces[1], normed.astype(BF), TN)
        sums[8:9, :] += column_sum(normed_grad * hat)
        sums[9:10, :] += column_sum(normed_grad)
        sums[10:11, :narrow] += column_sum(latent_grad)
        upstream[...] = norm_back(normed_grad, output_gain[0:1, :], hat, inverse)

    @pl.when(jnp.logical_not(encoder))
    def _():
        upstream[...] = cotangent[...].astype(F32)

    above = upstream[...]
    low = above.astype(BF)
    out_low[...] = low
    sums[4:5, :] += column_sum(low.astype(F32))
    normed_grad = None
    chunk = 1024
    for start in range(0, weight_in.shape[1], chunk):
        here = slice(start, start + chunk)
        active_grad = dot(low, weight_last[here, :], NT)
        inner = (active_grad * slope[:, here].astype(F32)).astype(BF)
        preact_low[:, here] = inner
        part = column_sum(inner.astype(F32))
        for at in range(0, chunk, min(chunk, width)):
            row, lane = (start + at) // width, (start + at) % width
            size = min(chunk, width)
            sums[row : row + 1, lane : lane + size] += part[:, at : at + size]
        term = dot(inner, weight_in[:, here], NT)
        normed_grad = term if normed_grad is None else normed_grad + term
    hat, inverse = norm_parts(mid[...])
    sums[6:7, :] += column_sum(normed_grad * hat)
    sums[7:8, :] += column_sum(normed_grad)
    middle = above + norm_back(normed_grad, gains[1:2, :], hat, inverse)
    mid_grad[...] = middle
    branch = middle.astype(BF)
    branch_low[...] = branch
    sums[5:6, :] += column_sum(branch.astype(F32))
    context_grad[...] = dot(branch, weight_out[...], NT).astype(BF)


def mark_grads(context_grad, context, grad_mark):
    count = context_grad.shape[0]
    lane_all = lanes((count, 128)) & 63
    across = (
        lax.broadcasted_iota(jnp.int32, (128, 128), 0) // 64 != lanes((128, 128)) // 64
    ).astype(BF)
    zero = jnp.zeros((count, 128), BF)
    for pair in range(context_grad.shape[1] // 128):
        here = slice(pair * 128, pair * 128 + 128)
        product = split(context_grad[:, here].astype(F32) * context[:, here].astype(F32))
        level = -(dot(product[0], across, NN) + dot(product[1], across, NN))
        first = level.astype(BF)
        second, third = split(level - first.astype(F32))
        grad_mark[:, here] = merge(
            lane_all == 0, first, merge(lane_all == 1, second, merge(lane_all == 2, third, zero))
        )


def attend_back_block(
    number, start, extent, base, pairs,
    query, marks, key, value, context_grad, key_mark, grad_mark, query_grad, key_total, value_total,
):
    size = TOKENS
    low_query = lanes((size, 128)) < 64
    rows = pl.ds(pl.multiple_of(number * size, size), size)
    keys = pl.ds(pl.multiple_of(start, WINDOW), extent)
    low_key = lanes((extent, 128)) < 64
    key_aug = key_mark[keys, :]
    ones = jnp.where((lanes((extent, 128)) & 63) < 3, 1.0, 0.0).astype(BF)
    none = jnp.zeros((extent, 128), BF)
    for pair in range(pairs):
        here = pl.ds(pl.multiple_of(base + pair * 128, 128), 128)
        query_pair, key_pair, value_pair = query[rows, here], key[keys, here], value[keys, here]
        grad_pair, query_aug, grad_aug = context_grad[rows, here], marks[rows, here], grad_mark[rows, here]
        found = []
        for swap in (False, True):

            def both(low, left, right):
                return merge(low, right, left) if swap else merge(low, left, right)

            scores = dot(both(low_key, key_pair, key_aug), both(low_query, query_pair, query_aug), NT)
            rise = dot(both(low_key, value_pair, ones), both(low_query, grad_pair, grad_aug), NT)
            chance = jnp.exp2(scores)
            score_grad = (chance * rise).astype(BF)
            found.append(
                (
                    dot(score_grad, query_pair, NN),
                    dot(chance.astype(BF), grad_pair, NN),
                    dot(score_grad, both(low_key, key_pair, none), TN),
                )
            )
        key_total[keys, here] += merge(low_key, found[0][0], found[1][0])
        value_total[keys, here] += merge(low_key, found[0][1], found[1][1])
        query_grad[rows, here] = ((found[0][2] + found[1][2]) * HEAD ** (-0.5)).astype(BF)


def attend_back_kernel(
    windows, query, marks, key, value, context_grad, context, key_mark,
    query_grad, key_grad, value_grad, grad_mark, key_total, value_total, *, row
):
    count = query.shape[0]
    steps = count // TOKENS
    pairs = query.shape[1] // 128
    mark_grads(context_grad, context, grad_mark)
    key_total[...] = jnp.zeros_like(key_total)
    value_total[...] = jnp.zeros_like(value_total)

    def one(turn, carry):
        number = turn
        at = (row * steps + number) * 2

        def run(start, extent):
            attend_back_block(
                number, start, extent, 0, pairs,
                query, marks, key, value, context_grad, key_mark, grad_mark, query_grad, key_total, value_total,
            )

        for_windows(windows[at], windows[at + 1], count, (640, 768), run)
        return carry

    lax.fori_loop(0, steps, one, 0)
    key_grad[...] = (key_total[...] * (1.0 / LOG2E)).astype(BF)
    value_grad[...] = value_total[...].astype(BF)


def entry_back_kernel(
    side, edge, wide, up, head_bias, unit, query_grad, key_grad, value_grad, weight, gains, biases,
    mid_grad, *refs, adding
):
    before, refs = refs[: 2 * adding], refs[2 * adding :]
    entry, latent_out, sums, head_weight = refs
    encoder = side[0] == 0
    width = edge.shape[1]
    narrow = unit.shape[1]

    @pl.when(pl.program_id(0) == 0)
    def _():
        sums[...] = before[0][...] if adding else jnp.zeros_like(sums)
        head_weight[...] = before[1][...] if adding else jnp.zeros_like(head_weight)

    values = entry_values(encoder, edge[...], wide[...], up[...], head_bias[...])
    normed_grad = (
        dot(query_grad[...], weight[:, :width], NT)
        + dot(key_grad[...], weight[:, width : 2 * width], NT)
        + dot(value_grad[...], weight[:, 2 * width :], NT)
    )
    hat, inverse = norm_parts(values)
    sums[0:1, :] += column_sum(query_grad[...].astype(F32))
    sums[1:2, :] += column_sum(value_grad[...].astype(F32))
    sums[2:3, :] += column_sum(normed_grad * hat)
    sums[3:4, :] += column_sum(normed_grad)
    total = mid_grad[...] + norm_back(normed_grad, gains[0:1, :], hat, inverse)
    entry[...] = total

    @pl.when(jnp.logical_not(encoder))
    def _():
        sums[4:5, :] += column_sum(total)
        latent_out[...] = code_product(total, up[...]).T
        codes, low_total = split(unit[...]), total.astype(BF)
        head_weight[...] += dot(codes[0], low_total, TN) + dot(codes[1], low_total, TN)


def hidden_weight_kernel(active, out_low, n2, preact_low, *refs):
    out = refs[-1]
    before = refs[0] if len(refs) > 1 else None
    step = pl.program_id(0)
    first = pl.num_programs(0) // 2
    width = n2.shape[1]

    def put(value, rows):
        out[rows, :] = value if before is None else value + before[rows, :]

    @pl.when(step < first)
    def _():
        put(dot(active[...], out_low[...], TN), slice(0, 2 * width))

    @pl.when(step >= first)
    def _():
        value = dot(n2[...], preact_low[...], TN)
        put(value[:, :width], slice(0, width))
        put(value[:, width:], slice(width, 2 * width))


def weight_call(kernel, operands, in_specs, steps, before):
    width = operands[1].shape[1]
    out_spec = pl.BlockSpec((2 * width, width), lambda step: (step, 0))
    aliases = {}
    if before is not None:
        aliases = {len(operands): 0}
        operands, in_specs = operands + [before], in_specs + [out_spec]
    return pl.pallas_call(
        kernel,
        grid=(steps,),
        in_specs=in_specs,
        out_specs=out_spec,
        out_shape=jax.ShapeDtypeStruct((2 * steps * width, width), F32),
        input_output_aliases=aliases,
        compiler_params=PARAMS,
    )(*operands)


def hidden_weights(kept, late, before=None):
    operands = [kept.active, late.out_low, kept.n2, late.preact_low]
    count, width = kept.n2.shape
    first = kept.active.shape[1] // (2 * width)
    full = pl.BlockSpec((count, width), lambda step: (0, 0))
    in_specs = [
        pl.BlockSpec((count, 2 * width), lambda step: (0, jnp.minimum(step, first - 1))),
        full,
        full,
        pl.BlockSpec((count, 2 * width), lambda step: (0, jnp.maximum(step - first, 0))),
    ]
    return weight_call(hidden_weight_kernel, operands, in_specs, 2 * first, before)


MESH = pl.DeviceIdType.MESH
LEAST_DEVICES = 4


def ring_chip(position, chips):
    odd = position // (chips // 2)
    return (1 - odd) * (2 * position) + odd * (2 * (chips - 1 - position) + 1)


class Ring:
    @staticmethod
    def scratch(arrays, ways, crossing):
        chips = lax.axis_size(DP) // 2
        sizes = [array.shape[0] // (2 * count * chips) for array, count in zip(arrays, ways)]
        shapes = [(count, chips, size, array.shape[1]) for array, count, size in zip(arrays, ways, sizes)]
        buffers = [pltpu.VMEM(shape, F32) for shape in shapes] * 3
        sems = [pltpu.SemaphoreType.DMA(shape[:2]) for shape in shapes] * 10
        far = []
        if crossing is not None:
            count, unused, size, width = shapes[crossing]
            far = [pltpu.VMEM((count, size, width), F32)] + [pltpu.SemaphoreType.DMA((count,))] * 2
        return buffers + sems + far

    def __init__(self, sources, results, ways, crossing, scratch):
        number = len(sources)
        take = lambda at: scratch[at * number : (at + 1) * number]
        self.chips = lax.axis_size(DP) // 2
        self.sources, self.results, self.ways, self.crossing = sources, results, ways, crossing
        self.own, self.pair, self.run = take(0), take(1), take(2)
        (
            self.load_sems, self.pair_send, self.pair_recv, self.run_send, self.run_recv,
            self.keep_sems, self.spread_send, self.spread_recv, self.side_send, self.side_recv,
        ) = (take(at) for at in range(3, 13))
        self.far = scratch[13 * number :]
        self.sizes = [run.shape[2] for run in self.run]
        self.lanes = [(which, way) for way in range(max(ways)) for which in range(number) if way < ways[which]]
        place = lax.axis_index(DP)
        chip, self.core = place // 2, place % 2
        column, odd = chip // 2, chip % 2
        chips = self.chips
        self.position = (1 - odd) * column + odd * (chips - 1 - column)
        self.other = {DP: chip * 2 + (1 - self.core)}
        self.across = {SECTION: 1 - lax.axis_index(SECTION)}
        self.targets = (
            {DP: ring_chip((self.position + 1) % chips, chips) * 2 + self.core},
            {DP: ring_chip((self.position + chips - 1) % chips, chips) * 2 + self.core},
        )

    def greet(self):
        self.barrier = pltpu.get_barrier_semaphore()
        devices = (self.other, self.across) + self.targets
        for device in devices:
            pl.semaphore_signal(self.barrier, inc=1, device_id=device, device_id_type=MESH)
        self.greeted = len(devices)

    def piece(self, step, way):
        return (self.position + (2 * self.chips - step if way % 2 == 0 else step)) % self.chips

    def rows(self, which, half, way, number):
        size = self.sizes[which]
        return pl.ds(pl.multiple_of(((half * self.ways[which] + way) * self.chips + number) * size, 8), size)

    def final(self, which, half, way, step):
        return self.results[which].at[self.rows(which, half, way, self.piece(step + self.chips - 1, way))]

    def load(self, which, way, step):
        return pltpu.make_async_copy(
            self.sources[which].at[self.rows(which, self.core, way, self.piece(step, way))],
            self.own[which].at[way, step],
            self.load_sems[which].at[way, step],
        )

    def remote(self, source, target, send, recv, device):
        return pltpu.make_async_remote_copy(
            src_ref=source, dst_ref=target, send_sem=send, recv_sem=recv, device_id=device, device_id_type=MESH
        )

    def swap(self, which, way, step):
        return self.remote(
            self.sources[which].at[self.rows(which, 1 - self.core, way, self.piece(step, way))],
            self.pair[which].at[way, step],
            self.pair_send[which].at[way, step],
            self.pair_recv[which].at[way, step],
            self.other,
        )

    def pass_on(self, which, way, step):
        return self.remote(
            self.run[which].at[way, step],
            self.run[which].at[way, step + 1],
            self.run_send[which].at[way, step],
            self.run_recv[which].at[way, step + 1],
            self.targets[way % 2],
        )

    def cross(self, way):
        return self.remote(
            self.run[self.crossing].at[way, self.chips - 1],
            self.far[0].at[way],
            self.far[1].at[way],
            self.far[2].at[way],
            self.across,
        )

    def keep(self, which, way):
        return pltpu.make_async_copy(
            self.run[which].at[way, self.chips - 1], self.final(which, self.core, way, 0), self.keep_sems[which].at[way, 0]
        )

    def spread(self, which, way, step, first=False):
        here = self.final(which, self.core, way, step)
        return self.remote(
            self.run[which].at[way, self.chips - 1] if first else here,
            here,
            self.spread_send[which].at[way, step],
            self.spread_recv[which].at[way, step],
            self.targets[way % 2],
        )

    def incoming(self, which, way, step):
        here = self.final(which, self.core, way, step)
        return self.remote(
            here, here, self.spread_send[which].at[way, step], self.spread_recv[which].at[way, step - 1],
            self.targets[way % 2],
        )

    def aside(self, which, way, step, first=False):
        here = self.final(which, self.core, way, step)
        return self.remote(
            self.run[which].at[way, self.chips - 1] if first else here,
            here,
            self.side_send[which].at[way, step],
            self.side_recv[which].at[way, step],
            self.other,
        )

    def beside(self, which, way, step):
        here = self.final(which, 1 - self.core, way, step)
        return self.remote(
            here, here, self.side_send[which].at[way, step], self.side_recv[which].at[way, step], self.other
        )

    def begin(self, waiting=True):
        def load(step, carry):
            for which, way in self.lanes:
                self.load(which, way, step).start()
            return carry

        def swap(step, carry):
            for which, way in self.lanes:
                self.swap(which, way, step).start()
            return carry

        lax.fori_loop(0, self.chips, load, 0)
        if waiting:
            pl.semaphore_wait(self.barrier, self.greeted)
        lax.fori_loop(0, self.chips, swap, 0)
        for which, way in self.lanes:
            self.load(which, way, 0).wait()
            self.swap(which, way, 0).wait_recv()
            self.run[which][way, 0] = self.own[which][way, 0] + self.pair[which][way, 0]
            self.pass_on(which, way, 0).start()

    def gather(self, step, lanes=None):
        for which, way in self.lanes if lanes is None else lanes:
            run, own, pair = self.run[which], self.own[which], self.pair[which]
            self.load(which, way, step).wait()
            self.swap(which, way, step).wait_recv()
            self.pass_on(which, way, step - 1).wait_recv()
            run[way, step] = run[way, step] + own[way, step] + pair[way, step]

            @pl.when(step < self.chips - 1)
            def _():
                self.pass_on(which, way, step).start()

    def turn(self):
        for which, way in self.lanes:
            if which == self.crossing:
                self.cross(way).start()
        for which, way in self.lanes:
            if which != self.crossing:
                self.hand_out(which, way)
        for which, way in self.lanes:
            if which == self.crossing:
                run = self.run[which]
                self.cross(way).wait()
                run[way, self.chips - 1] = run[way, self.chips - 1] + self.far[0][way]
                self.hand_out(which, way)

    def hand_out(self, which, way):
        self.spread(which, way, 0, True).start()
        self.aside(which, way, 0, True).start()
        self.keep(which, way).start()

    def pass_out(self, step, lanes=None):
        for which, way in self.lanes if lanes is None else lanes:
            self.incoming(which, way, step).wait_recv()

            @pl.when(step < self.chips - 1)
            def _():
                self.spread(which, way, step).start()

            self.aside(which, way, step).start()

    def finish(self):
        def one(step, carry):
            for which, way in self.lanes:
                self.swap(which, way, step).wait_send()
                self.beside(which, way, step).wait_recv()
                self.aside(which, way, step).wait_send()

                @pl.when(step < self.chips - 1)
                def _():
                    self.pass_on(which, way, step).wait_send()
                    self.spread(which, way, step).wait_send()

            return carry

        lax.fori_loop(0, self.chips, one, 0)
        for which, way in self.lanes:
            self.keep(which, way).wait()


def loop(start, stop, run):
    def one(step, carry):
        run(step)
        return carry

    if start < stop:
        lax.fori_loop(start, stop, one, 0)


HIDDEN_WAYS = (4,)
OTHER_WAYS = (4, 2)


def finish_kernel(*refs, held):
    (
        hidden, query, marks, key, value, context_grad, context, key_mark, edges, mid_grad, weight, branch_low, n1,
    ), refs = refs[:13], refs[13:]
    mine, others, refs = refs[:6], refs[6:18], refs[18:]
    (
        gains, book, down, up, late, early,
        hidden_out, attention_out, misc_out, entry,
        query_in, marks_in, key_in, value_in, grad_in, context_in, key_mark_in, edge_in, mid_in, weight_in, branch_in,
        n1_in, part, misc, grad_mark, query_grad, key_total, value_total, key_grad, value_grad, in_sems, out_sems,
    ), scratch = refs[:32], refs[32:]
    encoder = lax.axis_index(SECTION) == 0
    decoder = jnp.logical_not(encoder)
    ring = Ring((hidden,), (hidden_out,), HIDDEN_WAYS, None, scratch[:held]) if scratch else None
    last = Ring((part, misc), (attention_out, misc_out), OTHER_WAYS, 1, scratch[held:]) if scratch else None
    count, width = query.shape
    narrow = down.shape[0]
    steps = count // TOKENS
    pairs = width // 128
    row = edges.shape[0] - 1
    at = book.shape[0] + 2 * narrow
    inputs = (
        (query, query_in), (marks, marks_in), (key, key_in), (value, value_in), (context_grad, grad_in),
        (context, context_in), (key_mark.at[row], key_mark_in), (edges.at[row], edge_in), (mid_grad, mid_in),
        (weight, weight_in), (branch_low, branch_in), (n1, n1_in),
    )
    first_held = (query_in, marks_in, key_in, value_in, grad_in, grad_mark)
    second_held = (context_in, branch_in, n1_in, query_grad, key_grad, value_grad)

    def copies(pairs):
        return [pltpu.make_async_copy(*pair, in_sems.at[number]) for number, pair in enumerate(pairs)]

    loads = copies(inputs)
    other_loads = copies(zip(others, first_held + second_held))
    first_loads = copies(zip(mine, first_held))

    def start(copies):
        for copy in copies:
            copy.start()

    def wait(copies):
        for copy in copies:
            copy.wait()

    if ring:
        ring.greet()
    pl.when(encoder)(functools.partial(start, loads))
    pl.when(decoder)(functools.partial(start, other_loads))
    if ring:
        ring.begin()
    misc[...] = jnp.zeros_like(misc)

    def attention_piece(turn):
        attend_back_block(
            turn // pairs, 0, count, (turn % pairs) * 128, 1,
            query_in, marks_in, key_in, value_in, grad_in, key_mark_in, grad_mark, query_grad, key_total, value_total,
        )

    @pl.when(encoder)
    def _():
        misc[: book.shape[0], :] = book[...]
        misc[book.shape[0] : book.shape[0] + narrow, :] = down[...]
        misc[at : at + 16, :] = late[...]
        misc[at + 16 : at + 32, :] = early[...]
        wait(loads)
        mark_grads(grad_in, context_in, grad_mark)
        key_total[...] = jnp.zeros_like(key_total)
        value_total[...] = jnp.zeros_like(value_total)
        loop(0, 2, attention_piece)

    @pl.when(decoder)
    def _():
        misc[book.shape[0] + narrow : at, :] = up[...]
        misc[at + 32 : at + 48, :] = late[...]
        misc[at + 48 : at + 64, :] = early[...]
        wait(other_loads)

    def entry_piece(number):
        rows = pl.ds(pl.multiple_of(number * TOKENS, TOKENS), TOKENS)
        normed_grad = (
            dot(query_grad[rows, :], weight_in[:, :width], NT)
            + dot(key_grad[rows, :], weight_in[:, width : 2 * width], NT)
            + dot(value_grad[rows, :], weight_in[:, 2 * width :], NT)
        )
        hat, inverse = norm_parts(edge_in[rows, :].astype(F32))
        misc[at + 16 : at + 17, :] += column_sum(query_grad[rows, :].astype(F32))
        misc[at + 17 : at + 18, :] += column_sum(value_grad[rows, :].astype(F32))
        misc[at + 18 : at + 19, :] += column_sum(normed_grad * hat)
        misc[at + 19 : at + 20, :] += column_sum(normed_grad)
        mid_in[rows, :] = mid_in[rows, :] + norm_back(normed_grad, gains[0:1, :], hat, inverse)

    def weight_piece(number):
        def put(first, second):
            rows = pl.ds(pl.multiple_of(number * width, width), width)
            part[rows, :] = dot(first[0][...], first[1][...], TN) + dot(second[0][...], second[1][...], TN)

        for choice, places in enumerate(((0, 1), (2, 3), (2, 4), (2, 5))):
            both = [[held[place] for place in places] for held in (first_held, second_held)]
            pl.when(number == choice)(functools.partial(put, *both))

    halves = (ring.lanes[:2], ring.lanes[2:]) if ring else (None, None)
    chips = ring.chips if ring else 8
    pieces = steps * pairs

    def summing(step):
        for half in range(2):
            if ring:
                ring.gather(step, halves[half])

            @pl.when(encoder)
            def _():
                attention_piece(2 * step + half)

    inside = min(chips - 1, pieces // 2 - 1)
    loop(1, inside + 1, summing)
    if ring:
        loop(inside + 1, chips, ring.gather)
        ring.turn()

    @pl.when(encoder)
    def _():
        loop(2 * inside + 2, pieces, attention_piece)
        start(first_loads)
        key_grad[...] = (key_total[...] * (1.0 / LOG2E)).astype(BF)
        value_grad[...] = value_total[...].astype(BF)

    def spreading(step):
        if ring:
            ring.pass_out(step, halves[0])

        @pl.when(encoder)
        def _():
            entry_piece(step - 1)

        if ring:
            ring.pass_out(step, halves[1])
        pl.when(encoder & (step == 1))(functools.partial(wait, first_loads))
        weight_piece(step - 1)

    loop(1, steps + 1, spreading)
    store = pltpu.make_async_copy(mid_in, entry, out_sems.at[0])

    @pl.when(encoder)
    def _():
        store.start()

    if ring:
        last.begin(False)

        def both(step):
            ring.pass_out(step)
            last.gather(step - steps)

        loop(steps + 1, chips, both)
        loop(chips - steps, chips, last.gather)
        last.turn()
        loop(1, chips, last.pass_out)
        ring.finish()
        last.finish()
    else:
        stores = [
            pltpu.make_async_copy(part, attention_out, out_sems.at[1]),
            pltpu.make_async_copy(misc, misc_out, out_sems.at[2]),
        ]
        start(stores)
        wait(stores)

    @pl.when(encoder)
    def _():
        store.wait()


def finish_row(work, first_kept, kept, late, mine, book, others, hidden):
    count, width = kept.n1.shape
    alone = lax.axis_size(DP) < LEAST_DEVICES
    its_late, its_early = mine
    operands = [
        hidden, kept.query, kept.marks, kept.key, kept.value, late.context_grad,
        kept.context, work.key_mark, work.edges, late.mid_grad, work.attention_in, late.branch_low, kept.n1,
    ]
    for a_kept, a_late, a_early in ((first_kept, its_late, its_early),) + others:
        operands += [a_kept.context, a_late.branch_low, a_kept.n1, *a_early[:3]]
    operands += [work.gains, book, late.head, its_early.head, late.sums, its_early.sums]
    hbm, vmem = pl.BlockSpec(memory_space=pl.ANY), pl.BlockSpec(memory_space=pltpu.VMEM)
    rows = book.shape[0] + 2 * work.narrow + 64
    unit = 16 * lax.axis_size(DP)
    attention = jax.ShapeDtypeStruct((4 * width, width), F32)
    misc = jax.ShapeDtypeStruct((rows + (-rows % unit), width), F32)
    low = pltpu.VMEM((count, width), BF)
    wide = pltpu.VMEM((count, width), F32)
    scratch = [low] * 6 + [pltpu.VMEM((count, 128), BF), low, wide, pltpu.VMEM(work.attention_in.shape, BF), low, low]
    scratch += [pltpu.VMEM(attention.shape, F32), pltpu.VMEM(misc.shape, F32), low, low, wide, wide, low, low]
    scratch += [pltpu.SemaphoreType.DMA((12,)), pltpu.SemaphoreType.DMA((3,))]
    settings = {}
    held = 0
    if not alone:
        rings = Ring.scratch((hidden,), HIDDEN_WAYS, None)
        held = len(rings)
        scratch += rings + Ring.scratch((attention, misc), OTHER_WAYS, 1)
        settings = dict(collective_id=0, has_side_effects=True)
    outs = pl.pallas_call(
        functools.partial(finish_kernel, held=held),
        in_specs=[hbm] * 31 + [vmem] * 6,
        out_specs=[hbm] * 4,
        out_shape=(
            jax.ShapeDtypeStruct(hidden.shape, F32), attention, misc, jax.ShapeDtypeStruct((count, width), F32),
        ),
        scratch_shapes=scratch,
        compiler_params=pltpu.CompilerParams(vmem_limit_bytes=60 << 20, **settings),
    )(*operands)
    if alone:
        return hidden, outs[1], lax.psum(outs[2], SECTION), outs[3]
    return outs


def unpack_kernel(
    side, hidden, attention, misc, first_entry, second_entry, first_result, second_result,
    hidden_out, hidden_in, attention_out, attention_in, edge, book, gains, biases, bias, last_gain, head_bias, down, down_last,
    up, held, head, rows, ins, outs, row_ins, row_outs,
):
    width = hidden.shape[1]
    narrow = book.shape[0]
    steps = hidden_out.shape[0] // width
    targets = [hidden_out.at[pl.ds(number * width, width), :] for number in range(steps)]
    targets += [hidden_in.at[:, pl.ds(number * width, width)] for number in range(steps)]
    targets += [attention_out]
    targets += [attention_in.at[:, pl.ds(number * width, width)] for number in range(3)]
    sources = [hidden.at[pl.ds(number * width, width), :] for number in range(2 * steps)]
    sources += [attention.at[pl.ds(number * width, width), :] for number in range(4)]
    tiles = range(len(targets))
    for mine, pair in ((0, (first_entry, second_entry)), (1, (first_result, second_result))):

        @pl.when(side[0] == mine)
        def _():
            for row in range(2):
                pltpu.make_async_copy(pair[row], rows.at[row], row_ins.at[row]).start()

    loads = [pltpu.make_async_copy(sources[number], held.at[number], ins.at[number]) for number in tiles]
    loads.append(pltpu.make_async_copy(misc.at[pl.ds(0, head.shape[0]), :], head, ins.at[len(targets)]))
    for load in loads:
        load.start()
    stores = []
    for row in range(2):
        pltpu.make_async_copy(first_entry, rows.at[row], row_ins.at[row]).wait()
        stores.append(pltpu.make_async_copy(rows.at[row], edge.at[row], row_outs.at[row]))
        stores[-1].start()
    for number in tiles:
        loads[number].wait()
        stores.append(pltpu.make_async_copy(held.at[number], targets[number], outs.at[number]))
        stores[-1].start()
    loads[-1].wait()
    for number in range(book.shape[1] // width):
        book[:, number * width : (number + 1) * width] = head[number * narrow : (number + 1) * narrow, :]
    at = book.shape[0] * book.shape[1] // width
    down[...] = head[at : at + narrow, :]
    up[...] = head[at + narrow : at + 2 * narrow, :]
    at += 2 * narrow
    last_gain[...] = head[at + 8 : at + 9, :]
    head_bias[0:1, :] = head[at + 9 : at + 10, :]
    head_bias[1:2, :] = head[at + 52 : at + 53, :]
    down_last[...] = head[at + 10 : at + 11, :narrow]
    mine = jnp.where(side[0] == 0, head[at : at + 32, :], head[at + 32 : at + 64, :])
    for number in range(steps):
        bias[:, number * width : (number + 1) * width] = mine[number : number + 1, :]
    for number, place in enumerate((18, 6)):
        gains[number : number + 1, :] = mine[place : place + 1, :]
    for number, place in enumerate((16, 17, 5, 19, 7, 4)):
        biases[number] = mine[place : place + 1, :]
    for store in stores:
        store.wait()


def unpack(side, hidden, attention, misc, ends, table_turned):
    width = hidden.shape[1]
    features = hidden.shape[0] // 2
    tiles = (hidden.shape[0] + attention.shape[0]) // width
    narrow = table_turned.shape[0]
    rows = table_turned.size // width + 2 * narrow + 64
    shapes = (
        (features, width), (width, features), (width, width), (width, 3 * width), (2,) + ends[0].shape,
        table_turned.shape, (2, width), (6, 1, width), (1, features), (1, width), (2, width),
        (narrow, width), (1, narrow), (narrow, width),
    )
    hbm, vmem = pl.BlockSpec(memory_space=pl.ANY), pl.BlockSpec(memory_space=pltpu.VMEM)
    return pl.pallas_call(
        unpack_kernel,
        in_specs=[pl.BlockSpec(memory_space=pltpu.SMEM)] + [hbm] * 7,
        out_specs=[hbm] * 5 + [vmem] * 9,
        out_shape=tuple(jax.ShapeDtypeStruct(shape, F32) for shape in shapes),
        scratch_shapes=[
            pltpu.VMEM((tiles, width, width), F32),
            pltpu.VMEM((rows, width), F32),
            pltpu.VMEM((2,) + ends[0].shape, F32),
            pltpu.SemaphoreType.DMA((tiles + 1,)),
            pltpu.SemaphoreType.DMA((tiles,)),
            pltpu.SemaphoreType.DMA((2,)),
            pltpu.SemaphoreType.DMA((2,)),
        ],
        compiler_params=PARAMS,
    )(side, hidden, attention, misc, *ends)


def nothing_kernel(*refs):
    pass


def unwritten(shapes):
    leaves, tree = jax.tree.flatten(shapes)
    arrays = pl.pallas_call(
        nothing_kernel,
        out_specs=[pl.BlockSpec(memory_space=pl.ANY)] * len(leaves),
        out_shape=tuple(leaves),
    )()
    return jax.tree.unflatten(tree, arrays)


class Kept(NamedTuple):
    n1: Any
    query: Any
    key: Any
    value: Any
    context: Any
    marks: Any
    mid: Any
    n2: Any
    active: Any
    slope: Any
    result: Any
    latent: Any


class Late(NamedTuple):
    out_low: Any
    preact_low: Any
    mid_grad: Any
    branch_low: Any
    context_grad: Any
    sums: Any
    head: Any


class Early(NamedTuple):
    query_grad: Any
    key_grad: Any
    value_grad: Any
    entry: Any
    latent_out: Any
    sums: Any
    head: Any


class Rows:
    def __init__(self, side, edges, wide, unit, windows, query_mark, key_mark, weights, head):
        self.side, self.edges, self.wide, self.unit = side, edges, wide, unit
        self.windows, self.query_mark, self.key_mark = windows, query_mark, key_mark
        (
            self.attention_in, self.attention_out, self.hidden_in, self.hidden_out,
            self.gains, self.biases, self.hidden_bias,
        ) = weights
        (
            self.output_gain, self.head_bias, self.down, self.down_bias, self.up,
        ) = head
        self.rows, self.count, self.width = edges.shape
        self.hidden = self.hidden_in.shape[1]
        self.narrow = unit.shape[1]
        self.size = TOKENS
        n, d, f = self.count, self.width, self.hidden
        shape = jax.ShapeDtypeStruct
        low, tall, wide = shape((n, d), BF), shape((n, f), BF), shape((n, d), F32)
        sums, head = shape((16, d), F32), shape((self.narrow, d), F32)
        self.kept = Kept(low, low, low, low, low, low, wide, low, tall, tall, wide, shape((n, self.narrow), F32))
        self.late = Late(low, tall, wide, low, low, sums, head)
        self.early = Early(low, low, low, wide, shape((self.narrow, n), F32), sums, head)

    def side_spec(self):
        return pl.BlockSpec(memory_space=pltpu.SMEM)

    def tokens(self, array):
        return pl.BlockSpec((self.size, array.shape[1]), lambda step: (step, 0))

    def turned(self, array):
        return pl.BlockSpec((array.shape[0], self.size), lambda step: (0, step))

    def whole(self, array):
        return pl.BlockSpec(array.shape, lambda step: (0,) * len(array.shape))

    def entry_specs(self, row):
        steps = self.count // self.size
        return [
            pl.BlockSpec((None, self.size, self.width), lambda step: (row, step, 0)),
            pl.BlockSpec((self.size, self.wide.shape[1]), lambda step: (row * steps + step, 0)),
            self.whole(self.up),
            self.whole(self.head_bias),
        ]

    def unit_spec(self, row):
        steps = self.count // self.size
        return pl.BlockSpec((self.size, self.narrow), lambda step: (row * steps + step, 0))

    def call(self, kernel, in_specs, operands, outs, out_specs, scratch=()):
        return pl.pallas_call(
            kernel,
            grid=(self.count // self.size,),
            in_specs=in_specs,
            out_specs=out_specs,
            out_shape=tuple(outs),
            scratch_shapes=list(scratch),
            compiler_params=PARAMS,
        )(*operands)

    def attention_call(self, kernel, row, operands, outs, scratch=()):
        half = self.width // 2

        def spec(array):
            if array.ndim == 3:
                return pl.BlockSpec((None, self.count, array.shape[2]), lambda step, info: (row, 0, 0))
            return pl.BlockSpec((self.count, half), lambda step, info: (0, step))

        return pl.pallas_call(
            functools.partial(kernel, row=row),
            grid_spec=pltpu.PrefetchScalarGridSpec(
                num_scalar_prefetch=1,
                grid=(2,),
                in_specs=[spec(array) for array in operands],
                out_specs=[spec(array) for array in outs],
                scratch_shapes=list(scratch),
            ),
            out_shape=tuple(outs),
            compiler_params=PARAMS,
        )(self.windows, *operands)

    def forward(self, row):
        shapes = self.kept
        entry = (self.edges, self.wide, self.up, self.head_bias)
        outs = shapes[:4]
        self.size = 2 * TOKENS
        n1, query, key, value = self.call(
            project_kernel,
            [self.side_spec()] + self.entry_specs(row)
            + [self.whole(self.gains), self.whole(self.biases), self.whole(self.attention_in)],
            (self.side,) + entry + (self.gains, self.biases, self.attention_in),
            outs,
            [self.tokens(array) for array in outs],
        )
        self.size = TOKENS
        context, marks = self.attention_call(
            attend_kernel, row, (query, key, value, self.query_mark, self.key_mark), shapes[4:6]
        )
        consts = (
            self.attention_out, self.gains, self.biases, self.hidden_in, self.hidden_bias, self.hidden_out,
            self.output_gain, self.down, self.down_bias,
        )
        outs = shapes[6:]
        outs = self.call(
            hidden_kernel,
            [self.side_spec()] + self.entry_specs(row) + [self.tokens(context)]
            + [self.whole(array) for array in consts],
            (self.side,) + entry + (context,) + consts,
            outs,
            [self.tokens(array) for array in outs],
        )
        return Kept(n1, query, key, value, context, marks, *outs)

    def backward(self, row, kept, latent_in, former=(None, None)):
        late = self.backward_late(row, kept, latent_in, former[0])
        return late, self.backward_early(row, kept, late, former[1])

    def backward_late(self, row, kept, latent_in, former=None):
        prior = () if former is None else (former.sums, former.head)
        adding = int(former is not None)
        consts = (self.output_gain, self.head_bias, self.down, self.hidden_out)
        late = (self.gains, self.biases, self.attention_out)
        outs = self.late
        return Late(*self.call(
            functools.partial(tail_back_kernel, adding=adding),
            [self.side_spec(), self.tokens(kept.result), self.entry_specs(row)[0], self.unit_spec(row),
             self.turned(latent_in), self.tokens(kept.latent)]
            + [self.whole(array) for array in consts]
            + [self.tokens(kept.slope), self.whole(self.hidden_in), self.tokens(kept.mid)]
            + [self.whole(array) for array in late + prior],
            (self.side, kept.result, self.edges, self.unit, latent_in, kept.latent) + consts
            + (kept.slope, self.hidden_in, kept.mid) + late + prior,
            outs,
            [self.tokens(array) for array in outs[:5]] + [self.whole(array) for array in outs[5:]],
            scratch=[pltpu.VMEM((self.size, self.width), F32)],
        ))

    def backward_early(self, row, kept, late, former=None):
        adding = int(former is not None)
        half = self.width // 2
        grads = tuple(self.attention_call(
            attend_back_kernel, row,
            (kept.query, kept.marks, kept.key, kept.value, late.context_grad, kept.context, self.key_mark),
            self.early[:3],
            scratch=[
                pltpu.VMEM((self.count, half), BF),
                pltpu.VMEM((self.count, half), F32),
                pltpu.VMEM((self.count, half), F32),
            ],
        ))
        prior = () if former is None else (former.sums, former.head)
        outs = self.early[3:]
        outs = self.call(
            functools.partial(entry_back_kernel, adding=adding),
            [self.side_spec()] + self.entry_specs(row) + [self.unit_spec(row)]
            + [self.tokens(array) for array in grads]
            + [self.whole(self.attention_in), self.whole(self.gains), self.whole(self.biases),
               self.tokens(late.mid_grad)] + [self.whole(array) for array in prior],
            (self.side, self.edges, self.wide, self.up, self.head_bias, self.unit) + grads
            + (self.attention_in, self.gains, self.biases, late.mid_grad) + prior,
            outs,
            [self.tokens(outs[0]), self.turned(outs[1])] + [self.whole(array) for array in outs[2:]],
        )
        return Early(*grads, *outs)


def windows_of(segments):
    rows, count = segments.shape
    steps = count // WINDOW
    wide, blocks = (segments.reshape(rows, -1, size) for size in (TOKENS, WINDOW))
    meets = (wide[:, :, None, -1] >= blocks[:, None, :, 0]) & (wide[:, :, None, 0] <= blocks[:, None, :, -1])
    place = jnp.arange(steps)
    start = jnp.min(jnp.where(meets, place, steps), -1)
    stop = jnp.max(jnp.where(meets, place, -1), -1) + 1
    return jnp.stack([start, stop - start], -1).reshape(-1).astype(jnp.int32)


def on_device(
    boundary, segments, code_index, attention_in, attention_out, hidden_in, hidden_out, block_gains,
    block_biases, hidden_bias, output_gain, head_bias, down_weight, down_bias, up_weight, codebook,
):
    section = lax.axis_index(SECTION)
    encoder = section == 0
    side = section.astype(jnp.int32)[None]
    edges = boundary[0]
    rows, count, width = edges.shape
    hidden = hidden_in.shape[2]
    table_turned = codebook.T
    code_index = code_index.reshape(-1)
    unit, wide, query_mark, key_mark = gather_codes(code_index, table_turned, segments)
    work = Rows(
        side, edges, wide, unit, windows_of(segments), query_mark, key_mark,
        (
            attention_in[0], attention_out[0], hidden_in[0], hidden_out[0], block_gains[0], block_biases.transpose(1, 0, 2),
            hidden_bias,
        ),
        (output_gain[None], head_bias, down_weight.T, down_bias[None], up_weight),
    )
    book_out = book_shape(table_turned, width)
    hidden_shape = jax.ShapeDtypeStruct((2 * hidden, width), F32)
    quiet = unwritten(work.early.latent_out)
    first_kept = work.forward(0)

    def encoder_first():
        return (work.forward(1), *unwritten((work.late, work.early)))

    def decoder_first():
        return (unwritten(work.kept), *work.backward(0, first_kept, quiet))

    kept_a, late_a, early_a = lax.cond(encoder, encoder_first, decoder_first)
    latent_in = lax.ppermute(early_a.latent_out, SECTION, [(1, 0)])

    def encoder_second():
        late, early = work.backward(0, first_kept, latent_in)
        book = scatter_codes(code_index, unit, (first_kept.latent, kept_a.latent), table_turned, width)
        return unwritten(work.kept), late, early, hidden_weights(first_kept, late), book

    def decoder_second():
        kept = work.forward(1)
        weights, book = unwritten((hidden_shape, book_out))
        return (kept, *work.backward(1, kept, quiet, (late_a, early_a)), weights, book)

    kept_b, late_b, early_b, weights_b, book = lax.cond(encoder, encoder_second, decoder_second)
    latent_in_second = lax.ppermute(early_b.latent_out, SECTION, [(1, 0)])

    def decoder_fourth():
        total = hidden_weights(kept_b, late_b, hidden_weights(first_kept, late_a))
        return total, (*unwritten(work.late[2:5]), late_b.sums, late_b.head)

    def encoder_fourth():
        late = work.backward_late(1, kept_a, latent_in_second, late_b)
        return hidden_weights(kept_a, late, weights_b), late[2:]

    hidden_total, late = lax.cond(encoder, encoder_fourth, decoder_fourth)
    late = Late(None, None, *late)
    hidden_total, attention_total, misc, second_entry = finish_row(
        work, first_kept, kept_a, late, (late_b, early_b), book,
        ((first_kept, late_a, early_a), (kept_b, late_b, early_b)), hidden_total,
    )
    (
        hidden_out_grad, hidden_in_grad, attention_out_grad, attention_in_grad, edge, book, gains, biases, bias,
        last_gain, head, down_grad, down_last, up_grad,
    ) = unpack(
        side, hidden_total, attention_total, misc,
        (early_b.entry, second_entry, first_kept.result, kept_b.result), table_turned,
    )
    return (
        edge[None],
        attention_in_grad[None],
        attention_out_grad[None],
        hidden_in_grad[None],
        hidden_out_grad[None],
        gains[None],
        biases.transpose(1, 0, 2),
        bias,
        last_gain[0],
        head,
        down_grad.T,
        down_last[0],
        up_grad,
        book.T,
    )


def solution(mesh):
    wide, split_last, flat = P(SECTION, DP, None, None), P(SECTION, None, None), P(SECTION, None)
    blocks = (split_last,) * 6 + (flat,)
    return jax.shard_map(
        on_device,
        mesh=mesh,
        in_specs=(wide, P(DP, None), P(DP, None)) + blocks + (P(),) * 6,
        out_specs=(wide,) + blocks + (P(),) * 6,
        check_vma=False,
    )
```
